32 devices in a mesh: dp: 16 (over z, y, x), seq: 2 (over core).
Axes of the slice: x: 2, y: 2, z: 4, core: 2. Of those that a mesh axis runs over, the one named last changes fastest.
Arguments:
- tokens_in: bfloat16 [8192, 1536], P(('dp', 'seq')), may hold values from -6 to 6
- cotangent: bfloat16 [8192, 1536], P(('dp', 'seq')), may hold values from -6 to 6
- seq_lens: int32 [16, 4], P('dp'), may hold values from 0 to 512, as said below
- in_weight: float32 [1536, 6448], P(('dp', 'seq')), may hold values from -0.15625 to 0.15625
- in_first: float32 [1536, 6448], P(('dp', 'seq')), may hold values from -32 to 32
- in_second: float32 [1536, 6448], P(('dp', 'seq')), may hold values from 54.0672 to 860.16
- out_weight: float32 [3072, 1536], P(('dp', 'seq')), may hold values from -0.109375 to 0.109375
- out_first: float32 [3072, 1536], P(('dp', 'seq')), may hold values from -56 to 56
- out_second: float32 [3072, 1536], P(('dp', 'seq')), may hold values from 172.032 to 2785.28
- conv_weight: float32 [5, 3328], P(None, ('dp', 'seq')), may hold values from -3 to 3
- conv_first: float32 [5, 3328], P(None, ('dp', 'seq')), may hold values from -32 to 32
- conv_second: float32 [5, 3328], P(None, ('dp', 'seq')), may hold values from 77.824 to 1228.8
- gains: float32 [4608], P(('dp', 'seq')), may hold values from 0.25 to 1.75
- gain_first: float32 [4608], P(('dp', 'seq')), may hold values from -48 to 48
- gain_second: float32 [4608], P(('dp', 'seq')), may hold values from 139.264 to 2211.84
- head_params: float32 [3, 48], replicated, may hold values from -8 to 2.5, as said below
- head_first: float32 [3, 48], replicated, may hold values from -96.302287 to 96.302287, as said below
- head_second: float32 [3, 48], replicated, may hold values from 54.272 to 108926.075, as said below
Outputs:
- mixed_out: bfloat16 [8192, 1536], P(('dp', 'seq'))
- grad_input: float32 [8192, 1536], P(('dp', 'seq'))
- in_weight_new: float32 [1536, 6448], P(('dp', 'seq'))
- in_first_new: float32 [1536, 6448], P(('dp', 'seq'))
- in_second_new: float32 [1536, 6448], P(('dp', 'seq'))
- out_weight_new: float32 [3072, 1536], P(('dp', 'seq'))
- out_first_new: float32 [3072, 1536], P(('dp', 'seq'))
- out_second_new: float32 [3072, 1536], P(('dp', 'seq'))
- conv_weight_new: float32 [5, 3328], P(None, ('dp', 'seq'))
- conv_first_new: float32 [5, 3328], P(None, ('dp', 'seq'))
- conv_second_new: float32 [5, 3328], P(None, ('dp', 'seq'))
- gains_new: float32 [4608], P(('dp', 'seq'))
- gain_first_new: float32 [4608], P(('dp', 'seq'))
- gain_second_new: float32 [4608], P(('dp', 'seq'))
- head_params_new: float32 [3, 48], replicated
- head_first_new: float32 [3, 48], replicated
- head_second_new: float32 [3, 48], replicated
The draws below stay inside these ranges and needn't reach their ends.
Inputs may be any that keep to these rules, and one draw needn't show every extreme that they name: `seq_lens`: row g lists group g's sequences in order, 0 marking an unused slot. Each takes ceil(length / 256) whole blocks of 256 positions after the earlier ones, all within 512 positions; the first is longer than 256; in some group it fills all 512. `head_params`: row 0 shifts the step sizes, row 1 is the logarithm of the decay rates, row 2 holds positive skip gains. `head_first`: both signs. `head_second`: Positive.
All inputs are finite; a program needn't handle non-finite values.
Results may differ from the reference program's by a relative error of at most 0.012.
Values may be sent and summed in bfloat16 or wider, within the bound.
A program may use at most 256 MiB of HBM per device.

```python
import math
import jax
import jax.numpy as jnp
from jax import lax

D = 1536
HEADS = 48
HDIM = 64
NST = 128
KCONV = 4
BLOCK = 256
SLOTS = 4
STEP = 10
TOK_DEV = 256
DIN = 3072
CONVC = 3328
PROJ = 6448
GROUP_TOK = 512
GROUPS = 16
TOKENS = 8192


def draw_seq_lens(key, part):
    key = jax.random.fold_in(key, 11)
    keys = jax.random.split(key, 2 * SLOTS + 2)
    blocks_all = GROUP_TOK // BLOCK
    blocks_dev = TOK_DEV // BLOCK
    first_blocks = jax.random.randint(keys[0], (GROUPS,), blocks_all - blocks_dev + 1, blocks_all + 1)
    first_len = jax.random.randint(keys[1], (GROUPS,), (first_blocks - 1) * BLOCK + 1, first_blocks * BLOCK + 1)
    fullest = jax.random.randint(keys[2], (), 0, GROUPS)
    chosen = jnp.arange(GROUPS) == fullest
    first_len = jnp.where(chosen, GROUP_TOK, first_len)
    first_blocks = jnp.where(chosen, blocks_all, first_blocks)
    remaining = blocks_all - first_blocks
    columns = [first_len]
    for slot in range(1, SLOTS):
        taken = jax.random.randint(keys[2 * slot + 1], (GROUPS,), 0, remaining + 1)
        length = jax.random.randint(keys[2 * slot + 2], (GROUPS,), jnp.maximum(taken - 1, 0) * BLOCK + 1, jnp.maximum(taken, 1) * BLOCK + 1)
        columns.append(jnp.where(taken > 0, length, 0))
        remaining = remaining - taken
    return jnp.stack(columns, axis=1).astype(jnp.int32)


def draw_head_params(key, part):
    key = jax.random.fold_in(key, 23)
    keys = jax.random.split(key, 3)
    bias_row = jax.random.uniform(keys[0], (HEADS,), jnp.float32, -7.0, -3.0)
    decay_row = jax.random.uniform(keys[1], (HEADS,), jnp.float32, -1.0, 2.5)
    skip_row = jax.random.uniform(keys[2], (HEADS,), jnp.float32, 0.5, 1.5)
    return jnp.stack([bias_row, decay_row, skip_row], axis=0)


def head_scales():
    return jnp.array([2.0, 0.5, 0.7 * HDIM ** 0.5], jnp.float32) * TOKENS ** 0.5


def draw_head_first(key, part):
    key = jax.random.fold_in(key, 29)
    return 0.19 * head_scales()[:, None] * jax.random.uniform(key, (3, HEADS), jnp.float32, -1.0, 1.0)


def draw_head_second(key, part):
    key = jax.random.fold_in(key, 31)
    spread = jax.random.uniform(key, (3, HEADS), jnp.float32, jnp.log(0.5), jnp.log(8.0))
    scales = head_scales()
    return 0.053 * (scales * scales)[:, None] * jnp.exp(spread)


def steps_of(own_key, dims, pieces, low, high):
    level = 1.0
    for dim, blocks in pieces:
        steps = jax.random.uniform(jax.random.fold_in(jax.random.fold_in(own_key, 6), dim), (blocks,), jnp.float32, low / len(pieces), high / len(pieces))
        level = level * jnp.repeat(jnp.exp(steps), dims[dim] // blocks).reshape((-1,) + (1,) * (len(dims) - 1 - dim))
    return level


def bell_draw(own_key, shape, deviation, reach, shards=(), kind=jnp.bfloat16):
    drawn = jax.random.normal(own_key, shape, jnp.float32) * deviation
    if len(shards) > 0:
        drawn = steps_of(own_key, shape, shards, -0.22, 0.18) * drawn
    return jnp.clip(drawn, min=-reach, max=reach).astype(kind)


def setup_inputs(seed: int = 0) -> dict:
    splits = jax.random.split(jax.random.key(seed), 19)
    tokens_in = bell_draw(splits[0], (TOKENS, D), 1.0, 6.0, ((0, 32),))
    cotangent = bell_draw(splits[1], (TOKENS, D), 1.0, 6.0, ((0, 32),))
    seq_lens = draw_seq_lens(jax.random.fold_in(splits[18], 71), 0)
    in_weight = bell_draw(splits[3], (D, PROJ), D ** -0.5, 0.15625, ((0, 32),), jnp.float32)
    in_first = bell_draw(splits[4], (D, PROJ), (0.055 * TOKENS ** 0.5), 32.0, ((0, 32),), jnp.float32)
    in_second = jnp.clip(jnp.exp(math.log(860.16) - 2.7668907 * jax.random.uniform(splits[5], (D, PROJ), jnp.float32) ** steps_of(splits[5], (D, PROJ), ((0, 32),), -0.2, 0.2)), 54.0672, 860.16)
    out_weight = bell_draw(splits[6], (DIN, D), DIN ** -0.5, 0.109375, ((0, 32),), jnp.float32)
    out_first = bell_draw(splits[7], (DIN, D), (0.1 * TOKENS ** 0.5), 56.0, ((0, 32),), jnp.float32)
    out_second = jnp.clip(jnp.exp(math.log(2785.28) - 2.784423 * jax.random.uniform(splits[8], (DIN, D), jnp.float32) ** steps_of(splits[8], (DIN, D), ((0, 32),), -0.2, 0.2)), 172.032, 2785.28)
    conv_weight = bell_draw(splits[9], (KCONV + 1, CONVC), 0.5, 3.0, ((1, 32),), jnp.float32)
    conv_first = bell_draw(splits[10], (KCONV + 1, CONVC), (0.067 * TOKENS ** 0.5), 32.0, ((1, 32),), jnp.float32)
    conv_second = jnp.clip(jnp.exp(math.log(1228.8) - 2.7593436 * jax.random.uniform(splits[11], (KCONV + 1, CONVC), jnp.float32) ** steps_of(splits[11], (KCONV + 1, CONVC), ((1, 32),), -0.2, 0.2)), 77.824, 1228.8)
    gains = jnp.clip(1.0 + 0.15 * jax.random.normal(splits[12], (D + DIN,), jnp.float32), 0.25, 1.75)
    gain_first = bell_draw(splits[13], (D + DIN,), (0.089 * TOKENS ** 0.5), 48.0, ((0, 32),), jnp.float32)
    gain_second = jnp.clip(jnp.exp(math.log(2211.84) - 2.7652086 * jax.random.uniform(splits[14], (D + DIN,), jnp.float32) ** steps_of(splits[14], (D + DIN,), ((0, 32),), -0.2, 0.2)), 139.264, 2211.84)
    head_params = draw_head_params(jax.random.fold_in(splits[18], 71), 0)
    head_first = draw_head_first(jax.random.fold_in(splits[18], 71), 0)
    head_second = draw_head_second(jax.random.fold_in(splits[18], 71), 0)
    return dict(tokens_in=tokens_in, cotangent=cotangent, seq_lens=seq_lens, in_weight=in_weight, in_first=in_first, in_second=in_second, out_weight=out_weight, out_first=out_first, out_second=out_second, conv_weight=conv_weight, conv_first=conv_first, conv_second=conv_second, gains=gains, gain_first=gain_first, gain_second=gain_second, head_params=head_params, head_first=head_first, head_second=head_second)


@jax.custom_vjp
def low(v):
    return lax.optimization_barrier(v.astype(jnp.bfloat16)).astype(jnp.float32)

@jax.custom_vjp
def low_back(v):
    return v

def low_keep(v):
    return (low(v), None)

def low_pass(kept, grad):
    return (grad,)

def back_keep(v):
    return (v, None)

def back_low(kept, grad):
    return (low(grad),)
low.defvjp(low_keep, low_pass)
low_back.defvjp(back_keep, back_low)
highest = lax.Precision.HIGHEST
norm_eps = 1e-05
beta_first = 0.9
beta_second = 0.95
adam_eps = 1e-08
weight_decay = 0.1
rate_in = 0.01
rate_out = 0.008
rate_conv = 0.2
rate_gain = 0.4
rate_head = 0.5

def segment_of(seq_row, position):
    blocks = (seq_row + BLOCK - 1) // BLOCK
    ends = (jnp.cumsum(blocks) * BLOCK).astype(jnp.int32)
    starts = (ends - blocks * BLOCK).astype(jnp.int32)
    above = position[:, None] >= starts[None, :]
    inside = above & (position[:, None] < ends[None, :])
    numbers = jnp.arange(1, SLOTS + 1, dtype=jnp.int32)
    labels_of = lax.optimization_barrier(jnp.sum(jnp.where(inside, numbers[None, :], 0), axis=1)).astype(jnp.int32)
    live_rows = lax.optimization_barrier(jnp.sum((above & (position[:, None] < (starts + seq_row)[None, :])).astype(jnp.float32), axis=1))
    return (labels_of, live_rows)

def layout(seq_row, position):
    labels_of, live_rows = segment_of(seq_row, position)
    columns = []
    for conv_lag in range(KCONV):
        earlier, unused_live = segment_of(seq_row, position - conv_lag)
        columns.append(((earlier == labels_of) & (labels_of > 0)).astype(jnp.float32))
    return (live_rows, jnp.stack(columns, axis=1))

def pre_norm(token_rows, gain_row):
    scaling = lax.rsqrt(lax.optimization_barrier(jnp.mean(token_rows * token_rows, axis=1, keepdims=True)) + norm_eps)
    return token_rows * scaling * gain_row[None, :]

def gate_norm(mixed, gate_part, gain_row):
    gated = mixed * jax.nn.silu(gate_part)
    scaling = lax.rsqrt(lax.optimization_barrier(jnp.mean(gated * gated, axis=1, keepdims=True)) + norm_eps)
    return gated * scaling * gain_row[None, :]

def mixer_in(extended, step_raw, conv_par, head_values, factors, live_rows):
    row_count = step_raw.shape[0]
    preact = jnp.zeros((row_count, conv_par.shape[1]), jnp.float32) + conv_par[KCONV][None, :]
    for conv_tap in range(KCONV):
        window = lax.slice_in_dim(extended, conv_tap, conv_tap + row_count, axis=0)
        preact = preact + conv_par[conv_tap][None, :] * window * factors[:, KCONV - 1 - conv_tap][:, None]
    conv_act = jax.nn.silu(preact)
    step_size = jax.nn.softplus(step_raw + head_values[0][None, :]) * live_rows[:, None]
    logdec = -jnp.exp(head_values[1])[None, :] * step_size
    return (conv_act, step_size, logdec)

def lower_ones():
    row_ids = lax.broadcasted_iota(jnp.int32, (BLOCK, BLOCK), 0)
    col_ids = lax.broadcasted_iota(jnp.int32, (BLOCK, BLOCK), 1)
    return (row_ids >= col_ids).astype(jnp.float32)

def block_state(values, keys_in, step_size, logdec):
    cumul = jnp.dot(lower_ones(), logdec, precision=highest)
    totals = cumul[-1]
    weighting = jnp.exp(totals[None, :] - cumul) * step_size
    states = jnp.einsum('uhp,un->hpn', weighting[:, :, None] * values, keys_in, precision=highest)
    return (jnp.exp(totals), states)

def block_out(values, keys_in, queries, step_size, logdec, skip_gain, start_state):
    lower_tri = lower_ones()
    cumul = jnp.dot(lower_tri, logdec, precision=highest)
    across = cumul.T
    gap_matrix = across[:, :, None] - across[:, None, :]
    decays = jnp.exp(jnp.where(lower_tri[None, :, :] > 0, gap_matrix, -1e+30))
    gram_matrix = jnp.dot(queries, keys_in.T, precision=highest)
    mixing = gram_matrix[None, :, :] * decays * step_size.T[:, None, :]
    intra_part = jnp.einsum('htu,uhp->thp', mixing, values, precision=highest)
    carried = jnp.exp(cumul)[:, :, None] * jnp.einsum('tn,hpn->thp', queries, start_state, precision=highest)
    return intra_part + carried + skip_gain[None, :, None] * values

def block_full(values, keys_in, queries, step_size, logdec, skip_gain, start_state):
    factor_end, states = block_state(values, keys_in, step_size, logdec)
    outputs = block_out(values, keys_in, queries, step_size, logdec, skip_gain, start_state)
    return (outputs, factor_end[:, None, None] * start_state + states)

def group_layer(token_rows, seq_row, in_low, out_low, conv_low, gain_low, head_values):
    position = jnp.arange(GROUP_TOK, dtype=jnp.int32)
    live_rows, factors = layout(seq_row, position)
    normed = low(pre_norm(token_rows, gain_low[:D]))
    projected = low_back(jnp.dot(normed, in_low, precision=highest))
    gate_part = projected[:, :DIN]
    conv_in = projected[:, DIN:DIN + CONVC]
    step_raw = projected[:, DIN + CONVC:]
    extended = jnp.concatenate([jnp.zeros((KCONV - 1, CONVC), jnp.float32), conv_in], axis=0)
    conv_act, step_size, logdec = mixer_in(extended, step_raw, conv_low, head_values, factors, live_rows)
    conv_act = low(conv_act)
    block_count = GROUP_TOK // BLOCK
    values = conv_act[:, :DIN].reshape(block_count, BLOCK, HEADS, HDIM)
    keys_in = conv_act[:, DIN:DIN + NST].reshape(block_count, BLOCK, NST)
    queries = conv_act[:, DIN + NST:].reshape(block_count, BLOCK, NST)
    resets = factors[::BLOCK, 1]

    def advance(states, block_item):
        outputs, state_next = block_full(block_item[0], block_item[1], block_item[2], block_item[3], block_item[4], head_values[2], block_item[5] * states)
        return (state_next, outputs)
    start_state = jnp.zeros((HEADS, HDIM, NST), jnp.float32)
    unused_state, outputs = lax.scan(jax.checkpoint(advance), start_state, (values, keys_in, queries, step_size.reshape(block_count, BLOCK, HEADS), logdec.reshape(block_count, BLOCK, HEADS), resets))
    mixed = low_back(outputs.reshape(GROUP_TOK, DIN))
    normed_out = low(gate_norm(mixed, gate_part, gain_low[D:]))
    branch = jnp.dot(normed_out, out_low, precision=highest)
    return token_rows + live_rows[:, None] * branch

def make_forward(seq_lens):

    def forward(token_rows, in_weight, out_weight, conv_weight, gains, head_params):
        in_low = low(in_weight)
        out_low = low(out_weight)
        conv_low = low(conv_weight)
        gain_low = low(gains)
        grouped = token_rows.reshape(GROUPS, GROUP_TOK, D)

        def per_group(carried, group_item):
            return (carried, group_layer(group_item[0], group_item[1], in_low, out_low, conv_low, gain_low, head_params))
        unused_carry, group_outs = lax.scan(jax.checkpoint(per_group), jnp.zeros((), jnp.float32), (grouped, seq_lens))
        return group_outs.reshape(TOKENS, D)
    return forward

def adam_update(weight, first, second, gradient, step_rate):
    first_new = beta_first * first + (1.0 - beta_first) * gradient
    second_new = beta_second * second + (1.0 - beta_second) * gradient * gradient
    first_hat = first_new / (1.0 - beta_first ** STEP)
    second_hat = second_new / (1.0 - beta_second ** STEP)
    weight_new = weight - step_rate * (first_hat / (jnp.sqrt(second_hat) + adam_eps) + weight_decay * weight)
    return (weight_new, first_new, second_new)

def reference(tokens_in, cotangent, seq_lens, in_weight, in_first, in_second, out_weight, out_first, out_second, conv_weight, conv_first, conv_second, gains, gain_first, gain_second, head_params, head_first, head_second):
    token_rows = tokens_in.astype(jnp.float32)
    forward = make_forward(seq_lens)
    outputs, pull_back = jax.vjp(forward, token_rows, in_weight, out_weight, conv_weight, gains, head_params)
    grad_rows, grad_in, grad_out, grad_conv, grad_gain, grad_head = pull_back(cotangent.astype(jnp.float32))
    new_in = adam_update(in_weight, in_first, in_second, grad_in, rate_in)
    new_out = adam_update(out_weight, out_first, out_second, grad_out, rate_out)
    new_conv = adam_update(conv_weight, conv_first, conv_second, grad_conv, rate_conv)
    new_gain = adam_update(gains, gain_first, gain_second, grad_gain, rate_gain)
    new_head = adam_update(head_params, head_first, head_second, grad_head, rate_head)
    return (outputs.astype(jnp.bfloat16), grad_rows, new_in[0], new_in[1], new_in[2], new_out[0], new_out[1], new_out[2], new_conv[0], new_conv[1], new_conv[2], new_gain[0], new_gain[1], new_gain[2], new_head[0], new_head[1], new_head[2])
```

```python
import functools

import jax
import jax.numpy as jnp
from jax import lax
from jax.experimental import pallas as pl
from jax.experimental.pallas import tpu as pltpu
from jax.sharding import PartitionSpec as P

D = 1536
HEADS = 48
HDIM = 64
NST = 128
KCONV = 4
BLOCK = 256
SLOTS = 4
STEP = 10
DIN = 3072
CONVC = 3328


highest = lax.Precision.HIGHEST
norm_eps = 1e-05
beta_first = 0.9
beta_second = 0.95
adam_eps = 1e-08
weight_decay = 0.1
rate_in = 0.01
rate_out = 0.008
rate_conv = 0.2
rate_gain = 0.4
rate_head = 0.5


def from_behind(block, axis, distance):
    devices = range(lax.axis_size(axis))
    route = [(i - distance, i) for i in devices if i - distance in devices]
    return lax.ppermute(block, axis, route)


def prefix(value, axis, join, neutral):
    place = lax.axis_index(axis)
    gathered = jax.tree.map(
        lambda a, kind: lax.all_gather(a.astype(kind), axis),
        value,
        jax.tree.map(lambda a: jnp.bfloat16 if a.dtype == jnp.float32 else a.dtype, value),
    )
    state = jax.tree.map(lambda a, e: jnp.zeros_like(a) + jnp.asarray(e, a.dtype), value, neutral)

    def one(hop, state):
        return join(
            state,
            jax.tree.map(
                lambda a, own: lax.dynamic_index_in_dim(a, hop, 0, False).astype(own.dtype),
                gathered,
                value,
            ),
        )

    return lax.fori_loop(0, place, one, state)


def prefix_2(value, axis, combine, identity):
    devices, index = (lax.axis_size(axis), lax.axis_index(axis))
    everything = jax.tree.map(
        lambda part, kind: lax.all_gather(part.astype(kind), axis),
        value,
        (jnp.bfloat16, jnp.bfloat16),
    )
    start = jax.tree.map(
        lambda part, zero: jnp.broadcast_to(jnp.asarray(zero, part.dtype), part.shape),
        value,
        identity,
    )

    def hop(k, before):
        at = devices - 1 - k
        reached = at > index
        new = combine(
            before, jax.tree.map(lambda part, own: part[at].astype(own.dtype), everything, value)
        )
        return jax.tree.map(lambda a, b: jnp.where(reached, a, b), new, before)

    return lax.fori_loop(0, devices, hop, start)


def segment_of(seq_row, position):
    blocks = (seq_row + BLOCK - 1) // BLOCK
    ends = jnp.cumsum(blocks) * BLOCK
    starts = ends - blocks * BLOCK
    above = position[:, None] >= starts[None, :]
    inside = above & (position[:, None] < ends[None, :])
    numbers = jnp.arange(1, SLOTS + 1, dtype=jnp.int32)
    labels_of = jnp.sum(jnp.where(inside, numbers[None, :], 0), axis=1)
    live_rows = jnp.sum(
        (above & (position[:, None] < (starts + seq_row)[None, :])).astype(jnp.float32), axis=1
    )
    return (labels_of, live_rows)


def layout(seq_row, position):
    labels_of, live_rows = segment_of(seq_row, position)
    columns = []
    for conv_lag in range(KCONV):
        earlier, unused_live = segment_of(seq_row, position - conv_lag)
        columns.append(((earlier == labels_of) & (labels_of > 0)).astype(jnp.float32))
    return (live_rows, jnp.stack(columns, axis=1))


def pre_norm(token_rows, gain_row):
    scaling = lax.rsqrt(jnp.mean(token_rows * token_rows, axis=1, keepdims=True) + norm_eps)
    return token_rows * scaling * gain_row[None, :]


def gate_norm(mixed, gate_part, gain_row):
    gated = mixed * jax.nn.silu(gate_part)
    scaling = lax.rsqrt(jnp.mean(gated * gated, axis=1, keepdims=True) + norm_eps)
    return gated * scaling * gain_row[None, :]


def mixer_in(extended, step_raw, conv_par, head_values, factors, live_rows):
    row_count = step_raw.shape[0]
    preact = jnp.zeros((row_count, conv_par.shape[1]), jnp.float32) + conv_par[KCONV][None, :]
    for conv_tap in range(KCONV):
        window = lax.slice_in_dim(extended, conv_tap, conv_tap + row_count, axis=0)
        preact = (
            preact
            + conv_par[conv_tap][None, :] * window * factors[:, KCONV - 1 - conv_tap][:, None]
        )
    conv_act = jax.nn.silu(preact)
    step_size = jax.nn.softplus(step_raw + head_values[0][None, :]) * live_rows[:, None]
    logdec = -jnp.exp(head_values[1])[None, :] * step_size
    return (conv_act, step_size, logdec)


def lower_ones():
    row_ids = lax.broadcasted_iota(jnp.int32, (BLOCK, BLOCK), 0)
    col_ids = lax.broadcasted_iota(jnp.int32, (BLOCK, BLOCK), 1)
    return (row_ids >= col_ids).astype(jnp.float32)


def block_state(values, keys_in, step_size, logdec):
    cumul = jnp.dot(lower_ones(), logdec, precision=highest)
    totals = cumul[-1]
    weighting = jnp.exp(totals[None, :] - cumul) * step_size
    states = jnp.einsum("uhp,un->hpn", weighting[:, :, None] * values, keys_in, precision=highest)
    return (jnp.exp(totals), states)


def block_out(values, keys_in, queries, step_size, logdec, skip_gain, start_state):
    lower_tri = lower_ones()
    cumul = jnp.dot(lower_tri, logdec, precision=highest)
    across = cumul.T
    gap_matrix = across[:, :, None] - across[:, None, :]
    decays = jnp.exp(jnp.where(lower_tri[None, :, :] > 0, gap_matrix, -1e30))
    gram_matrix = jnp.dot(queries, keys_in.T, precision=highest)
    mixing = gram_matrix[None, :, :] * decays * step_size.T[:, None, :]
    intra_part = jnp.einsum("htu,uhp->thp", mixing, values, precision=highest)
    carried = jnp.exp(cumul)[:, :, None] * jnp.einsum(
        "tn,hpn->thp", queries, start_state, precision=highest
    )
    return intra_part + carried + skip_gain[None, :, None] * values


def block_full(values, keys_in, queries, step_size, logdec, skip_gain, start_state):
    factor_end, states = block_state(values, keys_in, step_size, logdec)
    outputs = block_out(values, keys_in, queries, step_size, logdec, skip_gain, start_state)
    return (outputs, factor_end[:, None, None] * start_state + states)


def adam_update(weight, first, second, gradient, step_rate):
    first_new = beta_first * first + (1.0 - beta_first) * gradient
    second_new = beta_second * second + (1.0 - beta_second) * gradient * gradient
    first_hat = first_new / (1.0 - beta_first**STEP)
    second_hat = second_new / (1.0 - beta_second**STEP)
    weight_new = weight - step_rate * (
        first_hat / (jnp.sqrt(second_hat) + adam_eps) + weight_decay * weight
    )
    return (weight_new, first_new, second_new)


def carry_join(earlier, later):
    return (earlier[0] * later[0], later[0][:, None, None] * earlier[1] + later[1])


def as_float(array_low):
    return lax.optimization_barrier(array_low).astype(jnp.float32)


def contract_rows(left, right):
    return lax.dot_general(
        left, right, (((0,), (0,)), ((), ())), preferred_element_type=jnp.float32
    )


def contract_cols(left, right):
    return lax.dot_general(
        left, right, (((1,), (1,)), ((), ())), preferred_element_type=jnp.float32
    )


def per_device(
    tokens_in,
    cotangent,
    seq_lens,
    in_weight,
    in_first,
    in_second,
    out_weight,
    out_first,
    out_second,
    conv_weight,
    conv_first,
    conv_second,
    gains,
    gain_first,
    gain_second,
    head_params,
    head_first,
    head_second,
):
    local_tok = tokens_in.shape[0]
    position = lax.axis_index("seq") * local_tok + jnp.arange(local_tok, dtype=jnp.int32)
    live_rows, factors = layout(seq_lens[0], position)
    low_weights = (
        in_weight.astype(jnp.bfloat16),
        out_weight.astype(jnp.bfloat16),
        conv_weight.astype(jnp.bfloat16),
        gains.astype(jnp.bfloat16),
    )
    in_full, out_full, conv_full, gain_full = (
        lax.all_gather(low_weights[0], ("dp", "seq"), axis=0, tiled=True),
        lax.all_gather(low_weights[1], ("dp", "seq"), axis=0, tiled=True),
        lax.all_gather(low_weights[2], ("dp", "seq"), axis=1, tiled=True),
        lax.all_gather(low_weights[3], ("dp", "seq"), axis=0, tiled=True),
    )
    conv_par = conv_full.astype(jnp.float32)
    gain_par = gain_full.astype(jnp.float32)
    token_rows = tokens_in.astype(jnp.float32)
    normed_value, pull_pre = jax.vjp(pre_norm, token_rows, gain_par[:D])
    normed = normed_value.astype(jnp.bfloat16)
    projected = jnp.dot(normed, in_full, preferred_element_type=jnp.float32)
    gate_part = projected[:, :DIN]
    conv_in = projected[:, DIN : DIN + CONVC]
    step_raw = projected[:, DIN + CONVC :]
    halo_rows = from_behind(conv_in[local_tok - KCONV + 1 :], "seq", 1)
    extended = jnp.concatenate([halo_rows, conv_in], axis=0)

    def mixer_local(extended_rows, raw_steps, conv_values, head_values):
        return mixer_in(extended_rows, raw_steps, conv_values, head_values, factors, live_rows)

    (conv_act, step_size, logdec), pull_mixer = jax.vjp(
        mixer_local, extended, step_raw, conv_par, head_params
    )
    conv_used = as_float(conv_act.astype(jnp.bfloat16))
    block_count = local_tok // BLOCK
    values = conv_used[:, :DIN].reshape(block_count, BLOCK, HEADS, HDIM)
    keys_in = conv_used[:, DIN : DIN + NST].reshape(block_count, BLOCK, NST)
    queries = conv_used[:, DIN + NST :].reshape(block_count, BLOCK, NST)
    steps_blk = step_size.reshape(block_count, BLOCK, HEADS)
    logdec_blk = logdec.reshape(block_count, BLOCK, HEADS)
    resets = factors[::BLOCK, 1]
    skip_gain = head_params[2]
    decays, block_states = jax.vmap(block_state)(values, keys_in, steps_blk, logdec_blk)

    def fold_local(carried, block_item):
        factor_now = block_item[0] * block_item[2]
        return (
            (carried[0] * factor_now, factor_now[:, None, None] * carried[1] + block_item[1]),
            None,
        )

    identity = (jnp.ones((HEADS,), jnp.float32), jnp.zeros((HEADS, HDIM, NST), jnp.float32))
    device_sum, unused_fold = lax.scan(fold_local, identity, (decays, block_states, resets))
    unused_dec, entering = prefix(device_sum, "seq", carry_join, identity)

    def start_states(states, block_item):
        begin = block_item[2] * states
        return (block_item[0][:, None, None] * begin + block_item[1], begin)

    unused_end, begins = lax.scan(start_states, entering, (decays, block_states, resets))

    def emit(block_item):
        return block_out(
            block_item[0],
            block_item[1],
            block_item[2],
            block_item[3],
            block_item[4],
            skip_gain,
            block_item[5],
        )

    mixed = lax.map(emit, (values, keys_in, queries, steps_blk, logdec_blk, begins)).reshape(
        local_tok, DIN
    )
    normed_out_value, pull_gate = jax.vjp(gate_norm, mixed, gate_part, gain_par[D:])
    normed_out = normed_out_value.astype(jnp.bfloat16)
    branch = jnp.dot(normed_out, out_full, preferred_element_type=jnp.float32)
    mixed_out = (token_rows + live_rows[:, None] * branch).astype(jnp.bfloat16)
    out_grad = (cotangent.astype(jnp.float32) * live_rows[:, None]).astype(jnp.bfloat16)
    in_back, out_back = (
        lax.all_gather(in_weight.astype(jnp.bfloat16), ("dp", "seq"), axis=0, tiled=True),
        lax.all_gather(out_weight.astype(jnp.bfloat16), ("dp", "seq"), axis=0, tiled=True),
    )
    grad_out_w = contract_rows(normed_out, out_grad)
    grad_normed_out = contract_cols(out_grad, out_back)
    grad_mixed, grad_gate, grad_gain_in = pull_gate(grad_normed_out)
    mixed_back = as_float(grad_mixed.astype(jnp.bfloat16)).reshape(block_count, BLOCK, HEADS, HDIM)

    def adjoint_local(carried, block_item):
        cumul = jnp.dot(lower_ones(), block_item[2], precision=highest)
        weighted = jnp.exp(cumul)[:, :, None] * block_item[0]
        direct = jnp.einsum("thp,tn->hpn", weighted, block_item[1], precision=highest)
        return (block_item[4] * (direct + block_item[3][:, None, None] * carried), None)

    local_adj, unused_adj = lax.scan(
        adjoint_local, identity[1], (mixed_back, queries, logdec_blk, decays, resets), reverse=True
    )
    unused_later, leaving = prefix_2((device_sum[0], local_adj), "seq", carry_join, identity)

    def adjoint_block(carried, block_item):
        unused_primal, pull_block = jax.vjp(
            block_full,
            block_item[0],
            block_item[1],
            block_item[2],
            block_item[3],
            block_item[4],
            skip_gain,
            block_item[5],
        )
        grads = pull_block((block_item[6], carried[0]))
        return ((block_item[7] * grads[6], carried[1] + grads[5]), grads[:5])

    (unused_state, grad_skip), block_grads = lax.scan(
        adjoint_block,
        (leaving, jnp.zeros((HEADS,), jnp.float32)),
        (values, keys_in, queries, steps_blk, logdec_blk, begins, mixed_back, resets),
        reverse=True,
    )
    grad_values, grad_keys, grad_queries, grad_step, grad_logdec = block_grads
    grad_act = jnp.concatenate(
        [
            grad_values.reshape(local_tok, DIN),
            grad_keys.reshape(local_tok, NST),
            grad_queries.reshape(local_tok, NST),
        ],
        axis=1,
    )
    grad_ext, grad_raw, grad_conv, grad_head_part = pull_mixer(
        (grad_act, grad_step.reshape(local_tok, HEADS), grad_logdec.reshape(local_tok, HEADS))
    )
    returned = from_behind(grad_ext[: KCONV - 1].astype(jnp.bfloat16), "seq", -1).astype(
        jnp.float32
    )
    grad_conv_in = grad_ext[KCONV - 1 :] + jnp.concatenate(
        [jnp.zeros((local_tok - KCONV + 1, CONVC), jnp.float32), returned], axis=0
    )
    grad_proj = jnp.concatenate([grad_gate, grad_conv_in, grad_raw], axis=1).astype(jnp.bfloat16)
    grad_normed = contract_cols(grad_proj, in_back)
    grad_rows, grad_gain_pre = pull_pre(grad_normed)
    grad_input = cotangent.astype(jnp.float32) + grad_rows
    grad_gains = jnp.concatenate([grad_gain_pre, grad_gain_in], axis=0)
    grad_head = jnp.concatenate(
        [grad_head_part[:2], (grad_head_part[2] + grad_skip)[None, :]], axis=0
    )
    grad_in_w = contract_rows(normed, grad_proj)
    in_sum, out_sum, conv_sum, gain_sum = (
        lax.psum_scatter(grad_in_w, ("dp", "seq"), scatter_dimension=0, tiled=True),
        lax.psum_scatter(grad_out_w, ("dp", "seq"), scatter_dimension=0, tiled=True),
        lax.psum_scatter(grad_conv, ("dp", "seq"), scatter_dimension=1, tiled=True),
        lax.psum_scatter(grad_gains, ("dp", "seq"), scatter_dimension=0, tiled=True),
    )
    head_sum = lax.psum(grad_head, ("dp", "seq"))
    new_in = adam_update(in_weight, in_first, in_second, in_sum, rate_in)
    new_out = adam_update(out_weight, out_first, out_second, out_sum, rate_out)
    new_conv = adam_update(conv_weight, conv_first, conv_second, conv_sum, rate_conv)
    new_gain = adam_update(gains, gain_first, gain_second, gain_sum, rate_gain)
    new_head = adam_update(head_params, head_first, head_second, head_sum, rate_head)
    return (
        mixed_out,
        grad_input,
        new_in[0],
        new_in[1],
        new_in[2],
        new_out[0],
        new_out[1],
        new_out[2],
        new_conv[0],
        new_conv[1],
        new_conv[2],
        new_gain[0],
        new_gain[1],
        new_gain[2],
        new_head[0],
        new_head[1],
        new_head[2],
    )


MESH_ID = pl.DeviceIdType.MESH
ANY = pl.BlockSpec(memory_space=pl.ANY)
PLANES = 4
QUADS = 4
RANKS = 8


def place():
    chip = lax.axis_index("dp")
    return (chip // QUADS, chip % QUADS, lax.axis_index("seq"))


def at(plane, quad, core):
    return (plane * QUADS + quad, core)


def flip(core):
    return 1 - core


def xor4(value, k):
    low, high = value % 2, value // 2
    if k % 2:
        low = 1 - low
    if k // 2:
        high = 1 - high
    return 2 * high + low


def greet(devices):
    barrier = pltpu.get_barrier_semaphore()
    for device in devices:
        pl.semaphore_signal(barrier, inc=1, device_id=device, device_id_type=MESH_ID)
    pl.semaphore_wait(barrier, len(devices))


def plane_mates(plane, quad, core):
    mates = []
    for k in range(QUADS):
        for other in (core, flip(core)):
            if not (k == 0 and other is core):
                mates.append(at(plane, xor4(quad, k), other))
    return mates


def plane_others(plane, quad, core):
    return [at(xor4(plane, k), quad, core) for k in range(1, PLANES)]


class Sems:
    def __init__(self, send, recv):
        self.send, self.recv, self.used = (send, recv, 0)

    def copy(self, source, target, device):
        index = self.used
        self.used += 1
        return pltpu.make_async_remote_copy(
            src_ref=source,
            dst_ref=target,
            send_sem=self.send.at[index],
            recv_sem=self.recv.at[index],
            device_id=device,
            device_id_type=MESH_ID,
        )


class PlaneGather:
    def __init__(self, sems, own, block, plane, quad, core):
        near_x, near_y, far = (xor4(quad, k) for k in (1, 2, 3))
        rank = 2 * quad + core
        rank_x, rank_y, rank_far = (2 * q + core for q in (near_x, near_y, far))
        to_x, to_y = (at(plane, near_x, core), at(plane, near_y, core))
        sibling = at(plane, quad, flip(core))
        whole = [0, 1]
        self.own = [
            sems.copy(own(h), block(rank, h), device)
            for device in (to_x, to_y, sibling)
            for h in whole
        ]
        self.relay_x = [
            sems.copy(block(rank_x, 0), block(rank_x, 0), to_y),
        ] + [sems.copy(block(rank_x, h), block(rank_x, h), sibling) for h in whole]
        self.relay_y = [
            sems.copy(block(rank_y, 1), block(rank_y, 1), to_x),
        ] + [sems.copy(block(rank_y, h), block(rank_y, h), sibling) for h in whole]
        self.relay_far = [
            sems.copy(block(rank_far, h), block(rank_far, h), sibling) for h in whole
        ]

    def start(self):
        for copy in self.own:
            copy.start()

    def forward(self):
        self.own[0].wait_recv()
        self.relay_x[0].start()
        self.own[3].wait_recv()
        self.relay_y[0].start()
        self.own[1].wait_recv()
        self.own[2].wait_recv()
        for copy in self.relay_x[1:] + self.relay_y[1:]:
            copy.start()

    def finish(self):
        for h, relay in ((0, self.relay_x[0]), (1, self.relay_y[0])):
            relay.wait_recv()
            self.relay_far[h].start()
        for copy in self.own[4:] + self.relay_x[1:] + self.relay_y[1:] + self.relay_far:
            copy.wait_recv()
        for copy in self.own + self.relay_x + self.relay_y + self.relay_far:
            copy.wait_send()


class LineGather:
    def __init__(self, sems, own, block, plane, quad, core):
        self.plane = plane
        self.right, self.left = ([], [])
        for hop in range(PLANES - 1):
            for copies, step in ((self.right, 1), (self.left, -1)):
                index = plane - step * hop
                source = own if hop == 0 else block(index)
                copies.append(sems.copy(source, block(index), at(plane + step, quad, core)))

    def sends(self, hop, step):
        if step > 0:
            return (self.plane - hop >= 0) & (self.plane < PLANES - 1)
        return (self.plane + hop < PLANES) & (self.plane > 0)

    def receives(self, hop, step):
        if step > 0:
            return self.plane - 1 - hop >= 0
        return self.plane + 1 + hop < PLANES

    def start(self, hop):
        for copies, step in ((self.right, 1), (self.left, -1)):

            @pl.when(self.sends(hop, step))
            def go():
                copies[hop].start()

    def arrive(self, hop):
        for copies, step in ((self.right, 1), (self.left, -1)):

            @pl.when(self.receives(hop, step))
            def landed():
                copies[hop].wait_recv()

    def sent(self):
        for hop in range(PLANES - 1):
            for copies, step in ((self.right, 1), (self.left, -1)):

                @pl.when(self.sends(hop, step))
                def left():
                    copies[hop].wait_send()


def gather_kernel(tok, cot, wz, wc, wo, o_tok, o_cot, o_wz, o_wc, s_wo, o_wo, send, recv, local):
    plane, quad, core = place()
    rank = 2 * quad + core
    sibling = at(plane, quad, flip(core))
    sems = Sems(send, recv)
    where = (plane, quad, core)
    locals_ = []

    def keep(source, target):
        copy = pltpu.make_async_copy(source, target, local.at[len(locals_)])
        locals_.append(copy)
        copy.start()
        return copy

    half = tok.shape[0] // 2
    rows = wc.shape[0]

    def token_block(buffer):
        return lambda r, h: buffer.at[r, pl.ds(h * half, half)]

    def token_own(buffer):
        return lambda h: buffer.at[pl.ds(h * half, half)]

    line_c = LineGather(sems, wc, lambda q: o_wc.at[q, rank], *where)
    line_o = LineGather(sems, wo, lambda q: s_wo.at[q], *where)
    shuffle = []
    for k in range(1, RANKS):
        other_core = flip(core) if k % 2 else core
        other_quad = xor4(quad, k // 2)
        shuffle.append(
            sems.copy(wz.at[2 * other_quad + other_core], o_wz.at[plane, rank], at(plane, other_quad, other_core))
        )
    halves = [
        LineGather(
            sems,
            o_wz.at[plane, pl.ds(4 * h, 4)],
            lambda q, h=h: o_wz.at[q, pl.ds(4 * h, 4)],
            *where,
        )
        for h in range(2)
    ]
    tokens = PlaneGather(sems, token_own(tok), token_block(o_tok), *where)
    grads = PlaneGather(sems, token_own(cot), token_block(o_cot), *where)
    common = PlaneGather(
        sems,
        lambda h: o_wc.at[pl.ds(2 * h, 2), rank],
        lambda r, h: o_wc.at[pl.ds(2 * h, 2), r],
        *where,
    )
    cross_o = [
        sems.copy(s_wo.at[2 * flip(core) + k], o_wo.at[k, core], sibling) for k in range(2)
    ]

    greet(plane_mates(*where) + plane_others(*where))
    line_c.start(0)
    for copy in shuffle:
        copy.start()
    line_o.start(0)
    tokens.start()
    own_wz = keep(wz.at[rank], o_wz.at[plane, rank])
    own_wc = keep(wc, o_wc.at[plane, rank])
    own_wo = keep(wo, s_wo.at[plane])
    own_tok = keep(tok, o_tok.at[rank])
    own_cot = keep(cot, o_cot.at[rank])
    own_wz.wait()
    for copy in shuffle:
        copy.wait_recv()
    halves[0].start(0)
    halves[1].start(0)
    for hop in range(PLANES - 1):
        line_c.arrive(hop)
        if hop < PLANES - 2:
            line_c.start(hop + 1)
    own_wc.wait()
    common.start()
    tokens.forward()
    grads.start()
    common.forward()
    for hop in range(PLANES - 1):
        for h in range(2):
            halves[h].arrive(hop)
            if hop < PLANES - 2:
                halves[h].start(hop + 1)
        line_o.arrive(hop)
        if hop < PLANES - 2:
            line_o.start(hop + 1)
        if hop == 0:
            tokens.finish()
            common.finish()
    own_wo.wait()
    keeps = []
    for copy in cross_o:
        copy.start()
    keeps = [keep(s_wo.at[2 * core + k], o_wo.at[k, core]) for k in range(2)]
    grads.forward()
    grads.finish()
    for copy in cross_o:
        copy.wait()
    for copy in shuffle:
        copy.wait_send()
    for line in halves + [line_c, line_o]:
        line.sent()
    for copy in [own_tok, own_cot] + keeps:
        copy.wait()


def gather_all(tok, cot, wz, wc, wo):
    bf16 = jnp.bfloat16
    shapes = (
        (RANKS,) + tok.shape,
        (RANKS,) + cot.shape,
        (PLANES,) + wz.shape,
        (PLANES, RANKS) + wc.shape,
        (PLANES,) + wo.shape,
        (2, 2) + wo.shape,
    )
    outs = pl.pallas_call(
        gather_kernel,
        out_shape=[jax.ShapeDtypeStruct(s, bf16) for s in shapes],
        in_specs=[ANY] * 5,
        out_specs=[ANY] * 6,
        scratch_shapes=[
            pltpu.SemaphoreType.DMA((80,)),
            pltpu.SemaphoreType.DMA((80,)),
            pltpu.SemaphoreType.DMA((8,)),
        ],
        compiler_params=pltpu.CompilerParams(collective_id=0, has_side_effects=True),
    )(tok, cot, wz, wc, wo)
    return (outs[0], outs[1], outs[2], outs[3], outs[5])


def core_kernel(*refs):
    count = (len(refs) - 2) // 2
    sources, targets, (send, recv) = (refs[:count], refs[count : 2 * count], refs[2 * count :])
    plane, quad, core = place()
    sibling = at(plane, quad, flip(core))
    sems = Sems(send, recv)
    copies = [sems.copy(s.at[flip(core)], t, sibling) for s, t in zip(sources, targets)]
    greet([sibling])
    for copy in copies:
        copy.start()
    for copy in copies:
        copy.wait()


def core_swap(ident, *arrays):
    count = len(arrays)
    return pl.pallas_call(
        core_kernel,
        out_shape=[jax.ShapeDtypeStruct(a.shape[1:], a.dtype) for a in arrays],
        in_specs=[ANY] * count,
        out_specs=[ANY] * count,
        scratch_shapes=[pltpu.SemaphoreType.DMA((count,)), pltpu.SemaphoreType.DMA((count,))],
        compiler_params=pltpu.CompilerParams(collective_id=ident, has_side_effects=True),
    )(*arrays)


def push_kernel(n_quad, n_plane, n_rank, with_out, *refs):
    count = n_quad + n_plane + n_rank + with_out
    sources, targets = (refs[:count], refs[count : 2 * count])
    send, recv, out_send, out_recv, local = refs[2 * count :]
    plane, quad, core = place()
    where = (plane, quad, core)
    rank = 2 * quad + core
    sems = Sems(send, recv)
    copies = []
    peers = []
    if n_plane or with_out:
        peers += plane_others(*where)
    if with_out:
        peers += [at(xor4(plane, k), quad, flip(core)) for k in range(PLANES)]
    if n_rank:
        peers += plane_mates(*where)
    elif n_quad:
        peers += [at(plane, xor4(quad, k), core) for k in range(1, QUADS)]
    index = n_quad
    for i in range(n_plane):
        for k in (2, 3, 1):
            other = xor4(plane, k)
            copies.append(
                sems.copy(sources[index + i].at[other], targets[index + i].at[k - 1], at(other, quad, core))
            )
    for i in range(n_quad):
        for k in (3, 1, 2):
            other = xor4(quad, k)
            copies.append(sems.copy(sources[i].at[other], targets[i].at[k - 1], at(plane, other, core)))
    index += n_plane
    for i in range(n_rank):
        for k in range(1, RANKS):
            other_core = flip(core) if k % 2 else core
            other_quad = xor4(quad, k // 2)
            copies.append(
                sems.copy(
                    sources[index + i].at[2 * other_quad + other_core],
                    targets[index + i].at[rank],
                    at(plane, other_quad, other_core),
                )
            )
    index += n_rank
    greet(peers)
    for copy in copies:
        copy.start()
    if with_out:
        source, target = (sources[index], targets[index])
        mine = (plane // 2 == core)
        for near in range(2):
            for side in range(2):
                to_plane = 2 * core + near
                itself = (to_plane == plane) & (core == side)
                remote = pltpu.make_async_remote_copy(
                    src_ref=source.at[near, side],
                    dst_ref=target.at[plane],
                    send_sem=out_send.at[2 * near + side],
                    recv_sem=out_recv.at[plane],
                    device_id=at(to_plane, quad, side),
                    device_id_type=MESH_ID,
                )

                @pl.when(jnp.logical_not(itself))
                def go():
                    remote.start()

                @pl.when(itself)
                def stay():
                    pltpu.make_async_copy(source.at[near, side], target.at[plane], local).start()

        for origin in range(PLANES):
            itself = (plane == origin) & mine
            landing = pltpu.make_async_remote_copy(
                src_ref=source.at[0, 0],
                dst_ref=target.at[origin],
                send_sem=out_send.at[0],
                recv_sem=out_recv.at[origin],
                device_id=at(plane, quad, flip(core)),
                device_id_type=MESH_ID,
            )

            @pl.when(jnp.logical_not(itself))
            def arrived():
                landing.wait_recv()

            @pl.when(itself)
            def kept():
                pltpu.make_async_copy(source.at[0, 0], target.at[origin], local).wait()

        for near in range(2):
            for side in range(2):
                itself = (2 * core + near == plane) & (core == side)

                @pl.when(jnp.logical_not(itself))
                def gone():
                    pltpu.make_async_remote_copy(
                        src_ref=source.at[near, side],
                        dst_ref=target.at[plane],
                        send_sem=out_send.at[2 * near + side],
                        recv_sem=out_recv.at[plane],
                        device_id=at(2 * core + near, quad, side),
                        device_id_type=MESH_ID,
                    ).wait_send()

    for copy in copies:
        copy.wait()


def push(ident, quads=(), planes=(), ranks=(), out=None):
    arrays = tuple(quads) + tuple(planes) + tuple(ranks) + (() if out is None else (out,))
    shapes = (
        [(QUADS - 1,) + a.shape[1:] for a in quads]
        + [(PLANES - 1,) + a.shape[1:] for a in planes]
        + [a.shape for a in ranks]
        + ([] if out is None else [(PLANES,) + out.shape[2:]])
    )
    copies = 3 * len(quads) + 3 * len(planes) + 7 * len(ranks)
    return pl.pallas_call(
        functools.partial(push_kernel, len(quads), len(planes), len(ranks), 0 if out is None else 1),
        out_shape=[jax.ShapeDtypeStruct(s, a.dtype) for s, a in zip(shapes, arrays)],
        in_specs=[ANY] * len(arrays),
        out_specs=[ANY] * len(arrays),
        scratch_shapes=[
            pltpu.SemaphoreType.DMA((copies,)),
            pltpu.SemaphoreType.DMA((copies,)),
            pltpu.SemaphoreType.DMA((4,)),
            pltpu.SemaphoreType.DMA((4,)),
            pltpu.SemaphoreType.DMA,
        ],
        compiler_params=pltpu.CompilerParams(collective_id=ident, has_side_effects=True),
    )(*arrays)


def owners_kernel(source, target, send, recv):
    plane, quad, core = place()
    mine = 2 * (plane * QUADS + quad) + core
    sems = Sems(send, recv)
    copies, peers = ([], [])
    for k in range(1, PLANES * RANKS):
        other_plane = xor4(plane, k // RANKS)
        other_quad = xor4(quad, (k % RANKS) // 2)
        other_core = flip(core) if k % 2 else core
        device = at(other_plane, other_quad, other_core)
        peers.append(device)
        index = 2 * (other_plane * QUADS + other_quad) + other_core
        copies.append(sems.copy(source.at[index], target.at[mine], device))
    greet(peers)
    for copy in copies:
        copy.start()
    for copy in copies:
        copy.wait()


def to_owners(ident, array):
    return pl.pallas_call(
        owners_kernel,
        out_shape=jax.ShapeDtypeStruct(array.shape, array.dtype),
        in_specs=[ANY],
        out_specs=ANY,
        scratch_shapes=[
            pltpu.SemaphoreType.DMA((PLANES * RANKS - 1,)),
            pltpu.SemaphoreType.DMA((PLANES * RANKS - 1,)),
        ],
        compiler_params=pltpu.CompilerParams(collective_id=ident, has_side_effects=True),
    )(array)


def share_kernel(source, target, send, recv):
    plane, quad, core = place()
    rank = 2 * quad + core
    sems = Sems(send, recv)
    mates = plane_mates(plane, quad, core)
    copies = [sems.copy(source, target.at[rank], device) for device in mates]
    greet(mates)
    for copy in copies:
        copy.start()
    for copy in copies:
        copy.wait()


def share(ident, array):
    return pl.pallas_call(
        share_kernel,
        out_shape=jax.ShapeDtypeStruct((RANKS,) + array.shape, array.dtype),
        in_specs=[ANY],
        out_specs=ANY,
        scratch_shapes=[pltpu.SemaphoreType.DMA((RANKS - 1,))] * 2,
        compiler_params=pltpu.CompilerParams(collective_id=ident, has_side_effects=True),
    )(array)


OWN_HEADS = HEADS // RANKS
OWN = OWN_HEADS * HDIM
RUN = OWN // 2
COMMON = 2 * NST + HEADS
COMMON_PAD = 384
GROUP = 2 * BLOCK


def pick_runs(array, plane_runs, quad, core):
    lead = array.shape[:-1]
    width = array.shape[-1] // (PLANES * QUADS)
    split = array.reshape(lead + (2, 2, QUADS, width))
    zero = 0
    n = len(lead)
    taken = lax.dynamic_slice(
        split, (zero,) * n + (core, 0, quad, 0), lead + (1, 2, 1, width)
    )
    return taken.reshape(lead + (2 * width,))


def put_runs(array, quad, core):
    lead = array.shape[:-1]
    width = array.shape[-1] // 2
    zeros = jnp.zeros(lead + (2, 2, QUADS, width), array.dtype)
    n = len(lead)
    full = lax.dynamic_update_slice(
        zeros, array.reshape(lead + (1, 2, 1, width)), (0,) * n + (core, 0, quad, 0)
    )
    return full.reshape(lead + (width * PLANES * QUADS,))


def rank_slices(array):
    rows = array.shape[0]
    split = array.reshape(rows, 2, 2, QUADS, RUN)
    return split.transpose(3, 1, 0, 2, 4).reshape(RANKS, rows, OWN)


def rank_join(array):
    rows = array.shape[1]
    split = array.reshape(QUADS, 2, rows, 2, RUN)
    return split.transpose(2, 1, 3, 0, 4).reshape(rows, DIN)


def mixer_quad(extended, step_raw, conv_par, head_values, live_rows):
    rows = step_raw.shape[1]
    preact = conv_par[KCONV][None, None, :]
    for tap in range(KCONV):
        preact = preact + conv_par[tap][None, None, :] * extended[:, tap : tap + rows]
    conv_act = jax.nn.silu(preact)
    step_size = jax.nn.softplus(step_raw + head_values[0]) * live_rows[:, :, None]
    logdec = -jnp.exp(head_values[1]) * step_size
    return (conv_act, step_size, logdec)


def two_blocks(values, keys_in, queries, step_size, logdec, skip_gain):
    start = jnp.zeros((OWN_HEADS, HDIM, NST), jnp.float32)
    outs = []
    for k in range(2):
        rows = slice(k * BLOCK, (k + 1) * BLOCK)
        out, start = block_full(
            values[rows], keys_in[rows], queries[rows], step_size[rows], logdec[rows], skip_gain, start
        )
        outs.append(out)
    return jnp.concatenate(outs, axis=0)


def per_device_quad(
    tokens_in,
    cotangent,
    seq_lens,
    in_weight,
    in_first,
    in_second,
    out_weight,
    out_first,
    out_second,
    conv_weight,
    conv_first,
    conv_second,
    gains,
    gain_first,
    gain_second,
    head_params,
    head_first,
    head_second,
):
    bf16, f32 = (jnp.bfloat16, jnp.float32)
    plane, quad, core = place()
    rank = 2 * quad + core
    rows = in_weight.shape[0]
    in_low = in_weight.astype(bf16)
    out_low = out_weight.astype(bf16)
    wz = jnp.concatenate([rank_slices(in_low[:, :DIN]), rank_slices(in_low[:, DIN : 2 * DIN])], axis=2)
    first_len = jnp.full((rows, 1), seq_lens[0, 0] - BLOCK).astype(bf16)
    conv_flat = jnp.pad(conv_weight.reshape(-1), (0, 8)).astype(bf16).reshape(rows, 11)
    wc = jnp.concatenate(
        [in_low[:, 2 * DIN :], gains.astype(bf16).reshape(rows, 3), conv_flat, first_len], axis=1
    )
    wc = jnp.pad(wc, ((0, 0), (0, COMMON_PAD - wc.shape[1])))
    tok, cot, w_own, w_com, w_out = gather_all(tokens_in, cotangent, wz, wc, out_low)
    tok = tok.reshape(RANKS * BLOCK, D)
    cot = cot.reshape(RANKS * BLOCK, D)
    w_own = w_own.reshape(D, 2 * OWN)
    w_out = w_out.reshape(OWN, D)
    extras = w_com[:, :, :, COMMON:].astype(f32)
    gain_par = extras[:, :, :, :3].reshape(D + DIN)
    conv_par = (
        extras[:, :, :, 3:14].reshape(PLANES * RANKS, 11 * rows)[:, : 5 * 104]
        .reshape(PLANES * RANKS, 5, 104).transpose(1, 0, 2).reshape(5, CONVC)
    )
    lens = lax.dynamic_index_in_dim(extras, plane, 0, False)[::2, 0, 14] + BLOCK
    w_com = w_com.reshape(D, COMMON_PAD)[:, :COMMON]
    live = (jnp.arange(GROUP)[None, :] < lens[:, None]).astype(f32)
    conv_own = jnp.concatenate([pick_runs(conv_par[:, :DIN], 2, quad, core), conv_par[:, DIN:]], axis=1)
    gain_out = pick_runs(gain_par[D:], 2, quad, core)
    head_own = pick_runs(head_params, 2, quad, core)

    scaling = lax.rsqrt(jnp.mean(jnp.square(tok.astype(f32)), axis=1, keepdims=True) + norm_eps)
    normed = (tok.astype(f32) * scaling * gain_par[:D]).astype(bf16)
    proj_own = jnp.dot(normed, w_own, preferred_element_type=f32)
    proj_com = jnp.dot(normed, w_com, preferred_element_type=f32)
    gate_part = proj_own[:, :OWN]
    conv_in = jnp.concatenate([proj_own[:, OWN:], proj_com[:, : 2 * NST]], axis=1)
    step_raw = pick_runs(proj_com[:, 2 * NST :], 2, quad, core)
    extended = jnp.pad(conv_in.reshape(QUADS, GROUP, -1), ((0, 0), (KCONV - 1, 0), (0, 0)))
    (conv_act, step_size, logdec), pull_mixer = jax.vjp(
        lambda *a: mixer_quad(*a, live), extended, step_raw.reshape(QUADS, GROUP, OWN_HEADS), conv_own, head_own
    )
    used = as_float(conv_act.astype(bf16))
    values = used[:, :, :OWN].reshape(QUADS, GROUP, OWN_HEADS, HDIM)
    keys_in = used[:, :, OWN : OWN + NST]
    queries = used[:, :, OWN + NST :]
    mixed, pull_ssd = jax.vjp(
        jax.vmap(two_blocks, in_axes=(0, 0, 0, 0, 0, None)), values, keys_in, queries, step_size, logdec, head_own[2]
    )
    mixed = mixed.reshape(RANKS * BLOCK, OWN)
    out_grad = (cot.astype(f32) * live.reshape(-1, 1)).astype(bf16)
    grad_normed_out = contract_cols(out_grad, w_out)
    sig = jax.nn.sigmoid(gate_part)
    gate_act = gate_part * sig
    gated = mixed * gate_act
    weighted = grad_normed_out * gain_out
    stats = jnp.stack([jnp.sum(gated * gated, axis=1), jnp.sum(weighted * gated, axis=1)])
    stats = stats.reshape(32, 128)
    shared = share(1, stats)
    ranks = lax.broadcasted_iota(jnp.int32, (RANKS, 1, 1), 0)
    total = jnp.sum(jnp.where(ranks == rank, stats[None], shared), axis=0).reshape(2, RANKS * BLOCK, 1)
    scale_out = lax.rsqrt(total[0] / DIN + norm_eps)
    normed_out = (gated * scale_out * gain_out).astype(bf16)
    branch = jnp.dot(normed_out, w_out, preferred_element_type=f32).astype(bf16)
    grad_out_w = contract_rows(normed_out, out_grad).astype(bf16)
    grad_gated = scale_out * weighted - gated * (scale_out**3 * total[1] / DIN)
    grad_gain_out = jnp.sum(grad_normed_out * gated * scale_out, axis=0)
    grad_gate = grad_gated * mixed * (sig * (1.0 + gate_part * (1.0 - sig)))
    mixed_back = as_float((grad_gated * gate_act).astype(bf16))
    grad_values, grad_keys, grad_queries, grad_step, grad_logdec, grad_skip = pull_ssd(
        mixed_back.reshape(QUADS, GROUP, OWN_HEADS, HDIM)
    )
    grad_act = jnp.concatenate([grad_values.reshape(QUADS, GROUP, OWN), grad_keys, grad_queries], axis=2)
    grad_ext, grad_raw, grad_conv_own, grad_head_own = pull_mixer((grad_act, grad_step, grad_logdec))
    grad_conv_in = grad_ext[:, KCONV - 1 :].reshape(RANKS * BLOCK, OWN + 2 * NST)
    grad_proj_own = jnp.concatenate([grad_gate, grad_conv_in[:, :OWN]], axis=1).astype(bf16)
    grad_raw = put_runs(grad_raw.reshape(RANKS * BLOCK, OWN_HEADS), quad, core)
    grad_proj_com = jnp.concatenate([grad_conv_in[:, OWN:], grad_raw], axis=1).astype(bf16)
    grad_normed = (contract_cols(grad_proj_own, w_own) + contract_cols(grad_proj_com, w_com)).astype(bf16)
    grad_own_w = contract_rows(normed, grad_proj_own).astype(bf16)
    grad_com_w = jnp.pad(contract_rows(normed, grad_proj_com), ((0, 0), (0, COMMON_PAD - COMMON))).astype(bf16)

    def by_core(array, lead):
        split = array.reshape((lead, 2) + array.shape[1:]) if array.shape[0] == 2 * lead else array
        return jnp.moveaxis(split, 1, 0)

    parts = (
        by_core(branch.reshape(RANKS, BLOCK, D), QUADS),
        by_core(grad_normed.reshape(RANKS, BLOCK, D), QUADS),
        by_core(grad_com_w.reshape(PLANES * QUADS * 2, rows, COMMON_PAD), PLANES * QUADS),
    )
    swapped = core_swap(2, *parts)

    def own_part(array, index):
        return lax.dynamic_index_in_dim(array, index, 0, False)

    sums = [
        (own_part(a, core).astype(f32) + b.astype(f32)).astype(bf16) for a, b in zip(parts, swapped)
    ]
    sums[2] = sums[2].reshape(PLANES, QUADS, rows, COMMON_PAD).transpose(1, 0, 2, 3)
    own_blocks = grad_own_w.reshape(PLANES, RANKS, rows, 2 * OWN)
    got = push(
        3,
        quads=sums,
        planes=(own_blocks,),
        out=grad_out_w.reshape(2, 2, out_weight.shape[0], D),
    )

    def add_up(own, index, others):
        return own_part(own, index).astype(f32) + jnp.sum(others.astype(f32), axis=0)

    branch_sum = add_up(sums[0], quad, got[0])
    normed_sum = add_up(sums[1], quad, got[1])
    com_sum = add_up(sums[2], quad, got[2]).astype(bf16)
    own_sum = add_up(own_blocks, plane, got[3]).astype(bf16)
    out_sum = jnp.sum(got[4].astype(f32), axis=0)
    com_got, own_got = push(4, planes=(com_sum,), ranks=(own_sum,))
    com_total = add_up(com_sum, plane, com_got)
    own_all = jnp.where(ranks == rank, own_sum, own_got).astype(f32)
    in_sum = jnp.concatenate(
        [rank_join(own_all[:, :, :OWN]), rank_join(own_all[:, :, OWN:]), com_total[:, :COMMON]], axis=1
    )

    token_rows = tokens_in.astype(f32)
    own_live = lax.dynamic_slice(live, (quad, core * BLOCK), (1, BLOCK)).reshape(BLOCK, 1)
    mixed_out = (token_rows + own_live * branch_sum).astype(bf16)
    normed_value, pull_pre = jax.vjp(pre_norm, token_rows, gain_par[:D])
    grad_rows, grad_gain_pre = pull_pre(normed_sum)
    grad_input = cotangent.astype(f32) + grad_rows

    grad_gains = jnp.concatenate([grad_gain_pre, put_runs(grad_gain_out, quad, core)]).reshape(32, 144)
    grad_conv = jnp.concatenate(
        [put_runs(grad_conv_own[:, :OWN], quad, core), grad_conv_own[:, OWN:]], axis=1
    ).reshape(5, 32, 104).transpose(1, 0, 2).reshape(32, 520)
    grad_head_own = grad_head_own + jnp.stack([jnp.zeros_like(grad_skip), jnp.zeros_like(grad_skip), grad_skip])
    grad_head = jnp.broadcast_to(put_runs(grad_head_own, quad, core).reshape(1, 144), (32, 144))
    small = jnp.concatenate([grad_gains, grad_conv, grad_head, jnp.zeros((32, 216), f32)], axis=1)
    small = small.reshape(32, 8, 128)
    small_got = to_owners(5, small)
    mine = rank + RANKS * plane
    owners = lax.broadcasted_iota(jnp.int32, (32, 1, 1), 0)
    small_sum = jnp.sum(jnp.where(owners == mine, small, small_got), axis=0).reshape(-1)
    gain_sum = small_sum[:144]
    conv_sum = small_sum[144:664].reshape(5, 104)
    head_sum = small_sum[664:808].reshape(3, 48)
    new_in = adam_update(in_weight, in_first, in_second, in_sum, rate_in)
    new_out = adam_update(out_weight, out_first, out_second, out_sum, rate_out)
    new_conv = adam_update(conv_weight, conv_first, conv_second, conv_sum, rate_conv)
    new_gain = adam_update(gains, gain_first, gain_second, gain_sum, rate_gain)
    new_head = adam_update(head_params, head_first, head_second, head_sum, rate_head)
    return (mixed_out, grad_input) + new_in + new_out + new_conv + new_gain + new_head


def solution(mesh):
    placed = (
        P(("dp", "seq"), None),
        P(("dp", "seq"), None),
        P("dp", None),
        P(("dp", "seq"), None),
        P(("dp", "seq"), None),
        P(("dp", "seq"), None),
        P(("dp", "seq"), None),
        P(("dp", "seq"), None),
        P(("dp", "seq"), None),
        P(None, ("dp", "seq")),
        P(None, ("dp", "seq")),
        P(None, ("dp", "seq")),
        P(("dp", "seq")),
        P(("dp", "seq")),
        P(("dp", "seq")),
        P(),
        P(),
        P(),
    )
    quad = dict(mesh.shape) == {"dp": PLANES * QUADS, "seq": 2}
    return jax.shard_map(
        per_device_quad if quad else per_device,
        mesh=mesh,
        in_specs=placed,
        out_specs=(
            P(("dp", "seq"), None),
            P(("dp", "seq"), None),
            P(("dp", "seq"), None),
            P(("dp", "seq"), None),
            P(("dp", "seq"), None),
            P(("dp", "seq"), None),
            P(("dp", "seq"), None),
            P(("dp", "seq"), None),
            P(None, ("dp", "seq")),
            P(None, ("dp", "seq")),
            P(None, ("dp", "seq")),
            P(("dp", "seq")),
            P(("dp", "seq")),
            P(("dp", "seq")),
            P(),
            P(),
            P(),
        ),
        check_vma=False,
    )
```

```python
import functools

import jax
import jax.numpy as jnp
from jax import lax
from jax.experimental import pallas as pl
from jax.experimental.pallas import tpu as pltpu
from jax.sharding import PartitionSpec as P

D = 1536
HEADS = 48
HDIM = 64
NST = 128
KCONV = 4
BLOCK = 256
SLOTS = 4
STEP = 10
DIN = 3072
CONVC = 3328


highest = lax.Precision.HIGHEST
norm_eps = 1e-05
beta_first = 0.9
beta_second = 0.95
adam_eps = 1e-08
weight_decay = 0.1
rate_in = 0.01
rate_out = 0.008
rate_conv = 0.2
rate_gain = 0.4
rate_head = 0.5


def from_behind(block, axis, distance):
    devices = range(lax.axis_size(axis))
    route = [(i - distance, i) for i in devices if i - distance in devices]
    return lax.ppermute(block, axis, route)


def prefix(value, axis, join, neutral):
    place = lax.axis_index(axis)
    gathered = jax.tree.map(
        lambda a, kind: lax.all_gather(a.astype(kind), axis),
        value,
        jax.tree.map(lambda a: jnp.bfloat16 if a.dtype == jnp.float32 else a.dtype, value),
    )
    state = jax.tree.map(lambda a, e: jnp.zeros_like(a) + jnp.asarray(e, a.dtype), value, neutral)

    def one(hop, state):
        return join(
            state,
            jax.tree.map(
                lambda a, own: lax.dynamic_index_in_dim(a, hop, 0, False).astype(own.dtype),
                gathered,
                value,
            ),
        )

    return lax.fori_loop(0, place, one, state)


def prefix_2(value, axis, combine, identity):
    devices, index = (lax.axis_size(axis), lax.axis_index(axis))
    everything = jax.tree.map(
        lambda part, kind: lax.all_gather(part.astype(kind), axis),
        value,
        (jnp.bfloat16, jnp.bfloat16),
    )
    start = jax.tree.map(
        lambda part, zero: jnp.broadcast_to(jnp.asarray(zero, part.dtype), part.shape),
        value,
        identity,
    )

    def hop(k, before):
        at = devices - 1 - k
        reached = at > index
        new = combine(
            before, jax.tree.map(lambda part, own: part[at].astype(own.dtype), everything, value)
        )
        return jax.tree.map(lambda a, b: jnp.where(reached, a, b), new, before)

    return lax.fori_loop(0, devices, hop, start)


def segment_of(seq_row, position):
    blocks = (seq_row + BLOCK - 1) // BLOCK
    ends = jnp.cumsum(blocks) * BLOCK
    starts = ends - blocks * BLOCK
    above = position[:, None] >= starts[None, :]
    inside = above & (position[:, None] < ends[None, :])
    numbers = jnp.arange(1, SLOTS + 1, dtype=jnp.int32)
    labels_of = jnp.sum(jnp.where(inside, numbers[None, :], 0), axis=1)
    live_rows = jnp.sum(
        (above & (position[:, None] < (starts + seq_row)[None, :])).astype(jnp.float32), axis=1
    )
    return (labels_of, live_rows)


def layout(seq_row, position):
    labels_of, live_rows = segment_of(seq_row, position)
    columns = []
    for conv_lag in range(KCONV):
        earlier, unused_live = segment_of(seq_row, position - conv_lag)
        columns.append(((earlier == labels_of) & (labels_of > 0)).astype(jnp.float32))
    return (live_rows, jnp.stack(columns, axis=1))


def pre_norm(token_rows, gain_row):
    scaling = lax.rsqrt(jnp.mean(token_rows * token_rows, axis=1, keepdims=True) + norm_eps)
    return token_rows * scaling * gain_row[None, :]


def gate_norm(mixed, gate_part, gain_row):
    gated = mixed * jax.nn.silu(gate_part)
    scaling = lax.rsqrt(jnp.mean(gated * gated, axis=1, keepdims=True) + norm_eps)
    return gated * scaling * gain_row[None, :]


def mixer_in(extended, step_raw, conv_par, head_values, factors, live_rows):
    row_count = step_raw.shape[0]
    preact = jnp.zeros((row_count, conv_par.shape[1]), jnp.float32) + conv_par[KCONV][None, :]
    for conv_tap in range(KCONV):
        window = lax.slice_in_dim(extended, conv_tap, conv_tap + row_count, axis=0)
        preact = (
            preact
            + conv_par[conv_tap][None, :] * window * factors[:, KCONV - 1 - conv_tap][:, None]
        )
    conv_act = jax.nn.silu(preact)
    step_size = jax.nn.softplus(step_raw + head_values[0][None, :]) * live_rows[:, None]
    logdec = -jnp.exp(head_values[1])[None, :] * step_size
    return (conv_act, step_size, logdec)


def lower_ones():
    row_ids = lax.broadcasted_iota(jnp.int32, (BLOCK, BLOCK), 0)
    col_ids = lax.broadcasted_iota(jnp.int32, (BLOCK, BLOCK), 1)
    return (row_ids >= col_ids).astype(jnp.float32)


def block_state(values, keys_in, step_size, logdec):
    cumul = jnp.dot(lower_ones(), logdec, precision=highest)
    totals = cumul[-1]
    weighting = jnp.exp(totals[None, :] - cumul) * step_size
    states = jnp.einsum("uhp,un->hpn", weighting[:, :, None] * values, keys_in, precision=highest)
    return (jnp.exp(totals), states)


def block_out(values, keys_in, queries, step_size, logdec, skip_gain, start_state):
    lower_tri = lower_ones()
    cumul = jnp.dot(lower_tri, logdec, precision=highest)
    across = cumul.T
    gap_matrix = across[:, :, None] - across[:, None, :]
    decays = jnp.exp(jnp.where(lower_tri[None, :, :] > 0, gap_matrix, -1e30))
    gram_matrix = jnp.dot(queries, keys_in.T, precision=highest)
    mixing = gram_matrix[None, :, :] * decays * step_size.T[:, None, :]
    intra_part = jnp.einsum("htu,uhp->thp", mixing, values, precision=highest)
    carried = jnp.exp(cumul)[:, :, None] * jnp.einsum(
        "tn,hpn->thp", queries, start_state, precision=highest
    )
    return intra_part + carried + skip_gain[None, :, None] * values


def block_full(values, keys_in, queries, step_size, logdec, skip_gain, start_state):
    factor_end, states = block_state(values, keys_in, step_size, logdec)
    outputs = block_out(values, keys_in, queries, step_size, logdec, skip_gain, start_state)
    return (outputs, factor_end[:, None, None] * start_state + states)


def adam_update(weight, first, second, gradient, step_rate):
    first_new = beta_first * first + (1.0 - beta_first) * gradient
    second_new = beta_second * second + (1.0 - beta_second) * gradient * gradient
    first_hat = first_new / (1.0 - beta_first**STEP)
    second_hat = second_new / (1.0 - beta_second**STEP)
    weight_new = weight - step_rate * (
        first_hat / (jnp.sqrt(second_hat) + adam_eps) + weight_decay * weight
    )
    return (weight_new, first_new, second_new)


def carry_join(earlier, later):
    return (earlier[0] * later[0], later[0][:, None, None] * earlier[1] + later[1])


def as_float(array_low):
    return lax.optimization_barrier(array_low).astype(jnp.float32)


def contract_rows(left, right):
    return lax.dot_general(
        left, right, (((0,), (0,)), ((), ())), preferred_element_type=jnp.float32
    )


def contract_cols(left, right):
    return lax.dot_general(
        left, right, (((1,), (1,)), ((), ())), preferred_element_type=jnp.float32
    )


def per_device(
    tokens_in,
    cotangent,
    seq_lens,
    in_weight,
    in_first,
    in_second,
    out_weight,
    out_first,
    out_second,
    conv_weight,
    conv_first,
    conv_second,
    gains,
    gain_first,
    gain_second,
    head_params,
    head_first,
    head_second,
):
    local_tok = tokens_in.shape[0]
    position = lax.axis_index("seq") * local_tok + jnp.arange(local_tok, dtype=jnp.int32)
    live_rows, factors = layout(seq_lens[0], position)
    low_weights = (
        in_weight.astype(jnp.bfloat16),
        out_weight.astype(jnp.bfloat16),
        conv_weight.astype(jnp.bfloat16),
        gains.astype(jnp.bfloat16),
    )
    in_full, out_full, conv_full, gain_full = (
        lax.all_gather(low_weights[0], ("dp", "seq"), axis=0, tiled=True),
        lax.all_gather(low_weights[1], ("dp", "seq"), axis=0, tiled=True),
        lax.all_gather(low_weights[2], ("dp", "seq"), axis=1, tiled=True),
        lax.all_gather(low_weights[3], ("dp", "seq"), axis=0, tiled=True),
    )
    conv_par = conv_full.astype(jnp.float32)
    gain_par = gain_full.astype(jnp.float32)
    token_rows = tokens_in.astype(jnp.float32)
    normed_value, pull_pre = jax.vjp(pre_norm, token_rows, gain_par[:D])
    normed = normed_value.astype(jnp.bfloat16)
    projected = jnp.dot(normed, in_full, preferred_element_type=jnp.float32)
    gate_part = projected[:, :DIN]
    conv_in = projected[:, DIN : DIN + CONVC]
    step_raw = projected[:, DIN + CONVC :]
    halo_rows = from_behind(conv_in[local_tok - KCONV + 1 :], "seq", 1)
    extended = jnp.concatenate([halo_rows, conv_in], axis=0)

    def mixer_local(extended_rows, raw_steps, conv_values, head_values):
        return mixer_in(extended_rows, raw_steps, conv_values, head_values, factors, live_rows)

    (conv_act, step_size, logdec), pull_mixer = jax.vjp(
        mixer_local, extended, step_raw, conv_par, head_params
    )
    conv_used = as_float(conv_act.astype(jnp.bfloat16))
    block_count = local_tok // BLOCK
    values = conv_used[:, :DIN].reshape(block_count, BLOCK, HEADS, HDIM)
    keys_in = conv_used[:, DIN : DIN + NST].reshape(block_count, BLOCK, NST)
    queries = conv_used[:, DIN + NST :].reshape(block_count, BLOCK, NST)
    steps_blk = step_size.reshape(block_count, BLOCK, HEADS)
    logdec_blk = logdec.reshape(block_count, BLOCK, HEADS)
    resets = factors[::BLOCK, 1]
    skip_gain = head_params[2]
    decays, block_states = jax.vmap(block_state)(values, keys_in, steps_blk, logdec_blk)

    def fold_local(carried, block_item):
        factor_now = block_item[0] * block_item[2]
        return (
            (carried[0] * factor_now, factor_now[:, None, None] * carried[1] + block_item[1]),
            None,
        )

    identity = (jnp.ones((HEADS,), jnp.float32), jnp.zeros((HEADS, HDIM, NST), jnp.float32))
    device_sum, unused_fold = lax.scan(fold_local, identity, (decays, block_states, resets))
    unused_dec, entering = prefix(device_sum, "seq", carry_join, identity)

    def start_states(states, block_item):
        begin = block_item[2] * states
        return (block_item[0][:, None, None] * begin + block_item[1], begin)

    unused_end, begins = lax.scan(start_states, entering, (decays, block_states, resets))

    def emit(block_item):
        return block_out(
            block_item[0],
            block_item[1],
            block_item[2],
            block_item[3],
            block_item[4],
            skip_gain,
            block_item[5],
        )

    mixed = lax.map(emit, (values, keys_in, queries, steps_blk, logdec_blk, begins)).reshape(
        local_tok, DIN
    )
    normed_out_value, pull_gate = jax.vjp(gate_norm, mixed, gate_part, gain_par[D:])
    normed_out = normed_out_value.astype(jnp.bfloat16)
    branch = jnp.dot(normed_out, out_full, preferred_element_type=jnp.float32)
    mixed_out = (token_rows + live_rows[:, None] * branch).astype(jnp.bfloat16)
    out_grad = (cotangent.astype(jnp.float32) * live_rows[:, None]).astype(jnp.bfloat16)
    in_back, out_back = (
        lax.all_gather(in_weight.astype(jnp.bfloat16), ("dp", "seq"), axis=0, tiled=True),
        lax.all_gather(out_weight.astype(jnp.bfloat16), ("dp", "seq"), axis=0, tiled=True),
    )
    grad_out_w = contract_rows(normed_out, out_grad)
    grad_normed_out = contract_cols(out_grad, out_back)
    grad_mixed, grad_gate, grad_gain_in = pull_gate(grad_normed_out)
    mixed_back = as_float(grad_mixed.astype(jnp.bfloat16)).reshape(block_count, BLOCK, HEADS, HDIM)

    def adjoint_local(carried, block_item):
        cumul = jnp.dot(lower_ones(), block_item[2], precision=highest)
        weighted = jnp.exp(cumul)[:, :, None] * block_item[0]
        direct = jnp.einsum("thp,tn->hpn", weighted, block_item[1], precision=highest)
        return (block_item[4] * (direct + block_item[3][:, None, None] * carried), None)

    local_adj, unused_adj = lax.scan(
        adjoint_local, identity[1], (mixed_back, queries, logdec_blk, decays, resets), reverse=True
    )
    unused_later, leaving = prefix_2((device_sum[0], local_adj), "seq", carry_join, identity)

    def adjoint_block(carried, block_item):
        unused_primal, pull_block = jax.vjp(
            block_full,
            block_item[0],
            block_item[1],
            block_item[2],
            block_item[3],
            block_item[4],
            skip_gain,
            block_item[5],
        )
        grads = pull_block((block_item[6], carried[0]))
        return ((block_item[7] * grads[6], carried[1] + grads[5]), grads[:5])

    (unused_state, grad_skip), block_grads = lax.scan(
        adjoint_block,
        (leaving, jnp.zeros((HEADS,), jnp.float32)),
        (values, keys_in, queries, steps_blk, logdec_blk, begins, mixed_back, resets),
        reverse=True,
    )
    grad_values, grad_keys, grad_queries, grad_step, grad_logdec = block_grads
    grad_act = jnp.concatenate(
        [
            grad_values.reshape(local_tok, DIN),
            grad_keys.reshape(local_tok, NST),
            grad_queries.reshape(local_tok, NST),
        ],
        axis=1,
    )
    grad_ext, grad_raw, grad_conv, grad_head_part = pull_mixer(
        (grad_act, grad_step.reshape(local_tok, HEADS), grad_logdec.reshape(local_tok, HEADS))
    )
    returned = from_behind(grad_ext[: KCONV - 1].astype(jnp.bfloat16), "seq", -1).astype(
        jnp.float32
    )
    grad_conv_in = grad_ext[KCONV - 1 :] + jnp.concatenate(
        [jnp.zeros((local_tok - KCONV + 1, CONVC), jnp.float32), returned], axis=0
    )
    grad_proj = jnp.concatenate([grad_gate, grad_conv_in, grad_raw], axis=1).astype(jnp.bfloat16)
    grad_normed = contract_cols(grad_proj, in_back)
    grad_rows, grad_gain_pre = pull_pre(grad_normed)
    grad_input = cotangent.astype(jnp.float32) + grad_rows
    grad_gains = jnp.concatenate([grad_gain_pre, grad_gain_in], axis=0)
    grad_head = jnp.concatenate(
        [grad_head_part[:2], (grad_head_part[2] + grad_skip)[None, :]], axis=0
    )
    grad_in_w = contract_rows(normed, grad_proj)
    in_sum, out_sum, conv_sum, gain_sum = (
        lax.psum_scatter(grad_in_w, ("dp", "seq"), scatter_dimension=0, tiled=True),
        lax.psum_scatter(grad_out_w, ("dp", "seq"), scatter_dimension=0, tiled=True),
        lax.psum_scatter(grad_conv, ("dp", "seq"), scatter_dimension=1, tiled=True),
        lax.psum_scatter(grad_gains, ("dp", "seq"), scatter_dimension=0, tiled=True),
    )
    head_sum = lax.psum(grad_head, ("dp", "seq"))
    new_in = adam_update(in_weight, in_first, in_second, in_sum, rate_in)
    new_out = adam_update(out_weight, out_first, out_second, out_sum, rate_out)
    new_conv = adam_update(conv_weight, conv_first, conv_second, conv_sum, rate_conv)
    new_gain = adam_update(gains, gain_first, gain_second, gain_sum, rate_gain)
    new_head = adam_update(head_params, head_first, head_second, head_sum, rate_head)
    return (
        mixed_out,
        grad_input,
        new_in[0],
        new_in[1],
        new_in[2],
        new_out[0],
        new_out[1],
        new_out[2],
        new_conv[0],
        new_conv[1],
        new_conv[2],
        new_gain[0],
        new_gain[1],
        new_gain[2],
        new_head[0],
        new_head[1],
        new_head[2],
    )


MESH_ID = pl.DeviceIdType.MESH
ANY = pl.BlockSpec(memory_space=pl.ANY)
PLANES = 4
QUADS = 4
RANKS = 8


def place():
    chip = lax.axis_index("dp")
    return (chip // QUADS, chip % QUADS, lax.axis_index("seq"))


def at(plane, quad, core):
    return (plane * QUADS + quad, core)


def flip(core):
    return 1 - core


def xor4(value, k):
    low, high = value % 2, value // 2
    if k % 2:
        low = 1 - low
    if k // 2:
        high = 1 - high
    return 2 * high + low


def greet(devices):
    barrier = pltpu.get_barrier_semaphore()
    for device in devices:
        pl.semaphore_signal(barrier, inc=1, device_id=device, device_id_type=MESH_ID)
    pl.semaphore_wait(barrier, len(devices))


def plane_mates(plane, quad, core):
    mates = []
    for k in range(QUADS):
        for other in (core, flip(core)):
            if not (k == 0 and other is core):
                mates.append(at(plane, xor4(quad, k), other))
    return mates


def plane_others(plane, quad, core):
    return [at(xor4(plane, k), quad, core) for k in range(1, PLANES)]


class Sems:
    def __init__(self, send, recv):
        self.send, self.recv, self.used = (send, recv, 0)

    def copy(self, source, target, device):
        index = self.used
        self.used += 1
        return pltpu.make_async_remote_copy(
            src_ref=source,
            dst_ref=target,
            send_sem=self.send.at[index],
            recv_sem=self.recv.at[index],
            device_id=device,
            device_id_type=MESH_ID,
        )


class PlaneGather:
    def __init__(self, sems, own, block, plane, quad, core):
        near_x, near_y, far = (xor4(quad, k) for k in (1, 2, 3))
        rank = 2 * quad + core
        rank_x, rank_y, rank_far = (2 * q + core for q in (near_x, near_y, far))
        to_x, to_y = (at(plane, near_x, core), at(plane, near_y, core))
        sibling = at(plane, quad, flip(core))
        whole = [0, 1]
        self.own = [
            sems.copy(own(h), block(rank, h), device)
            for device in (to_x, to_y, sibling)
            for h in whole
        ]
        self.relay_x = [
            sems.copy(block(rank_x, 0), block(rank_x, 0), to_y),
        ] + [sems.copy(block(rank_x, h), block(rank_x, h), sibling) for h in whole]
        self.relay_y = [
            sems.copy(block(rank_y, 1), block(rank_y, 1), to_x),
        ] + [sems.copy(block(rank_y, h), block(rank_y, h), sibling) for h in whole]
        self.relay_far = [
            sems.copy(block(rank_far, h), block(rank_far, h), sibling) for h in whole
        ]

    def start(self):
        for copy in self.own:
            copy.start()

    def forward(self):
        self.own[0].wait_recv()
        self.relay_x[0].start()
        self.own[3].wait_recv()
        self.relay_y[0].start()
        self.own[1].wait_recv()
        self.own[2].wait_recv()
        for copy in self.relay_x[1:] + self.relay_y[1:]:
            copy.start()

    def finish(self):
        for h, relay in ((0, self.relay_x[0]), (1, self.relay_y[0])):
            relay.wait_recv()
            self.relay_far[h].start()
        for copy in self.own[4:] + self.relay_x[1:] + self.relay_y[1:] + self.relay_far:
            copy.wait_recv()
        for copy in self.own + self.relay_x + self.relay_y + self.relay_far:
            copy.wait_send()


class LineGather:
    def __init__(self, sems, own, block, plane, quad, core):
        self.plane = plane
        self.right, self.left = ([], [])
        for hop in range(PLANES - 1):
            for copies, step in ((self.right, 1), (self.left, -1)):
                index = plane - step * hop
                source = own if hop == 0 else block(index)
                copies.append(sems.copy(source, block(index), at(plane + step, quad, core)))

    def sends(self, hop, step):
        if step > 0:
            return (self.plane - hop >= 0) & (self.plane < PLANES - 1)
        return (self.plane + hop < PLANES) & (self.plane > 0)

    def receives(self, hop, step):
        if step > 0:
            return self.plane - 1 - hop >= 0
        return self.plane + 1 + hop < PLANES

    def start(self, hop):
        for copies, step in ((self.right, 1), (self.left, -1)):

            @pl.when(self.sends(hop, step))
            def go():
                copies[hop].start()

    def arrive(self, hop):
        for copies, step in ((self.right, 1), (self.left, -1)):

            @pl.when(self.receives(hop, step))
            def landed():
                copies[hop].wait_recv()

    def sent(self):
        for hop in range(PLANES - 1):
            for copies, step in ((self.right, 1), (self.left, -1)):

                @pl.when(self.sends(hop, step))
                def left():
                    copies[hop].wait_send()


def gather_kernel(tok, cot, wz, wc, wo, o_tok, o_cot, o_wz, o_wc, s_wo, o_wo, send, recv, local):
    plane, quad, core = place()
    rank = 2 * quad + core
    sibling = at(plane, quad, flip(core))
    sems = Sems(send, recv)
    where = (plane, quad, core)
    locals_ = []

    def keep(source, target):
        copy = pltpu.make_async_copy(source, target, local.at[len(locals_)])
        locals_.append(copy)
        copy.start()
        return copy

    half = tok.shape[0] // 2
    rows = wc.shape[0]

    def token_block(buffer):
        return lambda r, h: buffer.at[r, pl.ds(h * half, half)]

    def token_own(buffer):
        return lambda h: buffer.at[pl.ds(h * half, half)]

    line_c = LineGather(sems, wc, lambda q: o_wc.at[q, rank], *where)
    line_o = LineGather(sems, wo, lambda q: s_wo.at[q], *where)
    shuffle = []
    for k in range(1, RANKS):
        other_core = flip(core) if k % 2 else core
        other_quad = xor4(quad, k // 2)
        shuffle.append(
            sems.copy(wz.at[2 * other_quad + other_core], o_wz.at[plane, rank], at(plane, other_quad, other_core))
        )
    halves = [
        LineGather(
            sems,
            o_wz.at[plane, pl.ds(4 * h, 4)],
            lambda q, h=h: o_wz.at[q, pl.ds(4 * h, 4)],
            *where,
        )
        for h in range(2)
    ]
    tokens = PlaneGather(sems, token_own(tok), token_block(o_tok), *where)
    grads = PlaneGather(sems, token_own(cot), token_block(o_cot), *where)
    common = PlaneGather(
        sems,
        lambda h: o_wc.at[pl.ds(2 * h, 2), rank],
        lambda r, h: o_wc.at[pl.ds(2 * h, 2), r],
        *where,
    )
    cross_o = [
        sems.copy(s_wo.at[2 * flip(core) + k], o_wo.at[k, core], sibling) for k in range(2)
    ]

    greet(plane_mates(*where) + plane_others(*where))
    line_c.start(0)
    for copy in shuffle:
        copy.start()
    line_o.start(0)
    tokens.start()
    own_wz = keep(wz.at[rank], o_wz.at[plane, rank])
    own_wc = keep(wc, o_wc.at[plane, rank])
    own_wo = keep(wo, s_wo.at[plane])
    own_tok = keep(tok, o_tok.at[rank])
    own_cot = keep(cot, o_cot.at[rank])
    own_wz.wait()
    for copy in shuffle:
        copy.wait_recv()
    halves[0].start(0)
    halves[1].start(0)
    for hop in range(PLANES - 1):
        line_c.arrive(hop)
        if hop < PLANES - 2:
            line_c.start(hop + 1)
    own_wc.wait()
    common.start()
    tokens.forward()
    grads.start()
    common.forward()
    for hop in range(PLANES - 1):
        for h in range(2):
            halves[h].arrive(hop)
            if hop < PLANES - 2:
                halves[h].start(hop + 1)
        line_o.arrive(hop)
        if hop < PLANES - 2:
            line_o.start(hop + 1)
        if hop == 0:
            tokens.finish()
            common.finish()
    own_wo.wait()
    keeps = []
    for copy in cross_o:
        copy.start()
    keeps = [keep(s_wo.at[2 * core + k], o_wo.at[k, core]) for k in range(2)]
    grads.forward()
    grads.finish()
    for copy in cross_o:
        copy.wait()
    for copy in shuffle:
        copy.wait_send()
    for line in halves + [line_c, line_o]:
        line.sent()
    for copy in [own_tok, own_cot] + keeps:
        copy.wait()


def gather_all(tok, cot, wz, wc, wo):
    bf16 = jnp.bfloat16
    shapes = (
        (RANKS,) + tok.shape,
        (RANKS,) + cot.shape,
        (PLANES,) + wz.shape,
        (PLANES, RANKS) + wc.shape,
        (PLANES,) + wo.shape,
        (2, 2) + wo.shape,
    )
    outs = pl.pallas_call(
        gather_kernel,
        out_shape=[jax.ShapeDtypeStruct(s, bf16) for s in shapes],
        in_specs=[ANY] * 5,
        out_specs=[ANY] * 6,
        scratch_shapes=[
            pltpu.SemaphoreType.DMA((80,)),
            pltpu.SemaphoreType.DMA((80,)),
            pltpu.SemaphoreType.DMA((8,)),
        ],
        compiler_params=pltpu.CompilerParams(collective_id=0, has_side_effects=True),
    )(tok, cot, wz, wc, wo)
    return (outs[0], outs[1], outs[2], outs[3], outs[5])


def core_kernel(*refs):
    count = (len(refs) - 2) // 2
    sources, targets, (send, recv) = (refs[:count], refs[count : 2 * count], refs[2 * count :])
    plane, quad, core = place()
    sibling = at(plane, quad, flip(core))
    sems = Sems(send, recv)
    copies = [sems.copy(s.at[flip(core)], t, sibling) for s, t in zip(sources, targets)]
    greet([sibling])
    for copy in copies:
        copy.start()
    for copy in copies:
        copy.wait()


def core_swap(ident, *arrays):
    count = len(arrays)
    return pl.pallas_call(
        core_kernel,
        out_shape=[jax.ShapeDtypeStruct(a.shape[1:], a.dtype) for a in arrays],
        in_specs=[ANY] * count,
        out_specs=[ANY] * count,
        scratch_shapes=[pltpu.SemaphoreType.DMA((count,)), pltpu.SemaphoreType.DMA((count,))],
        compiler_params=pltpu.CompilerParams(collective_id=ident, has_side_effects=True),
    )(*arrays)


def push_kernel(n_quad, n_plane, n_rank, with_out, *refs):
    count = n_quad + n_plane + n_rank + with_out
    sources, targets = (refs[:count], refs[count : 2 * count])
    send, recv, out_send, out_recv, local = refs[2 * count :]
    plane, quad, core = place()
    where = (plane, quad, core)
    rank = 2 * quad + core
    sems = Sems(send, recv)
    copies = []
    peers = []
    if n_plane or with_out:
        peers += plane_others(*where)
    if with_out:
        peers += [at(xor4(plane, k), quad, flip(core)) for k in range(PLANES)]
    if n_rank:
        peers += plane_mates(*where)
    elif n_quad:
        peers += [at(plane, xor4(quad, k), core) for k in range(1, QUADS)]
    index = n_quad
    for i in range(n_plane):
        for k in (2, 3, 1):
            other = xor4(plane, k)
            copies.append(
                sems.copy(sources[index + i].at[other], targets[index + i].at[k - 1], at(other, quad, core))
            )
    for i in range(n_quad):
        for k in (3, 1, 2):
            other = xor4(quad, k)
            copies.append(sems.copy(sources[i].at[other], targets[i].at[k - 1], at(plane, other, core)))
    index += n_plane
    for i in range(n_rank):
        for k in range(1, RANKS):
            other_core = flip(core) if k % 2 else core
            other_quad = xor4(quad, k // 2)
            copies.append(
                sems.copy(
                    sources[index + i].at[2 * other_quad + other_core],
                    targets[index + i].at[rank],
                    at(plane, other_quad, other_core),
                )
            )
    index += n_rank
    greet(peers)
    for copy in copies:
        copy.start()
    if with_out:
        source, target = (sources[index], targets[index])
        mine = (plane // 2 == core)
        for near in range(2):
            for side in range(2):
                to_plane = 2 * core + near
                itself = (to_plane == plane) & (core == side)
                remote = pltpu.make_async_remote_copy(
                    src_ref=source.at[near, side],
                    dst_ref=target.at[plane],
                    send_sem=out_send.at[2 * near + side],
                    recv_sem=out_recv.at[plane],
                    device_id=at(to_plane, quad, side),
                    device_id_type=MESH_ID,
                )

                @pl.when(jnp.logical_not(itself))
                def go():
                    remote.start()

                @pl.when(itself)
                def stay():
                    pltpu.make_async_copy(source.at[near, side], target.at[plane], local).start()

        for origin in range(PLANES):
            itself = (plane == origin) & mine
            landing = pltpu.make_async_remote_copy(
                src_ref=source.at[0, 0],
                dst_ref=target.at[origin],
                send_sem=out_send.at[0],
                recv_sem=out_recv.at[origin],
                device_id=at(plane, quad, flip(core)),
                device_id_type=MESH_ID,
            )

            @pl.when(jnp.logical_not(itself))
            def arrived():
                landing.wait_recv()

            @pl.when(itself)
            def kept():
                pltpu.make_async_copy(source.at[0, 0], target.at[origin], local).wait()

        for near in range(2):
            for side in range(2):
                itself = (2 * core + near == plane) & (core == side)

                @pl.when(jnp.logical_not(itself))
                def gone():
                    pltpu.make_async_remote_copy(
                        src_ref=source.at[near, side],
                        dst_ref=target.at[plane],
                        send_sem=out_send.at[2 * near + side],
                        recv_sem=out_recv.at[plane],
                        device_id=at(2 * core + near, quad, side),
                        device_id_type=MESH_ID,
                    ).wait_send()

    for copy in copies:
        copy.wait()


def push(ident, quads=(), planes=(), ranks=(), out=None):
    arrays = tuple(quads) + tuple(planes) + tuple(ranks) + (() if out is None else (out,))
    shapes = (
        [(QUADS - 1,) + a.shape[1:] for a in quads]
        + [(PLANES - 1,) + a.shape[1:] for a in planes]
        + [a.shape for a in ranks]
        + ([] if out is None else [(PLANES,) + out.shape[2:]])
    )
    copies = 3 * len(quads) + 3 * len(planes) + 7 * len(ranks)
    return pl.pallas_call(
        functools.partial(push_kernel, len(quads), len(planes), len(ranks), 0 if out is None else 1),
        out_shape=[jax.ShapeDtypeStruct(s, a.dtype) for s, a in zip(shapes, arrays)],
        in_specs=[ANY] * len(arrays),
        out_specs=[ANY] * len(arrays),
        scratch_shapes=[
            pltpu.SemaphoreType.DMA((copies,)),
            pltpu.SemaphoreType.DMA((copies,)),
            pltpu.SemaphoreType.DMA((4,)),
            pltpu.SemaphoreType.DMA((4,)),
            pltpu.SemaphoreType.DMA,
        ],
        compiler_params=pltpu.CompilerParams(collective_id=ident, has_side_effects=True),
    )(*arrays)


def owners_kernel(source, target, send, recv):
    plane, quad, core = place()
    mine = 2 * (plane * QUADS + quad) + core
    sems = Sems(send, recv)
    copies, peers = ([], [])
    for k in range(1, PLANES * RANKS):
        other_plane = xor4(plane, k // RANKS)
        other_quad = xor4(quad, (k % RANKS) // 2)
        other_core = flip(core) if k % 2 else core
        device = at(other_plane, other_quad, other_core)
        peers.append(device)
        index = 2 * (other_plane * QUADS + other_quad) + other_core
        copies.append(sems.copy(source.at[index], target.at[mine], device))
    greet(peers)
    for copy in copies:
        copy.start()
    for copy in copies:
        copy.wait()


def to_owners(ident, array):
    return pl.pallas_call(
        owners_kernel,
        out_shape=jax.ShapeDtypeStruct(array.shape, array.dtype),
        in_specs=[ANY],
        out_specs=ANY,
        scratch_shapes=[
            pltpu.SemaphoreType.DMA((PLANES * RANKS - 1,)),
            pltpu.SemaphoreType.DMA((PLANES * RANKS - 1,)),
        ],
        compiler_params=pltpu.CompilerParams(collective_id=ident, has_side_effects=True),
    )(array)


def share_kernel(source, target, send, recv):
    plane, quad, core = place()
    rank = 2 * quad + core
    sems = Sems(send, recv)
    mates = plane_mates(plane, quad, core)
    copies = [sems.copy(source, target.at[rank], device) for device in mates]
    greet(mates)
    for copy in copies:
        copy.start()
    for copy in copies:
        copy.wait()


def share(ident, array):
    return pl.pallas_call(
        share_kernel,
        out_shape=jax.ShapeDtypeStruct((RANKS,) + array.shape, array.dtype),
        in_specs=[ANY],
        out_specs=ANY,
        scratch_shapes=[pltpu.SemaphoreType.DMA((RANKS - 1,))] * 2,
        compiler_params=pltpu.CompilerParams(collective_id=ident, has_side_effects=True),
    )(array)


OWN_HEADS = HEADS // RANKS
OWN = OWN_HEADS * HDIM
PAIRS = OWN_HEADS // 2
RUN = OWN // 2
COMMON = 2 * NST + HEADS
COMMON_PAD = 384
GROUP = 2 * BLOCK
MIX = OWN + 2 * NST
LANES = 128


def mm(left, right):
    return lax.dot_general(left, right, (((1,), (0,)), ((), ())), preferred_element_type=jnp.float32)


def mm_t(left, right):
    return lax.dot_general(left, right, (((1,), (1,)), ((), ())), preferred_element_type=jnp.float32)


def t_mm(left, right):
    return lax.dot_general(left, right, (((0,), (0,)), ((), ())), preferred_element_type=jnp.float32)


def mm_full(left, right):
    return lax.dot_general(
        left, right, (((1,), (0,)), ((), ())), precision=highest, preferred_element_type=jnp.float32
    )


def low16(value):
    return value.astype(jnp.bfloat16)


def iota(shape, axis):
    return lax.broadcasted_iota(jnp.int32, shape, axis)


def head_spread():
    return (iota((LANES, OWN), 1) // HDIM == iota((LANES, OWN), 0)).astype(jnp.float32)


def head_gather():
    return (iota((OWN, LANES), 0) // HDIM == iota((OWN, LANES), 1)).astype(jnp.float32)


def lower_mask():
    return iota((BLOCK, BLOCK), 0) >= iota((BLOCK, BLOCK), 1)


def shift_down(value, k):
    if k == 0:
        return value
    rolled = pltpu.roll(value, k, 0)
    return jnp.where(iota(value.shape, 0) >= k, rolled, 0.0)


def shift_up(value, k):
    if k == 0:
        return value
    rows = value.shape[0]
    rolled = pltpu.roll(value, rows - k, 0)
    return jnp.where(iota(value.shape, 0) < rows - k, rolled, 0.0)


def sigmoid(value):
    return 1.0 / (1.0 + jnp.exp(-value))


def softplus(value):
    return jnp.maximum(value, 0.0) + jnp.log1p(jnp.exp(-jnp.abs(value)))


def preact_of(u, conv):
    total = u * conv[KCONV - 1 : KCONV] + conv[KCONV : KCONV + 1]
    for tap in range(KCONV - 1):
        total = total + shift_down(u, KCONV - 1 - tap) * conv[tap : tap + 1]
    return total


def steps_of(raw, heads, live):
    step = softplus(raw + heads[0:1]) * live * heads[3:4]
    return (step, -jnp.exp(heads[1:2]) * step)


def decay_of(cumul, cumul_t, h):
    return jnp.exp(jnp.minimum(cumul[:, h : h + 1] - cumul_t[h : h + 1, :], 0.0))


def lane_half(value, side):
    lanes = iota(value.shape, 1)
    return jnp.where((lanes >= HDIM) == (side == 1), value, jnp.zeros_like(value))


def block_parts(step, logdec, spread):
    cumul = mm_full(lower_mask().astype(jnp.float32), logdec)
    return (cumul, jnp.transpose(cumul), mm_full(step, spread), mm_full(cumul, spread))


def forward_group(live, tok, cot, w_own, w_com, w_out, gain_in, gain_out, conv, heads, skip, select):
    token_rows = tok[...].astype(jnp.float32)
    scaling = lax.rsqrt(jnp.mean(token_rows * token_rows, axis=1, keepdims=True) + norm_eps)
    normed = low16(token_rows * scaling * gain_in[...])
    gate_part = mm(normed, w_own[:, :OWN])
    conv_in = jnp.concatenate([mm(normed, w_own[:, OWN:]), mm(normed, w_com[:, : 2 * NST])], axis=1)
    raw = mm_full(mm(normed, w_com[:, 2 * NST :]), select[...])
    preact = preact_of(conv_in, conv[...])
    act = low16(preact * sigmoid(preact))
    step, logdec = steps_of(raw, heads[...], live)
    spread = head_spread()
    lower = lower_mask()
    outs = []
    state = None
    for k in range(2):
        rows = slice(k * BLOCK, (k + 1) * BLOCK)
        values, keys, queries = (act[rows, :OWN], act[rows, OWN : OWN + NST], act[rows, OWN + NST :])
        cumul, cumul_t, step_w, cumul_w = block_parts(step[rows], logdec[rows], spread)
        gram = jnp.where(lower, mm_t(queries, keys), 0.0)
        values_f = values.astype(jnp.float32)
        stepped = low16(values_f * step_w)
        pieces = []
        for pair in range(PAIRS):
            lanes = slice(pair * LANES, (pair + 1) * LANES)
            piece = 0.0
            for side in range(2):
                mixing = low16(gram * decay_of(cumul, cumul_t, 2 * pair + side))
                piece = piece + mm(mixing, lane_half(stepped[:, lanes], side))
            pieces.append(piece)
        out = jnp.concatenate(pieces, axis=1) + skip[...] * values_f
        if state is not None:
            out = out + jnp.exp(cumul_w) * mm(queries, state)
        else:
            weighting = jnp.exp(cumul_w[BLOCK - 1 :] - cumul_w) * step_w
            state = low16(t_mm(keys, low16(weighting * values_f)))
        outs.append(out)
    mixed = jnp.concatenate(outs, axis=0)
    grad = jnp.where(live > 0.0, cot[...], jnp.zeros_like(cot[...]))
    grad_normed_out = mm_t(grad, w_out[...])
    gated = mixed * gate_part * sigmoid(gate_part)
    stats = (
        jnp.sum(gated * gated, axis=1, keepdims=True),
        jnp.sum(grad_normed_out * gain_out[...] * gated, axis=1, keepdims=True),
    )
    return (normed, gate_part, conv_in, raw, act, mixed, grad_normed_out, stats)


def live_of(lens, g):
    rows = iota((GROUP, 1), 0).astype(jnp.float32)
    chosen = jnp.sum(jnp.where(iota(lens.shape, 0) == g, lens, 0.0), axis=0, keepdims=True)[:, :1]
    return (rows < chosen).astype(jnp.float32)


def forward_kernel(
    lens, tok, cot, w_own, w_com, w_out, gain_in, gain_out, conv, heads, skip, select,
    normed, gate_part, conv_in, raw, act, mixed, grad_normed_out, stats
):
    g = pl.program_id(0)
    live = live_of(lens[...], g)
    results = forward_group(
        live, tok, cot, w_own, w_com, w_out, gain_in, gain_out, conv, heads, skip, select
    )
    for ref, value in zip((normed, gate_part, conv_in, raw, act, mixed, grad_normed_out), results):
        ref[...] = value
    lanes = iota((GROUP, LANES), 1)
    columns = jnp.where(lanes == 2 * g, results[7][0], 0.0) + jnp.where(lanes == 2 * g + 1, results[7][1], 0.0)

    @pl.when(g == 0)
    def first():
        stats[...] = jnp.zeros_like(stats)

    stats[...] += jnp.transpose(columns)[:8]


def full_spec(shape):
    return pl.BlockSpec(shape, lambda g: (0,) * len(shape))


def group_spec(width):
    return pl.BlockSpec((GROUP, width), lambda g: (g, 0))


VMEM_GRANT = 60 * 1024 * 1024


def run_forward(lens, tok, cot, w_own, w_com, w_out, gain_in, gain_out, conv, heads, skip, select):
    f32, bf16 = (jnp.float32, jnp.bfloat16)
    rows = QUADS * GROUP
    widths = ((D, bf16), (OWN, f32), (MIX, f32), (LANES, f32), (MIX, bf16), (OWN, f32), (OWN, f32))
    return pl.pallas_call(
        forward_kernel,
        grid=(QUADS,),
        in_specs=[full_spec(lens.shape), group_spec(D), group_spec(D)]
        + [full_spec(a.shape) for a in (w_own, w_com, w_out, gain_in, gain_out, conv, heads, skip, select)],
        out_specs=[group_spec(w) for w, kind in widths] + [full_spec((8, GROUP))],
        out_shape=[jax.ShapeDtypeStruct((rows, w), kind) for w, kind in widths]
        + [jax.ShapeDtypeStruct((8, GROUP), f32)],
        compiler_params=pltpu.CompilerParams(vmem_limit_bytes=VMEM_GRANT),
    )(lens, tok, cot, w_own, w_com, w_out, gain_in, gain_out, conv, heads, skip, select)


def backward_block(k, act, dmix, step, logdec, skip, state, state_grad, spread, gather):
    values, keys, queries = (act[:, :OWN], act[:, OWN : OWN + NST], act[:, OWN + NST :])
    lower = lower_mask()
    cumul, cumul_t, step_w, cumul_w = block_parts(step, logdec, spread)
    step_t = jnp.transpose(step)
    gram = jnp.where(lower, mm_t(queries, keys), 0.0)
    values_f = values.astype(jnp.float32)
    dmix_f = dmix.astype(jnp.float32)
    lanes_h = iota((BLOCK, LANES), 1)
    rows_h = iota((8, BLOCK), 0)
    grad_gram = 0.0
    row_sums = jnp.zeros((BLOCK, LANES), jnp.float32)
    col_sums = jnp.zeros((8, BLOCK), jnp.float32)
    pieces = []
    for pair in range(PAIRS):
        lanes = slice(pair * LANES, (pair + 1) * LANES)
        piece = 0.0
        for side in range(2):
            h = 2 * pair + side
            decay = decay_of(cumul, cumul_t, h)
            dm_half = lane_half(dmix[:, lanes], side)
            grad_mixing = mm_t(dm_half, values[:, lanes])
            step_row = step_t[h : h + 1, :]
            grad_gram = grad_gram + grad_mixing * decay * step_row
            mixing = gram * decay
            piece = piece + t_mm(low16(mixing), dm_half)
            product = grad_mixing * mixing
            col_sums = jnp.where(rows_h == h, jnp.sum(product, axis=0, keepdims=True), col_sums)
            row_sums = jnp.where(
                lanes_h == h, jnp.sum(product * step_row, axis=1, keepdims=True), row_sums
            )
        pieces.append(piece)
    grad_values = jnp.concatenate(pieces, axis=1) * step_w + skip * dmix_f
    grad_skip = jnp.sum(dmix_f * values_f, axis=0, keepdims=True)
    grad_gram = low16(jnp.where(lower, grad_gram, 0.0))
    grad_queries = mm(grad_gram, keys)
    grad_keys = t_mm(grad_gram, queries)
    columns = jnp.transpose(jnp.concatenate([col_sums, jnp.zeros((LANES - 8, BLOCK), jnp.float32)], axis=0))
    grad_step = columns
    grad_cumul = row_sums - columns * step
    if k == 1:
        entering = jnp.exp(cumul_w) * dmix_f
        entering_low = low16(entering)
        crossed = mm(queries, state)
        grad_cumul = grad_cumul + mm_full(entering * crossed, gather)
        grad_queries = grad_queries + mm_t(entering_low, state)
        before = low16(t_mm(queries, entering_low))
    else:
        tail = jnp.exp(cumul_w[BLOCK - 1 :] - cumul_w)
        weighting = tail * step_w
        back = mm(keys, state_grad)
        grad_values = grad_values + weighting * back
        grad_keys = grad_keys + mm_t(low16(weighting * values_f), state_grad)
        grad_weight = mm_full(values_f * back, gather)
        tail_h = jnp.exp(cumul[BLOCK - 1 :] - cumul)
        grad_step = grad_step + grad_weight * tail_h
        part = grad_weight * tail_h * step
        last = iota((BLOCK, LANES), 0) == BLOCK - 1
        grad_cumul = grad_cumul - part + jnp.where(last, jnp.sum(part, axis=0, keepdims=True), 0.0)
        before = None
    upper = (iota((BLOCK, BLOCK), 0) <= iota((BLOCK, BLOCK), 1)).astype(jnp.float32)
    grad_logdec = mm_full(upper, grad_cumul)
    return (grad_values, grad_keys, grad_queries, grad_step, grad_logdec, grad_skip, before)


def backward_kernel(
    lens, stats, cot, normed, gate_part, conv_in, raw, act, mixed, grad_normed_out,
    w_own, w_com, w_out, gain_out, conv, heads, skip, select,
    branch, grad_normed, g_out, g_own, g_com, small_conv, small_head, small_wide,
    acc_out, acc_in
):
    g = pl.program_id(0)
    live = live_of(lens[...], g)

    @pl.when(g == 0)
    def first():
        acc_out[...] = jnp.zeros_like(acc_out)
        acc_in[...] = jnp.zeros_like(acc_in)
        small_conv[...] = jnp.zeros_like(small_conv)
        small_head[...] = jnp.zeros_like(small_head)
        small_wide[...] = jnp.zeros_like(small_wide)

    padded = jnp.concatenate([stats[...], jnp.zeros((LANES - 8, GROUP), jnp.float32)], axis=0)
    columns = jnp.transpose(padded)
    lanes = iota((GROUP, LANES), 1)
    power = jnp.sum(jnp.where(lanes == 2 * g, columns, 0.0), axis=1, keepdims=True)
    along = jnp.sum(jnp.where(lanes == 2 * g + 1, columns, 0.0), axis=1, keepdims=True)
    scale_out = lax.rsqrt(power * (1.0 / DIN) + norm_eps)
    gate_v, mixed_v, gno = (gate_part[...], mixed[...], grad_normed_out[...])
    sig = sigmoid(gate_v)
    gate_act = gate_v * sig
    gated = mixed_v * gate_act
    normed_out = low16(gated * scale_out * gain_out[...])
    branch[...] = low16(mm(normed_out, w_out[...]))
    grad = jnp.where(live > 0.0, cot[...], jnp.zeros_like(cot[...]))
    acc_out[...] += t_mm(normed_out, grad)
    scaled = gno * scale_out
    grad_gated = scaled * gain_out[...] - gated * (scale_out * scale_out * scale_out * along * (1.0 / DIN))
    gain_sum = jnp.sum(scaled * gated, axis=0, keepdims=True)
    grad_gate = grad_gated * mixed_v * (sig * (1.0 + gate_v * (1.0 - sig)))
    dmix = low16(grad_gated * gate_act)

    act_v = act[...]
    raw_v = raw[...]
    heads_v = heads[...]
    step, logdec = steps_of(raw_v, heads_v, live)
    spread, gather = (head_spread(), head_gather())
    rows0, rows1 = (slice(0, BLOCK), slice(BLOCK, GROUP))
    cumul0 = mm_full(lower_mask().astype(jnp.float32), logdec[rows0])
    cumul0_w = mm_full(cumul0, spread)
    weighting = jnp.exp(cumul0_w[BLOCK - 1 :] - cumul0_w) * mm_full(step[rows0], spread)
    state = low16(
        t_mm(act_v[rows0, OWN : OWN + NST], low16(weighting * act_v[rows0, :OWN].astype(jnp.float32)))
    )
    late = backward_block(
        1, act_v[rows1], dmix[rows1], step[rows1], logdec[rows1], skip[...], state, None, spread, gather
    )
    early = backward_block(
        0, act_v[rows0], dmix[rows0], step[rows0], logdec[rows0], skip[...], None, late[6], spread, gather
    )
    grad_act = jnp.concatenate([jnp.concatenate(part[:3], axis=1) for part in (early, late)], axis=0)
    grad_step = jnp.concatenate([early[3], late[3]], axis=0)
    grad_logdec = jnp.concatenate([early[4], late[4]], axis=0)
    rate = jnp.exp(heads_v[1:2])
    grad_raw = (grad_step - rate * grad_logdec) * live * heads_v[3:4] * sigmoid(raw_v + heads_v[0:1])
    u = conv_in[...]
    conv_v = conv[...]
    preact = preact_of(u, conv_v)
    sig_q = sigmoid(preact)
    grad_pre = grad_act * (sig_q * (1.0 + preact * (1.0 - sig_q)))
    grad_u = grad_pre * conv_v[KCONV - 1 : KCONV]
    taps = []
    for tap in range(KCONV):
        lag = KCONV - 1 - tap
        if lag:
            grad_u = grad_u + shift_up(grad_pre, lag) * conv_v[tap : tap + 1]
        taps.append(jnp.sum(grad_pre * shift_down(u, lag), axis=0, keepdims=True))
    taps.append(jnp.sum(grad_pre, axis=0, keepdims=True))
    small_conv[...] += jnp.concatenate(taps + [jnp.zeros((3, MIX), jnp.float32)], axis=0)
    small_head[...] += jnp.concatenate(
        [
            jnp.sum(grad_raw, axis=0, keepdims=True),
            jnp.sum(grad_logdec * logdec, axis=0, keepdims=True),
            jnp.zeros((6, LANES), jnp.float32),
        ],
        axis=0,
    )
    small_wide[...] += jnp.concatenate(
        [gain_sum, early[5] + late[5], jnp.zeros((6, OWN), jnp.float32)], axis=0
    )
    raw_wide = mm_t(low16(grad_raw), low16(select[...]))
    grad_proj = low16(jnp.concatenate([grad_gate, grad_u, raw_wide], axis=1))
    grad_normed[...] = low16(
        mm_t(grad_proj[:, : 2 * OWN], w_own[...]) + mm_t(grad_proj[:, 2 * OWN :], w_com[...])
    )
    acc_in[...] += t_mm(normed[...], grad_proj)

    @pl.when(g == QUADS - 1)
    def last():
        g_out[...] = low16(acc_out[...])
        g_own[...] = low16(acc_in[:, : 2 * OWN])
        g_com[...] = low16(acc_in[:, 2 * OWN :])


def run_backward(
    lens, stats, cot, normed, gate_part, conv_in, raw, act, mixed, grad_normed_out,
    w_own, w_com, w_out, gain_out, conv, heads, skip, select
):
    f32, bf16 = (jnp.float32, jnp.bfloat16)
    rows = QUADS * GROUP
    fixed = (w_own, w_com, w_out, gain_out, conv, heads, skip, select)
    grouped = (cot, normed, gate_part, conv_in, raw, act, mixed, grad_normed_out)
    ends = (
        ((OWN, D), bf16), ((D, 2 * OWN), bf16), ((D, COMMON_PAD), bf16),
        ((8, MIX), f32), ((8, LANES), f32), ((8, OWN), f32),
    )
    return pl.pallas_call(
        backward_kernel,
        grid=(QUADS,),
        in_specs=[full_spec(lens.shape), full_spec(stats.shape)]
        + [group_spec(a.shape[1]) for a in grouped]
        + [full_spec(a.shape) for a in fixed],
        out_specs=[group_spec(D), group_spec(D)] + [full_spec(s) for s, kind in ends],
        out_shape=[jax.ShapeDtypeStruct((rows, D), bf16)] * 2
        + [jax.ShapeDtypeStruct(s, kind) for s, kind in ends],
        scratch_shapes=[pltpu.VMEM((OWN, D), f32), pltpu.VMEM((D, 2 * OWN + COMMON_PAD), f32)],
        compiler_params=pltpu.CompilerParams(vmem_limit_bytes=VMEM_GRANT),
    )(lens, stats, *grouped, *fixed)


def pick_runs(array, plane_runs, quad, core):
    lead = array.shape[:-1]
    width = array.shape[-1] // (PLANES * QUADS)
    split = array.reshape(lead + (2, 2, QUADS, width))
    zero = 0
    n = len(lead)
    taken = lax.dynamic_slice(
        split, (zero,) * n + (core, 0, quad, 0), lead + (1, 2, 1, width)
    )
    return taken.reshape(lead + (2 * width,))


def put_runs(array, quad, core):
    lead = array.shape[:-1]
    width = array.shape[-1] // 2
    zeros = jnp.zeros(lead + (2, 2, QUADS, width), array.dtype)
    n = len(lead)
    full = lax.dynamic_update_slice(
        zeros, array.reshape(lead + (1, 2, 1, width)), (0,) * n + (core, 0, quad, 0)
    )
    return full.reshape(lead + (width * PLANES * QUADS,))


def rank_slices(array):
    rows = array.shape[0]
    split = array.reshape(rows, 2, 2, QUADS, RUN)
    return split.transpose(3, 1, 0, 2, 4).reshape(RANKS, rows, OWN)


def rank_join(array):
    rows = array.shape[1]
    split = array.reshape(QUADS, 2, rows, 2, RUN)
    return split.transpose(2, 1, 3, 0, 4).reshape(rows, DIN)


def per_device_quad(
    tokens_in,
    cotangent,
    seq_lens,
    in_weight,
    in_first,
    in_second,
    out_weight,
    out_first,
    out_second,
    conv_weight,
    conv_first,
    conv_second,
    gains,
    gain_first,
    gain_second,
    head_params,
    head_first,
    head_second,
):
    bf16, f32 = (jnp.bfloat16, jnp.float32)
    plane, quad, core = place()
    rank = 2 * quad + core
    rows = in_weight.shape[0]
    in_low = in_weight.astype(bf16)
    out_low = out_weight.astype(bf16)
    wz = jnp.concatenate([rank_slices(in_low[:, :DIN]), rank_slices(in_low[:, DIN : 2 * DIN])], axis=2)
    first_len = jnp.full((rows, 1), seq_lens[0, 0] - BLOCK).astype(bf16)
    conv_flat = jnp.pad(conv_weight.reshape(-1), (0, 8)).astype(bf16).reshape(rows, 11)
    wc = jnp.concatenate(
        [in_low[:, 2 * DIN :], gains.astype(bf16).reshape(rows, 3), conv_flat, first_len], axis=1
    )
    wc = jnp.pad(wc, ((0, 0), (0, COMMON_PAD - wc.shape[1])))
    tok, cot, w_own, w_com, w_out = gather_all(tokens_in, cotangent, wz, wc, out_low)
    tok = tok.reshape(RANKS * BLOCK, D)
    cot = cot.reshape(RANKS * BLOCK, D)
    w_own = w_own.reshape(D, 2 * OWN)
    w_out = w_out.reshape(OWN, D)
    extras = w_com[:, :, :, COMMON:].astype(f32)
    gain_par = extras[:, :, :, :3].reshape(D + DIN)
    conv_par = (
        extras[:, :, :, 3:14].reshape(PLANES * RANKS, 11 * rows)[:, : 5 * 104]
        .reshape(PLANES * RANKS, 5, 104).transpose(1, 0, 2).reshape(5, CONVC)
    )
    lens = lax.dynamic_index_in_dim(extras, plane, 0, False)[::2, 0, 14] + BLOCK
    w_com = w_com.reshape(D, COMMON_PAD)
    live = (jnp.arange(GROUP)[None, :] < lens[:, None]).astype(f32)
    lens_rows = jnp.pad(jnp.broadcast_to(lens[:, None], (QUADS, LANES)), ((0, 8 - QUADS), (0, 0)))
    conv_own = jnp.concatenate([pick_runs(conv_par[:, :DIN], 2, quad, core), conv_par[:, DIN:]], axis=1)
    conv_own = jnp.pad(conv_own, ((0, 3), (0, 0)))
    gain_out = pick_runs(gain_par[D:], 2, quad, core)[None, :]
    head_own = pick_runs(head_params, 2, quad, core)
    heads = jnp.pad(
        jnp.concatenate([head_own, jnp.ones((1, OWN_HEADS), f32)]), ((0, 4), (0, LANES - OWN_HEADS))
    )
    skip = jnp.repeat(head_own[2], HDIM)[None, :]
    head_index = pick_runs(jnp.arange(HEADS)[None, :], 2, quad, core)[0]
    select = (iota((LANES, OWN_HEADS), 0) == head_index[None, :]).astype(f32)
    select = jnp.pad(select, ((0, 0), (0, LANES - OWN_HEADS)))

    normed, gate_part, conv_in, raw, act, mixed, grad_normed_out, stats = run_forward(
        lens_rows, tok, cot, w_own, w_com, w_out, gain_par[None, :D], gain_out, conv_own, heads, skip, select
    )
    shared = share(1, stats)
    ranks = lax.broadcasted_iota(jnp.int32, (RANKS, 1, 1), 0)
    total = jnp.sum(jnp.where(ranks == rank, stats[None], shared), axis=0)
    branch, grad_normed, grad_out_w, grad_own_w, grad_com_w, small_conv, small_head, small_wide = run_backward(
        lens_rows, total, cot, normed, gate_part, conv_in, raw, act, mixed, grad_normed_out,
        w_own, w_com, w_out, gain_out, conv_own, heads, skip, select
    )
    grad_conv_own = small_conv[: KCONV + 1]
    grad_gain_out = small_wide[0]
    grad_skip = jnp.sum(small_wide[1].reshape(OWN_HEADS, HDIM), axis=1)
    grad_head_own = jnp.concatenate([small_head[:2, :OWN_HEADS], grad_skip[None, :]])

    def by_core(array, lead):
        split = array.reshape((lead, 2) + array.shape[1:]) if array.shape[0] == 2 * lead else array
        return jnp.moveaxis(split, 1, 0)

    parts = (
        by_core(branch.reshape(RANKS, BLOCK, D), QUADS),
        by_core(grad_normed.reshape(RANKS, BLOCK, D), QUADS),
        by_core(grad_com_w.reshape(PLANES * QUADS * 2, rows, COMMON_PAD), PLANES * QUADS),
    )
    swapped = core_swap(2, *parts)

    def own_part(array, index):
        return lax.dynamic_index_in_dim(array, index, 0, False)

    sums = [
        (own_part(a, core).astype(f32) + b.astype(f32)).astype(bf16) for a, b in zip(parts, swapped)
    ]
    sums[2] = sums[2].reshape(PLANES, QUADS, rows, COMMON_PAD).transpose(1, 0, 2, 3)
    own_blocks = grad_own_w.reshape(PLANES, RANKS, rows, 2 * OWN)
    got = push(
        3,
        quads=sums,
        planes=(own_blocks,),
        out=grad_out_w.reshape(2, 2, out_weight.shape[0], D),
    )

    def add_up(own, index, others):
        return own_part(own, index).astype(f32) + jnp.sum(others.astype(f32), axis=0)

    branch_sum = add_up(sums[0], quad, got[0])
    normed_sum = add_up(sums[1], quad, got[1])
    com_sum = add_up(sums[2], quad, got[2]).astype(bf16)
    own_sum = add_up(own_blocks, plane, got[3]).astype(bf16)
    out_sum = jnp.sum(got[4].astype(f32), axis=0)
    com_got, own_got = push(4, planes=(com_sum,), ranks=(own_sum,))
    com_total = add_up(com_sum, plane, com_got)
    own_all = jnp.where(ranks == rank, own_sum, own_got).astype(f32)
    in_sum = jnp.concatenate(
        [rank_join(own_all[:, :, :OWN]), rank_join(own_all[:, :, OWN:]), com_total[:, :COMMON]], axis=1
    )

    token_rows = tokens_in.astype(f32)
    own_live = lax.dynamic_slice(live, (quad, core * BLOCK), (1, BLOCK)).reshape(BLOCK, 1)
    mixed_out = (token_rows + own_live * branch_sum).astype(bf16)
    normed_value, pull_pre = jax.vjp(pre_norm, token_rows, gain_par[:D])
    grad_rows, grad_gain_pre = pull_pre(normed_sum)
    grad_input = cotangent.astype(f32) + grad_rows

    grad_gains = jnp.concatenate([grad_gain_pre, put_runs(grad_gain_out, quad, core)]).reshape(32, 144)
    grad_conv = jnp.concatenate(
        [put_runs(grad_conv_own[:, :OWN], quad, core), grad_conv_own[:, OWN:]], axis=1
    ).reshape(5, 32, 104).transpose(1, 0, 2).reshape(32, 520)
    grad_head = jnp.broadcast_to(put_runs(grad_head_own, quad, core).reshape(1, 144), (32, 144))
    small = jnp.concatenate([grad_gains, grad_conv, grad_head, jnp.zeros((32, 216), f32)], axis=1)
    small = small.reshape(32, 8, 128)
    small_got = to_owners(5, small)
    mine = rank + RANKS * plane
    owners = lax.broadcasted_iota(jnp.int32, (32, 1, 1), 0)
    small_sum = jnp.sum(jnp.where(owners == mine, small, small_got), axis=0).reshape(-1)
    gain_sum = small_sum[:144]
    conv_sum = small_sum[144:664].reshape(5, 104)
    head_sum = small_sum[664:808].reshape(3, 48)
    new_in = adam_update(in_weight, in_first, in_second, in_sum, rate_in)
    new_out = adam_update(out_weight, out_first, out_second, out_sum, rate_out)
    new_conv = adam_update(conv_weight, conv_first, conv_second, conv_sum, rate_conv)
    new_gain = adam_update(gains, gain_first, gain_second, gain_sum, rate_gain)
    new_head = adam_update(head_params, head_first, head_second, head_sum, rate_head)
    return (mixed_out, grad_input) + new_in + new_out + new_conv + new_gain + new_head


def solution(mesh):
    placed = (
        P(("dp", "seq"), None),
        P(("dp", "seq"), None),
        P("dp", None),
        P(("dp", "seq"), None),
        P(("dp", "seq"), None),
        P(("dp", "seq"), None),
        P(("dp", "seq"), None),
        P(("dp", "seq"), None),
        P(("dp", "seq"), None),
        P(None, ("dp", "seq")),
        P(None, ("dp", "seq")),
        P(None, ("dp", "seq")),
        P(("dp", "seq")),
        P(("dp", "seq")),
        P(("dp", "seq")),
        P(),
        P(),
        P(),
    )
    quad = dict(mesh.shape) == {"dp": PLANES * QUADS, "seq": 2}
    return jax.shard_map(
        per_device_quad if quad else per_device,
        mesh=mesh,
        in_specs=placed,
        out_specs=(
            P(("dp", "seq"), None),
            P(("dp", "seq"), None),
            P(("dp", "seq"), None),
            P(("dp", "seq"), None),
            P(("dp", "seq"), None),
            P(("dp", "seq"), None),
            P(("dp", "seq"), None),
            P(("dp", "seq"), None),
            P(None, ("dp", "seq")),
            P(None, ("dp", "seq")),
            P(None, ("dp", "seq")),
            P(("dp", "seq")),
            P(("dp", "seq")),
            P(("dp", "seq")),
            P(),
            P(),
            P(),
        ),
        check_vma=False,
    )
```

```python
import functools

import jax
import jax.numpy as jnp
from jax import lax
from jax.experimental import pallas as pl
from jax.experimental.pallas import tpu as pltpu
from jax.sharding import PartitionSpec as P

D = 1536
HEADS = 48
HDIM = 64
NST = 128
KCONV = 4
BLOCK = 256
SLOTS = 4
STEP = 10
DIN = 3072
CONVC = 3328


highest = lax.Precision.HIGHEST
norm_eps = 1e-05
beta_first = 0.9
beta_second = 0.95
adam_eps = 1e-08
weight_decay = 0.1
rate_in = 0.01
rate_out = 0.008
rate_conv = 0.2
rate_gain = 0.4
rate_head = 0.5


def from_behind(block, axis, distance):
    devices = range(lax.axis_size(axis))
    route = [(i - distance, i) for i in devices if i - distance in devices]
    return lax.ppermute(block, axis, route)


def prefix(value, axis, join, neutral):
    place = lax.axis_index(axis)
    gathered = jax.tree.map(
        lambda a, kind: lax.all_gather(a.astype(kind), axis),
        value,
        jax.tree.map(lambda a: jnp.bfloat16 if a.dtype == jnp.float32 else a.dtype, value),
    )
    state = jax.tree.map(lambda a, e: jnp.zeros_like(a) + jnp.asarray(e, a.dtype), value, neutral)

    def one(hop, state):
        return join(
            state,
            jax.tree.map(
                lambda a, own: lax.dynamic_index_in_dim(a, hop, 0, False).astype(own.dtype),
                gathered,
                value,
            ),
        )

    return lax.fori_loop(0, place, one, state)


def prefix_2(value, axis, combine, identity):
    devices, index = (lax.axis_size(axis), lax.axis_index(axis))
    everything = jax.tree.map(
        lambda part, kind: lax.all_gather(part.astype(kind), axis),
        value,
        (jnp.bfloat16, jnp.bfloat16),
    )
    start = jax.tree.map(
        lambda part, zero: jnp.broadcast_to(jnp.asarray(zero, part.dtype), part.shape),
        value,
        identity,
    )

    def hop(k, before):
        at = devices - 1 - k
        reached = at > index
        new = combine(
            before, jax.tree.map(lambda part, own: part[at].astype(own.dtype), everything, value)
        )
        return jax.tree.map(lambda a, b: jnp.where(reached, a, b), new, before)

    return lax.fori_loop(0, devices, hop, start)


def segment_of(seq_row, position):
    blocks = (seq_row + BLOCK - 1) // BLOCK
    ends = jnp.cumsum(blocks) * BLOCK
    starts = ends - blocks * BLOCK
    above = position[:, None] >= starts[None, :]
    inside = above & (position[:, None] < ends[None, :])
    numbers = jnp.arange(1, SLOTS + 1, dtype=jnp.int32)
    labels_of = jnp.sum(jnp.where(inside, numbers[None, :], 0), axis=1)
    live_rows = jnp.sum(
        (above & (position[:, None] < (starts + seq_row)[None, :])).astype(jnp.float32), axis=1
    )
    return (labels_of, live_rows)


def layout(seq_row, position):
    labels_of, live_rows = segment_of(seq_row, position)
    columns = []
    for conv_lag in range(KCONV):
        earlier, unused_live = segment_of(seq_row, position - conv_lag)
        columns.append(((earlier == labels_of) & (labels_of > 0)).astype(jnp.float32))
    return (live_rows, jnp.stack(columns, axis=1))


def pre_norm(token_rows, gain_row):
    scaling = lax.rsqrt(jnp.mean(token_rows * token_rows, axis=1, keepdims=True) + norm_eps)
    return token_rows * scaling * gain_row[None, :]


def gate_norm(mixed, gate_part, gain_row):
    gated = mixed * jax.nn.silu(gate_part)
    scaling = lax.rsqrt(jnp.mean(gated * gated, axis=1, keepdims=True) + norm_eps)
    return gated * scaling * gain_row[None, :]


def mixer_in(extended, step_raw, conv_par, head_values, factors, live_rows):
    row_count = step_raw.shape[0]
    preact = jnp.zeros((row_count, conv_par.shape[1]), jnp.float32) + conv_par[KCONV][None, :]
    for conv_tap in range(KCONV):
        window = lax.slice_in_dim(extended, conv_tap, conv_tap + row_count, axis=0)
        preact = (
            preact
            + conv_par[conv_tap][None, :] * window * factors[:, KCONV - 1 - conv_tap][:, None]
        )
    conv_act = jax.nn.silu(preact)
    step_size = jax.nn.softplus(step_raw + head_values[0][None, :]) * live_rows[:, None]
    logdec = -jnp.exp(head_values[1])[None, :] * step_size
    return (conv_act, step_size, logdec)


def lower_ones():
    row_ids = lax.broadcasted_iota(jnp.int32, (BLOCK, BLOCK), 0)
    col_ids = lax.broadcasted_iota(jnp.int32, (BLOCK, BLOCK), 1)
    return (row_ids >= col_ids).astype(jnp.float32)


def block_state(values, keys_in, step_size, logdec):
    cumul = jnp.dot(lower_ones(), logdec, precision=highest)
    totals = cumul[-1]
    weighting = jnp.exp(totals[None, :] - cumul) * step_size
    states = jnp.einsum("uhp,un->hpn", weighting[:, :, None] * values, keys_in, precision=highest)
    return (jnp.exp(totals), states)


def block_out(values, keys_in, queries, step_size, logdec, skip_gain, start_state):
    lower_tri = lower_ones()
    cumul = jnp.dot(lower_tri, logdec, precision=highest)
    across = cumul.T
    gap_matrix = across[:, :, None] - across[:, None, :]
    decays = jnp.exp(jnp.where(lower_tri[None, :, :] > 0, gap_matrix, -1e30))
    gram_matrix = jnp.dot(queries, keys_in.T, precision=highest)
    mixing = gram_matrix[None, :, :] * decays * step_size.T[:, None, :]
    intra_part = jnp.einsum("htu,uhp->thp", mixing, values, precision=highest)
    carried = jnp.exp(cumul)[:, :, None] * jnp.einsum(
        "tn,hpn->thp", queries, start_state, precision=highest
    )
    return intra_part + carried + skip_gain[None, :, None] * values


def block_full(values, keys_in, queries, step_size, logdec, skip_gain, start_state):
    factor_end, states = block_state(values, keys_in, step_size, logdec)
    outputs = block_out(values, keys_in, queries, step_size, logdec, skip_gain, start_state)
    return (outputs, factor_end[:, None, None] * start_state + states)


def adam_update(weight, first, second, gradient, step_rate):
    first_new = beta_first * first + (1.0 - beta_first) * gradient
    second_new = beta_second * second + (1.0 - beta_second) * gradient * gradient
    first_hat = first_new / (1.0 - beta_first**STEP)
    second_hat = second_new / (1.0 - beta_second**STEP)
    weight_new = weight - step_rate * (
        first_hat / (jnp.sqrt(second_hat) + adam_eps) + weight_decay * weight
    )
    return (weight_new, first_new, second_new)


def carry_join(earlier, later):
    return (earlier[0] * later[0], later[0][:, None, None] * earlier[1] + later[1])


def as_float(array_low):
    return lax.optimization_barrier(array_low).astype(jnp.float32)


def contract_rows(left, right):
    return lax.dot_general(
        left, right, (((0,), (0,)), ((), ())), preferred_element_type=jnp.float32
    )


def contract_cols(left, right):
    return lax.dot_general(
        left, right, (((1,), (1,)), ((), ())), preferred_element_type=jnp.float32
    )


def per_device(
    tokens_in,
    cotangent,
    seq_lens,
    in_weight,
    in_first,
    in_second,
    out_weight,
    out_first,
    out_second,
    conv_weight,
    conv_first,
    conv_second,
    gains,
    gain_first,
    gain_second,
    head_params,
    head_first,
    head_second,
):
    local_tok = tokens_in.shape[0]
    position = lax.axis_index("seq") * local_tok + jnp.arange(local_tok, dtype=jnp.int32)
    live_rows, factors = layout(seq_lens[0], position)
    low_weights = (
        in_weight.astype(jnp.bfloat16),
        out_weight.astype(jnp.bfloat16),
        conv_weight.astype(jnp.bfloat16),
        gains.astype(jnp.bfloat16),
    )
    in_full, out_full, conv_full, gain_full = (
        lax.all_gather(low_weights[0], ("dp", "seq"), axis=0, tiled=True),
        lax.all_gather(low_weights[1], ("dp", "seq"), axis=0, tiled=True),
        lax.all_gather(low_weights[2], ("dp", "seq"), axis=1, tiled=True),
        lax.all_gather(low_weights[3], ("dp", "seq"), axis=0, tiled=True),
    )
    conv_par = conv_full.astype(jnp.float32)
    gain_par = gain_full.astype(jnp.float32)
    token_rows = tokens_in.astype(jnp.float32)
    normed_value, pull_pre = jax.vjp(pre_norm, token_rows, gain_par[:D])
    normed = normed_value.astype(jnp.bfloat16)
    projected = jnp.dot(normed, in_full, preferred_element_type=jnp.float32)
    gate_part = projected[:, :DIN]
    conv_in = projected[:, DIN : DIN + CONVC]
    step_raw = projected[:, DIN + CONVC :]
    halo_rows = from_behind(conv_in[local_tok - KCONV + 1 :], "seq", 1)
    extended = jnp.concatenate([halo_rows, conv_in], axis=0)

    def mixer_local(extended_rows, raw_steps, conv_values, head_values):
        return mixer_in(extended_rows, raw_steps, conv_values, head_values, factors, live_rows)

    (conv_act, step_size, logdec), pull_mixer = jax.vjp(
        mixer_local, extended, step_raw, conv_par, head_params
    )
    conv_used = as_float(conv_act.astype(jnp.bfloat16))
    block_count = local_tok // BLOCK
    values = conv_used[:, :DIN].reshape(block_count, BLOCK, HEADS, HDIM)
    keys_in = conv_used[:, DIN : DIN + NST].reshape(block_count, BLOCK, NST)
    queries = conv_used[:, DIN + NST :].reshape(block_count, BLOCK, NST)
    steps_blk = step_size.reshape(block_count, BLOCK, HEADS)
    logdec_blk = logdec.reshape(block_count, BLOCK, HEADS)
    resets = factors[::BLOCK, 1]
    skip_gain = head_params[2]
    decays, block_states = jax.vmap(block_state)(values, keys_in, steps_blk, logdec_blk)

    def fold_local(carried, block_item):
        factor_now = block_item[0] * block_item[2]
        return (
            (carried[0] * factor_now, factor_now[:, None, None] * carried[1] + block_item[1]),
            None,
        )

    identity = (jnp.ones((HEADS,), jnp.float32), jnp.zeros((HEADS, HDIM, NST), jnp.float32))
    device_sum, unused_fold = lax.scan(fold_local, identity, (decays, block_states, resets))
    unused_dec, entering = prefix(device_sum, "seq", carry_join, identity)

    def start_states(states, block_item):
        begin = block_item[2] * states
        return (block_item[0][:, None, None] * begin + block_item[1], begin)

    unused_end, begins = lax.scan(start_states, entering, (decays, block_states, resets))

    def emit(block_item):
        return block_out(
            block_item[0],
            block_item[1],
            block_item[2],
            block_item[3],
            block_item[4],
            skip_gain,
            block_item[5],
        )

    mixed = lax.map(emit, (values, keys_in, queries, steps_blk, logdec_blk, begins)).reshape(
        local_tok, DIN
    )
    normed_out_value, pull_gate = jax.vjp(gate_norm, mixed, gate_part, gain_par[D:])
    normed_out = normed_out_value.astype(jnp.bfloat16)
    branch = jnp.dot(normed_out, out_full, preferred_element_type=jnp.float32)
    mixed_out = (token_rows + live_rows[:, None] * branch).astype(jnp.bfloat16)
    out_grad = (cotangent.astype(jnp.float32) * live_rows[:, None]).astype(jnp.bfloat16)
    in_back, out_back = (
        lax.all_gather(in_weight.astype(jnp.bfloat16), ("dp", "seq"), axis=0, tiled=True),
        lax.all_gather(out_weight.astype(jnp.bfloat16), ("dp", "seq"), axis=0, tiled=True),
    )
    grad_out_w = contract_rows(normed_out, out_grad)
    grad_normed_out = contract_cols(out_grad, out_back)
    grad_mixed, grad_gate, grad_gain_in = pull_gate(grad_normed_out)
    mixed_back = as_float(grad_mixed.astype(jnp.bfloat16)).reshape(block_count, BLOCK, HEADS, HDIM)

    def adjoint_local(carried, block_item):
        cumul = jnp.dot(lower_ones(), block_item[2], precision=highest)
        weighted = jnp.exp(cumul)[:, :, None] * block_item[0]
        direct = jnp.einsum("thp,tn->hpn", weighted, block_item[1], precision=highest)
        return (block_item[4] * (direct + block_item[3][:, None, None] * carried), None)

    local_adj, unused_adj = lax.scan(
        adjoint_local, identity[1], (mixed_back, queries, logdec_blk, decays, resets), reverse=True
    )
    unused_later, leaving = prefix_2((device_sum[0], local_adj), "seq", carry_join, identity)

    def adjoint_block(carried, block_item):
        unused_primal, pull_block = jax.vjp(
            block_full,
            block_item[0],
            block_item[1],
            block_item[2],
            block_item[3],
            block_item[4],
            skip_gain,
            block_item[5],
        )
        grads = pull_block((block_item[6], carried[0]))
        return ((block_item[7] * grads[6], carried[1] + grads[5]), grads[:5])

    (unused_state, grad_skip), block_grads = lax.scan(
        adjoint_block,
        (leaving, jnp.zeros((HEADS,), jnp.float32)),
        (values, keys_in, queries, steps_blk, logdec_blk, begins, mixed_back, resets),
        reverse=True,
    )
    grad_values, grad_keys, grad_queries, grad_step, grad_logdec = block_grads
    grad_act = jnp.concatenate(
        [
            grad_values.reshape(local_tok, DIN),
            grad_keys.reshape(local_tok, NST),
            grad_queries.reshape(local_tok, NST),
        ],
        axis=1,
    )
    grad_ext, grad_raw, grad_conv, grad_head_part = pull_mixer(
        (grad_act, grad_step.reshape(local_tok, HEADS), grad_logdec.reshape(local_tok, HEADS))
    )
    returned = from_behind(grad_ext[: KCONV - 1].astype(jnp.bfloat16), "seq", -1).astype(
        jnp.float32
    )
    grad_conv_in = grad_ext[KCONV - 1 :] + jnp.concatenate(
        [jnp.zeros((local_tok - KCONV + 1, CONVC), jnp.float32), returned], axis=0
    )
    grad_proj = jnp.concatenate([grad_gate, grad_conv_in, grad_raw], axis=1).astype(jnp.bfloat16)
    grad_normed = contract_cols(grad_proj, in_back)
    grad_rows, grad_gain_pre = pull_pre(grad_normed)
    grad_input = cotangent.astype(jnp.float32) + grad_rows
    grad_gains = jnp.concatenate([grad_gain_pre, grad_gain_in], axis=0)
    grad_head = jnp.concatenate(
        [grad_head_part[:2], (grad_head_part[2] + grad_skip)[None, :]], axis=0
    )
    grad_in_w = contract_rows(normed, grad_proj)
    in_sum, out_sum, conv_sum, gain_sum = (
        lax.psum_scatter(grad_in_w, ("dp", "seq"), scatter_dimension=0, tiled=True),
        lax.psum_scatter(grad_out_w, ("dp", "seq"), scatter_dimension=0, tiled=True),
        lax.psum_scatter(grad_conv, ("dp", "seq"), scatter_dimension=1, tiled=True),
        lax.psum_scatter(grad_gains, ("dp", "seq"), scatter_dimension=0, tiled=True),
    )
    head_sum = lax.psum(grad_head, ("dp", "seq"))
    new_in = adam_update(in_weight, in_first, in_second, in_sum, rate_in)
    new_out = adam_update(out_weight, out_first, out_second, out_sum, rate_out)
    new_conv = adam_update(conv_weight, conv_first, conv_second, conv_sum, rate_conv)
    new_gain = adam_update(gains, gain_first, gain_second, gain_sum, rate_gain)
    new_head = adam_update(head_params, head_first, head_second, head_sum, rate_head)
    return (
        mixed_out,
        grad_input,
        new_in[0],
        new_in[1],
        new_in[2],
        new_out[0],
        new_out[1],
        new_out[2],
        new_conv[0],
        new_conv[1],
        new_conv[2],
        new_gain[0],
        new_gain[1],
        new_gain[2],
        new_head[0],
        new_head[1],
        new_head[2],
    )


MESH_ID = pl.DeviceIdType.MESH
ANY = pl.BlockSpec(memory_space=pl.ANY)
PLANES = 4
QUADS = 4
RANKS = 8


def place():
    chip = lax.axis_index("dp")
    return (chip // QUADS, chip % QUADS, lax.axis_index("seq"))


def at(plane, quad, core):
    return (plane * QUADS + quad, core)


def flip(core):
    return 1 - core


def xor4(value, k):
    low, high = value % 2, value // 2
    if k % 2:
        low = 1 - low
    if k // 2:
        high = 1 - high
    return 2 * high + low


def greet(devices):
    barrier = pltpu.get_barrier_semaphore()
    for device in devices:
        pl.semaphore_signal(barrier, inc=1, device_id=device, device_id_type=MESH_ID)
    pl.semaphore_wait(barrier, len(devices))


def plane_mates(plane, quad, core):
    mates = []
    for k in range(QUADS):
        for other in (core, flip(core)):
            if not (k == 0 and other is core):
                mates.append(at(plane, xor4(quad, k), other))
    return mates


def plane_others(plane, quad, core):
    return [at(xor4(plane, k), quad, core) for k in range(1, PLANES)]


class Sems:
    def __init__(self, send, recv):
        self.send, self.recv, self.used = (send, recv, 0)

    def copy(self, source, target, device):
        index = self.used
        self.used += 1
        return pltpu.make_async_remote_copy(
            src_ref=source,
            dst_ref=target,
            send_sem=self.send.at[index],
            recv_sem=self.recv.at[index],
            device_id=device,
            device_id_type=MESH_ID,
        )


class PlaneGather:
    def __init__(self, sems, own, land, plane, quad, core):
        near_x, near_y, far = (xor4(quad, k) for k in (1, 2, 3))
        rank, rank_x, rank_y, rank_far = (2 * q + core for q in (quad, near_x, near_y, far))
        to_x, to_y = (at(plane, near_x, core), at(plane, near_y, core))
        sibling = at(plane, quad, flip(core))
        whole = [0, 1]
        self.own = [
            sems.copy(own(h), land(rank, slot, h), device)
            for device, slot in ((to_x, 1), (to_y, 2), (sibling, 0))
            for h in whole
        ]
        self.relay_x = [
            sems.copy(land(rank_x, 1, 0), land(rank_x, 3, 0), to_y),
        ] + [sems.copy(land(rank_x, 1, h), land(rank_x, 1, h), sibling) for h in whole]
        self.relay_y = [
            sems.copy(land(rank_y, 2, 1), land(rank_y, 3, 1), to_x),
        ] + [sems.copy(land(rank_y, 2, h), land(rank_y, 2, h), sibling) for h in whole]
        self.relay_far = [
            sems.copy(land(rank_far, 3, h), land(rank_far, 3, h), sibling) for h in whole
        ]

    def start(self):
        for copy in self.own:
            copy.start()

    def forward(self):
        self.own[0].wait_recv()
        self.relay_x[0].start()
        self.own[3].wait_recv()
        self.relay_y[0].start()
        self.own[1].wait_recv()
        self.own[2].wait_recv()
        for copy in self.relay_x[1:] + self.relay_y[1:]:
            copy.start()

    def finish(self):
        for h, relay in ((0, self.relay_x[0]), (1, self.relay_y[0])):
            relay.wait_recv()
            self.relay_far[h].start()
        for copy in self.own[4:] + self.relay_x[1:] + self.relay_y[1:] + self.relay_far:
            copy.wait_recv()
        for copy in self.own + self.relay_x + self.relay_y + self.relay_far:
            copy.wait_send()


class LineGather:
    def __init__(self, sems, own, block, plane, quad, core):
        self.plane = plane
        self.right, self.left = ([], [])
        for hop in range(PLANES - 1):
            for copies, step in ((self.right, 1), (self.left, -1)):
                index = plane - step * hop
                source = own if hop == 0 else block(index)
                copies.append(sems.copy(source, block(index), at(plane + step, quad, core)))

    def sends(self, hop, step):
        if step > 0:
            return (self.plane - hop >= 0) & (self.plane < PLANES - 1)
        return (self.plane + hop < PLANES) & (self.plane > 0)

    def receives(self, hop, step):
        if step > 0:
            return self.plane - 1 - hop >= 0
        return self.plane + 1 + hop < PLANES

    def start(self, hop):
        for copies, step in ((self.right, 1), (self.left, -1)):

            @pl.when(self.sends(hop, step))
            def go():
                copies[hop].start()

    def arrive(self, hop):
        for copies, step in ((self.right, 1), (self.left, -1)):

            @pl.when(self.receives(hop, step))
            def landed():
                copies[hop].wait_recv()

    def sent(self):
        for hop in range(PLANES - 1):
            for copies, step in ((self.right, 1), (self.left, -1)):

                @pl.when(self.sends(hop, step))
                def left():
                    copies[hop].wait_send()


def gather_kernel(tok, cot, wz, wc, wo, o_tok, o_cot, o_wz, o_wc, s_wo, o_wo, send, recv, local):
    plane, quad, core = place()
    rank = 2 * quad + core
    sibling = at(plane, quad, flip(core))
    sems = Sems(send, recv)
    where = (plane, quad, core)
    locals_ = []

    def keep(source, target):
        copy = pltpu.make_async_copy(source, target, local.at[len(locals_)])
        locals_.append(copy)
        copy.start()
        return copy

    half = tok.shape[0] // 2
    rows = wc.shape[0]

    def token_block(buffer):
        return lambda r, slot, h: buffer.at[slot, core, pl.ds(h * half, half)]

    def token_own(buffer):
        return lambda h: buffer.at[pl.ds(h * half, half)]

    line_c = LineGather(sems, wc, lambda q: o_wc.at[q, rank], *where)
    line_o = LineGather(sems, wo, lambda q: s_wo.at[q], *where)
    shuffle = []
    for k in range(1, RANKS):
        other_core = flip(core) if k % 2 else core
        other_quad = xor4(quad, k // 2)
        shuffle.append(
            sems.copy(wz.at[2 * other_quad + other_core], o_wz.at[plane, rank], at(plane, other_quad, other_core))
        )
    halves = [
        LineGather(
            sems,
            o_wz.at[plane, pl.ds(4 * h, 4)],
            lambda q, h=h: o_wz.at[q, pl.ds(4 * h, 4)],
            *where,
        )
        for h in range(2)
    ]
    tokens = PlaneGather(sems, token_own(tok), token_block(o_tok), *where)
    grads = PlaneGather(sems, token_own(cot), token_block(o_cot), *where)
    common = PlaneGather(
        sems,
        lambda h: o_wc.at[pl.ds(2 * h, 2), rank],
        lambda r, slot, h: o_wc.at[pl.ds(2 * h, 2), r],
        *where,
    )
    cross_o = [
        sems.copy(s_wo.at[2 * flip(core) + k], o_wo.at[k, core], sibling) for k in range(2)
    ]

    greet(plane_mates(*where) + plane_others(*where))
    line_c.start(0)
    for copy in shuffle:
        copy.start()
    line_o.start(0)
    tokens.start()
    own_wz = keep(wz.at[rank], o_wz.at[plane, rank])
    own_wc = keep(wc, o_wc.at[plane, rank])
    own_wo = keep(wo, s_wo.at[plane])
    own_tok = keep(tok, o_tok.at[0, core])
    own_cot = keep(cot, o_cot.at[0, core])
    own_wz.wait()
    for copy in shuffle:
        copy.wait_recv()
    halves[0].start(0)
    halves[1].start(0)
    for hop in range(PLANES - 1):
        line_c.arrive(hop)
        if hop < PLANES - 2:
            line_c.start(hop + 1)
    own_wc.wait()
    common.start()
    tokens.forward()
    grads.start()
    common.forward()
    for hop in range(PLANES - 1):
        for h in range(2):
            halves[h].arrive(hop)
            if hop < PLANES - 2:
                halves[h].start(hop + 1)
        line_o.arrive(hop)
        if hop < PLANES - 2:
            line_o.start(hop + 1)
        if hop == 0:
            tokens.finish()
            common.finish()
    own_wo.wait()
    keeps = []
    for copy in cross_o:
        copy.start()
    keeps = [keep(s_wo.at[2 * core + k], o_wo.at[k, core]) for k in range(2)]
    grads.forward()
    grads.finish()
    for copy in cross_o:
        copy.wait()
    for copy in shuffle:
        copy.wait_send()
    for line in halves + [line_c, line_o]:
        line.sent()
    for copy in [own_tok, own_cot] + keeps:
        copy.wait()


def gather_all(tok, cot, wz, wc, wo):
    bf16 = jnp.bfloat16
    shapes = (
        (QUADS, 2) + tok.shape,
        (QUADS, 2) + cot.shape,
        (PLANES,) + wz.shape,
        (PLANES, RANKS) + wc.shape,
        (PLANES,) + wo.shape,
        (2, 2) + wo.shape,
    )
    outs = pl.pallas_call(
        gather_kernel,
        out_shape=[jax.ShapeDtypeStruct(s, bf16) for s in shapes],
        in_specs=[ANY] * 5,
        out_specs=[ANY] * 6,
        scratch_shapes=[
            pltpu.SemaphoreType.DMA((80,)),
            pltpu.SemaphoreType.DMA((80,)),
            pltpu.SemaphoreType.DMA((8,)),
        ],
        compiler_params=pltpu.CompilerParams(collective_id=0, has_side_effects=True),
    )(tok, cot, wz, wc, wo)
    return (outs[0], outs[1], outs[2], outs[3], outs[5])


def share_kernel(source, target, send, recv):
    plane, quad, core = place()
    rank = 2 * quad + core
    sems = Sems(send, recv)
    mates = plane_mates(plane, quad, core)
    copies = [sems.copy(source, target.at[rank], device) for device in mates]
    greet(mates)
    for copy in copies:
        copy.start()
    for copy in copies:
        copy.wait()


def share(ident, array):
    return pl.pallas_call(
        share_kernel,
        out_shape=jax.ShapeDtypeStruct((RANKS,) + array.shape, array.dtype),
        in_specs=[ANY],
        out_specs=ANY,
        scratch_shapes=[pltpu.SemaphoreType.DMA((RANKS - 1,))] * 2,
        compiler_params=pltpu.CompilerParams(collective_id=ident, has_side_effects=True),
    )(array)


OWN_HEADS = HEADS // RANKS
OWN = OWN_HEADS * HDIM
PAIRS = OWN_HEADS // 2
RUN = OWN // 2
COMMON = 2 * NST + HEADS
COMMON_PAD = 384
GROUP = 2 * BLOCK
MIX = OWN + 2 * NST
LANES = 128


def mm(left, right):
    return lax.dot_general(left, right, (((1,), (0,)), ((), ())), preferred_element_type=jnp.float32)


def mm_t(left, right):
    return lax.dot_general(left, right, (((1,), (1,)), ((), ())), preferred_element_type=jnp.float32)


def t_mm(left, right):
    return lax.dot_general(left, right, (((0,), (0,)), ((), ())), preferred_element_type=jnp.float32)


def mm_full(left, right):
    return lax.dot_general(
        left, right, (((1,), (0,)), ((), ())), precision=highest, preferred_element_type=jnp.float32
    )


def low16(value):
    return value.astype(jnp.bfloat16)


def iota(shape, axis):
    return lax.broadcasted_iota(jnp.int32, shape, axis)


def head_spread():
    return (iota((LANES, OWN), 1) // HDIM == iota((LANES, OWN), 0)).astype(jnp.float32)


def head_gather():
    return (iota((OWN, LANES), 0) // HDIM == iota((OWN, LANES), 1)).astype(jnp.float32)


def lower_mask():
    return iota((BLOCK, BLOCK), 0) >= iota((BLOCK, BLOCK), 1)


def shift_down(value, k):
    if k == 0:
        return value
    rolled = pltpu.roll(value, k, 0)
    return jnp.where(iota(value.shape, 0) >= k, rolled, 0.0)


def shift_up(value, k):
    if k == 0:
        return value
    rows = value.shape[0]
    rolled = pltpu.roll(value, rows - k, 0)
    return jnp.where(iota(value.shape, 0) < rows - k, rolled, 0.0)


def sigmoid(value):
    return 1.0 / (1.0 + jnp.exp(-value))


def softplus(value):
    return jnp.maximum(value, 0.0) + jnp.log1p(jnp.exp(-jnp.abs(value)))


def preact_of(u, conv):
    total = u * conv[KCONV - 1 : KCONV] + conv[KCONV : KCONV + 1]
    for tap in range(KCONV - 1):
        total = total + shift_down(u, KCONV - 1 - tap) * conv[tap : tap + 1]
    return total


def steps_of(raw, heads, live):
    step = softplus(raw + heads[0:1]) * live * heads[3:4]
    return (step, -jnp.exp(heads[1:2]) * step)


def decay_of(cumul, cumul_t, h):
    return jnp.exp(jnp.minimum(cumul[:, h : h + 1] - cumul_t[h : h + 1, :], 0.0))


def lane_half(value, side):
    lanes = iota(value.shape, 1)
    return jnp.where((lanes >= HDIM) == (side == 1), value, jnp.zeros_like(value))


def block_parts(step, logdec, spread):
    cumul = mm_full(lower_mask().astype(jnp.float32), logdec)
    return (cumul, jnp.transpose(cumul), mm_full(step, spread), mm_full(cumul, spread))


def forward_group(live, tok, cot, w_own, w_com, w_out, gain_in, gain_out, conv, heads, skip, select):
    token_rows = tok[...].astype(jnp.float32)
    scaling = lax.rsqrt(jnp.mean(token_rows * token_rows, axis=1, keepdims=True) + norm_eps)
    normed = low16(token_rows * scaling * gain_in[...])
    gate_part = mm(normed, w_own[:, :OWN])
    conv_in = jnp.concatenate([mm(normed, w_own[:, OWN:]), mm(normed, w_com[:, : 2 * NST])], axis=1)
    raw = mm_full(mm(normed, w_com[:, 2 * NST :]), select[...])
    preact = preact_of(conv_in, conv[...])
    act = low16(preact * sigmoid(preact))
    step, logdec = steps_of(raw, heads[...], live)
    spread = head_spread()
    lower = lower_mask()
    outs = []
    state = None
    for k in range(2):
        rows = slice(k * BLOCK, (k + 1) * BLOCK)
        values, keys, queries = (act[rows, :OWN], act[rows, OWN : OWN + NST], act[rows, OWN + NST :])
        cumul, cumul_t, step_w, cumul_w = block_parts(step[rows], logdec[rows], spread)
        gram = jnp.where(lower, mm_t(queries, keys), 0.0)
        values_f = values.astype(jnp.float32)
        stepped = low16(values_f * step_w)
        pieces = []
        for pair in range(PAIRS):
            lanes = slice(pair * LANES, (pair + 1) * LANES)
            piece = 0.0
            for side in range(2):
                mixing = low16(gram * decay_of(cumul, cumul_t, 2 * pair + side))
                piece = piece + mm(mixing, lane_half(stepped[:, lanes], side))
            pieces.append(piece)
        out = jnp.concatenate(pieces, axis=1) + skip[...] * values_f
        if state is not None:
            out = out + jnp.exp(cumul_w) * mm(queries, state)
        else:
            weighting = jnp.exp(cumul_w[BLOCK - 1 :] - cumul_w) * step_w
            state = low16(t_mm(keys, low16(weighting * values_f)))
        outs.append(out)
    mixed = jnp.concatenate(outs, axis=0)
    grad = jnp.where(live > 0.0, cot[...], jnp.zeros_like(cot[...]))
    grad_normed_out = mm_t(grad, w_out[...])
    gated = mixed * gate_part * sigmoid(gate_part)
    stats = (
        jnp.sum(gated * gated, axis=1, keepdims=True),
        jnp.sum(grad_normed_out * gain_out[...] * gated, axis=1, keepdims=True),
    )
    return (normed, gate_part, conv_in, raw, act, mixed, grad_normed_out, stats)


def live_of(lens, g):
    rows = iota((GROUP, 1), 0).astype(jnp.float32)
    chosen = jnp.sum(jnp.where(iota(lens.shape, 0) == g, lens, 0.0), axis=0, keepdims=True)[:, :1]
    return (rows < chosen).astype(jnp.float32)


def forward_kernel(
    lens, tok, cot, w_own, w_com, w_out, gain_in, gain_out, conv, heads, skip, select,
    normed, gate_part, conv_in, raw, act, mixed, grad_normed_out, stats
):
    g = pl.program_id(0)
    live = live_of(lens[...], g)
    results = forward_group(
        live, tok, cot, w_own, w_com, w_out, gain_in, gain_out, conv, heads, skip, select
    )
    for ref, value in zip((normed, gate_part, conv_in, raw, act, mixed, grad_normed_out), results):
        ref[...] = value
    lanes = iota((GROUP, LANES), 1)
    seat = quad_of(g)
    columns = jnp.where(lanes == 2 * seat, results[7][0], 0.0) + jnp.where(lanes == 2 * seat + 1, results[7][1], 0.0)

    @pl.when(g == 0)
    def first():
        stats[...] = jnp.zeros_like(stats)

    stats[...] += jnp.transpose(columns)[:8]


def quad_of(slot):
    quad = lax.axis_index("dp") % QUADS
    return (quad % 2 + slot % 2) % 2 + 2 * ((quad // 2 + slot // 2) % 2)


def full_spec(shape):
    return pl.BlockSpec(shape, lambda g: (0,) * len(shape))


def group_spec(width):
    return pl.BlockSpec((GROUP, width), lambda g: (g, 0))


VMEM_GRANT = 60 * 1024 * 1024


def run_forward(lens, tok, cot, w_own, w_com, w_out, gain_in, gain_out, conv, heads, skip, select):
    f32, bf16 = (jnp.float32, jnp.bfloat16)
    rows = QUADS * GROUP
    widths = ((D, bf16), (OWN, f32), (MIX, f32), (LANES, f32), (MIX, bf16), (OWN, f32), (OWN, f32))
    return pl.pallas_call(
        forward_kernel,
        grid=(QUADS,),
        in_specs=[full_spec(lens.shape), group_spec(D), group_spec(D)]
        + [full_spec(a.shape) for a in (w_own, w_com, w_out, gain_in, gain_out, conv, heads, skip, select)],
        out_specs=[group_spec(w) for w, kind in widths] + [full_spec((8, GROUP))],
        out_shape=[jax.ShapeDtypeStruct((rows, w), kind) for w, kind in widths]
        + [jax.ShapeDtypeStruct((8, GROUP), f32)],
        compiler_params=pltpu.CompilerParams(vmem_limit_bytes=VMEM_GRANT),
    )(lens, tok, cot, w_own, w_com, w_out, gain_in, gain_out, conv, heads, skip, select)


def backward_block(k, act, dmix, step, logdec, skip, state, state_grad, spread, gather):
    values, keys, queries = (act[:, :OWN], act[:, OWN : OWN + NST], act[:, OWN + NST :])
    lower = lower_mask()
    cumul, cumul_t, step_w, cumul_w = block_parts(step, logdec, spread)
    step_t = jnp.transpose(step)
    gram = jnp.where(lower, mm_t(queries, keys), 0.0)
    values_f = values.astype(jnp.float32)
    dmix_f = dmix.astype(jnp.float32)
    lanes_h = iota((BLOCK, LANES), 1)
    rows_h = iota((8, BLOCK), 0)
    grad_gram = 0.0
    row_sums = jnp.zeros((BLOCK, LANES), jnp.float32)
    col_sums = jnp.zeros((8, BLOCK), jnp.float32)
    pieces = []
    for pair in range(PAIRS):
        lanes = slice(pair * LANES, (pair + 1) * LANES)
        piece = 0.0
        for side in range(2):
            h = 2 * pair + side
            decay = decay_of(cumul, cumul_t, h)
            dm_half = lane_half(dmix[:, lanes], side)
            grad_mixing = mm_t(dm_half, values[:, lanes])
            step_row = step_t[h : h + 1, :]
            grad_gram = grad_gram + grad_mixing * decay * step_row
            mixing = gram * decay
            piece = piece + t_mm(low16(mixing), dm_half)
            product = grad_mixing * mixing
            col_sums = jnp.where(rows_h == h, jnp.sum(product, axis=0, keepdims=True), col_sums)
            row_sums = jnp.where(
                lanes_h == h, jnp.sum(product * step_row, axis=1, keepdims=True), row_sums
            )
        pieces.append(piece)
    grad_values = jnp.concatenate(pieces, axis=1) * step_w + skip * dmix_f
    grad_skip = jnp.sum(dmix_f * values_f, axis=0, keepdims=True)
    grad_gram = low16(jnp.where(lower, grad_gram, 0.0))
    grad_queries = mm(grad_gram, keys)
    grad_keys = t_mm(grad_gram, queries)
    columns = jnp.transpose(jnp.concatenate([col_sums, jnp.zeros((LANES - 8, BLOCK), jnp.float32)], axis=0))
    grad_step = columns
    grad_cumul = row_sums - columns * step
    if k == 1:
        entering = jnp.exp(cumul_w) * dmix_f
        entering_low = low16(entering)
        crossed = mm(queries, state)
        grad_cumul = grad_cumul + mm_full(entering * crossed, gather)
        grad_queries = grad_queries + mm_t(entering_low, state)
        before = low16(t_mm(queries, entering_low))
    else:
        tail = jnp.exp(cumul_w[BLOCK - 1 :] - cumul_w)
        weighting = tail * step_w
        back = mm(keys, state_grad)
        grad_values = grad_values + weighting * back
        grad_keys = grad_keys + mm_t(low16(weighting * values_f), state_grad)
        grad_weight = mm_full(values_f * back, gather)
        tail_h = jnp.exp(cumul[BLOCK - 1 :] - cumul)
        grad_step = grad_step + grad_weight * tail_h
        part = grad_weight * tail_h * step
        last = iota((BLOCK, LANES), 0) == BLOCK - 1
        grad_cumul = grad_cumul - part + jnp.where(last, jnp.sum(part, axis=0, keepdims=True), 0.0)
        before = None
    upper = (iota((BLOCK, BLOCK), 0) <= iota((BLOCK, BLOCK), 1)).astype(jnp.float32)
    grad_logdec = mm_full(upper, grad_cumul)
    return (grad_values, grad_keys, grad_queries, grad_step, grad_logdec, grad_skip, before)


def gate_kernel(
    lens, stats, shared, cot, normed, gate_part, mixed, grad_normed_out, w_out, gain_out,
    branch, dgate, dmix, g_out, g_gate, g_gain, acc_out, acc_gate
):
    g = pl.program_id(0)
    live = live_of(lens[...], g)

    @pl.when(g == 0)
    def first():
        acc_out[...] = jnp.zeros_like(acc_out)
        acc_gate[...] = jnp.zeros_like(acc_gate)
        g_gain[...] = jnp.zeros_like(g_gain)

    total = stats[...]
    rank = 2 * (lax.axis_index("dp") % QUADS) + lax.axis_index("seq")
    for r in range(RANKS):
        total = total + jnp.where(rank == r, 0.0, shared[r])
    columns = jnp.transpose(jnp.concatenate([total, jnp.zeros((LANES - 8, GROUP), jnp.float32)], axis=0))
    lanes = iota((GROUP, LANES), 1)
    seat = quad_of(g)
    power = jnp.sum(jnp.where(lanes == 2 * seat, columns, 0.0), axis=1, keepdims=True)
    along = jnp.sum(jnp.where(lanes == 2 * seat + 1, columns, 0.0), axis=1, keepdims=True)
    scale_out = lax.rsqrt(power * (1.0 / DIN) + norm_eps)
    gate_v, mixed_v, gno = (gate_part[...], mixed[...], grad_normed_out[...])
    sig = sigmoid(gate_v)
    gate_act = gate_v * sig
    gated = mixed_v * gate_act
    normed_out = low16(gated * scale_out * gain_out[...])
    for half in range(2):
        rows = slice(half * BLOCK, (half + 1) * BLOCK)
        branch[0, half] = low16(mm(normed_out[rows], w_out[...]))
    grad = jnp.where(live > 0.0, cot[...], jnp.zeros_like(cot[...]))
    acc_out[...] += t_mm(normed_out, grad)
    scaled = gno * scale_out
    grad_gated = scaled * gain_out[...] - gated * (scale_out * scale_out * scale_out * along * (1.0 / DIN))
    gain_sum = jnp.sum(scaled * gated, axis=0, keepdims=True)
    g_gain[...] += jnp.concatenate([gain_sum, jnp.zeros((7, OWN), jnp.float32)], axis=0)
    grad_gate = low16(grad_gated * mixed_v * (sig * (1.0 + gate_v * (1.0 - sig))))
    dgate[...] = grad_gate
    dmix[...] = low16(grad_gated * gate_act)
    acc_gate[...] += t_mm(normed[...], grad_gate)

    @pl.when(g == QUADS - 1)
    def last():
        g_out[...] = low16(acc_out[...])
        g_gate[...] = low16(acc_gate[...])


def run_gate(lens, stats, shared, cot, normed, gate_part, mixed, grad_normed_out, w_out, gain_out):
    f32, bf16 = (jnp.float32, jnp.bfloat16)
    rows = QUADS * GROUP
    grouped = (cot, normed, gate_part, mixed, grad_normed_out)
    ends = (((OWN, D), bf16), ((D, OWN), bf16), ((8, OWN), f32))
    return pl.pallas_call(
        gate_kernel,
        grid=(QUADS,),
        in_specs=[full_spec(a.shape) for a in (lens, stats, shared)]
        + [group_spec(a.shape[1]) for a in grouped]
        + [full_spec(w_out.shape), full_spec(gain_out.shape)],
        out_specs=[pl.BlockSpec((1, 2, BLOCK, D), lambda g: (g, 0, 0, 0)), group_spec(OWN), group_spec(OWN)]
        + [full_spec(s) for s, kind in ends],
        out_shape=[
            jax.ShapeDtypeStruct((QUADS, 2, BLOCK, D), bf16),
            jax.ShapeDtypeStruct((rows, OWN), bf16),
            jax.ShapeDtypeStruct((rows, OWN), bf16),
        ]
        + [jax.ShapeDtypeStruct(s, kind) for s, kind in ends],
        scratch_shapes=[pltpu.VMEM((OWN, D), f32), pltpu.VMEM((D, OWN), f32)],
        compiler_params=pltpu.CompilerParams(vmem_limit_bytes=VMEM_GRANT),
    )(lens, stats, shared, *grouped, w_out, gain_out)


def backward_group(live, dmix, conv_in, raw, act, conv, heads, skip):
    act_v = act[...]
    raw_v = raw[...]
    heads_v = heads[...]
    step, logdec = steps_of(raw_v, heads_v, live)
    spread, gather = (head_spread(), head_gather())
    rows0, rows1 = (slice(0, BLOCK), slice(BLOCK, GROUP))
    cumul0 = mm_full(lower_mask().astype(jnp.float32), logdec[rows0])
    cumul0_w = mm_full(cumul0, spread)
    weighting = jnp.exp(cumul0_w[BLOCK - 1 :] - cumul0_w) * mm_full(step[rows0], spread)
    state = low16(
        t_mm(act_v[rows0, OWN : OWN + NST], low16(weighting * act_v[rows0, :OWN].astype(jnp.float32)))
    )
    late = backward_block(
        1, act_v[rows1], dmix[rows1], step[rows1], logdec[rows1], skip[...], state, None, spread, gather
    )
    early = backward_block(
        0, act_v[rows0], dmix[rows0], step[rows0], logdec[rows0], skip[...], None, late[6], spread, gather
    )
    grad_act = jnp.concatenate([jnp.concatenate(part[:3], axis=1) for part in (early, late)], axis=0)
    grad_step = jnp.concatenate([early[3], late[3]], axis=0)
    grad_logdec = jnp.concatenate([early[4], late[4]], axis=0)
    rate = jnp.exp(heads_v[1:2])
    grad_raw = (grad_step - rate * grad_logdec) * live * heads_v[3:4] * sigmoid(raw_v + heads_v[0:1])
    u = conv_in[...]
    conv_v = conv[...]
    preact = preact_of(u, conv_v)
    sig_q = sigmoid(preact)
    grad_pre = grad_act * (sig_q * (1.0 + preact * (1.0 - sig_q)))
    grad_u = grad_pre * conv_v[KCONV - 1 : KCONV]
    taps = []
    for tap in range(KCONV):
        lag = KCONV - 1 - tap
        if lag:
            grad_u = grad_u + shift_up(grad_pre, lag) * conv_v[tap : tap + 1]
        taps.append(jnp.sum(grad_pre * shift_down(u, lag), axis=0, keepdims=True))
    taps.append(jnp.sum(grad_pre, axis=0, keepdims=True))
    small = (
        jnp.concatenate(taps + [jnp.zeros((3, MIX), jnp.float32)], axis=0),
        jnp.sum(grad_raw, axis=0, keepdims=True),
        jnp.sum(grad_logdec * logdec, axis=0, keepdims=True),
        early[5] + late[5],
    )
    return (grad_u, grad_raw, small)


PACK = 48


def back_kernel(
    lens, gate_grads, out_grads, branch_all, w_own, w_com, conv, heads, skip, select, gain_in, g_gain, tok_own,
    branch, normed, dgate, dmix, conv_in, raw, act,
    r_out, all_gate, all_x, sum_com, packs, sum_branch, grad_rows,
    acc_x, acc_com, small_conv, small_head, small_skip,
    branch_sib, en_part, en_sib, branch_got, en_got, branch_relay, en_relay,
    gate_got, gate_own, sum_gate, x_send, x_got, sum_x, com_send, com_sib, com_quad, com_z, com_got,
    pack_send, pack_got, pack_sum,
    sends, recvs, out_send, out_recv, local
):
    s = pl.program_id(0)
    slot = QUADS - 1 - s
    plane, quad, core = place()
    where = (plane, quad, core)
    rank = 2 * quad + core
    sibling = at(plane, quad, flip(core))
    f32 = jnp.float32
    sems = Sems(sends, recvs)
    to_x, to_y = (at(plane, xor4(quad, 1), core), at(plane, xor4(quad, 2), core))
    half = BLOCK // 2

    swaps = [
        [sems.copy(source.at[k, flip(core)], target.at[k], sibling) for k in range(QUADS)]
        for source, target in ((branch_all, branch_sib), (en_part, en_sib))
    ]
    routes = []
    for sib, got, relay in ((branch_sib, branch_got, branch_relay), (en_sib, en_got, en_relay)):
        routes.append(
            {
                "relay_x": sems.copy(sib.at[3, pl.ds(0, half)], relay.at[0], to_x),
                "relay_y": sems.copy(sib.at[3, pl.ds(half, half)], relay.at[1], to_y),
                "x": sems.copy(sib.at[1], got.at[0], to_x),
                "y": sems.copy(sib.at[2], got.at[1], to_y),
            }
        )

    def z_push(source, target):
        return [
            sems.copy(source.at[xor4(plane, k)], target.at[k - 1], at(xor4(plane, k), quad, core))
            for k in (2, 3, 1)
        ]

    def rank_push(source, target):
        copies = []
        for k in range(1, RANKS):
            other_core = flip(core) if k % 2 else core
            other_quad = xor4(quad, k // 2)
            copies.append(
                sems.copy(source(2 * other_quad + other_core), target.at[rank], at(plane, other_quad, other_core))
            )
        return copies

    gate_z = z_push(gate_grads, gate_got)
    x_z = z_push(x_send, x_got)
    gate_ranks = rank_push(lambda r: sum_gate.at[r], all_gate)
    x_ranks = rank_push(lambda r: sum_x.at[r], all_x)
    com_swap = sems.copy(com_send.at[:, :, flip(core)], com_sib, sibling)
    com_quads = [
        sems.copy(com_sib.at[:, xor4(quad, k)], com_quad.at[k - 1], at(plane, xor4(quad, k), core))
        for k in (3, 1, 2)
    ]
    com_planes = z_push(com_z, com_got)
    pack_z = [
        sems.copy(pack_send, pack_got.at[k - 1], at(xor4(plane, k), quad, core)) for k in (2, 3, 1)
    ]
    pack_ranks = rank_push(lambda r: pack_sum, packs)

    def out_copy(near, side):
        return pltpu.make_async_remote_copy(
            src_ref=out_grads.at[near, side],
            dst_ref=r_out.at[plane],
            send_sem=out_send.at[2 * near + side],
            recv_sem=out_recv.at[plane],
            device_id=at(2 * core + near, quad, side),
            device_id_type=MESH_ID,
        )

    def out_landing(origin):
        return pltpu.make_async_remote_copy(
            src_ref=out_grads.at[0, 0],
            dst_ref=r_out.at[origin],
            send_sem=out_send.at[0],
            recv_sem=out_recv.at[origin],
            device_id=sibling,
            device_id_type=MESH_ID,
        )

    out_here = pltpu.make_async_copy(out_grads.at[plane % 2, core], r_out.at[plane], local.at[0])
    out_stays = plane // 2 == core
    gate_here = pltpu.make_async_copy(gate_grads.at[plane], gate_own, local.at[1])

    @pl.when(s == 0)
    def begin():
        peers = plane_mates(*where) + plane_others(*where)
        peers += [at(xor4(plane, k), quad, flip(core)) for k in range(1, PLANES)]
        greet(peers)
        for copy in gate_z:
            copy.start()
        for copy in swaps[0][::-1]:
            copy.start()
        for near in range(2):
            for side in range(2):

                @pl.when(jnp.logical_not((2 * core + near == plane) & (core == side)))
                def go():
                    out_copy(near, side).start()

        @pl.when(out_stays)
        def stay():
            out_here.start()

        gate_here.start()
        for ref in (acc_x, acc_com, small_conv, small_head, small_skip):
            ref[...] = jnp.zeros_like(ref)

    live = live_of(lens[...], slot)
    grad_u, grad_raw, small = backward_group(live, dmix[...], conv_in, raw, act, conv, heads, skip)
    small_conv[...] += small[0]
    small_head[0:1] += small[1]
    small_head[1:2] += small[2]
    small_skip[0:1] += small[3]
    raw_wide = mm_t(low16(grad_raw), low16(select[...]))
    grad_x = low16(grad_u[:, :OWN])
    grad_com = low16(jnp.concatenate([grad_u[:, OWN:], raw_wide], axis=1))
    for side in range(2):
        rows = slice(side * BLOCK, (side + 1) * BLOCK)
        en_part[slot, side] = low16(
            mm_t(dgate[rows], w_own[:, :OWN]) + mm_t(grad_x[rows], w_own[:, OWN:]) + mm_t(grad_com[rows], w_com[...])
        )
    for k in range(QUADS):

        @pl.when(slot == k)
        def swap_en():
            swaps[1][k].start()

    normed_v = normed[...]
    acc_x[...] += t_mm(normed_v, grad_x)
    acc_com[...] += t_mm(normed_v, grad_com)

    def settle(kind, k, own, sib):
        route = routes[kind]
        relay = (branch_relay, en_relay)[kind]
        swaps[kind][k].wait_recv()
        sib[k] = low16(own.astype(f32) + sib[k].astype(f32))
        if k == 3:
            route["relay_x"].start()
            route["relay_y"].start()
        if k == 2:
            route["relay_x"].wait_recv()
            sib[k, :half] = low16(sib[k, :half].astype(f32) + relay[0].astype(f32))
            route["y"].start()
        if k == 1:
            route["relay_y"].wait_recv()
            sib[k, half:] = low16(sib[k, half:].astype(f32) + relay[1].astype(f32))
            route["x"].start()

    for k in range(QUADS):

        @pl.when(slot == k)
        def settle_branch():
            settle(0, k, branch[0, core], branch_sib)

        if k < QUADS - 1:

            @pl.when(slot == k)
            def settle_en():
                settle(1, k + 1, en_part[k + 1, core], en_sib)

    @pl.when(s == QUADS - 1)
    def tail():
        x_send[...] = low16(acc_x[...]).reshape(x_send.shape)
        for copy in x_z:
            copy.start()
        com_send[...] = low16(acc_com[...]).reshape(com_send.shape)
        com_swap.start()
        settle(1, 0, en_part[0, core], en_sib)
        gate_here.wait()
        for copy in gate_z:
            copy.wait_recv()
        sum_gate[...] = low16(
            gate_own[...].astype(f32) + gate_got[0].astype(f32) + gate_got[1].astype(f32) + gate_got[2].astype(f32)
        )
        for copy in gate_ranks:
            copy.start()
        gate_keep = pltpu.make_async_copy(sum_gate.at[rank], all_gate.at[rank], local.at[2])
        gate_keep.start()
        com_swap.wait_recv()
        com_sib[...] = low16(com_sib[...].astype(f32) + com_send[:, :, core].astype(f32))
        for copy in com_quads:
            copy.start()
        for name in ("x", "y"):
            routes[0][name].wait_recv()
        sum_branch[...] = (
            branch_sib[0].astype(f32) + branch_got[0].astype(f32) + branch_got[1].astype(f32)
        )
        for copy in com_quads:
            copy.wait_recv()
        com_z[...] = low16(
            com_sib[:, quad].astype(f32)
            + com_quad[0].astype(f32) + com_quad[1].astype(f32) + com_quad[2].astype(f32)
        )
        for copy in com_planes:
            copy.start()
        for name in ("x", "y"):
            routes[1][name].wait_recv()
        en = en_sib[0].astype(f32) + en_got[0].astype(f32) + en_got[1].astype(f32)
        rows = tok_own[...].astype(f32)
        scaling = lax.rsqrt(jnp.mean(rows * rows, axis=1, keepdims=True) + norm_eps)
        scaled = rows * scaling
        gain_grad = jnp.sum(en * scaled, axis=0, keepdims=True)
        weighted = en * gain_in[...]
        inner = jnp.mean(weighted * scaled, axis=1, keepdims=True)
        grad_rows[...] = scaling * (weighted - scaled * inner)
        pack_send[...] = jnp.zeros_like(pack_send)
        for i in range(D // LANES):
            pack_send[i : i + 1] = gain_grad[:, i * LANES : (i + 1) * LANES]
        gain_out_grad = g_gain[0:1]
        skip_grad = small_skip[0:1]
        for i in range(PAIRS):
            lanes = slice(i * LANES, (i + 1) * LANES)
            pack_send[12 + i : 13 + i] = gain_out_grad[:, lanes]
            pack_send[42 + i : 43 + i] = skip_grad[:, lanes]
            for tap in range(KCONV + 1):
                pack_send[15 + 3 * tap + i : 16 + 3 * tap + i] = small_conv[tap : tap + 1, lanes]
        for tap in range(KCONV + 1):
            for i in range(2):
                lanes = slice(OWN + i * LANES, OWN + (i + 1) * LANES)
                pack_send[30 + 2 * tap + i : 31 + 2 * tap + i] = small_conv[tap : tap + 1, lanes]
        pack_send[40:42] = small_head[0:2]
        for copy in pack_z:
            copy.start()
        for copy in com_planes:
            copy.wait_recv()
        sum_com[...] = (
            com_z[plane].astype(f32)
            + com_got[0].astype(f32) + com_got[1].astype(f32) + com_got[2].astype(f32)
        )
        for copy in pack_z:
            copy.wait_recv()
        pack_sum[...] = pack_send[...] + pack_got[0] + pack_got[1] + pack_got[2]
        for copy in pack_ranks:
            copy.start()
        pack_keep = pltpu.make_async_copy(pack_sum, packs.at[rank], local.at[3])
        pack_keep.start()
        for copy in x_z:
            copy.wait_recv()
        sum_x[...] = low16(
            x_send[plane].astype(f32) + x_got[0].astype(f32) + x_got[1].astype(f32) + x_got[2].astype(f32)
        )
        for copy in x_ranks:
            copy.start()
        x_keep = pltpu.make_async_copy(sum_x.at[rank], all_x.at[rank], local.at[4])
        x_keep.start()
        for origin in range(PLANES):

            @pl.when(jnp.logical_not((plane == origin) & out_stays))
            def arrived():
                out_landing(origin).wait_recv()

        @pl.when(out_stays)
        def kept():
            out_here.wait()

        for near in range(2):
            for side in range(2):

                @pl.when(jnp.logical_not((2 * core + near == plane) & (core == side)))
                def gone():
                    out_copy(near, side).wait_send()

        for copy in gate_ranks + pack_ranks + x_ranks:
            copy.wait_recv()
        for copy in gate_z + x_z + gate_ranks + x_ranks + [com_swap] + com_quads + com_planes + pack_z + pack_ranks:
            copy.wait_send()
        for kind in range(2):
            for copy in swaps[kind] + list(routes[kind].values()):
                copy.wait_send()
        gate_keep.wait()
        pack_keep.wait()
        x_keep.wait()


def run_back(lens, gate_grads, out_grads, branch, w_own, w_com, conv, heads, skip, select, gain_in, g_gain, tok_own,
             normed, dgate, dmix, conv_in, raw, act):
    f32, bf16 = (jnp.float32, jnp.bfloat16)
    rows_in = D // (PLANES * RANKS)
    rows_out = DIN // (PLANES * RANKS)
    gate_grads = gate_grads.reshape(PLANES, RANKS, rows_in, OWN)
    out_grads = out_grads.reshape(2, 2, rows_out, D)
    fixed = (w_own, w_com, conv, heads, skip, select, gain_in, g_gain, tok_own)
    grouped = (normed, dgate, dmix, conv_in, raw, act)

    def turned(width):
        return pl.BlockSpec((GROUP, width), lambda s: (QUADS - 1 - s, 0))

    outs = (
        ((PLANES, rows_out, D), bf16, ANY),
        ((RANKS, rows_in, OWN), bf16, ANY),
        ((RANKS, rows_in, OWN), bf16, ANY),
        ((rows_in, COMMON_PAD), f32, None),
        ((RANKS, PACK, LANES), f32, ANY),
        ((BLOCK, D), f32, None),
        ((BLOCK, D), f32, None),
    )
    half = BLOCK // 2
    quarter = (RANKS, rows_in, OWN)
    com = (rows_in, COMMON_PAD)
    scratch = [
        ((D, OWN), f32), ((D, COMMON_PAD), f32), ((8, MIX), f32), ((8, LANES), f32), ((8, OWN), f32),
        ((QUADS, BLOCK, D), bf16), ((QUADS, 2, BLOCK, D), bf16), ((QUADS, BLOCK, D), bf16),
        ((2, BLOCK, D), bf16), ((2, BLOCK, D), bf16), ((2, half, D), bf16), ((2, half, D), bf16),
        ((PLANES - 1,) + quarter, bf16), (quarter, bf16), (quarter, bf16),
        ((PLANES,) + quarter, bf16), ((PLANES - 1,) + quarter, bf16), (quarter, bf16),
        ((PLANES, QUADS, 2) + com, bf16), ((PLANES, QUADS) + com, bf16), ((QUADS - 1, PLANES) + com, bf16),
        ((PLANES,) + com, bf16), ((PLANES - 1,) + com, bf16),
        ((PACK, LANES), f32), ((PLANES - 1, PACK, LANES), f32), ((PACK, LANES), f32),
    ]
    return pl.pallas_call(
        back_kernel,
        grid=(QUADS,),
        in_specs=[full_spec(lens.shape), ANY, ANY, ANY]
        + [full_spec(a.shape) for a in fixed]
        + [pl.BlockSpec((1, 2, BLOCK, D), lambda s: (QUADS - 1 - s, 0, 0, 0))]
        + [turned(a.shape[1]) for a in grouped],
        out_specs=[full_spec(s) if spec is None else spec for s, kind, spec in outs],
        out_shape=[jax.ShapeDtypeStruct(s, kind) for s, kind, spec in outs],
        scratch_shapes=[pltpu.VMEM(s, kind) for s, kind in scratch]
        + [
            pltpu.SemaphoreType.DMA((64,)),
            pltpu.SemaphoreType.DMA((64,)),
            pltpu.SemaphoreType.DMA((4,)),
            pltpu.SemaphoreType.DMA((4,)),
            pltpu.SemaphoreType.DMA((5,)),
        ],
        compiler_params=pltpu.CompilerParams(
            vmem_limit_bytes=VMEM_GRANT, collective_id=2, has_side_effects=True
        ),
    )(lens, gate_grads, out_grads, branch, *fixed, branch, *grouped)


def adam_refs(refs, index, gradient, rate):
    weight, first, second, weight_new, first_new, second_new = refs
    results = adam_update(weight[index], first[index], second[index], gradient, rate)
    for ref, value in zip((weight_new, first_new, second_new), results):
        ref[index] = value


def finish_kernel(
    lens, tok, cot, sum_branch, grad_rows, r_out, all_gate, all_x, sum_com,
    in_w, in_m, in_v, out_w, out_m, out_v,
    mixed_out, grad_input, in_wn, in_mn, in_vn, out_wn, out_mn, out_vn
):
    f32 = jnp.float32
    core = lax.axis_index("seq")
    position = (iota((BLOCK, 1), 0) + core * BLOCK).astype(f32)
    live = (position < lens[0:1, 0:1]).astype(f32)
    mixed_out[...] = (tok[...].astype(f32) + live * sum_branch[...]).astype(jnp.bfloat16)
    grad_input[...] = cot[...].astype(f32) + grad_rows[...]
    ins = (in_w, in_m, in_v, in_wn, in_mn, in_vn)
    rows = in_w.shape[0]
    lanes = iota((rows, LANES), 1)
    for part, source in ((0, all_gate), (1, all_x)):
        for run in range(PLANES):
            side, near = divmod(run, 2)
            tiles = []
            for t in range(2 * PAIRS):
                halves = []
                for b in range(2):
                    p, i = divmod(2 * t + b, 3)
                    index = 3 * near + i
                    tile = source[2 * p + side, :, (index // 2) * LANES : (index // 2 + 1) * LANES].astype(f32)
                    halves.append(tile if index % 2 == b else pltpu.roll(tile, HDIM, 1))
                tiles.append(jnp.where(lanes < HDIM, halves[0], halves[1]))
            start = part * DIN + run * 2 * OWN
            adam_refs(ins, (slice(None), slice(start, start + 2 * OWN)), jnp.concatenate(tiles, axis=1), rate_in)
    adam_refs(ins, (slice(None), slice(2 * DIN, 2 * DIN + COMMON)), sum_com[:, :COMMON], rate_in)
    total = r_out[0].astype(f32) + r_out[1].astype(f32) + r_out[2].astype(f32) + r_out[3].astype(f32)
    adam_refs((out_w, out_m, out_v, out_wn, out_mn, out_vn), (slice(None), slice(None)), total, rate_out)


def run_finish(*args):
    tok, cot, in_w, out_w = (args[1], args[2], args[9], args[12])
    shapes = [(tok.shape, jnp.bfloat16), (cot.shape, jnp.float32)]
    shapes += [(in_w.shape, jnp.float32)] * 3 + [(out_w.shape, jnp.float32)] * 3
    whole = pl.BlockSpec(memory_space=pltpu.VMEM)
    return pl.pallas_call(
        finish_kernel,
        in_specs=[whole] * len(args),
        out_specs=[whole] * len(shapes),
        out_shape=[jax.ShapeDtypeStruct(s, kind) for s, kind in shapes],
        compiler_params=pltpu.CompilerParams(vmem_limit_bytes=VMEM_GRANT),
    )(*args)


def pick_runs(array, plane_runs, quad, core):
    lead = array.shape[:-1]
    width = array.shape[-1] // (PLANES * QUADS)
    split = array.reshape(lead + (2, 2, QUADS, width))
    zero = 0
    n = len(lead)
    taken = lax.dynamic_slice(
        split, (zero,) * n + (core, 0, quad, 0), lead + (1, 2, 1, width)
    )
    return taken.reshape(lead + (2 * width,))


def put_runs(array, quad, core):
    lead = array.shape[:-1]
    width = array.shape[-1] // 2
    zeros = jnp.zeros(lead + (2, 2, QUADS, width), array.dtype)
    n = len(lead)
    full = lax.dynamic_update_slice(
        zeros, array.reshape(lead + (1, 2, 1, width)), (0,) * n + (core, 0, quad, 0)
    )
    return full.reshape(lead + (width * PLANES * QUADS,))


def rank_slices(array):
    rows = array.shape[0]
    split = array.reshape(rows, 2, 2, QUADS, RUN)
    return split.transpose(3, 1, 0, 2, 4).reshape(RANKS, rows, OWN)


def rank_join(array):
    rows = array.shape[1]
    split = array.reshape(QUADS, 2, rows, 2, RUN)
    return split.transpose(2, 1, 3, 0, 4).reshape(rows, DIN)


def per_device_quad(
    tokens_in,
    cotangent,
    seq_lens,
    in_weight,
    in_first,
    in_second,
    out_weight,
    out_first,
    out_second,
    conv_weight,
    conv_first,
    conv_second,
    gains,
    gain_first,
    gain_second,
    head_params,
    head_first,
    head_second,
):
    bf16, f32 = (jnp.bfloat16, jnp.float32)
    plane, quad, core = place()
    rank = 2 * quad + core
    rows = in_weight.shape[0]
    in_low = in_weight.astype(bf16)
    out_low = out_weight.astype(bf16)
    wz = jnp.concatenate([rank_slices(in_low[:, :DIN]), rank_slices(in_low[:, DIN : 2 * DIN])], axis=2)
    first_len = jnp.full((rows, 1), seq_lens[0, 0] - BLOCK).astype(bf16)
    conv_flat = jnp.pad(conv_weight.reshape(-1), (0, 8)).astype(bf16).reshape(rows, 11)
    wc = jnp.concatenate(
        [in_low[:, 2 * DIN :], gains.astype(bf16).reshape(rows, 3), conv_flat, first_len], axis=1
    )
    wc = jnp.pad(wc, ((0, 0), (0, COMMON_PAD - wc.shape[1])))
    tok, cot, w_own, w_com, w_out = gather_all(tokens_in, cotangent, wz, wc, out_low)
    tok = tok.reshape(RANKS * BLOCK, D)
    cot = cot.reshape(RANKS * BLOCK, D)
    w_own = w_own.reshape(D, 2 * OWN)
    w_out = w_out.reshape(OWN, D)
    extras = w_com[:, :, :, COMMON:].astype(f32)
    gain_par = extras[:, :, :, :3].reshape(D + DIN)
    conv_par = (
        extras[:, :, :, 3:14].reshape(PLANES * RANKS, 11 * rows)[:, : 5 * 104]
        .reshape(PLANES * RANKS, 5, 104).transpose(1, 0, 2).reshape(5, CONVC)
    )
    lens = lax.dynamic_index_in_dim(extras, plane, 0, False)[::2, 0, 14] + BLOCK
    lens = jnp.stack([lax.dynamic_index_in_dim(lens, xor4(quad, k), 0, False) for k in range(QUADS)])
    w_com = w_com.reshape(D, COMMON_PAD)
    lens_rows = jnp.pad(jnp.broadcast_to(lens[:, None], (QUADS, LANES)), ((0, 8 - QUADS), (0, 0)))
    conv_own = jnp.concatenate([pick_runs(conv_par[:, :DIN], 2, quad, core), conv_par[:, DIN:]], axis=1)
    conv_own = jnp.pad(conv_own, ((0, 3), (0, 0)))
    gain_out = pick_runs(gain_par[D:], 2, quad, core)[None, :]
    head_own = pick_runs(head_params, 2, quad, core)
    heads = jnp.pad(
        jnp.concatenate([head_own, jnp.ones((1, OWN_HEADS), f32)]), ((0, 4), (0, LANES - OWN_HEADS))
    )
    skip = jnp.repeat(head_own[2], HDIM)[None, :]
    head_index = pick_runs(jnp.arange(HEADS)[None, :], 2, quad, core)[0]
    select = (iota((LANES, OWN_HEADS), 0) == head_index[None, :]).astype(f32)
    select = jnp.pad(select, ((0, 0), (0, LANES - OWN_HEADS)))

    normed, gate_part, conv_in, raw, act, mixed, grad_normed_out, stats = run_forward(
        lens_rows, tok, cot, w_own, w_com, w_out, gain_par[None, :D], gain_out, conv_own, heads, skip, select
    )
    shared = share(1, stats)
    branch, dgate, dmix, g_out, g_gate, g_gain = run_gate(
        lens_rows, stats, shared, cot, normed, gate_part, mixed, grad_normed_out, w_out, gain_out
    )
    r_out, all_gate, all_x, sum_com, packs, sum_branch, grad_rows = run_back(
        lens_rows, g_gate, g_out, branch, w_own, w_com, conv_own, heads, skip, select, gain_par[None, :D], g_gain,
        tokens_in, normed, dgate, dmix, conv_in, raw, act
    )
    finished = run_finish(
        lens_rows, tokens_in, cotangent, sum_branch, grad_rows, r_out, all_gate, all_x, sum_com,
        in_weight, in_first, in_second, out_weight, out_first, out_second
    )
    mine = rank + RANKS * plane
    grad_gains = jnp.concatenate(
        [jnp.sum(packs[:, :12], axis=0).reshape(D), rank_join(packs[:, 12:15].reshape(RANKS, 1, OWN)).reshape(DIN)]
    )
    gain_sum = lax.dynamic_slice(grad_gains, (mine * gains.shape[0],), gains.shape)
    grad_conv = jnp.concatenate(
        [
            rank_join(packs[:, 15:30].reshape(RANKS, KCONV + 1, OWN)),
            jnp.sum(packs[:, 30:40], axis=0).reshape(KCONV + 1, 2 * NST),
        ],
        axis=1,
    )
    conv_sum = lax.dynamic_slice(grad_conv, (0, mine * conv_weight.shape[1]), conv_weight.shape)
    grad_skip = jnp.sum(packs[:, 42:45].reshape(RANKS, 1, OWN_HEADS, HDIM), axis=3)
    head_sum = jnp.concatenate([packs[:, 40:42, :OWN_HEADS], grad_skip], axis=1)
    head_sum = head_sum.reshape(QUADS, 2, 3, 2, 3).transpose(2, 1, 3, 0, 4).reshape(3, HEADS)
    new_conv = adam_update(conv_weight, conv_first, conv_second, conv_sum, rate_conv)
    new_gain = adam_update(gains, gain_first, gain_second, gain_sum, rate_gain)
    new_head = adam_update(head_params, head_first, head_second, head_sum, rate_head)
    return tuple(finished) + new_conv + new_gain + new_head


def solution(mesh):
    placed = (
        P(("dp", "seq"), None),
        P(("dp", "seq"), None),
        P("dp", None),
        P(("dp", "seq"), None),
        P(("dp", "seq"), None),
        P(("dp", "seq"), None),
        P(("dp", "seq"), None),
        P(("dp", "seq"), None),
        P(("dp", "seq"), None),
        P(None, ("dp", "seq")),
        P(None, ("dp", "seq")),
        P(None, ("dp", "seq")),
        P(("dp", "seq")),
        P(("dp", "seq")),
        P(("dp", "seq")),
        P(),
        P(),
        P(),
    )
    quad = dict(mesh.shape) == {"dp": PLANES * QUADS, "seq": 2}
    return jax.shard_map(
        per_device_quad if quad else per_device,
        mesh=mesh,
        in_specs=placed,
        out_specs=(
            P(("dp", "seq"), None),
            P(("dp", "seq"), None),
            P(("dp", "seq"), None),
            P(("dp", "seq"), None),
            P(("dp", "seq"), None),
            P(("dp", "seq"), None),
            P(("dp", "seq"), None),
            P(("dp", "seq"), None),
            P(None, ("dp", "seq")),
            P(None, ("dp", "seq")),
            P(None, ("dp", "seq")),
            P(("dp", "seq")),
            P(("dp", "seq")),
            P(("dp", "seq")),
            P(),
            P(),
            P(),
        ),
        check_vma=False,
    )
```

```python
import functools

import jax
import jax.numpy as jnp
from jax import lax
from jax.experimental import pallas as pl
from jax.experimental.pallas import tpu as pltpu
from jax.sharding import PartitionSpec as P

D = 1536
HEADS = 48
HDIM = 64
NST = 128
KCONV = 4
BLOCK = 256
SLOTS = 4
STEP = 10
DIN = 3072
CONVC = 3328


highest = lax.Precision.HIGHEST
norm_eps = 1e-05
beta_first = 0.9
beta_second = 0.95
adam_eps = 1e-08
weight_decay = 0.1
rate_in = 0.01
rate_out = 0.008
rate_conv = 0.2
rate_gain = 0.4
rate_head = 0.5


def from_behind(block, axis, distance):
    devices = range(lax.axis_size(axis))
    route = [(i - distance, i) for i in devices if i - distance in devices]
    return lax.ppermute(block, axis, route)


def prefix(value, axis, join, neutral):
    place = lax.axis_index(axis)
    gathered = jax.tree.map(
        lambda a, kind: lax.all_gather(a.astype(kind), axis),
        value,
        jax.tree.map(lambda a: jnp.bfloat16 if a.dtype == jnp.float32 else a.dtype, value),
    )
    state = jax.tree.map(lambda a, e: jnp.zeros_like(a) + jnp.asarray(e, a.dtype), value, neutral)

    def one(hop, state):
        return join(
            state,
            jax.tree.map(
                lambda a, own: lax.dynamic_index_in_dim(a, hop, 0, False).astype(own.dtype),
                gathered,
                value,
            ),
        )

    return lax.fori_loop(0, place, one, state)


def prefix_2(value, axis, combine, identity):
    devices, index = (lax.axis_size(axis), lax.axis_index(axis))
    everything = jax.tree.map(
        lambda part, kind: lax.all_gather(part.astype(kind), axis),
        value,
        (jnp.bfloat16, jnp.bfloat16),
    )
    start = jax.tree.map(
        lambda part, zero: jnp.broadcast_to(jnp.asarray(zero, part.dtype), part.shape),
        value,
        identity,
    )

    def hop(k, before):
        at = devices - 1 - k
        reached = at > index
        new = combine(
            before, jax.tree.map(lambda part, own: part[at].astype(own.dtype), everything, value)
        )
        return jax.tree.map(lambda a, b: jnp.where(reached, a, b), new, before)

    return lax.fori_loop(0, devices, hop, start)


def segment_of(seq_row, position):
    blocks = (seq_row + BLOCK - 1) // BLOCK
    ends = jnp.cumsum(blocks) * BLOCK
    starts = ends - blocks * BLOCK
    above = position[:, None] >= starts[None, :]
    inside = above & (position[:, None] < ends[None, :])
    numbers = jnp.arange(1, SLOTS + 1, dtype=jnp.int32)
    labels_of = jnp.sum(jnp.where(inside, numbers[None, :], 0), axis=1)
    live_rows = jnp.sum(
        (above & (position[:, None] < (starts + seq_row)[None, :])).astype(jnp.float32), axis=1
    )
    return (labels_of, live_rows)


def layout(seq_row, position):
    labels_of, live_rows = segment_of(seq_row, position)
    columns = []
    for conv_lag in range(KCONV):
        earlier, unused_live = segment_of(seq_row, position - conv_lag)
        columns.append(((earlier == labels_of) & (labels_of > 0)).astype(jnp.float32))
    return (live_rows, jnp.stack(columns, axis=1))


def pre_norm(token_rows, gain_row):
    scaling = lax.rsqrt(jnp.mean(token_rows * token_rows, axis=1, keepdims=True) + norm_eps)
    return token_rows * scaling * gain_row[None, :]


def gate_norm(mixed, gate_part, gain_row):
    gated = mixed * jax.nn.silu(gate_part)
    scaling = lax.rsqrt(jnp.mean(gated * gated, axis=1, keepdims=True) + norm_eps)
    return gated * scaling * gain_row[None, :]


def mixer_in(extended, step_raw, conv_par, head_values, factors, live_rows):
    row_count = step_raw.shape[0]
    preact = jnp.zeros((row_count, conv_par.shape[1]), jnp.float32) + conv_par[KCONV][None, :]
    for conv_tap in range(KCONV):
        window = lax.slice_in_dim(extended, conv_tap, conv_tap + row_count, axis=0)
        preact = (
            preact
            + conv_par[conv_tap][None, :] * window * factors[:, KCONV - 1 - conv_tap][:, None]
        )
    conv_act = jax.nn.silu(preact)
    step_size = jax.nn.softplus(step_raw + head_values[0][None, :]) * live_rows[:, None]
    logdec = -jnp.exp(head_values[1])[None, :] * step_size
    return (conv_act, step_size, logdec)


def lower_ones():
    row_ids = lax.broadcasted_iota(jnp.int32, (BLOCK, BLOCK), 0)
    col_ids = lax.broadcasted_iota(jnp.int32, (BLOCK, BLOCK), 1)
    return (row_ids >= col_ids).astype(jnp.float32)


def block_state(values, keys_in, step_size, logdec):
    cumul = jnp.dot(lower_ones(), logdec, precision=highest)
    totals = cumul[-1]
    weighting = jnp.exp(totals[None, :] - cumul) * step_size
    states = jnp.einsum("uhp,un->hpn", weighting[:, :, None] * values, keys_in, precision=highest)
    return (jnp.exp(totals), states)


def block_out(values, keys_in, queries, step_size, logdec, skip_gain, start_state):
    lower_tri = lower_ones()
    cumul = jnp.dot(lower_tri, logdec, precision=highest)
    across = cumul.T
    gap_matrix = across[:, :, None] - across[:, None, :]
    decays = jnp.exp(jnp.where(lower_tri[None, :, :] > 0, gap_matrix, -1e30))
    gram_matrix = jnp.dot(queries, keys_in.T, precision=highest)
    mixing = gram_matrix[None, :, :] * decays * step_size.T[:, None, :]
    intra_part = jnp.einsum("htu,uhp->thp", mixing, values, precision=highest)
    carried = jnp.exp(cumul)[:, :, None] * jnp.einsum(
        "tn,hpn->thp", queries, start_state, precision=highest
    )
    return intra_part + carried + skip_gain[None, :, None] * values


def block_full(values, keys_in, queries, step_size, logdec, skip_gain, start_state):
    factor_end, states = block_state(values, keys_in, step_size, logdec)
    outputs = block_out(values, keys_in, queries, step_size, logdec, skip_gain, start_state)
    return (outputs, factor_end[:, None, None] * start_state + states)


def adam_update(weight, first, second, gradient, step_rate):
    first_new = beta_first * first + (1.0 - beta_first) * gradient
    second_new = beta_second * second + (1.0 - beta_second) * gradient * gradient
    first_hat = first_new / (1.0 - beta_first**STEP)
    second_hat = second_new / (1.0 - beta_second**STEP)
    weight_new = weight - step_rate * (
        first_hat / (jnp.sqrt(second_hat) + adam_eps) + weight_decay * weight
    )
    return (weight_new, first_new, second_new)


def carry_join(earlier, later):
    return (earlier[0] * later[0], later[0][:, None, None] * earlier[1] + later[1])


def as_float(array_low):
    return lax.optimization_barrier(array_low).astype(jnp.float32)


def contract_rows(left, right):
    return lax.dot_general(
        left, right, (((0,), (0,)), ((), ())), preferred_element_type=jnp.float32
    )


def contract_cols(left, right):
    return lax.dot_general(
        left, right, (((1,), (1,)), ((), ())), preferred_element_type=jnp.float32
    )


def per_device(
    tokens_in,
    cotangent,
    seq_lens,
    in_weight,
    in_first,
    in_second,
    out_weight,
    out_first,
    out_second,
    conv_weight,
    conv_first,
    conv_second,
    gains,
    gain_first,
    gain_second,
    head_params,
    head_first,
    head_second,
):
    local_tok = tokens_in.shape[0]
    position = lax.axis_index("seq") * local_tok + jnp.arange(local_tok, dtype=jnp.int32)
    live_rows, factors = layout(seq_lens[0], position)
    low_weights = (
        in_weight.astype(jnp.bfloat16),
        out_weight.astype(jnp.bfloat16),
        conv_weight.astype(jnp.bfloat16),
        gains.astype(jnp.bfloat16),
    )
    in_full, out_full, conv_full, gain_full = (
        lax.all_gather(low_weights[0], ("dp", "seq"), axis=0, tiled=True),
        lax.all_gather(low_weights[1], ("dp", "seq"), axis=0, tiled=True),
        lax.all_gather(low_weights[2], ("dp", "seq"), axis=1, tiled=True),
        lax.all_gather(low_weights[3], ("dp", "seq"), axis=0, tiled=True),
    )
    conv_par = conv_full.astype(jnp.float32)
    gain_par = gain_full.astype(jnp.float32)
    token_rows = tokens_in.astype(jnp.float32)
    normed_value, pull_pre = jax.vjp(pre_norm, token_rows, gain_par[:D])
    normed = normed_value.astype(jnp.bfloat16)
    projected = jnp.dot(normed, in_full, preferred_element_type=jnp.float32)
    gate_part = projected[:, :DIN]
    conv_in = projected[:, DIN : DIN + CONVC]
    step_raw = projected[:, DIN + CONVC :]
    halo_rows = from_behind(conv_in[local_tok - KCONV + 1 :], "seq", 1)
    extended = jnp.concatenate([halo_rows, conv_in], axis=0)

    def mixer_local(extended_rows, raw_steps, conv_values, head_values):
        return mixer_in(extended_rows, raw_steps, conv_values, head_values, factors, live_rows)

    (conv_act, step_size, logdec), pull_mixer = jax.vjp(
        mixer_local, extended, step_raw, conv_par, head_params
    )
    conv_used = as_float(conv_act.astype(jnp.bfloat16))
    block_count = local_tok // BLOCK
    values = conv_used[:, :DIN].reshape(block_count, BLOCK, HEADS, HDIM)
    keys_in = conv_used[:, DIN : DIN + NST].reshape(block_count, BLOCK, NST)
    queries = conv_used[:, DIN + NST :].reshape(block_count, BLOCK, NST)
    steps_blk = step_size.reshape(block_count, BLOCK, HEADS)
    logdec_blk = logdec.reshape(block_count, BLOCK, HEADS)
    resets = factors[::BLOCK, 1]
    skip_gain = head_params[2]
    decays, block_states = jax.vmap(block_state)(values, keys_in, steps_blk, logdec_blk)

    def fold_local(carried, block_item):
        factor_now = block_item[0] * block_item[2]
        return (
            (carried[0] * factor_now, factor_now[:, None, None] * carried[1] + block_item[1]),
            None,
        )

    identity = (jnp.ones((HEADS,), jnp.float32), jnp.zeros((HEADS, HDIM, NST), jnp.float32))
    device_sum, unused_fold = lax.scan(fold_local, identity, (decays, block_states, resets))
    unused_dec, entering = prefix(device_sum, "seq", carry_join, identity)

    def start_states(states, block_item):
        begin = block_item[2] * states
        return (block_item[0][:, None, None] * begin + block_item[1], begin)

    unused_end, begins = lax.scan(start_states, entering, (decays, block_states, resets))

    def emit(block_item):
        return block_out(
            block_item[0],
            block_item[1],
            block_item[2],
            block_item[3],
            block_item[4],
            skip_gain,
            block_item[5],
        )

    mixed = lax.map(emit, (values, keys_in, queries, steps_blk, logdec_blk, begins)).reshape(
        local_tok, DIN
    )
    normed_out_value, pull_gate = jax.vjp(gate_norm, mixed, gate_part, gain_par[D:])
    normed_out = normed_out_value.astype(jnp.bfloat16)
    branch = jnp.dot(normed_out, out_full, preferred_element_type=jnp.float32)
    mixed_out = (token_rows + live_rows[:, None] * branch).astype(jnp.bfloat16)
    out_grad = (cotangent.astype(jnp.float32) * live_rows[:, None]).astype(jnp.bfloat16)
    in_back, out_back = (
        lax.all_gather(in_weight.astype(jnp.bfloat16), ("dp", "seq"), axis=0, tiled=True),
        lax.all_gather(out_weight.astype(jnp.bfloat16), ("dp", "seq"), axis=0, tiled=True),
    )
    grad_out_w = contract_rows(normed_out, out_grad)
    grad_normed_out = contract_cols(out_grad, out_back)
    grad_mixed, grad_gate, grad_gain_in = pull_gate(grad_normed_out)
    mixed_back = as_float(grad_mixed.astype(jnp.bfloat16)).reshape(block_count, BLOCK, HEADS, HDIM)

    def adjoint_local(carried, block_item):
        cumul = jnp.dot(lower_ones(), block_item[2], precision=highest)
        weighted = jnp.exp(cumul)[:, :, None] * block_item[0]
        direct = jnp.einsum("thp,tn->hpn", weighted, block_item[1], precision=highest)
        return (block_item[4] * (direct + block_item[3][:, None, None] * carried), None)

    local_adj, unused_adj = lax.scan(
        adjoint_local, identity[1], (mixed_back, queries, logdec_blk, decays, resets), reverse=True
    )
    unused_later, leaving = prefix_2((device_sum[0], local_adj), "seq", carry_join, identity)

    def adjoint_block(carried, block_item):
        unused_primal, pull_block = jax.vjp(
            block_full,
            block_item[0],
            block_item[1],
            block_item[2],
            block_item[3],
            block_item[4],
            skip_gain,
            block_item[5],
        )
        grads = pull_block((block_item[6], carried[0]))
        return ((block_item[7] * grads[6], carried[1] + grads[5]), grads[:5])

    (unused_state, grad_skip), block_grads = lax.scan(
        adjoint_block,
        (leaving, jnp.zeros((HEADS,), jnp.float32)),
        (values, keys_in, queries, steps_blk, logdec_blk, begins, mixed_back, resets),
        reverse=True,
    )
    grad_values, grad_keys, grad_queries, grad_step, grad_logdec = block_grads
    grad_act = jnp.concatenate(
        [
            grad_values.reshape(local_tok, DIN),
            grad_keys.reshape(local_tok, NST),
            grad_queries.reshape(local_tok, NST),
        ],
        axis=1,
    )
    grad_ext, grad_raw, grad_conv, grad_head_part = pull_mixer(
        (grad_act, grad_step.reshape(local_tok, HEADS), grad_logdec.reshape(local_tok, HEADS))
    )
    returned = from_behind(grad_ext[: KCONV - 1].astype(jnp.bfloat16), "seq", -1).astype(
        jnp.float32
    )
    grad_conv_in = grad_ext[KCONV - 1 :] + jnp.concatenate(
        [jnp.zeros((local_tok - KCONV + 1, CONVC), jnp.float32), returned], axis=0
    )
    grad_proj = jnp.concatenate([grad_gate, grad_conv_in, grad_raw], axis=1).astype(jnp.bfloat16)
    grad_normed = contract_cols(grad_proj, in_back)
    grad_rows, grad_gain_pre = pull_pre(grad_normed)
    grad_input = cotangent.astype(jnp.float32) + grad_rows
    grad_gains = jnp.concatenate([grad_gain_pre, grad_gain_in], axis=0)
    grad_head = jnp.concatenate(
        [grad_head_part[:2], (grad_head_part[2] + grad_skip)[None, :]], axis=0
    )
    grad_in_w = contract_rows(normed, grad_proj)
    in_sum, out_sum, conv_sum, gain_sum = (
        lax.psum_scatter(grad_in_w, ("dp", "seq"), scatter_dimension=0, tiled=True),
        lax.psum_scatter(grad_out_w, ("dp", "seq"), scatter_dimension=0, tiled=True),
        lax.psum_scatter(grad_conv, ("dp", "seq"), scatter_dimension=1, tiled=True),
        lax.psum_scatter(grad_gains, ("dp", "seq"), scatter_dimension=0, tiled=True),
    )
    head_sum = lax.psum(grad_head, ("dp", "seq"))
    new_in = adam_update(in_weight, in_first, in_second, in_sum, rate_in)
    new_out = adam_update(out_weight, out_first, out_second, out_sum, rate_out)
    new_conv = adam_update(conv_weight, conv_first, conv_second, conv_sum, rate_conv)
    new_gain = adam_update(gains, gain_first, gain_second, gain_sum, rate_gain)
    new_head = adam_update(head_params, head_first, head_second, head_sum, rate_head)
    return (
        mixed_out,
        grad_input,
        new_in[0],
        new_in[1],
        new_in[2],
        new_out[0],
        new_out[1],
        new_out[2],
        new_conv[0],
        new_conv[1],
        new_conv[2],
        new_gain[0],
        new_gain[1],
        new_gain[2],
        new_head[0],
        new_head[1],
        new_head[2],
    )


MESH_ID = pl.DeviceIdType.MESH
ANY = pl.BlockSpec(memory_space=pl.ANY)
PLANES = 4
QUADS = 4
RANKS = 8


def place():
    chip = lax.axis_index("dp")
    return (chip // QUADS, chip % QUADS, lax.axis_index("seq"))


def at(plane, quad, core):
    return (plane * QUADS + quad, core)


def flip(core):
    return 1 - core


def xor4(value, k):
    low, high = value % 2, value // 2
    if k % 2:
        low = 1 - low
    if k // 2:
        high = 1 - high
    return 2 * high + low


def greet(devices):
    barrier = pltpu.get_barrier_semaphore()
    for device in devices:
        pl.semaphore_signal(barrier, inc=1, device_id=device, device_id_type=MESH_ID)
    pl.semaphore_wait(barrier, len(devices))


def plane_mates(plane, quad, core):
    mates = []
    for k in range(QUADS):
        for other in (core, flip(core)):
            if not (k == 0 and other is core):
                mates.append(at(plane, xor4(quad, k), other))
    return mates


def plane_others(plane, quad, core):
    return [at(xor4(plane, k), quad, core) for k in range(1, PLANES)]


class Sems:
    def __init__(self, send, recv):
        self.send, self.recv, self.used = (send, recv, 0)

    def copy(self, source, target, device):
        index = self.used
        self.used += 1
        return pltpu.make_async_remote_copy(
            src_ref=source,
            dst_ref=target,
            send_sem=self.send.at[index],
            recv_sem=self.recv.at[index],
            device_id=device,
            device_id_type=MESH_ID,
        )


class PlaneGather:
    def __init__(self, sems, own, land, plane, quad, core):
        near_x, near_y, far = (xor4(quad, k) for k in (1, 2, 3))
        rank, rank_x, rank_y, rank_far = (2 * q + core for q in (quad, near_x, near_y, far))
        to_x, to_y = (at(plane, near_x, core), at(plane, near_y, core))
        sibling = at(plane, quad, flip(core))
        whole = [0, 1]
        self.own = [
            sems.copy(own(h), land(rank, slot, h), device)
            for device, slot in ((to_x, 1), (to_y, 2), (sibling, 0))
            for h in whole
        ]
        self.relay_x = [
            sems.copy(land(rank_x, 1, 0), land(rank_x, 3, 0), to_y),
        ] + [sems.copy(land(rank_x, 1, h), land(rank_x, 1, h), sibling) for h in whole]
        self.relay_y = [
            sems.copy(land(rank_y, 2, 1), land(rank_y, 3, 1), to_x),
        ] + [sems.copy(land(rank_y, 2, h), land(rank_y, 2, h), sibling) for h in whole]
        self.relay_far = [
            sems.copy(land(rank_far, 3, h), land(rank_far, 3, h), sibling) for h in whole
        ]

    def start(self):
        for copy in self.own:
            copy.start()

    def near(self):
        self.own[0].wait_recv()
        self.relay_x[0].start()
        self.own[3].wait_recv()
        self.relay_y[0].start()
        self.own[1].wait_recv()
        self.own[2].wait_recv()
        for copy in self.relay_x[1:] + self.relay_y[1:]:
            copy.start()

    def across(self):
        for h, relay in ((0, self.relay_x[0]), (1, self.relay_y[0])):
            relay.wait_recv()
            self.relay_far[h].start()

    def wait_slot(self, slot):
        for copy in (self.own[4:], self.relay_x[1:], self.relay_y[1:], self.relay_far)[slot]:
            copy.wait_recv()

    def sent(self):
        for copy in self.own + self.relay_x + self.relay_y + self.relay_far:
            copy.wait_send()


class LineGather:
    def __init__(self, sems, own, block, plane, quad, core):
        self.plane = plane
        self.right, self.left = ([], [])
        for hop in range(PLANES - 1):
            for copies, step in ((self.right, 1), (self.left, -1)):
                index = plane - step * hop
                source = own if hop == 0 else block(index)
                copies.append(sems.copy(source, block(index), at(plane + step, quad, core)))

    def sends(self, hop, step):
        if step > 0:
            return (self.plane - hop >= 0) & (self.plane < PLANES - 1)
        return (self.plane + hop < PLANES) & (self.plane > 0)

    def receives(self, hop, step):
        if step > 0:
            return self.plane - 1 - hop >= 0
        return self.plane + 1 + hop < PLANES

    def start(self, hop):
        for copies, step in ((self.right, 1), (self.left, -1)):

            @pl.when(self.sends(hop, step))
            def go():
                copies[hop].start()

    def arrive(self, hop):
        for copies, step in ((self.right, 1), (self.left, -1)):

            @pl.when(self.receives(hop, step))
            def landed():
                copies[hop].wait_recv()

    def sent(self):
        for hop in range(PLANES - 1):
            for copies, step in ((self.right, 1), (self.left, -1)):

                @pl.when(self.sends(hop, step))
                def left():
                    copies[hop].wait_send()


OWN_HEADS = HEADS // RANKS
OWN = OWN_HEADS * HDIM
PAIRS = OWN_HEADS // 2
RUN = OWN // 2
COMMON = 2 * NST + HEADS
COMMON_PAD = 384
GROUP = 2 * BLOCK
MIX = OWN + 2 * NST
LANES = 128


def mm(left, right):
    return lax.dot_general(left, right, (((1,), (0,)), ((), ())), preferred_element_type=jnp.float32)


def mm_t(left, right):
    return lax.dot_general(left, right, (((1,), (1,)), ((), ())), preferred_element_type=jnp.float32)


def t_mm(left, right):
    return lax.dot_general(left, right, (((0,), (0,)), ((), ())), preferred_element_type=jnp.float32)


def mm_full(left, right):
    return lax.dot_general(
        left, right, (((1,), (0,)), ((), ())), precision=highest, preferred_element_type=jnp.float32
    )


def low16(value):
    return value.astype(jnp.bfloat16)


def iota(shape, axis):
    return lax.broadcasted_iota(jnp.int32, shape, axis)


def head_spread():
    return (iota((LANES, OWN), 1) // HDIM == iota((LANES, OWN), 0)).astype(jnp.float32)


def head_gather():
    return (iota((OWN, LANES), 0) // HDIM == iota((OWN, LANES), 1)).astype(jnp.float32)


def lower_mask():
    return iota((BLOCK, BLOCK), 0) >= iota((BLOCK, BLOCK), 1)


def shift_down(value, k):
    if k == 0:
        return value
    rolled = pltpu.roll(value, k, 0)
    return jnp.where(iota(value.shape, 0) >= k, rolled, 0.0)


def shift_up(value, k):
    if k == 0:
        return value
    rows = value.shape[0]
    rolled = pltpu.roll(value, rows - k, 0)
    return jnp.where(iota(value.shape, 0) < rows - k, rolled, 0.0)


def sigmoid(value):
    return 1.0 / (1.0 + jnp.exp(-value))


def softplus(value):
    return jnp.maximum(value, 0.0) + jnp.log1p(jnp.exp(-jnp.abs(value)))


def preact_of(u, conv):
    total = u * conv[KCONV - 1 : KCONV] + conv[KCONV : KCONV + 1]
    for tap in range(KCONV - 1):
        total = total + shift_down(u, KCONV - 1 - tap) * conv[tap : tap + 1]
    return total


def steps_of(raw, heads, live):
    step = softplus(raw + heads[0:1]) * live * heads[3:4]
    return (step, -jnp.exp(heads[1:2]) * step)


def decay_of(cumul, cumul_t, h):
    return jnp.exp(jnp.minimum(cumul[:, h : h + 1] - cumul_t[h : h + 1, :], 0.0))


def lane_half(value, side):
    lanes = iota(value.shape, 1)
    return jnp.where((lanes >= HDIM) == (side == 1), value, jnp.zeros_like(value))


def block_parts(step, logdec, spread):
    cumul = mm_full(lower_mask().astype(jnp.float32), logdec)
    return (cumul, jnp.transpose(cumul), mm_full(step, spread), mm_full(cumul, spread))


def ssd_forward(act, step, logdec, skip):
    spread = head_spread()
    lower = lower_mask()
    outs = []
    state = None
    for k in range(2):
        rows = slice(k * BLOCK, (k + 1) * BLOCK)
        values, keys, queries = (act[rows, :OWN], act[rows, OWN : OWN + NST], act[rows, OWN + NST :])
        cumul, cumul_t, step_w, cumul_w = block_parts(step[rows], logdec[rows], spread)
        gram = jnp.where(lower, mm_t(queries, keys), 0.0)
        values_f = values.astype(jnp.float32)
        stepped = low16(values_f * step_w)
        pieces = []
        for pair in range(PAIRS):
            lanes = slice(pair * LANES, (pair + 1) * LANES)
            piece = 0.0
            for side in range(2):
                mixing = low16(gram * decay_of(cumul, cumul_t, 2 * pair + side))
                piece = piece + mm(mixing, lane_half(stepped[:, lanes], side))
            pieces.append(piece)
        out = jnp.concatenate(pieces, axis=1) + skip * values_f
        if state is not None:
            out = out + jnp.exp(cumul_w) * mm(queries, state)
        else:
            weighting = jnp.exp(cumul_w[BLOCK - 1 :] - cumul_w) * step_w
            state = low16(t_mm(keys, low16(weighting * values_f)))
        outs.append(out)
    return jnp.concatenate(outs, axis=0)


def live_of(lens, g):
    rows = iota((GROUP, 1), 0).astype(jnp.float32)
    chosen = jnp.sum(jnp.where(iota(lens.shape, 0) == g, lens, 0.0), axis=0, keepdims=True)[:, :1]
    return (rows < chosen).astype(jnp.float32)


def quad_of(slot):
    quad = lax.axis_index("dp") % QUADS
    return (quad % 2 + slot % 2) % 2 + 2 * ((quad // 2 + slot // 2) % 2)


def full_spec(shape):
    return pl.BlockSpec(shape, lambda g: (0,) * len(shape))


def group_spec(width):
    return pl.BlockSpec((GROUP, width), lambda g: (g, 0))


VMEM_GRANT = 60 * 1024 * 1024


def backward_block(k, act, dmix, step, logdec, skip, state, state_grad, spread, gather):
    values, keys, queries = (act[:, :OWN], act[:, OWN : OWN + NST], act[:, OWN + NST :])
    lower = lower_mask()
    cumul, cumul_t, step_w, cumul_w = block_parts(step, logdec, spread)
    step_t = jnp.transpose(step)
    gram = jnp.where(lower, mm_t(queries, keys), 0.0)
    values_f = values.astype(jnp.float32)
    dmix_f = dmix.astype(jnp.float32)
    lanes_h = iota((BLOCK, LANES), 1)
    rows_h = iota((8, BLOCK), 0)
    grad_gram = 0.0
    row_sums = jnp.zeros((BLOCK, LANES), jnp.float32)
    col_sums = jnp.zeros((8, BLOCK), jnp.float32)
    pieces = []
    for pair in range(PAIRS):
        lanes = slice(pair * LANES, (pair + 1) * LANES)
        piece = 0.0
        for side in range(2):
            h = 2 * pair + side
            decay = decay_of(cumul, cumul_t, h)
            dm_half = lane_half(dmix[:, lanes], side)
            grad_mixing = mm_t(dm_half, values[:, lanes])
            step_row = step_t[h : h + 1, :]
            grad_gram = grad_gram + grad_mixing * decay * step_row
            mixing = gram * decay
            piece = piece + t_mm(low16(mixing), dm_half)
            product = grad_mixing * mixing
            col_sums = jnp.where(rows_h == h, jnp.sum(product, axis=0, keepdims=True), col_sums)
            row_sums = jnp.where(
                lanes_h == h, jnp.sum(product * step_row, axis=1, keepdims=True), row_sums
            )
        pieces.append(piece)
    grad_values = jnp.concatenate(pieces, axis=1) * step_w + skip * dmix_f
    grad_skip = jnp.sum(dmix_f * values_f, axis=0, keepdims=True)
    grad_gram = low16(jnp.where(lower, grad_gram, 0.0))
    grad_queries = mm(grad_gram, keys)
    grad_keys = t_mm(grad_gram, queries)
    columns = jnp.transpose(jnp.concatenate([col_sums, jnp.zeros((LANES - 8, BLOCK), jnp.float32)], axis=0))
    grad_step = columns
    grad_cumul = row_sums - columns * step
    if k == 1:
        entering = jnp.exp(cumul_w) * dmix_f
        entering_low = low16(entering)
        crossed = mm(queries, state)
        grad_cumul = grad_cumul + mm_full(entering * crossed, gather)
        grad_queries = grad_queries + mm_t(entering_low, state)
        before = low16(t_mm(queries, entering_low))
    else:
        tail = jnp.exp(cumul_w[BLOCK - 1 :] - cumul_w)
        weighting = tail * step_w
        back = mm(keys, state_grad)
        grad_values = grad_values + weighting * back
        grad_keys = grad_keys + mm_t(low16(weighting * values_f), state_grad)
        grad_weight = mm_full(values_f * back, gather)
        tail_h = jnp.exp(cumul[BLOCK - 1 :] - cumul)
        grad_step = grad_step + grad_weight * tail_h
        part = grad_weight * tail_h * step
        last = iota((BLOCK, LANES), 0) == BLOCK - 1
        grad_cumul = grad_cumul - part + jnp.where(last, jnp.sum(part, axis=0, keepdims=True), 0.0)
        before = None
    upper = (iota((BLOCK, BLOCK), 0) <= iota((BLOCK, BLOCK), 1)).astype(jnp.float32)
    grad_logdec = mm_full(upper, grad_cumul)
    return (grad_values, grad_keys, grad_queries, grad_step, grad_logdec, grad_skip, before)


ROWS_IN = D // (PLANES * RANKS)
ROWS_OUT = DIN // (PLANES * RANKS)
ROWS_ALL = ROWS_IN + 16
SHARD_CONV = CONVC // (PLANES * RANKS)
SHARD_GAIN = (D + DIN) // (PLANES * RANKS)
RUN_HALVES = RUN // HDIM


def place_lanes(pieces, tiles, rows):
    lanes = iota((rows, LANES), 1)
    out = [jnp.zeros((rows, LANES), jnp.float32) for unused in range(tiles)]
    for value, width, offset in pieces:
        tile, lane = divmod(offset, LANES)
        moved = pltpu.roll(value, lane, 1) if lane else value
        end = lane + width
        out[tile] = jnp.where((lanes >= lane) & (lanes < end), moved, out[tile])
        if end > LANES:
            out[tile + 1] = jnp.where(lanes < end - LANES, moved, out[tile + 1])
    return out


def own_lanes(tiles, quad, core):
    rows = tiles[0].shape[0]
    lanes = iota((rows, LANES), 1)

    def half_of(index):
        tile, odd = (index // 2, index % 2)
        chosen = tiles[0]
        for t in range(1, len(tiles)):
            chosen = jnp.where(tile == t, tiles[t], chosen)
        return (chosen, odd)

    out = []
    for pair in range(PAIRS):
        sides = []
        for b in range(2):
            near, i = divmod(2 * pair + b, RUN_HALVES)
            value, odd = half_of(2 * PLANES * RUN_HALVES * core + PLANES * RUN_HALVES * near + RUN_HALVES * quad + i)
            sides.append(jnp.where(odd == b, value, pltpu.roll(value, HDIM, 1)))
        out.append(jnp.where(lanes < HDIM, sides[0], sides[1]))
    return jnp.concatenate(out, axis=1)


def fill_sends(in_w, out_w, conv_w, gains, lens, wz_send, wc_send, wo_send):
    lanes = iota((ROWS_IN, LANES), 1)
    for j in range(RANKS):
        quad, core = divmod(j, 2)
        for part in range(2):
            for pair in range(PAIRS):
                sides = []
                for b in range(2):
                    near, i = divmod(2 * pair + b, RUN_HALVES)
                    index = (2 * core + near) * PLANES * RUN_HALVES + RUN_HALVES * quad + i
                    start = part * DIN + index // 2 * LANES
                    tile = in_w[:, start : start + LANES]
                    sides.append(tile if index % 2 == b else pltpu.roll(tile, HDIM, 1))
                start = part * OWN + pair * LANES
                wz_send[j, :, start : start + LANES] = low16(jnp.where(lanes < HDIM, sides[0], sides[1]))


def fill_common(in_w, conv_w, gains, lens, wc_send):
    wc_send[...] = jnp.zeros_like(wc_send)
    wc_send[:ROWS_IN, : 2 * NST] = low16(in_w[:, 2 * DIN : 2 * DIN + 2 * NST])
    tail = in_w[:, 2 * DIN + 2 * NST : 2 * DIN + COMMON]
    wide = jnp.concatenate([tail, jnp.zeros((ROWS_IN, LANES - HEADS), jnp.float32)], axis=1)
    wc_send[:ROWS_IN, 2 * NST :] = low16(wide)
    conv_v = jnp.concatenate([conv_w[...], jnp.zeros((KCONV + 1, COMMON_PAD - SHARD_CONV), jnp.float32)], axis=1)
    gain_v = jnp.concatenate([gains[...], jnp.zeros((1, COMMON_PAD - SHARD_GAIN), jnp.float32)], axis=1)
    extra = jnp.broadcast_to(lens[:, 0:1].astype(jnp.float32) - BLOCK, (1, COMMON_PAD))
    rows = jnp.concatenate([conv_v, gain_v, extra, jnp.zeros((9, COMMON_PAD), jnp.float32)], axis=0)
    wc_send[ROWS_IN:] = low16(rows)


def select_heads(quad, core):
    rows, columns = (iota((LANES, LANES), 0), iota((LANES, LANES), 1))
    head = HEADS // 2 * core + HEADS // 4 * (columns // 3) + 3 * quad + columns % 3
    return ((rows == head) & (columns < OWN_HEADS)).astype(jnp.float32)


def fore_kernel(
    tok, cot, seq_lens, in_w, out_w, conv_w, gains, head_params,
    o_normed, o_cot, o_own, o_com, o_out, o_proj, o_proj_com, o_act, o_mixed, o_gno,
    stats, gain_in, gain_out, conv, heads, skip, select, lens,
    wz_send, wc_send, wo_send, all_tok, all_cot, normed, all_wz, all_wc, w_com, line_wo, w_out,
    proj, proj_com, act, mixed, gno, part, shared,
    send, recv, local
):
    plane, quad, core = place()
    where = (plane, quad, core)
    rank = 2 * quad + core
    sibling = at(plane, quad, flip(core))
    sems = Sems(send, recv)
    f32 = jnp.float32
    half = BLOCK // 2
    kept = []

    def keep(source, target):
        copy = pltpu.make_async_copy(source, target, local.at[len(kept)])
        kept.append(copy)
        copy.start()
        return copy

    def pieces(buffer):
        return lambda r, slot, h: buffer.at[slot, core, pl.ds(h * half, half)]

    def halves(buffer):
        return lambda h: buffer.at[pl.ds(h * half, half)]

    line_c = LineGather(sems, wc_send, lambda q: all_wc.at[q, rank], *where)
    line_o = LineGather(sems, wo_send, lambda q: line_wo.at[q], *where)
    line_w = LineGather(sems, all_wz.at[plane], lambda q: all_wz.at[q], *where)
    shuffle = []
    for k in range(1, RANKS):
        other_core = flip(core) if k % 2 else core
        other_quad = xor4(quad, k // 2)
        shuffle.append(
            sems.copy(
                wz_send.at[2 * other_quad + other_core], all_wz.at[plane, rank], at(plane, other_quad, other_core)
            )
        )
    tokens = PlaneGather(sems, halves(tok), pieces(all_tok), *where)
    grads = PlaneGather(sems, halves(cot), pieces(all_cot), *where)
    common = PlaneGather(
        sems,
        lambda h: all_wc.at[pl.ds(2 * h, 2), rank],
        lambda r, slot, h: all_wc.at[pl.ds(2 * h, 2), r],
        *where,
    )
    cross_o = [
        sems.copy(line_wo.at[2 * flip(core) + k], w_out.at[k, core], sibling) for k in range(2)
    ]
    mates = plane_mates(*where)
    swap = [sems.copy(part, shared.at[rank], device) for device in mates]

    greet(mates + plane_others(*where))
    fill_common(in_w, conv_w, gains, seq_lens, wc_send)
    line_c.start(0)
    fill_sends(in_w, out_w, conv_w, gains, seq_lens, wz_send, wc_send, wo_send)
    for copy in shuffle:
        copy.start()
    wo_send[...] = low16(out_w[...])
    line_o.start(0)
    tokens.start()
    own_wz = keep(wz_send.at[rank], all_wz.at[plane, rank])
    own_wc = keep(wc_send, all_wc.at[plane, rank])
    own_tok = keep(tok, all_tok.at[0, core])
    own_cot = keep(cot, all_cot.at[0, core])
    own_wo = keep(wo_send, line_wo.at[plane])
    select[...] = select_heads(quad, core)
    wide = jnp.concatenate([head_params[...], jnp.zeros((3, LANES - HEADS), f32)], axis=1)
    wide = jnp.concatenate([wide, jnp.ones((1, LANES), f32), jnp.zeros((4, LANES), f32)], axis=0)
    heads[...] = mm_full(wide * (iota((8, LANES), 1) < HEADS).astype(f32), select[...])
    skip[...] = mm_full(heads[2:3], head_spread())

    for hop in range(PLANES - 1):
        line_c.arrive(hop)
        if hop < PLANES - 2:
            line_c.start(hop + 1)
    own_wc.wait()
    common.start()
    own_wz.wait()
    for copy in shuffle:
        copy.wait_recv()
    line_w.start(0)
    common.near()
    common.across()
    for slot in range(QUADS):
        common.wait_slot(slot)
    for q in range(PLANES):
        for r in range(RANKS):
            start = (RANKS * q + r) * ROWS_IN
            w_com[start : start + ROWS_IN] = all_wc[q, r, :ROWS_IN]
    keep(w_com, o_com)
    extras = [all_wc[q, r, ROWS_IN:].astype(f32) for q in range(PLANES) for r in range(RANKS)]
    gain_tiles = place_lanes(
        [(e[5:6, :LANES], LANES, SHARD_GAIN * d) for d, e in enumerate(extras)]
        + [(e[5:6, LANES : 2 * LANES], SHARD_GAIN - LANES, SHARD_GAIN * d + LANES) for d, e in enumerate(extras)],
        (D + DIN) // LANES,
        1,
    )
    gain_in[...] = jnp.concatenate(gain_tiles[: D // LANES], axis=1)
    gain_out[...] = own_lanes(gain_tiles[D // LANES :], quad, core)
    conv_tiles = place_lanes(
        [(e[:8, :LANES], SHARD_CONV, SHARD_CONV * d) for d, e in enumerate(extras)], CONVC // LANES, 8
    )
    conv[...] = jnp.concatenate(
        [own_lanes(conv_tiles[: DIN // LANES], quad, core)] + conv_tiles[DIN // LANES :], axis=1
    )
    seats = []
    for slot in range(QUADS):
        chosen = jnp.zeros((1, LANES), f32)
        for q in range(PLANES):
            for p in range(QUADS):
                here = (plane == q) & (quad_of(slot) == p)
                chosen = jnp.where(here, extras[RANKS * q + 2 * p][6:7, :LANES], chosen)
        seats.append(chosen + BLOCK)
    lens[...] = jnp.concatenate(seats + [jnp.zeros((8 - QUADS, LANES), f32)], axis=0)

    def norm(slot):
        for side in range(2):
            rows = all_tok[slot, side].astype(f32)
            scaling = lax.rsqrt(jnp.mean(rows * rows, axis=1, keepdims=True) + norm_eps)
            normed[slot, pl.ds(side * BLOCK, BLOCK)] = low16(rows * scaling * gain_in[...])

    def project(plane_from, slots, first=False):
        columns = pl.ds(pl.multiple_of(plane_from * (D // PLANES), LANES), D // PLANES)

        @pl.loop(slots[0], slots[1])
        def one(slot):
            product = mm(normed[slot, :, columns], all_wz[plane_from].reshape(D // PLANES, 2 * OWN))
            proj[slot] = product if first else proj[slot] + product

    own_tok.wait()
    tokens.wait_slot(0)
    norm(0)
    project(plane, (0, 1), first=True)
    line_w.arrive(0)
    line_w.start(1)
    tokens.near()
    grads.start()
    tokens.wait_slot(1)
    norm(1)
    tokens.wait_slot(2)
    norm(2)
    project(plane, (1, 3), first=True)
    line_w.arrive(1)
    line_w.start(2)
    tokens.across()
    tokens.wait_slot(3)
    norm(3)
    project(plane, (3, 4), first=True)
    for slot in range(QUADS):
        keep(normed.at[slot], o_normed.at[pl.ds(slot * GROUP, GROUP)])

    def arrivals(hop):
        for step in (1, -1):

            @pl.when(line_w.receives(hop, step))
            def multiply():
                project(plane - step * (hop + 1), (0, QUADS))

    arrivals(0)
    arrivals(1)
    line_w.arrive(2)
    line_o.arrive(0)
    line_o.start(1)
    arrivals(2)
    keep(all_wz, o_own)

    @pl.loop(0, QUADS)
    def each(slot):
        @pl.when(slot == 1)
        def onward():
            line_o.arrive(1)
            line_o.start(2)

        @pl.when(slot == 2)
        def pass_on():
            grads.near()

        @pl.when(slot == 3)
        def pass_across():
            grads.across()
            line_o.arrive(2)
            own_wo.wait()
            for copy in cross_o:
                copy.start()
            for k in range(2):
                w_out[k, core] = line_wo[2 * core + k]

        proj_com[slot] = mm(normed[slot], w_com[...])
        conv_in = jnp.concatenate([proj[slot, :, OWN:], proj_com[slot, :, : 2 * NST]], axis=1)
        raw = mm_full(proj_com[slot, :, 2 * NST :], select[...])
        preact = preact_of(conv_in, conv[...])
        active = low16(preact * sigmoid(preact))
        act[slot] = active
        step, logdec = steps_of(raw, heads[...], live_of(lens[...], slot))
        mixed[slot] = ssd_forward(active, step, logdec, skip[...])

    for source, target in ((proj, o_proj), (proj_com, o_proj_com), (act, o_act), (mixed, o_mixed)):
        keep(source, target)
    own_cot.wait()
    for copy in cross_o:
        copy.wait_recv()
    for slot in range(QUADS):
        grads.wait_slot(slot)
    keep(all_cot, o_cot)
    keep(w_out, o_out)
    part[...] = jnp.zeros_like(part)

    @pl.loop(0, QUADS)
    def measure(slot):
        live = live_of(lens[...], slot)
        grad = all_cot[slot].reshape(GROUP, D)
        grad = jnp.where(live > 0.0, grad, jnp.zeros_like(grad))
        gno_v = mm_t(grad, w_out[...].reshape(OWN, D))
        gno[slot] = gno_v
        gate_part = proj[slot, :, :OWN]
        gated = mixed[slot] * gate_part * sigmoid(gate_part)
        squares = jnp.sum(gated * gated, axis=1, keepdims=True)
        inner = jnp.sum(gno_v * gain_out[...] * gated, axis=1, keepdims=True)
        lanes = iota((GROUP, LANES), 1)
        seat = quad_of(slot)
        columns = jnp.where(lanes == 2 * seat, squares, 0.0) + jnp.where(lanes == 2 * seat + 1, inner, 0.0)
        part[...] += jnp.transpose(columns)[:8]

    keep(gno, o_gno)
    for copy in swap:
        copy.start()
    shared[rank] = part[...]
    for copy in swap:
        copy.wait_recv()
    stats[...] = jnp.sum(shared[...], axis=0)
    for copy in shuffle + cross_o + swap:
        copy.wait_send()
    for line in (line_c, line_o, line_w):
        line.sent()
    for gather in (tokens, grads, common):
        gather.sent()
    for copy in kept:
        if not any(copy is done for done in (own_wz, own_wc, own_tok, own_cot, own_wo)):
            copy.wait()


def run_fore(tok, cot, seq_lens, in_w, out_w, conv_w, gains, head_params):
    f32, bf16 = (jnp.float32, jnp.bfloat16)
    whole = pl.BlockSpec(memory_space=pltpu.VMEM)
    outs = (
        ((QUADS * GROUP, D), bf16), ((QUADS, 2, BLOCK, D), bf16), ((PLANES, RANKS, ROWS_IN, 2 * OWN), bf16),
        ((D, COMMON_PAD), bf16), ((2, 2, ROWS_OUT, D), bf16),
        ((QUADS, GROUP, 2 * OWN), f32), ((QUADS, GROUP, COMMON_PAD), f32), ((QUADS, GROUP, MIX), bf16),
        ((QUADS, GROUP, OWN), f32), ((QUADS, GROUP, OWN), f32),
    )
    small = (
        (8, GROUP), (1, D), (1, OWN), (8, MIX), (8, LANES), (1, OWN), (LANES, LANES), (8, LANES),
    )
    scratch = (
        ((RANKS, ROWS_IN, 2 * OWN), bf16), ((ROWS_ALL, COMMON_PAD), bf16), ((ROWS_OUT, D), bf16),
        ((QUADS, 2, BLOCK, D), bf16), ((QUADS, 2, BLOCK, D), bf16), ((QUADS, GROUP, D), bf16),
        ((PLANES, RANKS, ROWS_IN, 2 * OWN), bf16), ((PLANES, RANKS, ROWS_ALL, COMMON_PAD), bf16),
        ((D, COMMON_PAD), bf16), ((PLANES, ROWS_OUT, D), bf16), ((2, 2, ROWS_OUT, D), bf16),
        ((QUADS, GROUP, 2 * OWN), f32), ((QUADS, GROUP, COMMON_PAD), f32), ((QUADS, GROUP, MIX), bf16),
        ((QUADS, GROUP, OWN), f32), ((QUADS, GROUP, OWN), f32), ((8, GROUP), f32), ((RANKS, 8, GROUP), f32),
    )
    args = (tok, cot, seq_lens, in_w, out_w, conv_w, gains.reshape(1, -1), head_params)
    results = pl.pallas_call(
        fore_kernel,
        in_specs=[ANY, ANY] + [whole] * 6,
        out_specs=[ANY] * len(outs) + [whole] * len(small),
        out_shape=[jax.ShapeDtypeStruct(s, kind) for s, kind in outs]
        + [jax.ShapeDtypeStruct(s, f32) for s in small],
        scratch_shapes=[pltpu.VMEM(s, kind) for s, kind in scratch]
        + [
            pltpu.SemaphoreType.DMA((80,)),
            pltpu.SemaphoreType.DMA((80,)),
            pltpu.SemaphoreType.DMA((24,)),
        ],
        compiler_params=pltpu.CompilerParams(
            vmem_limit_bytes=VMEM_GRANT, collective_id=0, has_side_effects=True
        ),
    )(*args)
    rows = QUADS * GROUP
    widths = (D, D, None, None, None, 2 * OWN, COMMON_PAD, MIX, OWN, OWN)
    flat = [a if w is None else a.reshape(rows, w) for a, w in zip(results, widths)]
    flat[2] = flat[2].reshape(D, 2 * OWN)
    flat[4] = flat[4].reshape(OWN, D)
    return flat + list(results[len(outs) :])


def gate_kernel(
    lens, stats, cot, normed, gate_part, mixed, grad_normed_out, w_out, gain_out,
    branch, dgate, dmix, g_out, g_gate, g_gain, acc_out, acc_gate
):
    g = pl.program_id(0)
    live = live_of(lens[...], g)

    @pl.when(g == 0)
    def first():
        acc_out[...] = jnp.zeros_like(acc_out)
        acc_gate[...] = jnp.zeros_like(acc_gate)
        g_gain[...] = jnp.zeros_like(g_gain)

    columns = jnp.transpose(jnp.concatenate([stats[...], jnp.zeros((LANES - 8, GROUP), jnp.float32)], axis=0))
    lanes = iota((GROUP, LANES), 1)
    seat = quad_of(g)
    power = jnp.sum(jnp.where(lanes == 2 * seat, columns, 0.0), axis=1, keepdims=True)
    along = jnp.sum(jnp.where(lanes == 2 * seat + 1, columns, 0.0), axis=1, keepdims=True)
    scale_out = lax.rsqrt(power * (1.0 / DIN) + norm_eps)
    gate_v, mixed_v, gno = (gate_part[...], mixed[...], grad_normed_out[...])
    sig = sigmoid(gate_v)
    gate_act = gate_v * sig
    gated = mixed_v * gate_act
    normed_out = low16(gated * scale_out * gain_out[...])
    for half in range(2):
        rows = slice(half * BLOCK, (half + 1) * BLOCK)
        branch[0, half] = low16(mm(normed_out[rows], w_out[...]))
    grad = jnp.where(live > 0.0, cot[...], jnp.zeros_like(cot[...]))
    acc_out[...] += t_mm(normed_out, grad)
    scaled = gno * scale_out
    grad_gated = scaled * gain_out[...] - gated * (scale_out * scale_out * scale_out * along * (1.0 / DIN))
    gain_sum = jnp.sum(scaled * gated, axis=0, keepdims=True)
    g_gain[...] += jnp.concatenate([gain_sum, jnp.zeros((7, OWN), jnp.float32)], axis=0)
    grad_gate = low16(grad_gated * mixed_v * (sig * (1.0 + gate_v * (1.0 - sig))))
    dgate[...] = grad_gate
    dmix[...] = low16(grad_gated * gate_act)
    acc_gate[...] += t_mm(normed[...], grad_gate)

    @pl.when(g == QUADS - 1)
    def last():
        g_out[...] = low16(acc_out[...])
        g_gate[...] = low16(acc_gate[...])


def run_gate(lens, stats, cot, normed, proj_own, mixed, grad_normed_out, w_out, gain_out):
    f32, bf16 = (jnp.float32, jnp.bfloat16)
    rows = QUADS * GROUP
    grouped = (cot, normed, proj_own, mixed, grad_normed_out)
    ends = (((OWN, D), bf16), ((D, OWN), bf16), ((8, OWN), f32))
    return pl.pallas_call(
        gate_kernel,
        grid=(QUADS,),
        in_specs=[full_spec(a.shape) for a in (lens, stats)]
        + [group_spec(w) for w in (D, D, OWN, OWN, OWN)]
        + [full_spec(w_out.shape), full_spec(gain_out.shape)],
        out_specs=[pl.BlockSpec((1, 2, BLOCK, D), lambda g: (g, 0, 0, 0)), group_spec(OWN), group_spec(OWN)]
        + [full_spec(s) for s, kind in ends],
        out_shape=[
            jax.ShapeDtypeStruct((QUADS, 2, BLOCK, D), bf16),
            jax.ShapeDtypeStruct((rows, OWN), bf16),
            jax.ShapeDtypeStruct((rows, OWN), bf16),
        ]
        + [jax.ShapeDtypeStruct(s, kind) for s, kind in ends],
        scratch_shapes=[pltpu.VMEM((OWN, D), f32), pltpu.VMEM((D, OWN), f32)],
        compiler_params=pltpu.CompilerParams(vmem_limit_bytes=VMEM_GRANT),
    )(lens, stats, *grouped, w_out, gain_out)


def backward_group(live, dmix, conv_in, raw, act, conv, heads, skip):
    act_v = act[...]
    raw_v = raw[...]
    heads_v = heads[...]
    step, logdec = steps_of(raw_v, heads_v, live)
    spread, gather = (head_spread(), head_gather())
    rows0, rows1 = (slice(0, BLOCK), slice(BLOCK, GROUP))
    cumul0 = mm_full(lower_mask().astype(jnp.float32), logdec[rows0])
    cumul0_w = mm_full(cumul0, spread)
    weighting = jnp.exp(cumul0_w[BLOCK - 1 :] - cumul0_w) * mm_full(step[rows0], spread)
    state = low16(
        t_mm(act_v[rows0, OWN : OWN + NST], low16(weighting * act_v[rows0, :OWN].astype(jnp.float32)))
    )
    late = backward_block(
        1, act_v[rows1], dmix[rows1], step[rows1], logdec[rows1], skip[...], state, None, spread, gather
    )
    early = backward_block(
        0, act_v[rows0], dmix[rows0], step[rows0], logdec[rows0], skip[...], None, late[6], spread, gather
    )
    grad_act = jnp.concatenate([jnp.concatenate(part[:3], axis=1) for part in (early, late)], axis=0)
    grad_step = jnp.concatenate([early[3], late[3]], axis=0)
    grad_logdec = jnp.concatenate([early[4], late[4]], axis=0)
    rate = jnp.exp(heads_v[1:2])
    grad_raw = (grad_step - rate * grad_logdec) * live * heads_v[3:4] * sigmoid(raw_v + heads_v[0:1])
    u = conv_in[...]
    conv_v = conv[...]
    preact = preact_of(u, conv_v)
    sig_q = sigmoid(preact)
    grad_pre = grad_act * (sig_q * (1.0 + preact * (1.0 - sig_q)))
    grad_u = grad_pre * conv_v[KCONV - 1 : KCONV]
    taps = []
    for tap in range(KCONV):
        lag = KCONV - 1 - tap
        if lag:
            grad_u = grad_u + shift_up(grad_pre, lag) * conv_v[tap : tap + 1]
        taps.append(jnp.sum(grad_pre * shift_down(u, lag), axis=0, keepdims=True))
    taps.append(jnp.sum(grad_pre, axis=0, keepdims=True))
    small = (
        jnp.concatenate(taps + [jnp.zeros((3, MIX), jnp.float32)], axis=0),
        jnp.sum(grad_raw, axis=0, keepdims=True),
        jnp.sum(grad_logdec * logdec, axis=0, keepdims=True),
        early[5] + late[5],
    )
    return (grad_u, grad_raw, small)


PACK = 48


def back_kernel(
    lens, gate_grads, out_grads, branch_all, w_own, w_com, conv, heads, skip, select, gain_in, g_gain, tok_own,
    branch, normed, dgate, dmix, proj_x, proj_com, act,
    r_out, all_gate, all_x, sum_com, packs, sum_branch, grad_rows,
    acc_x, acc_com, small_conv, small_head, small_skip,
    branch_sib, en_part, en_sib, branch_got, en_got, branch_relay, en_relay,
    gate_got, gate_own, sum_gate, x_send, x_got, sum_x, com_send, com_sib, com_quad, com_z, com_got,
    pack_send, pack_got, pack_sum,
    sends, recvs, out_send, out_recv, local
):
    s = pl.program_id(0)
    slot = QUADS - 1 - s
    plane, quad, core = place()
    where = (plane, quad, core)
    rank = 2 * quad + core
    sibling = at(plane, quad, flip(core))
    f32 = jnp.float32
    sems = Sems(sends, recvs)
    to_x, to_y = (at(plane, xor4(quad, 1), core), at(plane, xor4(quad, 2), core))
    half = BLOCK // 2

    swaps = [
        [sems.copy(source.at[k, flip(core)], target.at[k], sibling) for k in range(QUADS)]
        for source, target in ((branch_all, branch_sib), (en_part, en_sib))
    ]
    routes = []
    for sib, got, relay in ((branch_sib, branch_got, branch_relay), (en_sib, en_got, en_relay)):
        routes.append(
            {
                "relay_x": sems.copy(sib.at[3, pl.ds(0, half)], relay.at[0], to_x),
                "relay_y": sems.copy(sib.at[3, pl.ds(half, half)], relay.at[1], to_y),
                "x": sems.copy(sib.at[1], got.at[0], to_x),
                "y": sems.copy(sib.at[2], got.at[1], to_y),
            }
        )

    def z_push(source, target):
        return [
            sems.copy(source.at[xor4(plane, k)], target.at[k - 1], at(xor4(plane, k), quad, core))
            for k in (2, 3, 1)
        ]

    def rank_push(source, target):
        copies = []
        for k in range(1, RANKS):
            other_core = flip(core) if k % 2 else core
            other_quad = xor4(quad, k // 2)
            copies.append(
                sems.copy(source(2 * other_quad + other_core), target.at[rank], at(plane, other_quad, other_core))
            )
        return copies

    gate_z = z_push(gate_grads, gate_got)
    x_z = z_push(x_send, x_got)
    gate_ranks = rank_push(lambda r: sum_gate.at[r], all_gate)
    x_ranks = rank_push(lambda r: sum_x.at[r], all_x)
    com_swap = sems.copy(com_send.at[:, :, flip(core)], com_sib, sibling)
    com_quads = [
        sems.copy(com_sib.at[:, xor4(quad, k)], com_quad.at[k - 1], at(plane, xor4(quad, k), core))
        for k in (3, 1, 2)
    ]
    com_planes = z_push(com_z, com_got)
    pack_z = [
        sems.copy(pack_send, pack_got.at[k - 1], at(xor4(plane, k), quad, core)) for k in (2, 3, 1)
    ]
    pack_ranks = rank_push(lambda r: pack_sum, packs)

    def out_copy(near, side):
        return pltpu.make_async_remote_copy(
            src_ref=out_grads.at[near, side],
            dst_ref=r_out.at[plane],
            send_sem=out_send.at[2 * near + side],
            recv_sem=out_recv.at[plane],
            device_id=at(2 * core + near, quad, side),
            device_id_type=MESH_ID,
        )

    def out_landing(origin):
        return pltpu.make_async_remote_copy(
            src_ref=out_grads.at[0, 0],
            dst_ref=r_out.at[origin],
            send_sem=out_send.at[0],
            recv_sem=out_recv.at[origin],
            device_id=sibling,
            device_id_type=MESH_ID,
        )

    out_here = pltpu.make_async_copy(out_grads.at[plane % 2, core], r_out.at[plane], local.at[0])
    out_stays = plane // 2 == core
    gate_here = pltpu.make_async_copy(gate_grads.at[plane], gate_own, local.at[1])

    @pl.when(s == 0)
    def begin():
        peers = plane_mates(*where) + plane_others(*where)
        peers += [at(xor4(plane, k), quad, flip(core)) for k in range(1, PLANES)]
        greet(peers)
        for copy in gate_z:
            copy.start()
        for copy in swaps[0][::-1]:
            copy.start()
        for near in range(2):
            for side in range(2):

                @pl.when(jnp.logical_not((2 * core + near == plane) & (core == side)))
                def go():
                    out_copy(near, side).start()

        @pl.when(out_stays)
        def stay():
            out_here.start()

        gate_here.start()
        for ref in (acc_x, acc_com, small_conv, small_head, small_skip):
            ref[...] = jnp.zeros_like(ref)

    live = live_of(lens[...], slot)
    conv_in = jnp.concatenate([proj_x[...], proj_com[:, : 2 * NST]], axis=1)
    raw = mm_full(proj_com[:, 2 * NST :], select[...])
    grad_u, grad_raw, small = backward_group(live, dmix[...], conv_in, raw, act, conv, heads, skip)
    small_conv[...] += small[0]
    small_head[0:1] += small[1]
    small_head[1:2] += small[2]
    small_skip[0:1] += small[3]
    raw_wide = mm_t(low16(grad_raw), low16(select[...]))
    grad_x = low16(grad_u[:, :OWN])
    grad_com = low16(jnp.concatenate([grad_u[:, OWN:], raw_wide], axis=1))
    for side in range(2):
        rows = slice(side * BLOCK, (side + 1) * BLOCK)
        en_part[slot, side] = low16(
            mm_t(dgate[rows], w_own[:, :OWN]) + mm_t(grad_x[rows], w_own[:, OWN:]) + mm_t(grad_com[rows], w_com[...])
        )
    for k in range(QUADS):

        @pl.when(slot == k)
        def swap_en():
            swaps[1][k].start()

    normed_v = normed[...]
    acc_x[...] += t_mm(normed_v, grad_x)
    acc_com[...] += t_mm(normed_v, grad_com)

    def settle(kind, k, own, sib):
        route = routes[kind]
        relay = (branch_relay, en_relay)[kind]
        swaps[kind][k].wait_recv()
        sib[k] = low16(own.astype(f32) + sib[k].astype(f32))
        if k == 3:
            route["relay_x"].start()
            route["relay_y"].start()
        if k == 2:
            route["relay_x"].wait_recv()
            sib[k, :half] = low16(sib[k, :half].astype(f32) + relay[0].astype(f32))
            route["y"].start()
        if k == 1:
            route["relay_y"].wait_recv()
            sib[k, half:] = low16(sib[k, half:].astype(f32) + relay[1].astype(f32))
            route["x"].start()

    for k in range(QUADS):

        @pl.when(slot == k)
        def settle_branch():
            settle(0, k, branch[0, core], branch_sib)

        if k < QUADS - 1:

            @pl.when(slot == k)
            def settle_en():
                settle(1, k + 1, en_part[k + 1, core], en_sib)

    @pl.when(s == QUADS - 1)
    def tail():
        x_send[...] = low16(acc_x[...]).reshape(x_send.shape)
        for copy in x_z:
            copy.start()
        com_send[...] = low16(acc_com[...]).reshape(com_send.shape)
        com_swap.start()
        settle(1, 0, en_part[0, core], en_sib)
        gate_here.wait()
        for copy in gate_z:
            copy.wait_recv()
        sum_gate[...] = low16(
            gate_own[...].astype(f32) + gate_got[0].astype(f32) + gate_got[1].astype(f32) + gate_got[2].astype(f32)
        )
        for copy in gate_ranks:
            copy.start()
        gate_keep = pltpu.make_async_copy(sum_gate.at[rank], all_gate.at[rank], local.at[2])
        gate_keep.start()
        com_swap.wait_recv()
        com_sib[...] = low16(com_sib[...].astype(f32) + com_send[:, :, core].astype(f32))
        for copy in com_quads:
            copy.start()
        for name in ("x", "y"):
            routes[0][name].wait_recv()
        sum_branch[...] = (
            branch_sib[0].astype(f32) + branch_got[0].astype(f32) + branch_got[1].astype(f32)
        )
        for copy in com_quads:
            copy.wait_recv()
        com_z[...] = low16(
            com_sib[:, quad].astype(f32)
            + com_quad[0].astype(f32) + com_quad[1].astype(f32) + com_quad[2].astype(f32)
        )
        for copy in com_planes:
            copy.start()
        for name in ("x", "y"):
            routes[1][name].wait_recv()
        en = en_sib[0].astype(f32) + en_got[0].astype(f32) + en_got[1].astype(f32)
        rows = tok_own[...].astype(f32)
        scaling = lax.rsqrt(jnp.mean(rows * rows, axis=1, keepdims=True) + norm_eps)
        scaled = rows * scaling
        gain_grad = jnp.sum(en * scaled, axis=0, keepdims=True)
        weighted = en * gain_in[...]
        inner = jnp.mean(weighted * scaled, axis=1, keepdims=True)
        grad_rows[...] = scaling * (weighted - scaled * inner)
        pack_send[...] = jnp.zeros_like(pack_send)
        for i in range(D // LANES):
            pack_send[i : i + 1] = gain_grad[:, i * LANES : (i + 1) * LANES]
        gain_out_grad = g_gain[0:1]
        skip_grad = small_skip[0:1]
        for i in range(PAIRS):
            lanes = slice(i * LANES, (i + 1) * LANES)
            pack_send[12 + i : 13 + i] = gain_out_grad[:, lanes]
            pack_send[42 + i : 43 + i] = skip_grad[:, lanes]
            for tap in range(KCONV + 1):
                pack_send[15 + 3 * tap + i : 16 + 3 * tap + i] = small_conv[tap : tap + 1, lanes]
        for tap in range(KCONV + 1):
            for i in range(2):
                lanes = slice(OWN + i * LANES, OWN + (i + 1) * LANES)
                pack_send[30 + 2 * tap + i : 31 + 2 * tap + i] = small_conv[tap : tap + 1, lanes]
        pack_send[40:42] = small_head[0:2]
        for copy in pack_z:
            copy.start()
        for copy in com_planes:
            copy.wait_recv()
        sum_com[...] = (
            com_z[plane].astype(f32)
            + com_got[0].astype(f32) + com_got[1].astype(f32) + com_got[2].astype(f32)
        )
        for copy in pack_z:
            copy.wait_recv()
        pack_sum[...] = pack_send[...] + pack_got[0] + pack_got[1] + pack_got[2]
        for copy in pack_ranks:
            copy.start()
        pack_keep = pltpu.make_async_copy(pack_sum, packs.at[rank], local.at[3])
        pack_keep.start()
        for copy in x_z:
            copy.wait_recv()
        sum_x[...] = low16(
            x_send[plane].astype(f32) + x_got[0].astype(f32) + x_got[1].astype(f32) + x_got[2].astype(f32)
        )
        for copy in x_ranks:
            copy.start()
        x_keep = pltpu.make_async_copy(sum_x.at[rank], all_x.at[rank], local.at[4])
        x_keep.start()
        for origin in range(PLANES):

            @pl.when(jnp.logical_not((plane == origin) & out_stays))
            def arrived():
                out_landing(origin).wait_recv()

        @pl.when(out_stays)
        def kept():
            out_here.wait()

        for near in range(2):
            for side in range(2):

                @pl.when(jnp.logical_not((2 * core + near == plane) & (core == side)))
                def gone():
                    out_copy(near, side).wait_send()

        for copy in gate_ranks + pack_ranks + x_ranks:
            copy.wait_recv()
        for copy in gate_z + x_z + gate_ranks + x_ranks + [com_swap] + com_quads + com_planes + pack_z + pack_ranks:
            copy.wait_send()
        for kind in range(2):
            for copy in swaps[kind] + list(routes[kind].values()):
                copy.wait_send()
        gate_keep.wait()
        pack_keep.wait()
        x_keep.wait()


def run_back(lens, gate_grads, out_grads, branch, w_own, w_com, conv, heads, skip, select, gain_in, g_gain, tok_own,
             normed, dgate, dmix, proj_own, proj_com, act):
    f32, bf16 = (jnp.float32, jnp.bfloat16)
    rows_in = D // (PLANES * RANKS)
    rows_out = DIN // (PLANES * RANKS)
    gate_grads = gate_grads.reshape(PLANES, RANKS, rows_in, OWN)
    out_grads = out_grads.reshape(2, 2, rows_out, D)
    fixed = (w_own, w_com, conv, heads, skip, select, gain_in, g_gain, tok_own)
    grouped = (normed, dgate, dmix, proj_own, proj_com, act)

    def turned(width, place=0):
        return pl.BlockSpec((GROUP, width), lambda s: (QUADS - 1 - s, place))

    outs = (
        ((PLANES, rows_out, D), bf16, ANY),
        ((RANKS, rows_in, OWN), bf16, ANY),
        ((RANKS, rows_in, OWN), bf16, ANY),
        ((rows_in, COMMON_PAD), f32, None),
        ((RANKS, PACK, LANES), f32, ANY),
        ((BLOCK, D), f32, None),
        ((BLOCK, D), f32, None),
    )
    half = BLOCK // 2
    quarter = (RANKS, rows_in, OWN)
    com = (rows_in, COMMON_PAD)
    scratch = [
        ((D, OWN), f32), ((D, COMMON_PAD), f32), ((8, MIX), f32), ((8, LANES), f32), ((8, OWN), f32),
        ((QUADS, BLOCK, D), bf16), ((QUADS, 2, BLOCK, D), bf16), ((QUADS, BLOCK, D), bf16),
        ((2, BLOCK, D), bf16), ((2, BLOCK, D), bf16), ((2, half, D), bf16), ((2, half, D), bf16),
        ((PLANES - 1,) + quarter, bf16), (quarter, bf16), (quarter, bf16),
        ((PLANES,) + quarter, bf16), ((PLANES - 1,) + quarter, bf16), (quarter, bf16),
        ((PLANES, QUADS, 2) + com, bf16), ((PLANES, QUADS) + com, bf16), ((QUADS - 1, PLANES) + com, bf16),
        ((PLANES,) + com, bf16), ((PLANES - 1,) + com, bf16),
        ((PACK, LANES), f32), ((PLANES - 1, PACK, LANES), f32), ((PACK, LANES), f32),
    ]
    return pl.pallas_call(
        back_kernel,
        grid=(QUADS,),
        in_specs=[full_spec(lens.shape), ANY, ANY, ANY]
        + [full_spec(a.shape) for a in fixed]
        + [pl.BlockSpec((1, 2, BLOCK, D), lambda s: (QUADS - 1 - s, 0, 0, 0))]
        + [turned(D), turned(OWN), turned(OWN), turned(OWN, 1), turned(COMMON_PAD), turned(MIX)],
        out_specs=[full_spec(s) if spec is None else spec for s, kind, spec in outs],
        out_shape=[jax.ShapeDtypeStruct(s, kind) for s, kind, spec in outs],
        scratch_shapes=[pltpu.VMEM(s, kind) for s, kind in scratch]
        + [
            pltpu.SemaphoreType.DMA((64,)),
            pltpu.SemaphoreType.DMA((64,)),
            pltpu.SemaphoreType.DMA((4,)),
            pltpu.SemaphoreType.DMA((4,)),
            pltpu.SemaphoreType.DMA((5,)),
        ],
        compiler_params=pltpu.CompilerParams(
            vmem_limit_bytes=VMEM_GRANT, collective_id=2, has_side_effects=True
        ),
    )(lens, gate_grads, out_grads, branch, *fixed, branch, *grouped)


def adam_refs(refs, index, gradient, rate):
    weight, first, second, weight_new, first_new, second_new = refs
    results = adam_update(weight[index], first[index], second[index], gradient, rate)
    for ref, value in zip((weight_new, first_new, second_new), results):
        ref[index] = value


def finish_kernel(
    lens, tok, cot, sum_branch, grad_rows, r_out, all_gate, all_x, sum_com,
    in_w, in_m, in_v, out_w, out_m, out_v,
    mixed_out, grad_input, in_wn, in_mn, in_vn, out_wn, out_mn, out_vn
):
    f32 = jnp.float32
    core = lax.axis_index("seq")
    position = (iota((BLOCK, 1), 0) + core * BLOCK).astype(f32)
    live = (position < lens[0:1, 0:1]).astype(f32)
    mixed_out[...] = (tok[...].astype(f32) + live * sum_branch[...]).astype(jnp.bfloat16)
    grad_input[...] = cot[...].astype(f32) + grad_rows[...]
    ins = (in_w, in_m, in_v, in_wn, in_mn, in_vn)
    rows = in_w.shape[0]
    lanes = iota((rows, LANES), 1)
    for part, source in ((0, all_gate), (1, all_x)):
        for run in range(PLANES):
            side, near = divmod(run, 2)
            tiles = []
            for t in range(2 * PAIRS):
                halves = []
                for b in range(2):
                    p, i = divmod(2 * t + b, 3)
                    index = 3 * near + i
                    tile = source[2 * p + side, :, (index // 2) * LANES : (index // 2 + 1) * LANES].astype(f32)
                    halves.append(tile if index % 2 == b else pltpu.roll(tile, HDIM, 1))
                tiles.append(jnp.where(lanes < HDIM, halves[0], halves[1]))
            start = part * DIN + run * 2 * OWN
            adam_refs(ins, (slice(None), slice(start, start + 2 * OWN)), jnp.concatenate(tiles, axis=1), rate_in)
    adam_refs(ins, (slice(None), slice(2 * DIN, 2 * DIN + COMMON)), sum_com[:, :COMMON], rate_in)
    total = r_out[0].astype(f32) + r_out[1].astype(f32) + r_out[2].astype(f32) + r_out[3].astype(f32)
    adam_refs((out_w, out_m, out_v, out_wn, out_mn, out_vn), (slice(None), slice(None)), total, rate_out)


def run_finish(*args):
    tok, cot, in_w, out_w = (args[1], args[2], args[9], args[12])
    shapes = [(tok.shape, jnp.bfloat16), (cot.shape, jnp.float32)]
    shapes += [(in_w.shape, jnp.float32)] * 3 + [(out_w.shape, jnp.float32)] * 3
    whole = pl.BlockSpec(memory_space=pltpu.VMEM)
    return pl.pallas_call(
        finish_kernel,
        in_specs=[whole] * len(args),
        out_specs=[whole] * len(shapes),
        out_shape=[jax.ShapeDtypeStruct(s, kind) for s, kind in shapes],
        compiler_params=pltpu.CompilerParams(vmem_limit_bytes=VMEM_GRANT),
    )(*args)


def pick_runs(array, plane_runs, quad, core):
    lead = array.shape[:-1]
    width = array.shape[-1] // (PLANES * QUADS)
    split = array.reshape(lead + (2, 2, QUADS, width))
    zero = 0
    n = len(lead)
    taken = lax.dynamic_slice(
        split, (zero,) * n + (core, 0, quad, 0), lead + (1, 2, 1, width)
    )
    return taken.reshape(lead + (2 * width,))


def put_runs(array, quad, core):
    lead = array.shape[:-1]
    width = array.shape[-1] // 2
    zeros = jnp.zeros(lead + (2, 2, QUADS, width), array.dtype)
    n = len(lead)
    full = lax.dynamic_update_slice(
        zeros, array.reshape(lead + (1, 2, 1, width)), (0,) * n + (core, 0, quad, 0)
    )
    return full.reshape(lead + (width * PLANES * QUADS,))


def rank_slices(array):
    rows = array.shape[0]
    split = array.reshape(rows, 2, 2, QUADS, RUN)
    return split.transpose(3, 1, 0, 2, 4).reshape(RANKS, rows, OWN)


def rank_join(array):
    rows = array.shape[1]
    split = array.reshape(QUADS, 2, rows, 2, RUN)
    return split.transpose(2, 1, 3, 0, 4).reshape(rows, DIN)


def per_device_quad(
    tokens_in,
    cotangent,
    seq_lens,
    in_weight,
    in_first,
    in_second,
    out_weight,
    out_first,
    out_second,
    conv_weight,
    conv_first,
    conv_second,
    gains,
    gain_first,
    gain_second,
    head_params,
    head_first,
    head_second,
):
    plane, quad, core = place()
    rank = 2 * quad + core
    (
        normed, cot, w_own, w_com, w_out, proj_own, proj_com, act, mixed, grad_normed_out,
        stats, gain_in, gain_out, conv, heads, skip, select, lens
    ) = run_fore(tokens_in, cotangent, seq_lens, in_weight, out_weight, conv_weight, gains, head_params)
    branch, dgate, dmix, g_out, g_gate, g_gain = run_gate(
        lens, stats, cot, normed, proj_own, mixed, grad_normed_out, w_out, gain_out
    )
    r_out, all_gate, all_x, sum_com, packs, sum_branch, grad_rows = run_back(
        lens, g_gate, g_out, branch, w_own, w_com, conv, heads, skip, select, gain_in, g_gain,
        tokens_in, normed, dgate, dmix, proj_own, proj_com, act
    )
    finished = run_finish(
        lens, tokens_in, cotangent, sum_branch, grad_rows, r_out, all_gate, all_x, sum_com,
        in_weight, in_first, in_second, out_weight, out_first, out_second
    )
    mine = rank + RANKS * plane
    grad_gains = jnp.concatenate(
        [jnp.sum(packs[:, :12], axis=0).reshape(D), rank_join(packs[:, 12:15].reshape(RANKS, 1, OWN)).reshape(DIN)]
    )
    gain_sum = lax.dynamic_slice(grad_gains, (mine * gains.shape[0],), gains.shape)
    grad_conv = jnp.concatenate(
        [
            rank_join(packs[:, 15:30].reshape(RANKS, KCONV + 1, OWN)),
            jnp.sum(packs[:, 30:40], axis=0).reshape(KCONV + 1, 2 * NST),
        ],
        axis=1,
    )
    conv_sum = lax.dynamic_slice(grad_conv, (0, mine * conv_weight.shape[1]), conv_weight.shape)
    grad_skip = jnp.sum(packs[:, 42:45].reshape(RANKS, 1, OWN_HEADS, HDIM), axis=3)
    head_sum = jnp.concatenate([packs[:, 40:42, :OWN_HEADS], grad_skip], axis=1)
    head_sum = head_sum.reshape(QUADS, 2, 3, 2, 3).transpose(2, 1, 3, 0, 4).reshape(3, HEADS)
    new_conv = adam_update(conv_weight, conv_first, conv_second, conv_sum, rate_conv)
    new_gain = adam_update(gains, gain_first, gain_second, gain_sum, rate_gain)
    new_head = adam_update(head_params, head_first, head_second, head_sum, rate_head)
    return tuple(finished) + new_conv + new_gain + new_head


def solution(mesh):
    placed = (
        P(("dp", "seq"), None),
        P(("dp", "seq"), None),
        P("dp", None),
        P(("dp", "seq"), None),
        P(("dp", "seq"), None),
        P(("dp", "seq"), None),
        P(("dp", "seq"), None),
        P(("dp", "seq"), None),
        P(("dp", "seq"), None),
        P(None, ("dp", "seq")),
        P(None, ("dp", "seq")),
        P(None, ("dp", "seq")),
        P(("dp", "seq")),
        P(("dp", "seq")),
        P(("dp", "seq")),
        P(),
        P(),
        P(),
    )
    quad = dict(mesh.shape) == {"dp": PLANES * QUADS, "seq": 2}
    return jax.shard_map(
        per_device_quad if quad else per_device,
        mesh=mesh,
        in_specs=placed,
        out_specs=(
            P(("dp", "seq"), None),
            P(("dp", "seq"), None),
            P(("dp", "seq"), None),
            P(("dp", "seq"), None),
            P(("dp", "seq"), None),
            P(("dp", "seq"), None),
            P(("dp", "seq"), None),
            P(("dp", "seq"), None),
            P(None, ("dp", "seq")),
            P(None, ("dp", "seq")),
            P(None, ("dp", "seq")),
            P(("dp", "seq")),
            P(("dp", "seq")),
            P(("dp", "seq")),
            P(),
            P(),
            P(),
        ),
        check_vma=False,
    )
```

```python
import functools

import jax
import jax.numpy as jnp
from jax import lax
from jax.experimental import pallas as pl
from jax.experimental.pallas import tpu as pltpu
from jax.sharding import PartitionSpec as P

D = 1536
HEADS = 48
HDIM = 64
NST = 128
KCONV = 4
BLOCK = 256
SLOTS = 4
STEP = 10
DIN = 3072
CONVC = 3328


highest = lax.Precision.HIGHEST
norm_eps = 1e-05
beta_first = 0.9
beta_second = 0.95
adam_eps = 1e-08
weight_decay = 0.1
rate_in = 0.01
rate_out = 0.008
rate_conv = 0.2
rate_gain = 0.4
rate_head = 0.5


def from_behind(block, axis, distance):
    devices = range(lax.axis_size(axis))
    route = [(i - distance, i) for i in devices if i - distance in devices]
    return lax.ppermute(block, axis, route)


def prefix(value, axis, join, neutral):
    place = lax.axis_index(axis)
    gathered = jax.tree.map(
        lambda a, kind: lax.all_gather(a.astype(kind), axis),
        value,
        jax.tree.map(lambda a: jnp.bfloat16 if a.dtype == jnp.float32 else a.dtype, value),
    )
    state = jax.tree.map(lambda a, e: jnp.zeros_like(a) + jnp.asarray(e, a.dtype), value, neutral)

    def one(hop, state):
        return join(
            state,
            jax.tree.map(
                lambda a, own: lax.dynamic_index_in_dim(a, hop, 0, False).astype(own.dtype),
                gathered,
                value,
            ),
        )

    return lax.fori_loop(0, place, one, state)


def prefix_2(value, axis, combine, identity):
    devices, index = (lax.axis_size(axis), lax.axis_index(axis))
    everything = jax.tree.map(
        lambda part, kind: lax.all_gather(part.astype(kind), axis),
        value,
        (jnp.bfloat16, jnp.bfloat16),
    )
    start = jax.tree.map(
        lambda part, zero: jnp.broadcast_to(jnp.asarray(zero, part.dtype), part.shape),
        value,
        identity,
    )

    def hop(k, before):
        at = devices - 1 - k
        reached = at > index
        new = combine(
            before, jax.tree.map(lambda part, own: part[at].astype(own.dtype), everything, value)
        )
        return jax.tree.map(lambda a, b: jnp.where(reached, a, b), new, before)

    return lax.fori_loop(0, devices, hop, start)


def segment_of(seq_row, position):
    blocks = (seq_row + BLOCK - 1) // BLOCK
    ends = jnp.cumsum(blocks) * BLOCK
    starts = ends - blocks * BLOCK
    above = position[:, None] >= starts[None, :]
    inside = above & (position[:, None] < ends[None, :])
    numbers = jnp.arange(1, SLOTS + 1, dtype=jnp.int32)
    labels_of = jnp.sum(jnp.where(inside, numbers[None, :], 0), axis=1)
    live_rows = jnp.sum(
        (above & (position[:, None] < (starts + seq_row)[None, :])).astype(jnp.float32), axis=1
    )
    return (labels_of, live_rows)


def layout(seq_row, position):
    labels_of, live_rows = segment_of(seq_row, position)
    columns = []
    for conv_lag in range(KCONV):
        earlier, unused_live = segment_of(seq_row, position - conv_lag)
        columns.append(((earlier == labels_of) & (labels_of > 0)).astype(jnp.float32))
    return (live_rows, jnp.stack(columns, axis=1))


def pre_norm(token_rows, gain_row):
    scaling = lax.rsqrt(jnp.mean(token_rows * token_rows, axis=1, keepdims=True) + norm_eps)
    return token_rows * scaling * gain_row[None, :]


def gate_norm(mixed, gate_part, gain_row):
    gated = mixed * jax.nn.silu(gate_part)
    scaling = lax.rsqrt(jnp.mean(gated * gated, axis=1, keepdims=True) + norm_eps)
    return gated * scaling * gain_row[None, :]


def mixer_in(extended, step_raw, conv_par, head_values, factors, live_rows):
    row_count = step_raw.shape[0]
    preact = jnp.zeros((row_count, conv_par.shape[1]), jnp.float32) + conv_par[KCONV][None, :]
    for conv_tap in range(KCONV):
        window = lax.slice_in_dim(extended, conv_tap, conv_tap + row_count, axis=0)
        preact = (
            preact
            + conv_par[conv_tap][None, :] * window * factors[:, KCONV - 1 - conv_tap][:, None]
        )
    conv_act = jax.nn.silu(preact)
    step_size = jax.nn.softplus(step_raw + head_values[0][None, :]) * live_rows[:, None]
    logdec = -jnp.exp(head_values[1])[None, :] * step_size
    return (conv_act, step_size, logdec)


def lower_ones():
    row_ids = lax.broadcasted_iota(jnp.int32, (BLOCK, BLOCK), 0)
    col_ids = lax.broadcasted_iota(jnp.int32, (BLOCK, BLOCK), 1)
    return (row_ids >= col_ids).astype(jnp.float32)


def block_state(values, keys_in, step_size, logdec):
    cumul = jnp.dot(lower_ones(), logdec, precision=highest)
    totals = cumul[-1]
    weighting = jnp.exp(totals[None, :] - cumul) * step_size
    states = jnp.einsum("uhp,un->hpn", weighting[:, :, None] * values, keys_in, precision=highest)
    return (jnp.exp(totals), states)


def block_out(values, keys_in, queries, step_size, logdec, skip_gain, start_state):
    lower_tri = lower_ones()
    cumul = jnp.dot(lower_tri, logdec, precision=highest)
    across = cumul.T
    gap_matrix = across[:, :, None] - across[:, None, :]
    decays = jnp.exp(jnp.where(lower_tri[None, :, :] > 0, gap_matrix, -1e30))
    gram_matrix = jnp.dot(queries, keys_in.T, precision=highest)
    mixing = gram_matrix[None, :, :] * decays * step_size.T[:, None, :]
    intra_part = jnp.einsum("htu,uhp->thp", mixing, values, precision=highest)
    carried = jnp.exp(cumul)[:, :, None] * jnp.einsum(
        "tn,hpn->thp", queries, start_state, precision=highest
    )
    return intra_part + carried + skip_gain[None, :, None] * values


def block_full(values, keys_in, queries, step_size, logdec, skip_gain, start_state):
    factor_end, states = block_state(values, keys_in, step_size, logdec)
    outputs = block_out(values, keys_in, queries, step_size, logdec, skip_gain, start_state)
    return (outputs, factor_end[:, None, None] * start_state + states)


def adam_update(weight, first, second, gradient, step_rate):
    first_new = beta_first * first + (1.0 - beta_first) * gradient
    second_new = beta_second * second + (1.0 - beta_second) * gradient * gradient
    first_hat = first_new / (1.0 - beta_first**STEP)
    second_hat = second_new / (1.0 - beta_second**STEP)
    weight_new = weight - step_rate * (
        first_hat / (jnp.sqrt(second_hat) + adam_eps) + weight_decay * weight
    )
    return (weight_new, first_new, second_new)


def carry_join(earlier, later):
    return (earlier[0] * later[0], later[0][:, None, None] * earlier[1] + later[1])


def as_float(array_low):
    return lax.optimization_barrier(array_low).astype(jnp.float32)


def contract_rows(left, right):
    return lax.dot_general(
        left, right, (((0,), (0,)), ((), ())), preferred_element_type=jnp.float32
    )


def contract_cols(left, right):
    return lax.dot_general(
        left, right, (((1,), (1,)), ((), ())), preferred_element_type=jnp.float32
    )


def per_device(
    tokens_in,
    cotangent,
    seq_lens,
    in_weight,
    in_first,
    in_second,
    out_weight,
    out_first,
    out_second,
    conv_weight,
    conv_first,
    conv_second,
    gains,
    gain_first,
    gain_second,
    head_params,
    head_first,
    head_second,
):
    local_tok = tokens_in.shape[0]
    position = lax.axis_index("seq") * local_tok + jnp.arange(local_tok, dtype=jnp.int32)
    live_rows, factors = layout(seq_lens[0], position)
    low_weights = (
        in_weight.astype(jnp.bfloat16),
        out_weight.astype(jnp.bfloat16),
        conv_weight.astype(jnp.bfloat16),
        gains.astype(jnp.bfloat16),
    )
    in_full, out_full, conv_full, gain_full = (
        lax.all_gather(low_weights[0], ("dp", "seq"), axis=0, tiled=True),
        lax.all_gather(low_weights[1], ("dp", "seq"), axis=0, tiled=True),
        lax.all_gather(low_weights[2], ("dp", "seq"), axis=1, tiled=True),
        lax.all_gather(low_weights[3], ("dp", "seq"), axis=0, tiled=True),
    )
    conv_par = conv_full.astype(jnp.float32)
    gain_par = gain_full.astype(jnp.float32)
    token_rows = tokens_in.astype(jnp.float32)
    normed_value, pull_pre = jax.vjp(pre_norm, token_rows, gain_par[:D])
    normed = normed_value.astype(jnp.bfloat16)
    projected = jnp.dot(normed, in_full, preferred_element_type=jnp.float32)
    gate_part = projected[:, :DIN]
    conv_in = projected[:, DIN : DIN + CONVC]
    step_raw = projected[:, DIN + CONVC :]
    halo_rows = from_behind(conv_in[local_tok - KCONV + 1 :], "seq", 1)
    extended = jnp.concatenate([halo_rows, conv_in], axis=0)

    def mixer_local(extended_rows, raw_steps, conv_values, head_values):
        return mixer_in(extended_rows, raw_steps, conv_values, head_values, factors, live_rows)

    (conv_act, step_size, logdec), pull_mixer = jax.vjp(
        mixer_local, extended, step_raw, conv_par, head_params
    )
    conv_used = as_float(conv_act.astype(jnp.bfloat16))
    block_count = local_tok // BLOCK
    values = conv_used[:, :DIN].reshape(block_count, BLOCK, HEADS, HDIM)
    keys_in = conv_used[:, DIN : DIN + NST].reshape(block_count, BLOCK, NST)
    queries = conv_used[:, DIN + NST :].reshape(block_count, BLOCK, NST)
    steps_blk = step_size.reshape(block_count, BLOCK, HEADS)
    logdec_blk = logdec.reshape(block_count, BLOCK, HEADS)
    resets = factors[::BLOCK, 1]
    skip_gain = head_params[2]
    decays, block_states = jax.vmap(block_state)(values, keys_in, steps_blk, logdec_blk)

    def fold_local(carried, block_item):
        factor_now = block_item[0] * block_item[2]
        return (
            (carried[0] * factor_now, factor_now[:, None, None] * carried[1] + block_item[1]),
            None,
        )

    identity = (jnp.ones((HEADS,), jnp.float32), jnp.zeros((HEADS, HDIM, NST), jnp.float32))
    device_sum, unused_fold = lax.scan(fold_local, identity, (decays, block_states, resets))
    unused_dec, entering = prefix(device_sum, "seq", carry_join, identity)

    def start_states(states, block_item):
        begin = block_item[2] * states
        return (block_item[0][:, None, None] * begin + block_item[1], begin)

    unused_end, begins = lax.scan(start_states, entering, (decays, block_states, resets))

    def emit(block_item):
        return block_out(
            block_item[0],
            block_item[1],
            block_item[2],
            block_item[3],
            block_item[4],
            skip_gain,
            block_item[5],
        )

    mixed = lax.map(emit, (values, keys_in, queries, steps_blk, logdec_blk, begins)).reshape(
        local_tok, DIN
    )
    normed_out_value, pull_gate = jax.vjp(gate_norm, mixed, gate_part, gain_par[D:])
    normed_out = normed_out_value.astype(jnp.bfloat16)
    branch = jnp.dot(normed_out, out_full, preferred_element_type=jnp.float32)
    mixed_out = (token_rows + live_rows[:, None] * branch).astype(jnp.bfloat16)
    out_grad = (cotangent.astype(jnp.float32) * live_rows[:, None]).astype(jnp.bfloat16)
    in_back, out_back = (
        lax.all_gather(in_weight.astype(jnp.bfloat16), ("dp", "seq"), axis=0, tiled=True),
        lax.all_gather(out_weight.astype(jnp.bfloat16), ("dp", "seq"), axis=0, tiled=True),
    )
    grad_out_w = contract_rows(normed_out, out_grad)
    grad_normed_out = contract_cols(out_grad, out_back)
    grad_mixed, grad_gate, grad_gain_in = pull_gate(grad_normed_out)
    mixed_back = as_float(grad_mixed.astype(jnp.bfloat16)).reshape(block_count, BLOCK, HEADS, HDIM)

    def adjoint_local(carried, block_item):
        cumul = jnp.dot(lower_ones(), block_item[2], precision=highest)
        weighted = jnp.exp(cumul)[:, :, None] * block_item[0]
        direct = jnp.einsum("thp,tn->hpn", weighted, block_item[1], precision=highest)
        return (block_item[4] * (direct + block_item[3][:, None, None] * carried), None)

    local_adj, unused_adj = lax.scan(
        adjoint_local, identity[1], (mixed_back, queries, logdec_blk, decays, resets), reverse=True
    )
    unused_later, leaving = prefix_2((device_sum[0], local_adj), "seq", carry_join, identity)

    def adjoint_block(carried, block_item):
        unused_primal, pull_block = jax.vjp(
            block_full,
            block_item[0],
            block_item[1],
            block_item[2],
            block_item[3],
            block_item[4],
            skip_gain,
            block_item[5],
        )
        grads = pull_block((block_item[6], carried[0]))
        return ((block_item[7] * grads[6], carried[1] + grads[5]), grads[:5])

    (unused_state, grad_skip), block_grads = lax.scan(
        adjoint_block,
        (leaving, jnp.zeros((HEADS,), jnp.float32)),
        (values, keys_in, queries, steps_blk, logdec_blk, begins, mixed_back, resets),
        reverse=True,
    )
    grad_values, grad_keys, grad_queries, grad_step, grad_logdec = block_grads
    grad_act = jnp.concatenate(
        [
            grad_values.reshape(local_tok, DIN),
            grad_keys.reshape(local_tok, NST),
            grad_queries.reshape(local_tok, NST),
        ],
        axis=1,
    )
    grad_ext, grad_raw, grad_conv, grad_head_part = pull_mixer(
        (grad_act, grad_step.reshape(local_tok, HEADS), grad_logdec.reshape(local_tok, HEADS))
    )
    returned = from_behind(grad_ext[: KCONV - 1].astype(jnp.bfloat16), "seq", -1).astype(
        jnp.float32
    )
    grad_conv_in = grad_ext[KCONV - 1 :] + jnp.concatenate(
        [jnp.zeros((local_tok - KCONV + 1, CONVC), jnp.float32), returned], axis=0
    )
    grad_proj = jnp.concatenate([grad_gate, grad_conv_in, grad_raw], axis=1).astype(jnp.bfloat16)
    grad_normed = contract_cols(grad_proj, in_back)
    grad_rows, grad_gain_pre = pull_pre(grad_normed)
    grad_input = cotangent.astype(jnp.float32) + grad_rows
    grad_gains = jnp.concatenate([grad_gain_pre, grad_gain_in], axis=0)
    grad_head = jnp.concatenate(
        [grad_head_part[:2], (grad_head_part[2] + grad_skip)[None, :]], axis=0
    )
    grad_in_w = contract_rows(normed, grad_proj)
    in_sum, out_sum, conv_sum, gain_sum = (
        lax.psum_scatter(grad_in_w, ("dp", "seq"), scatter_dimension=0, tiled=True),
        lax.psum_scatter(grad_out_w, ("dp", "seq"), scatter_dimension=0, tiled=True),
        lax.psum_scatter(grad_conv, ("dp", "seq"), scatter_dimension=1, tiled=True),
        lax.psum_scatter(grad_gains, ("dp", "seq"), scatter_dimension=0, tiled=True),
    )
    head_sum = lax.psum(grad_head, ("dp", "seq"))
    new_in = adam_update(in_weight, in_first, in_second, in_sum, rate_in)
    new_out = adam_update(out_weight, out_first, out_second, out_sum, rate_out)
    new_conv = adam_update(conv_weight, conv_first, conv_second, conv_sum, rate_conv)
    new_gain = adam_update(gains, gain_first, gain_second, gain_sum, rate_gain)
    new_head = adam_update(head_params, head_first, head_second, head_sum, rate_head)
    return (
        mixed_out,
        grad_input,
        new_in[0],
        new_in[1],
        new_in[2],
        new_out[0],
        new_out[1],
        new_out[2],
        new_conv[0],
        new_conv[1],
        new_conv[2],
        new_gain[0],
        new_gain[1],
        new_gain[2],
        new_head[0],
        new_head[1],
        new_head[2],
    )


MESH_ID = pl.DeviceIdType.MESH
ANY = pl.BlockSpec(memory_space=pl.ANY)
PLANES = 4
QUADS = 4
RANKS = 8


def place():
    chip = lax.axis_index("dp")
    return (chip // QUADS, chip % QUADS, lax.axis_index("seq"))


def at(plane, quad, core):
    return (plane * QUADS + quad, core)


def flip(core):
    return 1 - core


def xor4(value, k):
    low, high = value % 2, value // 2
    if k % 2:
        low = 1 - low
    if k // 2:
        high = 1 - high
    return 2 * high + low


def greet(devices):
    barrier = pltpu.get_barrier_semaphore()
    for device in devices:
        pl.semaphore_signal(barrier, inc=1, device_id=device, device_id_type=MESH_ID)
    pl.semaphore_wait(barrier, len(devices))


def plane_mates(plane, quad, core):
    mates = []
    for k in range(QUADS):
        for other in (core, flip(core)):
            if not (k == 0 and other is core):
                mates.append(at(plane, xor4(quad, k), other))
    return mates


def plane_others(plane, quad, core):
    return [at(xor4(plane, k), quad, core) for k in range(1, PLANES)]


class Sems:
    def __init__(self, send, recv):
        self.send, self.recv, self.used = (send, recv, 0)

    def copy(self, source, target, device):
        index = self.used
        self.used += 1
        return pltpu.make_async_remote_copy(
            src_ref=source,
            dst_ref=target,
            send_sem=self.send.at[index],
            recv_sem=self.recv.at[index],
            device_id=device,
            device_id_type=MESH_ID,
        )


class PlaneGather:
    def __init__(self, sems, own, land, plane, quad, core):
        near_x, near_y, far = (xor4(quad, k) for k in (1, 2, 3))
        rank, rank_x, rank_y, rank_far = (2 * q + core for q in (quad, near_x, near_y, far))
        to_x, to_y = (at(plane, near_x, core), at(plane, near_y, core))
        sibling = at(plane, quad, flip(core))
        whole = [0, 1]
        self.own = [
            sems.copy(own(h), land(rank, slot, h), device)
            for device, slot in ((to_x, 1), (to_y, 2), (sibling, 0))
            for h in whole
        ]
        self.relay_x = [
            sems.copy(land(rank_x, 1, 0), land(rank_x, 3, 0), to_y),
        ] + [sems.copy(land(rank_x, 1, h), land(rank_x, 1, h), sibling) for h in whole]
        self.relay_y = [
            sems.copy(land(rank_y, 2, 1), land(rank_y, 3, 1), to_x),
        ] + [sems.copy(land(rank_y, 2, h), land(rank_y, 2, h), sibling) for h in whole]
        self.relay_far = [
            sems.copy(land(rank_far, 3, h), land(rank_far, 3, h), sibling) for h in whole
        ]

    def start(self):
        for copy in self.own:
            copy.start()

    def near(self):
        self.own[0].wait_recv()
        self.relay_x[0].start()
        self.own[3].wait_recv()
        self.relay_y[0].start()
        self.own[1].wait_recv()
        self.own[2].wait_recv()
        for copy in self.relay_x[1:] + self.relay_y[1:]:
            copy.start()

    def across(self):
        for h, relay in ((0, self.relay_x[0]), (1, self.relay_y[0])):
            relay.wait_recv()
            self.relay_far[h].start()

    def wait_slot(self, slot):
        for copy in (self.own[4:], self.relay_x[1:], self.relay_y[1:], self.relay_far)[slot]:
            copy.wait_recv()

    def sent(self):
        for copy in self.own + self.relay_x + self.relay_y + self.relay_far:
            copy.wait_send()


class LineGather:
    def __init__(self, sems, own, block, plane, quad, core):
        self.plane = plane
        self.right, self.left = ([], [])
        for hop in range(PLANES - 1):
            for copies, step in ((self.right, 1), (self.left, -1)):
                index = plane - step * hop
                source = own if hop == 0 else block(index)
                copies.append(sems.copy(source, block(index), at(plane + step, quad, core)))

    def sends(self, hop, step):
        if step > 0:
            return (self.plane - hop >= 0) & (self.plane < PLANES - 1)
        return (self.plane + hop < PLANES) & (self.plane > 0)

    def receives(self, hop, step):
        if step > 0:
            return self.plane - 1 - hop >= 0
        return self.plane + 1 + hop < PLANES

    def start(self, hop):
        for copies, step in ((self.right, 1), (self.left, -1)):

            @pl.when(self.sends(hop, step))
            def go():
                copies[hop].start()

    def arrive(self, hop):
        for copies, step in ((self.right, 1), (self.left, -1)):

            @pl.when(self.receives(hop, step))
            def landed():
                copies[hop].wait_recv()

    def sent(self):
        for hop in range(PLANES - 1):
            for copies, step in ((self.right, 1), (self.left, -1)):

                @pl.when(self.sends(hop, step))
                def left():
                    copies[hop].wait_send()


OWN_HEADS = HEADS // RANKS
OWN = OWN_HEADS * HDIM
PAIRS = OWN_HEADS // 2
RUN = OWN // 2
COMMON = 2 * NST + HEADS
COMMON_PAD = 384
GROUP = 2 * BLOCK
MIX = OWN + 2 * NST
LANES = 128


def mm(left, right):
    return lax.dot_general(left, right, (((1,), (0,)), ((), ())), preferred_element_type=jnp.float32)


def mm_t(left, right):
    return lax.dot_general(left, right, (((1,), (1,)), ((), ())), preferred_element_type=jnp.float32)


def t_mm(left, right):
    return lax.dot_general(left, right, (((0,), (0,)), ((), ())), preferred_element_type=jnp.float32)


def mm_full(left, right):
    return lax.dot_general(
        left, right, (((1,), (0,)), ((), ())), precision=highest, preferred_element_type=jnp.float32
    )


def low16(value):
    return value.astype(jnp.bfloat16)


def iota(shape, axis):
    return lax.broadcasted_iota(jnp.int32, shape, axis)


def head_spread():
    return (iota((LANES, OWN), 1) // HDIM == iota((LANES, OWN), 0)).astype(jnp.float32)


def head_gather():
    return (iota((OWN, LANES), 0) // HDIM == iota((OWN, LANES), 1)).astype(jnp.float32)


def lower_mask():
    return iota((BLOCK, BLOCK), 0) >= iota((BLOCK, BLOCK), 1)


def shift_down(value, k):
    if k == 0:
        return value
    rolled = pltpu.roll(value, k, 0)
    return jnp.where(iota(value.shape, 0) >= k, rolled, 0.0)


def shift_up(value, k):
    if k == 0:
        return value
    rows = value.shape[0]
    rolled = pltpu.roll(value, rows - k, 0)
    return jnp.where(iota(value.shape, 0) < rows - k, rolled, 0.0)


def sigmoid(value):
    return 1.0 / (1.0 + jnp.exp(-value))


def softplus(value):
    return jnp.maximum(value, 0.0) + jnp.log1p(jnp.exp(-jnp.abs(value)))


def preact_of(u, conv):
    total = u * conv[KCONV - 1 : KCONV] + conv[KCONV : KCONV + 1]
    for tap in range(KCONV - 1):
        total = total + shift_down(u, KCONV - 1 - tap) * conv[tap : tap + 1]
    return total


def steps_of(raw, heads, live):
    step = softplus(raw + heads[0:1]) * live * heads[3:4]
    return (step, -jnp.exp(heads[1:2]) * step)


def lane_half(value, side):
    lanes = iota(value.shape, 1)
    return jnp.where((lanes >= HDIM) == (side == 1), value, jnp.zeros_like(value))


def block_parts(step, logdec, spread):
    cumul = mm_full(lower_mask().astype(jnp.float32), logdec)
    return (cumul, jnp.transpose(cumul), mm_full(step, spread), mm_full(cumul, spread))


def ssd_forward(act, step, logdec, skip, out):
    spread = head_spread()
    lower = lower_mask()
    state = None
    for k in range(2):
        rows = slice(k * BLOCK, (k + 1) * BLOCK)
        values, keys, queries = (act[rows, :OWN], act[rows, OWN : OWN + NST], act[rows, OWN + NST :])
        cumul, cumul_t, step_w, cumul_w = block_parts(step[rows], logdec[rows], spread)
        gram = jnp.where(lower, mm_t(queries, keys), 0.0)
        values_f = values.astype(jnp.float32)
        stepped = low16(values_f * step_w)
        base = skip * values_f
        if state is not None:
            base = base + jnp.exp(cumul_w) * mm(queries, state)
        else:
            weighting = jnp.exp(cumul_w[BLOCK - 1 :] - cumul_w) * step_w
            state = low16(t_mm(keys, low16(weighting * values_f)))

        for pair in range(PAIRS):
            lanes = slice(pair * LANES, (pair + 1) * LANES)
            piece = 0.0
            for side in range(2):
                h = 2 * pair + side
                decay = jnp.exp(jnp.minimum(cumul[:, h : h + 1] - cumul_t[h : h + 1, :], 0.0))
                piece = piece + mm(low16(gram * decay), lane_half(stepped[:, lanes], side))
            out[rows, lanes] = base[:, lanes] + piece


def live_of(lens, g):
    rows = iota((GROUP, 1), 0).astype(jnp.float32)
    chosen = jnp.sum(jnp.where(iota(lens.shape, 0) == g, lens, 0.0), axis=0, keepdims=True)[:, :1]
    return (rows < chosen).astype(jnp.float32)


def quad_of(slot):
    quad = lax.axis_index("dp") % QUADS
    return (quad % 2 + slot % 2) % 2 + 2 * ((quad // 2 + slot // 2) % 2)


def full_spec(shape):
    return pl.BlockSpec(shape, lambda g: (0,) * len(shape))


def group_spec(width):
    return pl.BlockSpec((GROUP, width), lambda g: (g, 0))


VMEM_GRANT = 60 * 1024 * 1024


def backward_block(k, act, dmix, step, logdec, skip, state, state_grad, spread, gather):
    rows = slice(k * BLOCK, (k + 1) * BLOCK)
    values, keys, queries = (act[rows, :OWN], act[rows, OWN : OWN + NST], act[rows, OWN + NST :])
    step, logdec = (step[rows], logdec[rows])
    lower = lower_mask()
    cumul, cumul_t, step_w, cumul_w = block_parts(step, logdec, spread)
    step_t = jnp.transpose(step)
    gram = jnp.where(lower, mm_t(queries, keys), 0.0)
    values_f = values.astype(jnp.float32)
    dmix_f = dmix[rows].astype(jnp.float32)
    lanes_h = iota((BLOCK, LANES), 1)

    rows_h = iota((8, BLOCK), 0)
    grad_gram = 0.0
    row_sums = jnp.zeros((BLOCK, LANES), jnp.float32)
    col_sums = jnp.zeros((8, BLOCK), jnp.float32)
    pieces = []
    for pair in range(PAIRS):
        lanes = slice(pair * LANES, (pair + 1) * LANES)
        dm, value = (dmix[rows, lanes], act[rows, lanes])
        piece = 0.0
        for side in range(2):
            h = 2 * pair + side
            decay = jnp.exp(jnp.minimum(cumul[:, h : h + 1] - cumul_t[h : h + 1, :], 0.0))
            dm_half = lane_half(dm, side)
            grad_mixing = mm_t(dm_half, value)
            step_row = step_t[h : h + 1, :]
            mixing = gram * decay
            piece = piece + t_mm(low16(mixing), dm_half)
            grad_gram = grad_gram + grad_mixing * decay * step_row
            product = grad_mixing * mixing
            col_sums = jnp.where(rows_h == h, jnp.sum(product, axis=0, keepdims=True), col_sums)
            row_sums = jnp.where(
                lanes_h == h, jnp.sum(product * step_row, axis=1, keepdims=True), row_sums
            )
        pieces.append(piece)
    grad_values = jnp.concatenate(pieces, axis=1) * step_w + skip * dmix_f
    grad_skip = jnp.sum(dmix_f * values_f, axis=0, keepdims=True)
    grad_gram = low16(jnp.where(lower, grad_gram, 0.0))
    grad_queries = mm(grad_gram, keys)
    grad_keys = t_mm(grad_gram, queries)
    columns = jnp.transpose(
        jnp.concatenate([col_sums, jnp.zeros((LANES - 8, BLOCK), jnp.float32)], axis=0)
    )
    grad_step = columns
    grad_cumul = row_sums - columns * step
    if k == 1:
        entering = jnp.exp(cumul_w) * dmix_f
        entering_low = low16(entering)
        crossed = mm(queries, state)
        grad_cumul = grad_cumul + mm_full(entering * crossed, gather)
        grad_queries = grad_queries + mm_t(entering_low, state)
        before = low16(t_mm(queries, entering_low))
    else:
        tail = jnp.exp(cumul_w[BLOCK - 1 :] - cumul_w)
        weighting = tail * step_w
        back = mm(keys, state_grad)
        grad_values = grad_values + weighting * back
        grad_keys = grad_keys + mm_t(low16(weighting * values_f), state_grad)
        grad_weight = mm_full(values_f * back, gather)
        tail_h = jnp.exp(cumul[BLOCK - 1 :] - cumul)
        grad_step = grad_step + grad_weight * tail_h
        part = grad_weight * tail_h * step
        last = iota((BLOCK, LANES), 0) == BLOCK - 1
        grad_cumul = grad_cumul - part + jnp.where(last, jnp.sum(part, axis=0, keepdims=True), 0.0)
        before = None
    upper = (iota((BLOCK, BLOCK), 0) <= iota((BLOCK, BLOCK), 1)).astype(jnp.float32)
    grad_logdec = mm_full(upper, grad_cumul)
    return (grad_values, grad_keys, grad_queries, grad_step, grad_logdec, grad_skip, before)


ROWS_IN = D // (PLANES * RANKS)
ROWS_OUT = DIN // (PLANES * RANKS)
ROWS_ALL = ROWS_IN + 16
SHARD_CONV = CONVC // (PLANES * RANKS)
SHARD_GAIN = (D + DIN) // (PLANES * RANKS)
RUN_HALVES = RUN // HDIM


def place_lanes(pieces, tiles, rows):
    lanes = iota((rows, LANES), 1)
    out = [jnp.zeros((rows, LANES), jnp.float32) for unused in range(tiles)]
    for value, width, offset in pieces:
        tile, lane = divmod(offset, LANES)
        moved = pltpu.roll(value, lane, 1) if lane else value
        end = lane + width
        out[tile] = jnp.where((lanes >= lane) & (lanes < end), moved, out[tile])
        if end > LANES:
            out[tile + 1] = jnp.where(lanes < end - LANES, moved, out[tile + 1])
    return out


def own_lanes(tiles, quad, core):
    rows = tiles[0].shape[0]
    lanes = iota((rows, LANES), 1)

    def half_of(index):
        tile, odd = (index // 2, index % 2)
        chosen = tiles[0]
        for t in range(1, len(tiles)):
            chosen = jnp.where(tile == t, tiles[t], chosen)
        return (chosen, odd)

    out = []
    for pair in range(PAIRS):
        sides = []
        for b in range(2):
            near, i = divmod(2 * pair + b, RUN_HALVES)
            value, odd = half_of(2 * PLANES * RUN_HALVES * core + PLANES * RUN_HALVES * near + RUN_HALVES * quad + i)
            sides.append(jnp.where(odd == b, value, pltpu.roll(value, HDIM, 1)))
        out.append(jnp.where(lanes < HDIM, sides[0], sides[1]))
    return jnp.concatenate(out, axis=1)


def fill_sends(in_w, part, target):
    lanes = iota((ROWS_IN, LANES), 1)
    for j in range(RANKS):
        quad, core = divmod(j, 2)
        for pair in range(PAIRS):
            sides = []
            for b in range(2):
                near, i = divmod(2 * pair + b, RUN_HALVES)
                index = (2 * core + near) * PLANES * RUN_HALVES + RUN_HALVES * quad + i
                start = part * DIN + index // 2 * LANES
                tile = in_w[:, start : start + LANES]
                sides.append(tile if index % 2 == b else pltpu.roll(tile, HDIM, 1))
            lane = pair * LANES
            target[j, :, lane : lane + LANES] = low16(jnp.where(lanes < HDIM, sides[0], sides[1]))


def fill_common(in_w, conv_w, gains, lens, wc_send):
    wc_send[...] = jnp.zeros_like(wc_send)
    wc_send[:ROWS_IN, : 2 * NST] = low16(in_w[:, 2 * DIN : 2 * DIN + 2 * NST])
    tail = in_w[:, 2 * DIN + 2 * NST : 2 * DIN + COMMON]
    wide = jnp.concatenate([tail, jnp.zeros((ROWS_IN, LANES - HEADS), jnp.float32)], axis=1)
    wc_send[:ROWS_IN, 2 * NST :] = low16(wide)
    conv_v = jnp.concatenate([conv_w[...], jnp.zeros((KCONV + 1, COMMON_PAD - SHARD_CONV), jnp.float32)], axis=1)
    gain_v = jnp.concatenate([gains[...], jnp.zeros((1, COMMON_PAD - SHARD_GAIN), jnp.float32)], axis=1)
    extra = jnp.broadcast_to(lens[:, 0:1].astype(jnp.float32) - BLOCK, (1, COMMON_PAD))
    rows = jnp.concatenate([conv_v, gain_v, extra, jnp.zeros((9, COMMON_PAD), jnp.float32)], axis=0)
    wc_send[ROWS_IN:] = low16(rows)


def select_heads(quad, core):
    rows, columns = (iota((LANES, LANES), 0), iota((LANES, LANES), 1))
    head = HEADS // 2 * core + HEADS // 4 * (columns // 3) + 3 * quad + columns % 3
    return ((rows == head) & (columns < OWN_HEADS)).astype(jnp.float32)


def fore_kernel(
    tok, cot, seq_lens, in_w, out_w, conv_w, gains, head_params,
    o_normed, o_cot, o_gate_w, o_x_w, o_com, o_out, o_gate, o_proj, o_proj_com, o_act, o_mixed, o_gno,
    stats, gain_in, gain_out, conv, heads, skip, select, lens,
    wx_send, wg_send, wc_send, wo_send, all_tok, all_cot, normed, all_wx, all_wg, all_wc, w_com, line_wo, w_out,
    proj, gate, proj_com, act, mixed, gno, part, shared,
    send, recv, local
):
    plane, quad, core = place()
    where = (plane, quad, core)
    rank = 2 * quad + core
    sibling = at(plane, quad, flip(core))
    sems = Sems(send, recv)
    f32 = jnp.float32
    half = BLOCK // 2
    kept = []

    def keep(source, target):
        copy = pltpu.make_async_copy(source, target, local.at[len(kept)])
        kept.append(copy)
        copy.start()
        return copy

    def pieces(buffer):
        return lambda r, slot, h: buffer.at[slot, core, pl.ds(h * half, half)]

    def halves(buffer):
        return lambda h: buffer.at[pl.ds(h * half, half)]

    push_c = [
        sems.copy(wc_send, all_wc.at[plane, rank], at(xor4(plane, k), quad, core)) for k in (2, 3, 1)
    ]
    line_o = LineGather(sems, wo_send, lambda q: line_wo.at[q], *where)
    line_x = LineGather(sems, all_wx.at[plane], lambda q: all_wx.at[q], *where)
    line_g = LineGather(sems, all_wg.at[plane], lambda q: all_wg.at[q], *where)
    shuffles = []
    for source, target in ((wx_send, all_wx), (wg_send, all_wg)):
        copies = []
        for k in range(1, RANKS):
            other_core = flip(core) if k % 2 else core
            other_quad = xor4(quad, k // 2)
            copies.append(
                sems.copy(
                    source.at[2 * other_quad + other_core], target.at[plane, rank], at(plane, other_quad, other_core)
                )
            )
        shuffles.append(copies)
    tokens = PlaneGather(sems, halves(tok), pieces(all_tok), *where)
    grads = PlaneGather(sems, halves(cot), pieces(all_cot), *where)
    common = PlaneGather(
        sems,
        lambda h: all_wc.at[pl.ds(2 * h, 2), rank],
        lambda r, slot, h: all_wc.at[pl.ds(2 * h, 2), r],
        *where,
    )
    cross_o = [
        sems.copy(line_wo.at[2 * flip(core) + k], w_out.at[k, core], sibling) for k in range(2)
    ]
    mates = plane_mates(*where)
    swap = [sems.copy(part, shared.at[rank], device) for device in mates]

    greet(mates + plane_others(*where))
    fill_common(in_w, conv_w, gains, seq_lens, wc_send)
    for copy in push_c:
        copy.start()
    fill_sends(in_w, 1, wx_send)
    for copy in shuffles[0]:
        copy.start()
    wo_send[...] = low16(out_w[...])
    line_o.start(0)
    fill_sends(in_w, 0, wg_send)
    for copy in shuffles[1]:
        copy.start()
    own_wx = keep(wx_send.at[rank], all_wx.at[plane, rank])
    own_wg = keep(wg_send.at[rank], all_wg.at[plane, rank])
    own_wc = keep(wc_send, all_wc.at[plane, rank])
    own_tok = keep(tok, all_tok.at[0, core])
    own_cot = keep(cot, all_cot.at[0, core])
    own_wo = keep(wo_send, line_wo.at[plane])
    own_wc.wait()
    for copy in push_c:
        copy.wait_recv()
    common.start()
    own_wx.wait()
    for copy in shuffles[0]:
        copy.wait_recv()
    line_x.start(0)
    tokens.start()
    select[...] = select_heads(quad, core)
    wide = jnp.concatenate([head_params[...], jnp.zeros((3, LANES - HEADS), f32)], axis=1)
    wide = jnp.concatenate([wide, jnp.ones((1, LANES), f32), jnp.zeros((4, LANES), f32)], axis=0)
    heads[...] = mm_full(wide * (iota((8, LANES), 1) < HEADS).astype(f32), select[...])
    skip[...] = mm_full(heads[2:3], head_spread())

    common.near()
    common.across()
    for slot in range(QUADS):
        common.wait_slot(slot)
    line_x.arrive(0)
    line_x.start(1)
    for q in range(PLANES):
        for r in range(RANKS):
            start = (RANKS * q + r) * ROWS_IN
            w_com[start : start + ROWS_IN] = all_wc[q, r, :ROWS_IN]
    keep(w_com, o_com)
    extras = [all_wc[q, r, ROWS_IN:].astype(f32) for q in range(PLANES) for r in range(RANKS)]
    gain_tiles = place_lanes(
        [(e[5:6, :LANES], LANES, SHARD_GAIN * d) for d, e in enumerate(extras)]
        + [(e[5:6, LANES : 2 * LANES], SHARD_GAIN - LANES, SHARD_GAIN * d + LANES) for d, e in enumerate(extras)],
        (D + DIN) // LANES,
        1,
    )
    gain_in[...] = jnp.concatenate(gain_tiles[: D // LANES], axis=1)
    gain_out[...] = own_lanes(gain_tiles[D // LANES :], quad, core)
    conv_tiles = place_lanes(
        [(e[:8, :LANES], SHARD_CONV, SHARD_CONV * d) for d, e in enumerate(extras)], CONVC // LANES, 8
    )
    conv[...] = jnp.concatenate(
        [own_lanes(conv_tiles[: DIN // LANES], quad, core)] + conv_tiles[DIN // LANES :], axis=1
    )
    seats = []
    for slot in range(QUADS):
        chosen = jnp.zeros((1, LANES), f32)
        for q in range(PLANES):
            for p in range(QUADS):
                here = (plane == q) & (quad_of(slot) == p)
                chosen = jnp.where(here, extras[RANKS * q + 2 * p][6:7, :LANES], chosen)
        seats.append(chosen + BLOCK)
    lens[...] = jnp.concatenate(seats + [jnp.zeros((8 - QUADS, LANES), f32)], axis=0)

    def norm(slot):
        for side in range(2):
            rows = all_tok[slot, side].astype(f32)
            scaling = lax.rsqrt(jnp.mean(rows * rows, axis=1, keepdims=True) + norm_eps)
            normed[slot, pl.ds(side * BLOCK, BLOCK)] = low16(rows * scaling * gain_in[...])

    own_tok.wait()
    tokens.wait_slot(0)
    norm(0)
    line_x.arrive(1)
    line_x.start(2)
    own_wg.wait()
    for copy in shuffles[1]:
        copy.wait_recv()
    line_g.start(0)
    tokens.near()
    grads.start()
    line_x.arrive(2)
    keep(all_wx, o_x_w)

    @pl.loop(0, QUADS)
    def each(slot):
        @pl.when(slot == 1)
        def first():
            tokens.wait_slot(1)
            norm(1)
            line_g.arrive(0)
            line_g.start(1)

        @pl.when(slot == 2)
        def second():
            tokens.wait_slot(2)
            norm(2)
            tokens.across()
            line_g.arrive(1)
            line_g.start(2)

        @pl.when(slot == 3)
        def third():
            tokens.wait_slot(3)
            norm(3)
            line_o.arrive(0)
            line_o.start(1)

        proj[slot] = mm(normed[slot], all_wx[...].reshape(D, OWN))
        proj_com[slot] = mm(normed[slot], w_com[...])
        conv_in = jnp.concatenate([proj[slot], proj_com[slot, :, : 2 * NST]], axis=1)
        raw = mm_full(proj_com[slot, :, 2 * NST :], select[...])
        preact = preact_of(conv_in, conv[...])
        act[slot] = low16(preact * sigmoid(preact))
        step, logdec = steps_of(raw, heads[...], live_of(lens[...], slot))
        ssd_forward(act.at[slot], step, logdec, skip[...], mixed.at[slot])

    for slot in range(QUADS):
        keep(normed.at[slot], o_normed.at[pl.ds(slot * GROUP, GROUP)])
    for source, target in ((proj, o_proj), (proj_com, o_proj_com), (act, o_act), (mixed, o_mixed)):
        keep(source, target)
    line_g.arrive(2)
    line_o.arrive(1)
    line_o.start(2)
    keep(all_wg, o_gate_w)
    grads.near()

    @pl.loop(0, QUADS)
    def gates(slot):
        gate[slot] = mm(normed[slot], all_wg[...].reshape(D, OWN))

    keep(gate, o_gate)
    line_o.arrive(2)
    own_wo.wait()
    for copy in cross_o:
        copy.start()
    for k in range(2):
        w_out[k, core] = line_wo[2 * core + k]
    own_cot.wait()
    for copy in cross_o:
        copy.wait_recv()
    keep(w_out, o_out)
    part[...] = jnp.zeros_like(part)

    @pl.loop(0, QUADS)
    def measure(slot):
        for k in range(QUADS):

            @pl.when(slot == k)
            def here():
                if k == 1:
                    grads.across()
                grads.wait_slot(k)

        live = live_of(lens[...], slot)
        grad = all_cot[slot].reshape(GROUP, D)
        grad = jnp.where(live > 0.0, grad, jnp.zeros_like(grad))
        gno_v = mm_t(grad, w_out[...].reshape(OWN, D))
        gno[slot] = gno_v
        gate_part = gate[slot]
        gated = mixed[slot] * gate_part * sigmoid(gate_part)
        squares = jnp.sum(gated * gated, axis=1, keepdims=True)
        inner = jnp.sum(gno_v * gain_out[...] * gated, axis=1, keepdims=True)
        lanes = iota((GROUP, LANES), 1)
        seat = quad_of(slot)
        columns = jnp.where(lanes == 2 * seat, squares, 0.0) + jnp.where(lanes == 2 * seat + 1, inner, 0.0)
        part[...] += jnp.transpose(columns)[:8]

    for copy in swap:
        copy.start()
    keep(all_cot, o_cot)
    keep(gno, o_gno)
    shared[rank] = part[...]
    for copy in swap:
        copy.wait_recv()
    stats[...] = jnp.sum(shared[...], axis=0)
    for copy in shuffles[0] + shuffles[1] + push_c + cross_o + swap:
        copy.wait_send()
    for line in (line_o, line_x, line_g):
        line.sent()
    for gather in (tokens, grads, common):
        gather.sent()
    for copy in kept:
        if not any(copy is done for done in (own_wx, own_wg, own_wc, own_tok, own_cot, own_wo)):
            copy.wait()


def run_fore(tok, cot, seq_lens, in_w, out_w, conv_w, gains, head_params):
    f32, bf16 = (jnp.float32, jnp.bfloat16)
    whole = pl.BlockSpec(memory_space=pltpu.VMEM)
    outs = (
        ((QUADS * GROUP, D), bf16), ((QUADS, 2, BLOCK, D), bf16), ((PLANES, RANKS, ROWS_IN, OWN), bf16),
        ((PLANES, RANKS, ROWS_IN, OWN), bf16), ((D, COMMON_PAD), bf16), ((2, 2, ROWS_OUT, D), bf16),
        ((QUADS, GROUP, OWN), f32), ((QUADS, GROUP, OWN), f32), ((QUADS, GROUP, COMMON_PAD), f32), ((QUADS, GROUP, MIX), bf16),
        ((QUADS, GROUP, OWN), f32), ((QUADS, GROUP, OWN), f32),
    )
    small = (
        (8, GROUP), (1, D), (1, OWN), (8, MIX), (8, LANES), (1, OWN), (LANES, LANES), (8, LANES),
    )
    scratch = (
        ((RANKS, ROWS_IN, OWN), bf16), ((RANKS, ROWS_IN, OWN), bf16), ((ROWS_ALL, COMMON_PAD), bf16), ((ROWS_OUT, D), bf16),
        ((QUADS, 2, BLOCK, D), bf16), ((QUADS, 2, BLOCK, D), bf16), ((QUADS, GROUP, D), bf16),
        ((PLANES, RANKS, ROWS_IN, OWN), bf16), ((PLANES, RANKS, ROWS_IN, OWN), bf16),
        ((PLANES, RANKS, ROWS_ALL, COMMON_PAD), bf16),
        ((D, COMMON_PAD), bf16), ((PLANES, ROWS_OUT, D), bf16), ((2, 2, ROWS_OUT, D), bf16),
        ((QUADS, GROUP, OWN), f32), ((QUADS, GROUP, OWN), f32), ((QUADS, GROUP, COMMON_PAD), f32),
        ((QUADS, GROUP, MIX), bf16), ((QUADS, GROUP, OWN), f32), ((QUADS, GROUP, OWN), f32), ((8, GROUP), f32),
        ((RANKS, 8, GROUP), f32),
    )
    args = (tok, cot, seq_lens, in_w, out_w, conv_w, gains.reshape(1, -1), head_params)
    results = pl.pallas_call(
        fore_kernel,
        in_specs=[ANY, ANY] + [whole] * 6,
        out_specs=[ANY] * len(outs) + [whole] * len(small),
        out_shape=[jax.ShapeDtypeStruct(s, kind) for s, kind in outs]
        + [jax.ShapeDtypeStruct(s, f32) for s in small],
        scratch_shapes=[pltpu.VMEM(s, kind) for s, kind in scratch]
        + [
            pltpu.SemaphoreType.DMA((96,)),
            pltpu.SemaphoreType.DMA((96,)),
            pltpu.SemaphoreType.DMA((24,)),
        ],
        compiler_params=pltpu.CompilerParams(
            vmem_limit_bytes=VMEM_GRANT, collective_id=0, has_side_effects=True
        ),
    )(*args)
    rows = QUADS * GROUP
    widths = (D, D, None, None, None, None, OWN, OWN, COMMON_PAD, MIX, OWN, OWN)
    flat = [a if w is None else a.reshape(rows, w) for a, w in zip(results, widths)]
    flat[2], flat[3] = (flat[2].reshape(D, OWN), flat[3].reshape(D, OWN))
    flat[5] = flat[5].reshape(OWN, D)
    return flat + list(results[len(outs) :])


def gate_kernel(
    lens, stats, cot, normed, gate_part, mixed, grad_normed_out, w_out, gain_out,
    branch, dgate, dmix, g_out, g_gate, g_gain, acc_out, acc_gate
):
    g = pl.program_id(0)
    live = live_of(lens[...], g)

    @pl.when(g == 0)
    def first():
        acc_out[...] = jnp.zeros_like(acc_out)
        acc_gate[...] = jnp.zeros_like(acc_gate)
        g_gain[...] = jnp.zeros_like(g_gain)

    columns = jnp.transpose(jnp.concatenate([stats[...], jnp.zeros((LANES - 8, GROUP), jnp.float32)], axis=0))
    lanes = iota((GROUP, LANES), 1)
    seat = quad_of(g)
    power = jnp.sum(jnp.where(lanes == 2 * seat, columns, 0.0), axis=1, keepdims=True)
    along = jnp.sum(jnp.where(lanes == 2 * seat + 1, columns, 0.0), axis=1, keepdims=True)
    scale_out = lax.rsqrt(power * (1.0 / DIN) + norm_eps)
    gate_v, mixed_v, gno = (gate_part[...], mixed[...], grad_normed_out[...])
    sig = sigmoid(gate_v)
    gate_act = gate_v * sig
    gated = mixed_v * gate_act
    normed_out = low16(gated * scale_out * gain_out[...])
    for half in range(2):
        rows = slice(half * BLOCK, (half + 1) * BLOCK)
        branch[0, half] = low16(mm(normed_out[rows], w_out[...]))
    grad = jnp.where(live > 0.0, cot[...], jnp.zeros_like(cot[...]))
    acc_out[...] += t_mm(normed_out, grad)
    scaled = gno * scale_out
    grad_gated = scaled * gain_out[...] - gated * (scale_out * scale_out * scale_out * along * (1.0 / DIN))
    gain_sum = jnp.sum(scaled * gated, axis=0, keepdims=True)
    g_gain[...] += jnp.concatenate([gain_sum, jnp.zeros((7, OWN), jnp.float32)], axis=0)
    grad_gate = low16(grad_gated * mixed_v * (sig * (1.0 + gate_v * (1.0 - sig))))
    dgate[...] = grad_gate
    dmix[...] = low16(grad_gated * gate_act)
    acc_gate[...] += t_mm(normed[...], grad_gate)

    @pl.when(g == QUADS - 1)
    def last():
        g_out[...] = low16(acc_out[...])
        g_gate[...] = low16(acc_gate[...])


def run_gate(lens, stats, cot, normed, gate_part, mixed, grad_normed_out, w_out, gain_out):
    f32, bf16 = (jnp.float32, jnp.bfloat16)
    rows = QUADS * GROUP
    grouped = (cot, normed, gate_part, mixed, grad_normed_out)
    ends = (((OWN, D), bf16), ((D, OWN), bf16), ((8, OWN), f32))
    return pl.pallas_call(
        gate_kernel,
        grid=(QUADS,),
        in_specs=[full_spec(a.shape) for a in (lens, stats)]
        + [group_spec(a.shape[1]) for a in grouped]
        + [full_spec(w_out.shape), full_spec(gain_out.shape)],
        out_specs=[pl.BlockSpec((1, 2, BLOCK, D), lambda g: (g, 0, 0, 0)), group_spec(OWN), group_spec(OWN)]
        + [full_spec(s) for s, kind in ends],
        out_shape=[
            jax.ShapeDtypeStruct((QUADS, 2, BLOCK, D), bf16),
            jax.ShapeDtypeStruct((rows, OWN), bf16),
            jax.ShapeDtypeStruct((rows, OWN), bf16),
        ]
        + [jax.ShapeDtypeStruct(s, kind) for s, kind in ends],
        scratch_shapes=[pltpu.VMEM((OWN, D), f32), pltpu.VMEM((D, OWN), f32)],
        compiler_params=pltpu.CompilerParams(vmem_limit_bytes=VMEM_GRANT),
    )(lens, stats, *grouped, w_out, gain_out)


def backward_group(live, dmix, conv_in, raw, act, conv, heads, skip, between):
    raw_v = raw[...]
    heads_v = heads[...]
    step, logdec = steps_of(raw_v, heads_v, live)
    spread, gather = (head_spread(), head_gather())
    rows0 = slice(0, BLOCK)
    cumul0 = mm_full(lower_mask().astype(jnp.float32), logdec[rows0])
    cumul0_w = mm_full(cumul0, spread)
    weighting = jnp.exp(cumul0_w[BLOCK - 1 :] - cumul0_w) * mm_full(step[rows0], spread)
    state = low16(
        t_mm(act[rows0, OWN : OWN + NST], low16(weighting * act[rows0, :OWN].astype(jnp.float32)))
    )
    late = backward_block(1, act, dmix, step, logdec, skip[...], state, None, spread, gather)
    between()
    early = backward_block(0, act, dmix, step, logdec, skip[...], None, late[6], spread, gather)
    grad_act = jnp.concatenate([jnp.concatenate(part[:3], axis=1) for part in (early, late)], axis=0)
    grad_step = jnp.concatenate([early[3], late[3]], axis=0)
    grad_logdec = jnp.concatenate([early[4], late[4]], axis=0)
    rate = jnp.exp(heads_v[1:2])
    grad_raw = (grad_step - rate * grad_logdec) * live * heads_v[3:4] * sigmoid(raw_v + heads_v[0:1])
    u = conv_in[...]
    conv_v = conv[...]
    preact = preact_of(u, conv_v)
    sig_q = sigmoid(preact)
    grad_pre = grad_act * (sig_q * (1.0 + preact * (1.0 - sig_q)))
    grad_u = grad_pre * conv_v[KCONV - 1 : KCONV]
    taps = []
    for tap in range(KCONV):
        lag = KCONV - 1 - tap
        if lag:
            grad_u = grad_u + shift_up(grad_pre, lag) * conv_v[tap : tap + 1]
        taps.append(jnp.sum(grad_pre * shift_down(u, lag), axis=0, keepdims=True))
    taps.append(jnp.sum(grad_pre, axis=0, keepdims=True))
    small = (
        jnp.concatenate(taps + [jnp.zeros((3, MIX), jnp.float32)], axis=0),
        jnp.sum(grad_raw, axis=0, keepdims=True),
        jnp.sum(grad_logdec * logdec, axis=0, keepdims=True),
        early[5] + late[5],
    )
    return (grad_u, grad_raw, small)


PACK = 48


def back_kernel(
    lens, gate_grads, out_grads, branch_all, w_gate, w_x, w_com, conv, heads, skip, select, gain_in, g_gain,
    tok_own, normed, dgate, dmix, proj_x, proj_com, act,
    r_out, all_gate, all_x, sum_com, packs, sum_branch, grad_rows,
    acc_x, acc_com, small_conv, small_head, small_skip,
    branch_own, branch_sib, en_part, en_sib, branch_got, en_got, branch_relay, en_relay,
    gate_got, gate_own, sum_gate, x_send, x_got, x_passed, sum_x, com_send, com_sib, com_quad, com_z, com_got,
    pack_send, pack_got, pack_sum,
    sends, recvs, out_send, out_recv, local
):
    s = pl.program_id(0)
    slot = QUADS - 1 - s
    plane, quad, core = place()
    where = (plane, quad, core)
    rank = 2 * quad + core
    sibling = at(plane, quad, flip(core))
    f32 = jnp.float32
    sems = Sems(sends, recvs)
    to_x, to_y = (at(plane, xor4(quad, 1), core), at(plane, xor4(quad, 2), core))
    half = BLOCK // 2

    swaps = [
        [sems.copy(branch_all.at[k, flip(core)], branch_sib.at[k], sibling) for k in range(QUADS)],
        [sems.copy(en_part.at[k % 2, flip(core)], en_sib.at[k], sibling) for k in range(QUADS)],
    ]
    routes = []
    for sib, got, relay in ((branch_sib, branch_got, branch_relay), (en_sib, en_got, en_relay)):
        routes.append(
            {
                "relay_x": sems.copy(sib.at[3, pl.ds(0, half)], relay.at[0], to_x),
                "relay_y": sems.copy(sib.at[3, pl.ds(half, half)], relay.at[1], to_y),
                "x": sems.copy(sib.at[1], got.at[0], to_x),
                "y": sems.copy(sib.at[2], got.at[1], to_y),
            }
        )

    def z_push(source, target):
        return [
            sems.copy(source.at[xor4(plane, k)], target.at[k - 1], at(xor4(plane, k), quad, core))
            for k in (2, 3, 1)
        ]

    def rank_push(source, target):
        copies = []
        for k in range(1, RANKS):
            other_core = flip(core) if k % 2 else core
            other_quad = xor4(quad, k // 2)
            copies.append(
                sems.copy(source(2 * other_quad + other_core), target.at[rank], at(plane, other_quad, other_core))
            )
        return copies

    gate_z = z_push(gate_grads, gate_got)
    x_z = z_push(x_send, x_got)
    x_relay = sems.copy(x_send.at[xor4(plane, 3)], x_passed, at(xor4(plane, 1), quad, core))
    at_end = plane % (PLANES - 1) == 0
    part_rows = D // PLANES
    gate_ranks = rank_push(lambda r: sum_gate.at[r], all_gate)
    x_ranks = rank_push(lambda r: sum_x.at[r], all_x)
    com_swap = sems.copy(com_send.at[:, :, flip(core)], com_sib, sibling)
    com_quads = [
        sems.copy(com_sib.at[:, xor4(quad, k)], com_quad.at[k - 1], at(plane, xor4(quad, k), core))
        for k in (3, 1, 2)
    ]
    com_planes = z_push(com_z, com_got)
    pack_z = [
        sems.copy(pack_send, pack_got.at[k - 1], at(xor4(plane, k), quad, core)) for k in (2, 3, 1)
    ]
    pack_ranks = rank_push(lambda r: pack_sum, packs)

    def out_copy(near, side):
        return pltpu.make_async_remote_copy(
            src_ref=out_grads.at[near, side],
            dst_ref=r_out.at[plane],
            send_sem=out_send.at[2 * near + side],
            recv_sem=out_recv.at[plane],
            device_id=at(2 * core + near, quad, side),
            device_id_type=MESH_ID,
        )

    def out_landing(origin):
        return pltpu.make_async_remote_copy(
            src_ref=out_grads.at[0, 0],
            dst_ref=r_out.at[origin],
            send_sem=out_send.at[0],
            recv_sem=out_recv.at[origin],
            device_id=sibling,
            device_id_type=MESH_ID,
        )

    out_here = pltpu.make_async_copy(out_grads.at[plane % 2, core], r_out.at[plane], local.at[0])
    out_stays = plane // 2 == core
    gate_here = pltpu.make_async_copy(gate_grads.at[plane], gate_own, local.at[1])
    branch_here = [
        pltpu.make_async_copy(branch_all.at[k, core], branch_own.at[k], local.at[5 + k]) for k in range(QUADS)
    ]

    @pl.when(s == 0)
    def begin():
        peers = plane_mates(*where) + plane_others(*where)
        peers += [at(xor4(plane, k), quad, flip(core)) for k in range(1, PLANES)]
        greet(peers)
        for copy in gate_z:
            copy.start()
        for copy in swaps[0][::-1]:
            copy.start()
        for near in range(2):
            for side in range(2):

                @pl.when(jnp.logical_not((2 * core + near == plane) & (core == side)))
                def go():
                    out_copy(near, side).start()

        @pl.when(out_stays)
        def stay():
            out_here.start()

        for copy in branch_here[::-1]:
            copy.start()
        gate_here.start()
        for ref in (acc_x, acc_com, small_conv, small_head, small_skip):
            ref[...] = jnp.zeros_like(ref)

    def settle(kind, k, own, sib):
        route = routes[kind]
        relay = (branch_relay, en_relay)[kind]
        swaps[kind][k].wait_recv()
        sib[k] = low16(own.astype(f32) + sib[k].astype(f32))
        if k == 3:
            route["relay_x"].start()
            route["relay_y"].start()
        if k == 2:
            route["relay_x"].wait_recv()
            sib[k, :half] = low16(sib[k, :half].astype(f32) + relay[0].astype(f32))
            route["y"].start()
        if k == 1:
            route["relay_y"].wait_recv()
            sib[k, half:] = low16(sib[k, half:].astype(f32) + relay[1].astype(f32))
            route["x"].start()

    def settle_branch(k):
        branch_here[k].wait()
        settle(0, k, branch_own[k], branch_sib)

    def between():
        for k in range(QUADS):

            @pl.when(slot == k)
            def sums():
                if k < QUADS - 1:
                    settle(1, k + 1, en_part[(k + 1) % 2, core], en_sib)
                if k == 3:
                    settle_branch(3)
                if k == 2:
                    settle_branch(1)

    live = live_of(lens[...], slot)
    conv_in = jnp.concatenate([proj_x[...], proj_com[:, : 2 * NST]], axis=1)
    raw = mm_full(proj_com[:, 2 * NST :], select[...])
    grad_u, grad_raw, small = backward_group(
        live, dmix, conv_in, raw, act, conv, heads, skip, between
    )
    small_conv[...] += small[0]
    small_head[0:1] += small[1]
    small_head[1:2] += small[2]
    small_skip[0:1] += small[3]
    raw_wide = mm_t(low16(grad_raw), low16(select[...]))
    grad_x = low16(grad_u[:, :OWN])
    grad_com = low16(jnp.concatenate([grad_u[:, OWN:], raw_wide], axis=1))
    normed_v = normed[...]
    acc_x[...] += t_mm(normed_v, grad_x)

    @pl.when(s == QUADS - 1)
    def send_x():
        x_send[...] = low16(acc_x[...]).reshape(x_send.shape)

        @pl.when(at_end)
        def from_end():
            x_relay.start()

        @pl.when(jnp.logical_not(at_end))
        def from_middle():
            x_z[1].start()
            x_z[2].start()

    acc_com[...] += t_mm(normed_v, grad_com)

    @pl.when(s == QUADS - 1)
    def send_com():
        com_send[...] = low16(acc_com[...]).reshape(com_send.shape)
        com_swap.start()

    for k in range(2):

        @pl.when(slot == k)
        def free():
            swaps[1][k + 2].wait_send()

    for side in range(2):
        rows = slice(side * BLOCK, (side + 1) * BLOCK)
        en_part[slot % 2, side] = low16(
            mm_t(dgate[rows], w_gate[...]) + mm_t(grad_x[rows], w_x[...]) + mm_t(grad_com[rows], w_com[...])
        )
    for k in range(QUADS):

        @pl.when(slot == k)
        def swap_en():
            swaps[1][k].start()

    for k, done in ((3, 2), (2, 0)):

        @pl.when(slot == k)
        def settle_late():
            settle_branch(done)

    @pl.when(s == QUADS - 1)
    def tail():
        @pl.when(at_end)
        def rest_from_end():
            x_relay.wait_send()
            x_z[0].start()
            x_z[2].start()

        @pl.when(jnp.logical_not(at_end))
        def pass_on():
            x_relay.wait_recv()
            far = xor4(plane, 2)
            x_send[far] = low16(x_send[far].astype(f32) + x_passed[...].astype(f32))
            x_z[0].start()

        settle(1, 0, en_part[0, core], en_sib)
        gate_here.wait()
        for copy in gate_z:
            copy.wait_recv()
        sum_gate[...] = low16(
            gate_own[...].astype(f32) + gate_got[0].astype(f32) + gate_got[1].astype(f32) + gate_got[2].astype(f32)
        )
        for copy in gate_ranks:
            copy.start()
        gate_keep = pltpu.make_async_copy(sum_gate.at[rank], all_gate.at[rank], local.at[2])
        gate_keep.start()
        com_swap.wait_recv()
        com_sib[...] = low16(com_sib[...].astype(f32) + com_send[:, :, core].astype(f32))
        for copy in com_quads:
            copy.start()
        for name in ("x", "y"):
            routes[0][name].wait_recv()
        sum_branch[...] = (
            branch_sib[0].astype(f32) + branch_got[0].astype(f32) + branch_got[1].astype(f32)
        )
        for copy in com_quads:
            copy.wait_recv()
        com_z[...] = low16(
            com_sib[:, quad].astype(f32)
            + com_quad[0].astype(f32) + com_quad[1].astype(f32) + com_quad[2].astype(f32)
        )
        for copy in com_planes:
            copy.start()
        for name in ("x", "y"):
            routes[1][name].wait_recv()
        en = en_sib[0].astype(f32) + en_got[0].astype(f32) + en_got[1].astype(f32)
        rows = tok_own[...].astype(f32)
        scaling = lax.rsqrt(jnp.mean(rows * rows, axis=1, keepdims=True) + norm_eps)
        scaled = rows * scaling
        gain_grad = jnp.sum(en * scaled, axis=0, keepdims=True)
        weighted = en * gain_in[...]
        inner = jnp.mean(weighted * scaled, axis=1, keepdims=True)
        grad_rows[...] = scaling * (weighted - scaled * inner)
        pack_send[...] = jnp.zeros_like(pack_send)
        for i in range(D // LANES):
            pack_send[i : i + 1] = gain_grad[:, i * LANES : (i + 1) * LANES]
        gain_out_grad = g_gain[0:1]
        skip_grad = small_skip[0:1]
        for i in range(PAIRS):
            lanes = slice(i * LANES, (i + 1) * LANES)
            pack_send[12 + i : 13 + i] = gain_out_grad[:, lanes]
            pack_send[42 + i : 43 + i] = skip_grad[:, lanes]
            for tap in range(KCONV + 1):
                pack_send[15 + 3 * tap + i : 16 + 3 * tap + i] = small_conv[tap : tap + 1, lanes]
        for tap in range(KCONV + 1):
            for i in range(2):
                lanes = slice(OWN + i * LANES, OWN + (i + 1) * LANES)
                pack_send[30 + 2 * tap + i : 31 + 2 * tap + i] = small_conv[tap : tap + 1, lanes]
        pack_send[40:42] = small_head[0:2]
        for copy in pack_z:
            copy.start()
        for copy in com_planes:
            copy.wait_recv()
        sum_com[...] = (
            com_z[plane].astype(f32)
            + com_got[0].astype(f32) + com_got[1].astype(f32) + com_got[2].astype(f32)
        )
        for copy in pack_z:
            copy.wait_recv()
        pack_sum[...] = pack_send[...] + pack_got[0] + pack_got[1] + pack_got[2]
        for copy in pack_ranks:
            copy.start()
        pack_keep = pltpu.make_async_copy(pack_sum, packs.at[rank], local.at[3])
        pack_keep.start()
        x_z[0].wait_recv()
        x_z[2].wait_recv()
        acc_x[:part_rows] = (
            x_send[plane].astype(f32) + x_got[0].astype(f32) + x_got[1].astype(f32)
        ).reshape(part_rows, OWN)

        @pl.when(jnp.logical_not(at_end))
        def one_more():
            x_z[1].wait_recv()
            acc_x[:part_rows] += x_got[2].astype(f32).reshape(part_rows, OWN)

        sum_x[...] = low16(acc_x[:part_rows]).reshape(sum_x.shape)
        for copy in x_ranks:
            copy.start()
        x_keep = pltpu.make_async_copy(sum_x.at[rank], all_x.at[rank], local.at[4])
        x_keep.start()
        for origin in range(PLANES):

            @pl.when(jnp.logical_not((plane == origin) & out_stays))
            def arrived():
                out_landing(origin).wait_recv()

        @pl.when(out_stays)
        def kept():
            out_here.wait()

        for near in range(2):
            for side in range(2):

                @pl.when(jnp.logical_not((2 * core + near == plane) & (core == side)))
                def gone():
                    out_copy(near, side).wait_send()

        for copy in gate_ranks + pack_ranks + x_ranks:
            copy.wait_recv()
        @pl.when(jnp.logical_not(at_end))
        def middle_sent():
            x_z[1].wait_send()

        for copy in gate_z + [x_z[0], x_z[2]] + gate_ranks + x_ranks + [com_swap] + com_quads + com_planes + pack_z + pack_ranks:
            copy.wait_send()
        for copy in swaps[0] + swaps[1][:2] + list(routes[0].values()) + list(routes[1].values()):
            copy.wait_send()
        gate_keep.wait()
        pack_keep.wait()
        x_keep.wait()


def run_back(lens, gate_grads, out_grads, branch, w_gate, w_x, w_com, conv, heads, skip, select, gain_in, g_gain, tok_own,
             normed, dgate, dmix, proj_x, proj_com, act):
    f32, bf16 = (jnp.float32, jnp.bfloat16)
    rows_in = D // (PLANES * RANKS)
    rows_out = DIN // (PLANES * RANKS)
    gate_grads = gate_grads.reshape(PLANES, RANKS, rows_in, OWN)
    out_grads = out_grads.reshape(2, 2, rows_out, D)
    fixed = (w_gate, w_x, w_com, conv, heads, skip, select, gain_in, g_gain, tok_own)
    grouped = (normed, dgate, dmix, proj_x, proj_com, act)

    def turned(width):
        return pl.BlockSpec((GROUP, width), lambda s: (QUADS - 1 - s, 0))

    outs = (
        ((PLANES, rows_out, D), bf16, ANY),
        ((RANKS, rows_in, OWN), bf16, ANY),
        ((RANKS, rows_in, OWN), bf16, ANY),
        ((rows_in, COMMON_PAD), f32, None),
        ((RANKS, PACK, LANES), f32, ANY),
        ((BLOCK, D), f32, None),
        ((BLOCK, D), f32, None),
    )
    half = BLOCK // 2
    quarter = (RANKS, rows_in, OWN)
    com = (rows_in, COMMON_PAD)
    scratch = [
        ((D, OWN), f32), ((D, COMMON_PAD), f32), ((8, MIX), f32), ((8, LANES), f32), ((8, OWN), f32),
        ((QUADS, BLOCK, D), bf16),
        ((QUADS, BLOCK, D), bf16), ((2, 2, BLOCK, D), bf16), ((QUADS, BLOCK, D), bf16),
        ((2, BLOCK, D), bf16), ((2, BLOCK, D), bf16), ((2, half, D), bf16), ((2, half, D), bf16),
        ((PLANES - 1,) + quarter, bf16), (quarter, bf16), (quarter, bf16),
        ((PLANES,) + quarter, bf16), ((PLANES - 1,) + quarter, bf16), (quarter, bf16), (quarter, bf16),
        ((PLANES, QUADS, 2) + com, bf16), ((PLANES, QUADS) + com, bf16), ((QUADS - 1, PLANES) + com, bf16),
        ((PLANES,) + com, bf16), ((PLANES - 1,) + com, bf16),
        ((PACK, LANES), f32), ((PLANES - 1, PACK, LANES), f32), ((PACK, LANES), f32),
    ]
    return pl.pallas_call(
        back_kernel,
        grid=(QUADS,),
        in_specs=[full_spec(lens.shape), ANY, ANY, ANY]
        + [full_spec(a.shape) for a in fixed]
        + [turned(a.shape[1]) for a in grouped],
        out_specs=[full_spec(s) if spec is None else spec for s, kind, spec in outs],
        out_shape=[jax.ShapeDtypeStruct(s, kind) for s, kind, spec in outs],
        scratch_shapes=[pltpu.VMEM(s, kind) for s, kind in scratch]
        + [
            pltpu.SemaphoreType.DMA((64,)),
            pltpu.SemaphoreType.DMA((64,)),
            pltpu.SemaphoreType.DMA((4,)),
            pltpu.SemaphoreType.DMA((4,)),
            pltpu.SemaphoreType.DMA((9,)),
        ],
        compiler_params=pltpu.CompilerParams(
            vmem_limit_bytes=VMEM_GRANT, collective_id=2, has_side_effects=True
        ),
    )(lens, gate_grads, out_grads, branch, *fixed, *grouped)


def adam_refs(refs, index, gradient, rate):
    weight, first, second, weight_new, first_new, second_new = refs
    results = adam_update(weight[index], first[index], second[index], gradient, rate)
    for ref, value in zip((weight_new, first_new, second_new), results):
        ref[index] = value


def finish_kernel(
    lens, tok, cot, sum_branch, grad_rows, r_out, all_gate, all_x, sum_com,
    in_w, in_m, in_v, out_w, out_m, out_v,
    mixed_out, grad_input, in_wn, in_mn, in_vn, out_wn, out_mn, out_vn
):
    f32 = jnp.float32
    core = lax.axis_index("seq")
    position = (iota((BLOCK, 1), 0) + core * BLOCK).astype(f32)
    live = (position < lens[0:1, 0:1]).astype(f32)
    mixed_out[...] = (tok[...].astype(f32) + live * sum_branch[...]).astype(jnp.bfloat16)
    grad_input[...] = cot[...].astype(f32) + grad_rows[...]
    ins = (in_w, in_m, in_v, in_wn, in_mn, in_vn)
    rows = in_w.shape[0]
    lanes = iota((rows, LANES), 1)
    for part, source in ((0, all_gate), (1, all_x)):
        for run in range(PLANES):
            side, near = divmod(run, 2)
            tiles = []
            for t in range(2 * PAIRS):
                halves = []
                for b in range(2):
                    p, i = divmod(2 * t + b, 3)
                    index = 3 * near + i
                    tile = source[2 * p + side, :, (index // 2) * LANES : (index // 2 + 1) * LANES].astype(f32)
                    halves.append(tile if index % 2 == b else pltpu.roll(tile, HDIM, 1))
                tiles.append(jnp.where(lanes < HDIM, halves[0], halves[1]))
            start = part * DIN + run * 2 * OWN
            adam_refs(ins, (slice(None), slice(start, start + 2 * OWN)), jnp.concatenate(tiles, axis=1), rate_in)
    adam_refs(ins, (slice(None), slice(2 * DIN, 2 * DIN + COMMON)), sum_com[:, :COMMON], rate_in)
    total = r_out[0].astype(f32) + r_out[1].astype(f32) + r_out[2].astype(f32) + r_out[3].astype(f32)
    adam_refs((out_w, out_m, out_v, out_wn, out_mn, out_vn), (slice(None), slice(None)), total, rate_out)


def run_finish(*args):
    tok, cot, in_w, out_w = (args[1], args[2], args[9], args[12])
    shapes = [(tok.shape, jnp.bfloat16), (cot.shape, jnp.float32)]
    shapes += [(in_w.shape, jnp.float32)] * 3 + [(out_w.shape, jnp.float32)] * 3
    whole = pl.BlockSpec(memory_space=pltpu.VMEM)
    return pl.pallas_call(
        finish_kernel,
        in_specs=[whole] * len(args),
        out_specs=[whole] * len(shapes),
        out_shape=[jax.ShapeDtypeStruct(s, kind) for s, kind in shapes],
        compiler_params=pltpu.CompilerParams(vmem_limit_bytes=VMEM_GRANT),
    )(*args)


def pick_runs(array, plane_runs, quad, core):
    lead = array.shape[:-1]
    width = array.shape[-1] // (PLANES * QUADS)
    split = array.reshape(lead + (2, 2, QUADS, width))
    zero = 0
    n = len(lead)
    taken = lax.dynamic_slice(
        split, (zero,) * n + (core, 0, quad, 0), lead + (1, 2, 1, width)
    )
    return taken.reshape(lead + (2 * width,))


def put_runs(array, quad, core):
    lead = array.shape[:-1]
    width = array.shape[-1] // 2
    zeros = jnp.zeros(lead + (2, 2, QUADS, width), array.dtype)
    n = len(lead)
    full = lax.dynamic_update_slice(
        zeros, array.reshape(lead + (1, 2, 1, width)), (0,) * n + (core, 0, quad, 0)
    )
    return full.reshape(lead + (width * PLANES * QUADS,))


def rank_slices(array):
    rows = array.shape[0]
    split = array.reshape(rows, 2, 2, QUADS, RUN)
    return split.transpose(3, 1, 0, 2, 4).reshape(RANKS, rows, OWN)


def rank_join(array):
    rows = array.shape[1]
    split = array.reshape(QUADS, 2, rows, 2, RUN)
    return split.transpose(2, 1, 3, 0, 4).reshape(rows, DIN)


def per_device_quad(
    tokens_in,
    cotangent,
    seq_lens,
    in_weight,
    in_first,
    in_second,
    out_weight,
    out_first,
    out_second,
    conv_weight,
    conv_first,
    conv_second,
    gains,
    gain_first,
    gain_second,
    head_params,
    head_first,
    head_second,
):
    plane, quad, core = place()
    rank = 2 * quad + core
    (
        normed, cot, w_gate, w_x, w_com, w_out, gate_part, proj_x, proj_com, act, mixed, grad_normed_out,
        stats, gain_in, gain_out, conv, heads, skip, select, lens
    ) = run_fore(tokens_in, cotangent, seq_lens, in_weight, out_weight, conv_weight, gains, head_params)
    branch, dgate, dmix, g_out, g_gate, g_gain = run_gate(
        lens, stats, cot, normed, gate_part, mixed, grad_normed_out, w_out, gain_out
    )
    r_out, all_gate, all_x, sum_com, packs, sum_branch, grad_rows = run_back(
        lens, g_gate, g_out, branch, w_gate, w_x, w_com, conv, heads, skip, select, gain_in, g_gain,
        tokens_in, normed, dgate, dmix, proj_x, proj_com, act
    )
    finished = run_finish(
        lens, tokens_in, cotangent, sum_branch, grad_rows, r_out, all_gate, all_x, sum_com,
        in_weight, in_first, in_second, out_weight, out_first, out_second
    )
    mine = rank + RANKS * plane
    grad_gains = jnp.concatenate(
        [jnp.sum(packs[:, :12], axis=0).reshape(D), rank_join(packs[:, 12:15].reshape(RANKS, 1, OWN)).reshape(DIN)]
    )
    gain_sum = lax.dynamic_slice(grad_gains, (mine * gains.shape[0],), gains.shape)
    grad_conv = jnp.concatenate(
        [
            rank_join(packs[:, 15:30].reshape(RANKS, KCONV + 1, OWN)),
            jnp.sum(packs[:, 30:40], axis=0).reshape(KCONV + 1, 2 * NST),
        ],
        axis=1,
    )
    conv_sum = lax.dynamic_slice(grad_conv, (0, mine * conv_weight.shape[1]), conv_weight.shape)
    grad_skip = jnp.sum(packs[:, 42:45].reshape(RANKS, 1, OWN_HEADS, HDIM), axis=3)
    head_sum = jnp.concatenate([packs[:, 40:42, :OWN_HEADS], grad_skip], axis=1)
    head_sum = head_sum.reshape(QUADS, 2, 3, 2, 3).transpose(2, 1, 3, 0, 4).reshape(3, HEADS)
    new_conv = adam_update(conv_weight, conv_first, conv_second, conv_sum, rate_conv)
    new_gain = adam_update(gains, gain_first, gain_second, gain_sum, rate_gain)
    new_head = adam_update(head_params, head_first, head_second, head_sum, rate_head)
    return tuple(finished) + new_conv + new_gain + new_head


def solution(mesh):
    placed = (
        P(("dp", "seq"), None),
        P(("dp", "seq"), None),
        P("dp", None),
        P(("dp", "seq"), None),
        P(("dp", "seq"), None),
        P(("dp", "seq"), None),
        P(("dp", "seq"), None),
        P(("dp", "seq"), None),
        P(("dp", "seq"), None),
        P(None, ("dp", "seq")),
        P(None, ("dp", "seq")),
        P(None, ("dp", "seq")),
        P(("dp", "seq")),
        P(("dp", "seq")),
        P(("dp", "seq")),
        P(),
        P(),
        P(),
    )
    quad = dict(mesh.shape) == {"dp": PLANES * QUADS, "seq": 2}
    return jax.shard_map(
        per_device_quad if quad else per_device,
        mesh=mesh,
        in_specs=placed,
        out_specs=(
            P(("dp", "seq"), None),
            P(("dp", "seq"), None),
            P(("dp", "seq"), None),
            P(("dp", "seq"), None),
            P(("dp", "seq"), None),
            P(("dp", "seq"), None),
            P(("dp", "seq"), None),
            P(("dp", "seq"), None),
            P(None, ("dp", "seq")),
            P(None, ("dp", "seq")),
            P(None, ("dp", "seq")),
            P(("dp", "seq")),
            P(("dp", "seq")),
            P(("dp", "seq")),
            P(),
            P(),
            P(),
        ),
        check_vma=False,
    )
```

```python
import functools

import jax
import jax.numpy as jnp
from jax import lax
from jax.experimental import pallas as pl
from jax.experimental.pallas import tpu as pltpu
from jax.sharding import PartitionSpec as P

D = 1536
HEADS = 48
HDIM = 64
NST = 128
KCONV = 4
BLOCK = 256
SLOTS = 4
STEP = 10
DIN = 3072
CONVC = 3328


highest = lax.Precision.HIGHEST
norm_eps = 1e-05
beta_first = 0.9
beta_second = 0.95
adam_eps = 1e-08
weight_decay = 0.1
rate_in = 0.01
rate_out = 0.008
rate_conv = 0.2
rate_gain = 0.4
rate_head = 0.5


def from_behind(block, axis, distance):
    devices = range(lax.axis_size(axis))
    route = [(i - distance, i) for i in devices if i - distance in devices]
    return lax.ppermute(block, axis, route)


def prefix(value, axis, join, neutral):
    place = lax.axis_index(axis)
    gathered = jax.tree.map(
        lambda a, kind: lax.all_gather(a.astype(kind), axis),
        value,
        jax.tree.map(lambda a: jnp.bfloat16 if a.dtype == jnp.float32 else a.dtype, value),
    )
    state = jax.tree.map(lambda a, e: jnp.zeros_like(a) + jnp.asarray(e, a.dtype), value, neutral)

    def one(hop, state):
        return join(
            state,
            jax.tree.map(
                lambda a, own: lax.dynamic_index_in_dim(a, hop, 0, False).astype(own.dtype),
                gathered,
                value,
            ),
        )

    return lax.fori_loop(0, place, one, state)


def prefix_2(value, axis, combine, identity):
    devices, index = (lax.axis_size(axis), lax.axis_index(axis))
    everything = jax.tree.map(
        lambda part, kind: lax.all_gather(part.astype(kind), axis),
        value,
        (jnp.bfloat16, jnp.bfloat16),
    )
    start = jax.tree.map(
        lambda part, zero: jnp.broadcast_to(jnp.asarray(zero, part.dtype), part.shape),
        value,
        identity,
    )

    def hop(k, before):
        at = devices - 1 - k
        reached = at > index
        new = combine(
            before, jax.tree.map(lambda part, own: part[at].astype(own.dtype), everything, value)
        )
        return jax.tree.map(lambda a, b: jnp.where(reached, a, b), new, before)

    return lax.fori_loop(0, devices, hop, start)


def segment_of(seq_row, position):
    blocks = (seq_row + BLOCK - 1) // BLOCK
    ends = jnp.cumsum(blocks) * BLOCK
    starts = ends - blocks * BLOCK
    above = position[:, None] >= starts[None, :]
    inside = above & (position[:, None] < ends[None, :])
    numbers = jnp.arange(1, SLOTS + 1, dtype=jnp.int32)
    labels_of = jnp.sum(jnp.where(inside, numbers[None, :], 0), axis=1)
    live_rows = jnp.sum(
        (above & (position[:, None] < (starts + seq_row)[None, :])).astype(jnp.float32), axis=1
    )
    return (labels_of, live_rows)


def layout(seq_row, position):
    labels_of, live_rows = segment_of(seq_row, position)
    columns = []
    for conv_lag in range(KCONV):
        earlier, unused_live = segment_of(seq_row, position - conv_lag)
        columns.append(((earlier == labels_of) & (labels_of > 0)).astype(jnp.float32))
    return (live_rows, jnp.stack(columns, axis=1))


def pre_norm(token_rows, gain_row):
    scaling = lax.rsqrt(jnp.mean(token_rows * token_rows, axis=1, keepdims=True) + norm_eps)
    return token_rows * scaling * gain_row[None, :]


def gate_norm(mixed, gate_part, gain_row):
    gated = mixed * jax.nn.silu(gate_part)
    scaling = lax.rsqrt(jnp.mean(gated * gated, axis=1, keepdims=True) + norm_eps)
    return gated * scaling * gain_row[None, :]


def mixer_in(extended, step_raw, conv_par, head_values, factors, live_rows):
    row_count = step_raw.shape[0]
    preact = jnp.zeros((row_count, conv_par.shape[1]), jnp.float32) + conv_par[KCONV][None, :]
    for conv_tap in range(KCONV):
        window = lax.slice_in_dim(extended, conv_tap, conv_tap + row_count, axis=0)
        preact = (
            preact
            + conv_par[conv_tap][None, :] * window * factors[:, KCONV - 1 - conv_tap][:, None]
        )
    conv_act = jax.nn.silu(preact)
    step_size = jax.nn.softplus(step_raw + head_values[0][None, :]) * live_rows[:, None]
    logdec = -jnp.exp(head_values[1])[None, :] * step_size
    return (conv_act, step_size, logdec)


def lower_ones():
    row_ids = lax.broadcasted_iota(jnp.int32, (BLOCK, BLOCK), 0)
    col_ids = lax.broadcasted_iota(jnp.int32, (BLOCK, BLOCK), 1)
    return (row_ids >= col_ids).astype(jnp.float32)


def block_state(values, keys_in, step_size, logdec):
    cumul = jnp.dot(lower_ones(), logdec, precision=highest)
    totals = cumul[-1]
    weighting = jnp.exp(totals[None, :] - cumul) * step_size
    states = jnp.einsum("uhp,un->hpn", weighting[:, :, None] * values, keys_in, precision=highest)
    return (jnp.exp(totals), states)


def block_out(values, keys_in, queries, step_size, logdec, skip_gain, start_state):
    lower_tri = lower_ones()
    cumul = jnp.dot(lower_tri, logdec, precision=highest)
    across = cumul.T
    gap_matrix = across[:, :, None] - across[:, None, :]
    decays = jnp.exp(jnp.where(lower_tri[None, :, :] > 0, gap_matrix, -1e30))
    gram_matrix = jnp.dot(queries, keys_in.T, precision=highest)
    mixing = gram_matrix[None, :, :] * decays * step_size.T[:, None, :]
    intra_part = jnp.einsum("htu,uhp->thp", mixing, values, precision=highest)
    carried = jnp.exp(cumul)[:, :, None] * jnp.einsum(
        "tn,hpn->thp", queries, start_state, precision=highest
    )
    return intra_part + carried + skip_gain[None, :, None] * values


def block_full(values, keys_in, queries, step_size, logdec, skip_gain, start_state):
    factor_end, states = block_state(values, keys_in, step_size, logdec)
    outputs = block_out(values, keys_in, queries, step_size, logdec, skip_gain, start_state)
    return (outputs, factor_end[:, None, None] * start_state + states)


def adam_update(weight, first, second, gradient, step_rate):
    first_new = beta_first * first + (1.0 - beta_first) * gradient
    second_new = beta_second * second + (1.0 - beta_second) * gradient * gradient
    first_hat = first_new / (1.0 - beta_first**STEP)
    second_hat = second_new / (1.0 - beta_second**STEP)
    weight_new = weight - step_rate * (
        first_hat / (jnp.sqrt(second_hat) + adam_eps) + weight_decay * weight
    )
    return (weight_new, first_new, second_new)


def carry_join(earlier, later):
    return (earlier[0] * later[0], later[0][:, None, None] * earlier[1] + later[1])


def as_float(array_low):
    return lax.optimization_barrier(array_low).astype(jnp.float32)


def contract_rows(left, right):
    return lax.dot_general(
        left, right, (((0,), (0,)), ((), ())), preferred_element_type=jnp.float32
    )


def contract_cols(left, right):
    return lax.dot_general(
        left, right, (((1,), (1,)), ((), ())), preferred_element_type=jnp.float32
    )


def per_device(
    tokens_in,
    cotangent,
    seq_lens,
    in_weight,
    in_first,
    in_second,
    out_weight,
    out_first,
    out_second,
    conv_weight,
    conv_first,
    conv_second,
    gains,
    gain_first,
    gain_second,
    head_params,
    head_first,
    head_second,
):
    local_tok = tokens_in.shape[0]
    position = lax.axis_index("seq") * local_tok + jnp.arange(local_tok, dtype=jnp.int32)
    live_rows, factors = layout(seq_lens[0], position)
    low_weights = (
        in_weight.astype(jnp.bfloat16),
        out_weight.astype(jnp.bfloat16),
        conv_weight.astype(jnp.bfloat16),
        gains.astype(jnp.bfloat16),
    )
    in_full, out_full, conv_full, gain_full = (
        lax.all_gather(low_weights[0], ("dp", "seq"), axis=0, tiled=True),
        lax.all_gather(low_weights[1], ("dp", "seq"), axis=0, tiled=True),
        lax.all_gather(low_weights[2], ("dp", "seq"), axis=1, tiled=True),
        lax.all_gather(low_weights[3], ("dp", "seq"), axis=0, tiled=True),
    )
    conv_par = conv_full.astype(jnp.float32)
    gain_par = gain_full.astype(jnp.float32)
    token_rows = tokens_in.astype(jnp.float32)
    normed_value, pull_pre = jax.vjp(pre_norm, token_rows, gain_par[:D])
    normed = normed_value.astype(jnp.bfloat16)
    projected = jnp.dot(normed, in_full, preferred_element_type=jnp.float32)
    gate_part = projected[:, :DIN]
    conv_in = projected[:, DIN : DIN + CONVC]
    step_raw = projected[:, DIN + CONVC :]
    halo_rows = from_behind(conv_in[local_tok - KCONV + 1 :], "seq", 1)
    extended = jnp.concatenate([halo_rows, conv_in], axis=0)

    def mixer_local(extended_rows, raw_steps, conv_values, head_values):
        return mixer_in(extended_rows, raw_steps, conv_values, head_values, factors, live_rows)

    (conv_act, step_size, logdec), pull_mixer = jax.vjp(
        mixer_local, extended, step_raw, conv_par, head_params
    )
    conv_used = as_float(conv_act.astype(jnp.bfloat16))
    block_count = local_tok // BLOCK
    values = conv_used[:, :DIN].reshape(block_count, BLOCK, HEADS, HDIM)
    keys_in = conv_used[:, DIN : DIN + NST].reshape(block_count, BLOCK, NST)
    queries = conv_used[:, DIN + NST :].reshape(block_count, BLOCK, NST)
    steps_blk = step_size.reshape(block_count, BLOCK, HEADS)
    logdec_blk = logdec.reshape(block_count, BLOCK, HEADS)
    resets = factors[::BLOCK, 1]
    skip_gain = head_params[2]
    decays, block_states = jax.vmap(block_state)(values, keys_in, steps_blk, logdec_blk)

    def fold_local(carried, block_item):
        factor_now = block_item[0] * block_item[2]
        return (
            (carried[0] * factor_now, factor_now[:, None, None] * carried[1] + block_item[1]),
            None,
        )

    identity = (jnp.ones((HEADS,), jnp.float32), jnp.zeros((HEADS, HDIM, NST), jnp.float32))
    device_sum, unused_fold = lax.scan(fold_local, identity, (decays, block_states, resets))
    unused_dec, entering = prefix(device_sum, "seq", carry_join, identity)

    def start_states(states, block_item):
        begin = block_item[2] * states
        return (block_item[0][:, None, None] * begin + block_item[1], begin)

    unused_end, begins = lax.scan(start_states, entering, (decays, block_states, resets))

    def emit(block_item):
        return block_out(
            block_item[0],
            block_item[1],
            block_item[2],
            block_item[3],
            block_item[4],
            skip_gain,
            block_item[5],
        )

    mixed = lax.map(emit, (values, keys_in, queries, steps_blk, logdec_blk, begins)).reshape(
        local_tok, DIN
    )
    normed_out_value, pull_gate = jax.vjp(gate_norm, mixed, gate_part, gain_par[D:])
    normed_out = normed_out_value.astype(jnp.bfloat16)
    branch = jnp.dot(normed_out, out_full, preferred_element_type=jnp.float32)
    mixed_out = (token_rows + live_rows[:, None] * branch).astype(jnp.bfloat16)
    out_grad = (cotangent.astype(jnp.float32) * live_rows[:, None]).astype(jnp.bfloat16)
    in_back, out_back = (
        lax.all_gather(in_weight.astype(jnp.bfloat16), ("dp", "seq"), axis=0, tiled=True),
        lax.all_gather(out_weight.astype(jnp.bfloat16), ("dp", "seq"), axis=0, tiled=True),
    )
    grad_out_w = contract_rows(normed_out, out_grad)
    grad_normed_out = contract_cols(out_grad, out_back)
    grad_mixed, grad_gate, grad_gain_in = pull_gate(grad_normed_out)
    mixed_back = as_float(grad_mixed.astype(jnp.bfloat16)).reshape(block_count, BLOCK, HEADS, HDIM)

    def adjoint_local(carried, block_item):
        cumul = jnp.dot(lower_ones(), block_item[2], precision=highest)
        weighted = jnp.exp(cumul)[:, :, None] * block_item[0]
        direct = jnp.einsum("thp,tn->hpn", weighted, block_item[1], precision=highest)
        return (block_item[4] * (direct + block_item[3][:, None, None] * carried), None)

    local_adj, unused_adj = lax.scan(
        adjoint_local, identity[1], (mixed_back, queries, logdec_blk, decays, resets), reverse=True
    )
    unused_later, leaving = prefix_2((device_sum[0], local_adj), "seq", carry_join, identity)

    def adjoint_block(carried, block_item):
        unused_primal, pull_block = jax.vjp(
            block_full,
            block_item[0],
            block_item[1],
            block_item[2],
            block_item[3],
            block_item[4],
            skip_gain,
            block_item[5],
        )
        grads = pull_block((block_item[6], carried[0]))
        return ((block_item[7] * grads[6], carried[1] + grads[5]), grads[:5])

    (unused_state, grad_skip), block_grads = lax.scan(
        adjoint_block,
        (leaving, jnp.zeros((HEADS,), jnp.float32)),
        (values, keys_in, queries, steps_blk, logdec_blk, begins, mixed_back, resets),
        reverse=True,
    )
    grad_values, grad_keys, grad_queries, grad_step, grad_logdec = block_grads
    grad_act = jnp.concatenate(
        [
            grad_values.reshape(local_tok, DIN),
            grad_keys.reshape(local_tok, NST),
            grad_queries.reshape(local_tok, NST),
        ],
        axis=1,
    )
    grad_ext, grad_raw, grad_conv, grad_head_part = pull_mixer(
        (grad_act, grad_step.reshape(local_tok, HEADS), grad_logdec.reshape(local_tok, HEADS))
    )
    returned = from_behind(grad_ext[: KCONV - 1].astype(jnp.bfloat16), "seq", -1).astype(
        jnp.float32
    )
    grad_conv_in = grad_ext[KCONV - 1 :] + jnp.concatenate(
        [jnp.zeros((local_tok - KCONV + 1, CONVC), jnp.float32), returned], axis=0
    )
    grad_proj = jnp.concatenate([grad_gate, grad_conv_in, grad_raw], axis=1).astype(jnp.bfloat16)
    grad_normed = contract_cols(grad_proj, in_back)
    grad_rows, grad_gain_pre = pull_pre(grad_normed)
    grad_input = cotangent.astype(jnp.float32) + grad_rows
    grad_gains = jnp.concatenate([grad_gain_pre, grad_gain_in], axis=0)
    grad_head = jnp.concatenate(
        [grad_head_part[:2], (grad_head_part[2] + grad_skip)[None, :]], axis=0
    )
    grad_in_w = contract_rows(normed, grad_proj)
    in_sum, out_sum, conv_sum, gain_sum = (
        lax.psum_scatter(grad_in_w, ("dp", "seq"), scatter_dimension=0, tiled=True),
        lax.psum_scatter(grad_out_w, ("dp", "seq"), scatter_dimension=0, tiled=True),
        lax.psum_scatter(grad_conv, ("dp", "seq"), scatter_dimension=1, tiled=True),
        lax.psum_scatter(grad_gains, ("dp", "seq"), scatter_dimension=0, tiled=True),
    )
    head_sum = lax.psum(grad_head, ("dp", "seq"))
    new_in = adam_update(in_weight, in_first, in_second, in_sum, rate_in)
    new_out = adam_update(out_weight, out_first, out_second, out_sum, rate_out)
    new_conv = adam_update(conv_weight, conv_first, conv_second, conv_sum, rate_conv)
    new_gain = adam_update(gains, gain_first, gain_second, gain_sum, rate_gain)
    new_head = adam_update(head_params, head_first, head_second, head_sum, rate_head)
    return (
        mixed_out,
        grad_input,
        new_in[0],
        new_in[1],
        new_in[2],
        new_out[0],
        new_out[1],
        new_out[2],
        new_conv[0],
        new_conv[1],
        new_conv[2],
        new_gain[0],
        new_gain[1],
        new_gain[2],
        new_head[0],
        new_head[1],
        new_head[2],
    )


MESH_ID = pl.DeviceIdType.MESH
ANY = pl.BlockSpec(memory_space=pl.ANY)
PLANES = 4
QUADS = 4
RANKS = 8


def place():
    chip = lax.axis_index("dp")
    return (chip // QUADS, chip % QUADS, lax.axis_index("seq"))


def at(plane, quad, core):
    return (plane * QUADS + quad, core)


def flip(core):
    return 1 - core


def xor4(value, k):
    low, high = value % 2, value // 2
    if k % 2:
        low = 1 - low
    if k // 2:
        high = 1 - high
    return 2 * high + low


def greet(devices):
    barrier = pltpu.get_barrier_semaphore()
    for device in devices:
        pl.semaphore_signal(barrier, inc=1, device_id=device, device_id_type=MESH_ID)
    pl.semaphore_wait(barrier, len(devices))


def plane_mates(plane, quad, core):
    mates = []
    for k in range(QUADS):
        for other in (core, flip(core)):
            if not (k == 0 and other is core):
                mates.append(at(plane, xor4(quad, k), other))
    return mates


def plane_others(plane, quad, core):
    return [at(xor4(plane, k), quad, core) for k in range(1, PLANES)]


class Sems:
    def __init__(self, send, recv):
        self.send, self.recv, self.used = (send, recv, 0)

    def copy(self, source, target, device):
        index = self.used
        self.used += 1
        return pltpu.make_async_remote_copy(
            src_ref=source,
            dst_ref=target,
            send_sem=self.send.at[index],
            recv_sem=self.recv.at[index],
            device_id=device,
            device_id_type=MESH_ID,
        )


class PlaneGather:
    def __init__(self, sems, own, land, plane, quad, core):
        near_x, near_y, far = (xor4(quad, k) for k in (1, 2, 3))
        rank, rank_x, rank_y, rank_far = (2 * q + core for q in (quad, near_x, near_y, far))
        to_x, to_y = (at(plane, near_x, core), at(plane, near_y, core))
        sibling = at(plane, quad, flip(core))
        whole = [0, 1]
        self.own = [
            sems.copy(own(h), land(rank, slot, h), device)
            for device, slot in ((to_x, 1), (to_y, 2), (sibling, 0))
            for h in whole
        ]
        self.relay_x = [
            sems.copy(land(rank_x, 1, 0), land(rank_x, 3, 0), to_y),
        ] + [sems.copy(land(rank_x, 1, h), land(rank_x, 1, h), sibling) for h in whole]
        self.relay_y = [
            sems.copy(land(rank_y, 2, 1), land(rank_y, 3, 1), to_x),
        ] + [sems.copy(land(rank_y, 2, h), land(rank_y, 2, h), sibling) for h in whole]
        self.relay_far = [
            sems.copy(land(rank_far, 3, h), land(rank_far, 3, h), sibling) for h in whole
        ]

    def start(self):
        for copy in self.own:
            copy.start()

    def near(self):
        self.own[0].wait_recv()
        self.relay_x[0].start()
        self.own[3].wait_recv()
        self.relay_y[0].start()
        self.own[1].wait_recv()
        self.own[2].wait_recv()
        for copy in self.relay_x[1:] + self.relay_y[1:]:
            copy.start()

    def across(self):
        for h, relay in ((0, self.relay_x[0]), (1, self.relay_y[0])):
            relay.wait_recv()
            self.relay_far[h].start()

    def wait_slot(self, slot):
        for copy in (self.own[4:], self.relay_x[1:], self.relay_y[1:], self.relay_far)[slot]:
            copy.wait_recv()

    def sent(self):
        for copy in self.own + self.relay_x + self.relay_y + self.relay_far:
            copy.wait_send()


class LineGather:
    def __init__(self, sems, own, block, plane, quad, core):
        self.plane = plane
        self.right, self.left = ([], [])
        for hop in range(PLANES - 1):
            for copies, step in ((self.right, 1), (self.left, -1)):
                index = plane - step * hop
                source = own if hop == 0 else block(index)
                copies.append(sems.copy(source, block(index), at(plane + step, quad, core)))

    def sends(self, hop, step):
        if step > 0:
            return (self.plane - hop >= 0) & (self.plane < PLANES - 1)
        return (self.plane + hop < PLANES) & (self.plane > 0)

    def receives(self, hop, step):
        if step > 0:
            return self.plane - 1 - hop >= 0
        return self.plane + 1 + hop < PLANES

    def start(self, hop):
        for copies, step in ((self.right, 1), (self.left, -1)):

            @pl.when(self.sends(hop, step))
            def go():
                copies[hop].start()

    def arrive(self, hop):
        for copies, step in ((self.right, 1), (self.left, -1)):

            @pl.when(self.receives(hop, step))
            def landed():
                copies[hop].wait_recv()

    def sent(self):
        for hop in range(PLANES - 1):
            for copies, step in ((self.right, 1), (self.left, -1)):

                @pl.when(self.sends(hop, step))
                def left():
                    copies[hop].wait_send()


OWN_HEADS = HEADS // RANKS
OWN = OWN_HEADS * HDIM
PAIRS = OWN_HEADS // 2
RUN = OWN // 2
COMMON = 2 * NST + HEADS
COMMON_PAD = 384
GROUP = 2 * BLOCK
MIX = OWN + 2 * NST
LANES = 128
STRIP = 128


def mm(left, right):
    return lax.dot_general(left, right, (((1,), (0,)), ((), ())), preferred_element_type=jnp.float32)


def mm_t(left, right):
    return lax.dot_general(left, right, (((1,), (1,)), ((), ())), preferred_element_type=jnp.float32)


def t_mm(left, right):
    return lax.dot_general(left, right, (((0,), (0,)), ((), ())), preferred_element_type=jnp.float32)


def mm_full(left, right):
    return lax.dot_general(
        left, right, (((1,), (0,)), ((), ())), precision=highest, preferred_element_type=jnp.float32
    )


def low16(value):
    return value.astype(jnp.bfloat16)


def parts_of(value, terms):
    parts = []
    for unused in range(terms):
        parts.append(low16(value))
        value = value - parts[-1].astype(jnp.float32)
    return parts


def mm_right(left, ones, terms=3):
    return sum(mm(part, ones) for part in parts_of(left, terms))


def mm_left(ones, right, terms=3):
    return sum(mm(ones, part) for part in parts_of(right, terms))


def iota(shape, axis):
    return lax.broadcasted_iota(jnp.int32, shape, axis)


def head_spread():
    return low16((iota((LANES, OWN), 1) // HDIM == iota((LANES, OWN), 0)).astype(jnp.float32))


def head_gather():
    return low16((iota((OWN, LANES), 0) // HDIM == iota((OWN, LANES), 1)).astype(jnp.float32))


def lower_mask():
    return iota((BLOCK, BLOCK), 0) >= iota((BLOCK, BLOCK), 1)


def shift_down(value, k):
    if k == 0:
        return value
    rolled = pltpu.roll(value, k, 0)
    return jnp.where(iota(value.shape, 0) >= k, rolled, 0.0)


def shift_up(value, k):
    if k == 0:
        return value
    rows = value.shape[0]
    rolled = pltpu.roll(value, rows - k, 0)
    return jnp.where(iota(value.shape, 0) < rows - k, rolled, 0.0)


def sigmoid(value):
    return 1.0 / (1.0 + jnp.exp(-value))


def softplus(value):
    return jnp.maximum(value, 0.0) + jnp.log1p(jnp.exp(-jnp.abs(value)))


def preact_of(u, conv):
    total = u * conv[KCONV - 1 : KCONV] + conv[KCONV : KCONV + 1]
    for tap in range(KCONV - 1):
        total = total + shift_down(u, KCONV - 1 - tap) * conv[tap : tap + 1]
    return total


def steps_of(raw, heads, live):
    step = softplus(raw + heads[0:1]) * live * heads[3:4]
    return (step, -jnp.exp(heads[1:2]) * step)


def lane_half(value, side):
    lanes = iota(value.shape, 1)
    return jnp.where((lanes >= HDIM) == (side == 1), value, jnp.zeros_like(value))


def block_parts(step, logdec, spread):
    cumul = mm_left(low16(lower_mask().astype(jnp.float32)), logdec)
    return (cumul, jnp.transpose(cumul), mm_right(step, spread, 2), mm_right(cumul, spread))


def ssd_forward(act, step, logdec, skip, out):
    spread = head_spread()
    lower = lower_mask()
    state = None
    for k in range(2):
        rows = slice(k * BLOCK, (k + 1) * BLOCK)
        values, keys, queries = (act[rows, :OWN], act[rows, OWN : OWN + NST], act[rows, OWN + NST :])
        cumul, cumul_t, step_w, cumul_w = block_parts(step[rows], logdec[rows], spread)
        gram = jnp.where(lower, mm_t(queries, keys), 0.0)
        values_f = values.astype(jnp.float32)
        stepped = low16(values_f * step_w)
        base = skip * values_f
        if state is not None:
            base = base + jnp.exp(cumul_w) * mm(queries, state)
        else:
            weighting = jnp.exp(cumul_w[BLOCK - 1 :] - cumul_w) * step_w
            state = low16(t_mm(keys, low16(weighting * values_f)))

        for pair in range(PAIRS):
            lanes = slice(pair * LANES, (pair + 1) * LANES)
            sides = [lane_half(stepped[:, lanes], side) for side in range(2)]
            for start in range(0, BLOCK, STRIP):
                strip, wide = (slice(start, start + STRIP), start + STRIP)
                piece = base[strip, lanes]
                for side in range(2):
                    h = 2 * pair + side
                    decay = jnp.exp(jnp.minimum(cumul[strip, h : h + 1] - cumul_t[h : h + 1, :wide], 0.0))
                    piece = piece + mm(low16(gram[strip, :wide] * decay), sides[side][:wide])
                out[k * BLOCK + start : k * BLOCK + wide, lanes] = piece


def live_of(lens, g):
    rows = iota((GROUP, 1), 0).astype(jnp.float32)
    chosen = jnp.sum(jnp.where(iota(lens.shape, 0) == g, lens, 0.0), axis=0, keepdims=True)[:, :1]
    return (rows < chosen).astype(jnp.float32)


def quad_of(slot):
    quad = lax.axis_index("dp") % QUADS
    return (quad % 2 + slot % 2) % 2 + 2 * ((quad // 2 + slot // 2) % 2)


def full_spec(shape):
    return pl.BlockSpec(shape, lambda g: (0,) * len(shape))


def group_spec(width):
    return pl.BlockSpec((GROUP, width), lambda g: (g, 0))


VMEM_GRANT = 60 * 1024 * 1024


def backward_block(k, act, dmix, step, logdec, skip, state, state_grad, spread, gather):
    rows = slice(k * BLOCK, (k + 1) * BLOCK)
    values, keys, queries = (act[rows, :OWN], act[rows, OWN : OWN + NST], act[rows, OWN + NST :])
    step, logdec = (step[rows], logdec[rows])
    lower = lower_mask()
    cumul, cumul_t, step_w, cumul_w = block_parts(step, logdec, spread)
    step_t = jnp.transpose(step)
    gram = jnp.where(lower, mm_t(queries, keys), 0.0)
    values_f = values.astype(jnp.float32)
    dmix_f = dmix[rows].astype(jnp.float32)
    lanes_h = iota((BLOCK, LANES), 1)

    rows_h = iota((8, BLOCK), 0)
    strips = [slice(i * STRIP, (i + 1) * STRIP) for i in range(BLOCK // STRIP)]
    widths = [-(-strip.stop // LANES) * LANES for strip in strips]
    grams = [gram[strip, :wide] for strip, wide in zip(strips, widths)]
    grad_grams = [0.0] * len(strips)
    row_sums = [jnp.zeros((STRIP, LANES), jnp.float32)] * len(strips)
    lanes_h = iota((STRIP, LANES), 1)
    col_sums = jnp.zeros((8, BLOCK), jnp.float32)
    pieces = []
    for pair in range(PAIRS):
        lanes = slice(pair * LANES, (pair + 1) * LANES)
        dm, value = (dmix[rows, lanes], act[rows, lanes])
        piece = [0.0] * (BLOCK // LANES)
        for side in range(2):
            h = 2 * pair + side
            dm_half = lane_half(dm, side)
            sums = [0.0] * (BLOCK // LANES)
            for i, (strip, wide) in enumerate(zip(strips, widths)):
                decay = jnp.exp(jnp.minimum(cumul[strip, h : h + 1] - cumul_t[h : h + 1, :wide], 0.0))
                grad_mixing = mm_t(dm_half[strip], value[:wide])
                mixing = grams[i] * decay
                step_row = step_t[h : h + 1, :wide]
                grad_grams[i] = grad_grams[i] + grad_mixing * decay * step_row
                product = grad_mixing * mixing
                row_sums[i] = jnp.where(
                    lanes_h == h, jnp.sum(product * step_row, axis=1, keepdims=True), row_sums[i]
                )
                column = jnp.sum(product, axis=0, keepdims=True)
                part = t_mm(low16(mixing), dm_half[strip])
                for c in range(wide // LANES):
                    own = slice(c * LANES, (c + 1) * LANES)
                    sums[c] = sums[c] + column[:, own]
                    piece[c] = piece[c] + part[own]
            col_sums = jnp.where(rows_h == h, jnp.concatenate(sums, axis=1), col_sums)
        pieces.append(jnp.concatenate(piece, axis=0))
    row_sums = jnp.concatenate(row_sums, axis=0)
    grad_values = jnp.concatenate(pieces, axis=1) * step_w + skip * dmix_f
    grad_skip = jnp.sum(dmix_f * values_f, axis=0, keepdims=True)
    grad_queries, grad_keys = ([], [0.0] * (BLOCK // LANES))
    for strip, wide, grad_gram in zip(strips, widths, grad_grams):
        kept = low16(jnp.where(lower[strip, :wide], grad_gram, 0.0))
        grad_queries.append(mm(kept, keys[:wide]))
        part = t_mm(kept, queries[strip])
        for c in range(wide // LANES):
            grad_keys[c] = grad_keys[c] + part[c * LANES : (c + 1) * LANES]
    grad_queries = jnp.concatenate(grad_queries, axis=0)
    grad_keys = jnp.concatenate(grad_keys, axis=0)
    columns = jnp.transpose(
        jnp.concatenate([col_sums, jnp.zeros((LANES - 8, BLOCK), jnp.float32)], axis=0)
    )
    grad_step = columns
    grad_cumul = row_sums - columns * step
    if k == 1:
        entering = jnp.exp(cumul_w) * dmix_f
        entering_low = low16(entering)
        crossed = mm(queries, state)
        grad_cumul = grad_cumul + mm_right(entering * crossed, gather, 2)
        grad_queries = grad_queries + mm_t(entering_low, state)
        before = low16(t_mm(queries, entering_low))
    else:
        tail = jnp.exp(cumul_w[BLOCK - 1 :] - cumul_w)
        weighting = tail * step_w
        back = mm(keys, state_grad)
        grad_values = grad_values + weighting * back
        grad_keys = grad_keys + mm_t(low16(weighting * values_f), state_grad)
        grad_weight = mm_right(values_f * back, gather, 2)
        tail_h = jnp.exp(cumul[BLOCK - 1 :] - cumul)
        grad_step = grad_step + grad_weight * tail_h
        part = grad_weight * tail_h * step
        last = iota((BLOCK, LANES), 0) == BLOCK - 1
        grad_cumul = grad_cumul - part + jnp.where(last, jnp.sum(part, axis=0, keepdims=True), 0.0)
        before = None
    upper = low16((iota((BLOCK, BLOCK), 0) <= iota((BLOCK, BLOCK), 1)).astype(jnp.float32))
    grad_logdec = mm_left(upper, grad_cumul)
    return (grad_values, grad_keys, grad_queries, grad_step, grad_logdec, grad_skip, before)


ROWS_IN = D // (PLANES * RANKS)
ROWS_OUT = DIN // (PLANES * RANKS)
ROWS_ALL = ROWS_IN + 16
SHARD_CONV = CONVC // (PLANES * RANKS)
SHARD_GAIN = (D + DIN) // (PLANES * RANKS)
RUN_HALVES = RUN // HDIM


def place_lanes(pieces, tiles, rows):
    lanes = iota((rows, LANES), 1)
    out = [jnp.zeros((rows, LANES), jnp.float32) for unused in range(tiles)]
    for value, width, offset in pieces:
        tile, lane = divmod(offset, LANES)
        moved = pltpu.roll(value, lane, 1) if lane else value
        end = lane + width
        out[tile] = jnp.where((lanes >= lane) & (lanes < end), moved, out[tile])
        if end > LANES:
            out[tile + 1] = jnp.where(lanes < end - LANES, moved, out[tile + 1])
    return out


def own_lanes(tiles, quad, core):
    rows = tiles[0].shape[0]
    lanes = iota((rows, LANES), 1)

    def half_of(index):
        tile, odd = (index // 2, index % 2)
        chosen = tiles[0]
        for t in range(1, len(tiles)):
            chosen = jnp.where(tile == t, tiles[t], chosen)
        return (chosen, odd)

    out = []
    for pair in range(PAIRS):
        sides = []
        for b in range(2):
            near, i = divmod(2 * pair + b, RUN_HALVES)
            value, odd = half_of(2 * PLANES * RUN_HALVES * core + PLANES * RUN_HALVES * near + RUN_HALVES * quad + i)
            sides.append(jnp.where(odd == b, value, pltpu.roll(value, HDIM, 1)))
        out.append(jnp.where(lanes < HDIM, sides[0], sides[1]))
    return jnp.concatenate(out, axis=1)


def fill_sends(in_w, part, target):
    lanes = iota((ROWS_IN, LANES), 1)
    for j in range(RANKS):
        quad, core = divmod(j, 2)
        for pair in range(PAIRS):
            sides = []
            for b in range(2):
                near, i = divmod(2 * pair + b, RUN_HALVES)
                index = (2 * core + near) * PLANES * RUN_HALVES + RUN_HALVES * quad + i
                start = part * DIN + index // 2 * LANES
                tile = in_w[:, start : start + LANES]
                sides.append(tile if index % 2 == b else pltpu.roll(tile, HDIM, 1))
            lane = pair * LANES
            target[j, :, lane : lane + LANES] = low16(jnp.where(lanes < HDIM, sides[0], sides[1]))


def fill_common(in_w, conv_w, gains, lens, wc_send):
    wc_send[...] = jnp.zeros_like(wc_send)
    wc_send[:ROWS_IN, : 2 * NST] = low16(in_w[:, 2 * DIN : 2 * DIN + 2 * NST])
    tail = in_w[:, 2 * DIN + 2 * NST : 2 * DIN + COMMON]
    wide = jnp.concatenate([tail, jnp.zeros((ROWS_IN, LANES - HEADS), jnp.float32)], axis=1)
    wc_send[:ROWS_IN, 2 * NST :] = low16(wide)
    conv_v = jnp.concatenate([conv_w[...], jnp.zeros((KCONV + 1, COMMON_PAD - SHARD_CONV), jnp.float32)], axis=1)
    gain_v = jnp.concatenate([gains[...], jnp.zeros((1, COMMON_PAD - SHARD_GAIN), jnp.float32)], axis=1)
    extra = jnp.broadcast_to(lens[:, 0:1].astype(jnp.float32) - BLOCK, (1, COMMON_PAD))
    rows = jnp.concatenate([conv_v, gain_v, extra, jnp.zeros((9, COMMON_PAD), jnp.float32)], axis=0)
    wc_send[ROWS_IN:] = low16(rows)


def select_heads(quad, core):
    rows, columns = (iota((LANES, LANES), 0), iota((LANES, LANES), 1))
    head = HEADS // 2 * core + HEADS // 4 * (columns // 3) + 3 * quad + columns % 3
    return ((rows == head) & (columns < OWN_HEADS)).astype(jnp.float32)


def fore_kernel(
    tok, cot, seq_lens, in_w, out_w, conv_w, gains, head_params,
    o_normed, o_cot, o_gate_w, o_x_w, o_com, o_out, o_gate, o_proj, o_proj_com, o_act, o_mixed, o_gno,
    stats, gain_in, gain_out, conv, heads, skip, select, lens,
    wx_send, wg_send, wc_send, wo_send, all_tok, all_cot, normed, all_wx, all_wg, all_wc, w_com, line_wo, w_out,
    proj, gate, proj_com, act, mixed, gno, part, shared,
    send, recv, local
):
    plane, quad, core = place()
    where = (plane, quad, core)
    rank = 2 * quad + core
    sibling = at(plane, quad, flip(core))
    sems = Sems(send, recv)
    f32 = jnp.float32
    half = BLOCK // 2
    kept = []

    def keep(source, target):
        copy = pltpu.make_async_copy(source, target, local.at[len(kept)])
        kept.append(copy)
        copy.start()
        return copy

    def pieces(buffer):
        return lambda r, slot, h: buffer.at[slot, core, pl.ds(h * half, half)]

    def halves(buffer):
        return lambda h: buffer.at[pl.ds(h * half, half)]

    push_c = [
        sems.copy(wc_send, all_wc.at[plane, rank], at(xor4(plane, k), quad, core)) for k in (2, 3, 1)
    ]
    line_o = LineGather(sems, wo_send, lambda q: line_wo.at[q], *where)
    line_x = LineGather(sems, all_wx.at[plane], lambda q: all_wx.at[q], *where)
    line_g = LineGather(sems, all_wg.at[plane], lambda q: all_wg.at[q], *where)
    shuffles = []
    for source, target in ((wx_send, all_wx), (wg_send, all_wg)):
        copies = []
        for k in range(1, RANKS):
            other_core = flip(core) if k % 2 else core
            other_quad = xor4(quad, k // 2)
            copies.append(
                sems.copy(
                    source.at[2 * other_quad + other_core], target.at[plane, rank], at(plane, other_quad, other_core)
                )
            )
        shuffles.append(copies)
    tokens = PlaneGather(sems, halves(tok), pieces(all_tok), *where)
    grads = PlaneGather(sems, halves(cot), pieces(all_cot), *where)
    common = PlaneGather(
        sems,
        lambda h: all_wc.at[pl.ds(2 * h, 2), rank],
        lambda r, slot, h: all_wc.at[pl.ds(2 * h, 2), r],
        *where,
    )
    cross_o = [
        sems.copy(line_wo.at[2 * flip(core) + k], w_out.at[k, core], sibling) for k in range(2)
    ]
    mates = plane_mates(*where)
    swap = [sems.copy(part, shared.at[rank], device) for device in mates]

    greet(mates + plane_others(*where))
    fill_common(in_w, conv_w, gains, seq_lens, wc_send)
    for copy in push_c:
        copy.start()
    fill_sends(in_w, 1, wx_send)
    for copy in shuffles[0]:
        copy.start()
    wo_send[...] = low16(out_w[...])
    line_o.start(0)
    fill_sends(in_w, 0, wg_send)
    for copy in shuffles[1]:
        copy.start()
    own_wx = keep(wx_send.at[rank], all_wx.at[plane, rank])
    own_wg = keep(wg_send.at[rank], all_wg.at[plane, rank])
    own_wc = keep(wc_send, all_wc.at[plane, rank])
    own_tok = keep(tok, all_tok.at[0, core])
    own_cot = keep(cot, all_cot.at[0, core])
    own_wo = keep(wo_send, line_wo.at[plane])
    own_wc.wait()
    for copy in push_c:
        copy.wait_recv()
    common.start()
    own_wx.wait()
    for copy in shuffles[0]:
        copy.wait_recv()
    line_x.start(0)
    tokens.start()
    select[...] = select_heads(quad, core)
    wide = jnp.concatenate([head_params[...], jnp.zeros((3, LANES - HEADS), f32)], axis=1)
    wide = jnp.concatenate([wide, jnp.ones((1, LANES), f32), jnp.zeros((4, LANES), f32)], axis=0)
    heads[...] = mm_full(wide * (iota((8, LANES), 1) < HEADS).astype(f32), select[...])
    skip[...] = mm_right(heads[2:3], head_spread())

    common.near()
    common.across()
    for slot in range(QUADS):
        common.wait_slot(slot)
    line_x.arrive(0)
    line_x.start(1)
    for q in range(PLANES):
        for r in range(RANKS):
            start = (RANKS * q + r) * ROWS_IN
            w_com[start : start + ROWS_IN] = all_wc[q, r, :ROWS_IN]
    keep(w_com, o_com)
    extras = [all_wc[q, r, ROWS_IN:].astype(f32) for q in range(PLANES) for r in range(RANKS)]
    gain_tiles = place_lanes(
        [(e[5:6, :LANES], LANES, SHARD_GAIN * d) for d, e in enumerate(extras)]
        + [(e[5:6, LANES : 2 * LANES], SHARD_GAIN - LANES, SHARD_GAIN * d + LANES) for d, e in enumerate(extras)],
        (D + DIN) // LANES,
        1,
    )
    gain_in[...] = jnp.concatenate(gain_tiles[: D // LANES], axis=1)
    gain_out[...] = own_lanes(gain_tiles[D // LANES :], quad, core)
    conv_tiles = place_lanes(
        [(e[:8, :LANES], SHARD_CONV, SHARD_CONV * d) for d, e in enumerate(extras)], CONVC // LANES, 8
    )
    conv[...] = jnp.concatenate(
        [own_lanes(conv_tiles[: DIN // LANES], quad, core)] + conv_tiles[DIN // LANES :], axis=1
    )
    seats = []
    for slot in range(QUADS):
        chosen = jnp.zeros((1, LANES), f32)
        for q in range(PLANES):
            for p in range(QUADS):
                here = (plane == q) & (quad_of(slot) == p)
                chosen = jnp.where(here, extras[RANKS * q + 2 * p][6:7, :LANES], chosen)
        seats.append(chosen + BLOCK)
    lens[...] = jnp.concatenate(seats + [jnp.zeros((8 - QUADS, LANES), f32)], axis=0)

    def norm(slot):
        for side in range(2):
            rows = all_tok[slot, side].astype(f32)
            scaling = lax.rsqrt(jnp.mean(rows * rows, axis=1, keepdims=True) + norm_eps)
            normed[slot, pl.ds(side * BLOCK, BLOCK)] = low16(rows * scaling * gain_in[...])

    own_tok.wait()
    tokens.wait_slot(0)
    norm(0)
    line_x.arrive(1)
    line_x.start(2)
    own_wg.wait()
    for copy in shuffles[1]:
        copy.wait_recv()
    line_g.start(0)
    tokens.near()
    grads.start()
    line_x.arrive(2)
    keep(all_wx, o_x_w)

    @pl.loop(0, QUADS)
    def each(slot):
        @pl.when(slot == 1)
        def first():
            tokens.wait_slot(1)
            norm(1)
            line_g.arrive(0)
            line_g.start(1)

        @pl.when(slot == 2)
        def second():
            tokens.wait_slot(2)
            norm(2)
            tokens.across()
            line_g.arrive(1)
            line_g.start(2)

        @pl.when(slot == 3)
        def third():
            tokens.wait_slot(3)
            norm(3)
            line_o.arrive(0)
            line_o.start(1)

        proj[slot] = mm(normed[slot], all_wx[...].reshape(D, OWN))
        proj_com[slot] = mm(normed[slot], w_com[...])
        conv_in = jnp.concatenate([proj[slot], proj_com[slot, :, : 2 * NST]], axis=1)
        raw = mm_right(proj_com[slot, :, 2 * NST :], low16(select[...]))
        preact = preact_of(conv_in, conv[...])
        act[slot] = low16(preact * sigmoid(preact))
        step, logdec = steps_of(raw, heads[...], live_of(lens[...], slot))
        ssd_forward(act.at[slot], step, logdec, skip[...], mixed.at[slot])

    for slot in range(QUADS):
        keep(normed.at[slot], o_normed.at[pl.ds(slot * GROUP, GROUP)])
    for source, target in ((proj, o_proj), (proj_com, o_proj_com), (act, o_act), (mixed, o_mixed)):
        keep(source, target)
    line_g.arrive(2)
    line_o.arrive(1)
    line_o.start(2)
    keep(all_wg, o_gate_w)
    grads.near()

    @pl.loop(0, QUADS)
    def gates(slot):
        gate[slot] = mm(normed[slot], all_wg[...].reshape(D, OWN))

    keep(gate, o_gate)
    line_o.arrive(2)
    own_wo.wait()
    for copy in cross_o:
        copy.start()
    for k in range(2):
        w_out[k, core] = line_wo[2 * core + k]
    own_cot.wait()
    for copy in cross_o:
        copy.wait_recv()
    keep(w_out, o_out)
    part[...] = jnp.zeros_like(part)

    @pl.loop(0, QUADS)
    def measure(slot):
        for k in range(QUADS):

            @pl.when(slot == k)
            def here():
                if k == 1:
                    grads.across()
                grads.wait_slot(k)

        live = live_of(lens[...], slot)
        grad = all_cot[slot].reshape(GROUP, D)
        grad = jnp.where(live > 0.0, grad, jnp.zeros_like(grad))
        gno_v = mm_t(grad, w_out[...].reshape(OWN, D))
        gno[slot] = gno_v
        gate_part = gate[slot]
        gated = mixed[slot] * gate_part * sigmoid(gate_part)
        squares = jnp.sum(gated * gated, axis=1, keepdims=True)
        inner = jnp.sum(gno_v * gain_out[...] * gated, axis=1, keepdims=True)
        lanes = iota((GROUP, LANES), 1)
        seat = quad_of(slot)
        columns = jnp.where(lanes == 2 * seat, squares, 0.0) + jnp.where(lanes == 2 * seat + 1, inner, 0.0)
        part[...] += jnp.transpose(columns)[:8]

    for copy in swap:
        copy.start()
    keep(all_cot, o_cot)
    keep(gno, o_gno)
    shared[rank] = part[...]
    for copy in swap:
        copy.wait_recv()
    stats[...] = jnp.sum(shared[...], axis=0)
    for copy in shuffles[0] + shuffles[1] + push_c + cross_o + swap:
        copy.wait_send()
    for line in (line_o, line_x, line_g):
        line.sent()
    for gather in (tokens, grads, common):
        gather.sent()
    for copy in kept:
        if not any(copy is done for done in (own_wx, own_wg, own_wc, own_tok, own_cot, own_wo)):
            copy.wait()


def run_fore(tok, cot, seq_lens, in_w, out_w, conv_w, gains, head_params):
    f32, bf16 = (jnp.float32, jnp.bfloat16)
    whole = pl.BlockSpec(memory_space=pltpu.VMEM)
    outs = (
        ((QUADS * GROUP, D), bf16), ((QUADS, 2, BLOCK, D), bf16), ((PLANES, RANKS, ROWS_IN, OWN), bf16),
        ((PLANES, RANKS, ROWS_IN, OWN), bf16), ((D, COMMON_PAD), bf16), ((2, 2, ROWS_OUT, D), bf16),
        ((QUADS, GROUP, OWN), f32), ((QUADS, GROUP, OWN), f32), ((QUADS, GROUP, COMMON_PAD), f32), ((QUADS, GROUP, MIX), bf16),
        ((QUADS, GROUP, OWN), f32), ((QUADS, GROUP, OWN), f32),
    )
    small = (
        (8, GROUP), (1, D), (1, OWN), (8, MIX), (8, LANES), (1, OWN), (LANES, LANES), (8, LANES),
    )
    scratch = (
        ((RANKS, ROWS_IN, OWN), bf16), ((RANKS, ROWS_IN, OWN), bf16), ((ROWS_ALL, COMMON_PAD), bf16), ((ROWS_OUT, D), bf16),
        ((QUADS, 2, BLOCK, D), bf16), ((QUADS, 2, BLOCK, D), bf16), ((QUADS, GROUP, D), bf16),
        ((PLANES, RANKS, ROWS_IN, OWN), bf16), ((PLANES, RANKS, ROWS_IN, OWN), bf16),
        ((PLANES, RANKS, ROWS_ALL, COMMON_PAD), bf16),
        ((D, COMMON_PAD), bf16), ((PLANES, ROWS_OUT, D), bf16), ((2, 2, ROWS_OUT, D), bf16),
        ((QUADS, GROUP, OWN), f32), ((QUADS, GROUP, OWN), f32), ((QUADS, GROUP, COMMON_PAD), f32),
        ((QUADS, GROUP, MIX), bf16), ((QUADS, GROUP, OWN), f32), ((QUADS, GROUP, OWN), f32), ((8, GROUP), f32),
        ((RANKS, 8, GROUP), f32),
    )
    args = (tok, cot, seq_lens, in_w, out_w, conv_w, gains.reshape(1, -1), head_params)
    results = pl.pallas_call(
        fore_kernel,
        in_specs=[ANY, ANY] + [whole] * 6,
        out_specs=[ANY] * len(outs) + [whole] * len(small),
        out_shape=[jax.ShapeDtypeStruct(s, kind) for s, kind in outs]
        + [jax.ShapeDtypeStruct(s, f32) for s in small],
        scratch_shapes=[pltpu.VMEM(s, kind) for s, kind in scratch]
        + [
            pltpu.SemaphoreType.DMA((96,)),
            pltpu.SemaphoreType.DMA((96,)),
            pltpu.SemaphoreType.DMA((24,)),
        ],
        compiler_params=pltpu.CompilerParams(
            vmem_limit_bytes=VMEM_GRANT, collective_id=0, has_side_effects=True
        ),
    )(*args)
    rows = QUADS * GROUP
    widths = (D, D, None, None, None, None, OWN, OWN, COMMON_PAD, MIX, OWN, OWN)
    flat = [a if w is None else a.reshape(rows, w) for a, w in zip(results, widths)]
    flat[2], flat[3] = (flat[2].reshape(D, OWN), flat[3].reshape(D, OWN))
    flat[5] = flat[5].reshape(OWN, D)
    return flat + list(results[len(outs) :])


def gate_kernel(
    lens, stats, cot, normed, gate_part, mixed, grad_normed_out, w_out, gain_out,
    branch, dgate, dmix, g_out, g_gate, g_gain, acc_out, acc_gate, tmp_out_t, tmp_grad
):
    g = pl.program_id(0)
    live = live_of(lens[...], g)

    @pl.when(g == 0)
    def first():
        acc_out[...] = jnp.zeros_like(acc_out)
        acc_gate[...] = jnp.zeros_like(acc_gate)
        g_gain[...] = jnp.zeros_like(g_gain)

    columns = jnp.transpose(jnp.concatenate([stats[...], jnp.zeros((LANES - 8, GROUP), jnp.float32)], axis=0))
    lanes = iota((GROUP, LANES), 1)
    seat = quad_of(g)
    power = jnp.sum(jnp.where(lanes == 2 * seat, columns, 0.0), axis=1, keepdims=True)
    along = jnp.sum(jnp.where(lanes == 2 * seat + 1, columns, 0.0), axis=1, keepdims=True)
    scale_out = lax.rsqrt(power * (1.0 / DIN) + norm_eps)
    gate_v, mixed_v, gno = (gate_part[...], mixed[...], grad_normed_out[...])
    sig = sigmoid(gate_v)
    gate_act = gate_v * sig
    gated = mixed_v * gate_act
    normed_out = low16(gated * scale_out * gain_out[...])
    tmp_out_t[...] = jnp.transpose(normed_out)
    tmp_grad[...] = jnp.where(live > 0.0, cot[...], jnp.zeros_like(cot[...]))
    scaled = gno * scale_out
    grad_gated = scaled * gain_out[...] - gated * (scale_out * scale_out * scale_out * along * (1.0 / DIN))
    gain_sum = jnp.sum(scaled * gated, axis=0, keepdims=True)
    g_gain[...] += jnp.concatenate([gain_sum, jnp.zeros((7, OWN), jnp.float32)], axis=0)
    grad_gate = low16(grad_gated * mixed_v * (sig * (1.0 + gate_v * (1.0 - sig))))
    dgate[...] = grad_gate
    dmix[...] = low16(grad_gated * gate_act)
    wide = 4 * LANES
    for side in range(2):
        branch[0, side] = low16(mm(normed_out[side * BLOCK : (side + 1) * BLOCK], w_out[...]))

    @pl.loop(0, D // wide)
    def tile(i):
        lanes = pl.ds(pl.multiple_of(i * wide, wide), wide)
        acc_out[:, lanes] += mm(tmp_out_t[...], tmp_grad[:, lanes])
        acc_gate[lanes, :] += t_mm(normed[:, lanes], dgate[...])

    @pl.when(g == QUADS - 1)
    def last():
        g_out[...] = low16(acc_out[...])
        g_gate[...] = low16(acc_gate[...])


def run_gate(lens, stats, cot, normed, gate_part, mixed, grad_normed_out, w_out, gain_out):
    f32, bf16 = (jnp.float32, jnp.bfloat16)
    rows = QUADS * GROUP
    grouped = (cot, normed, gate_part, mixed, grad_normed_out)
    ends = (((OWN, D), bf16), ((D, OWN), bf16), ((8, OWN), f32))
    return pl.pallas_call(
        gate_kernel,
        grid=(QUADS,),
        in_specs=[full_spec(a.shape) for a in (lens, stats)]
        + [group_spec(a.shape[1]) for a in grouped]
        + [full_spec(w_out.shape), full_spec(gain_out.shape)],
        out_specs=[pl.BlockSpec((1, 2, BLOCK, D), lambda g: (g, 0, 0, 0)), group_spec(OWN), group_spec(OWN)]
        + [full_spec(s) for s, kind in ends],
        out_shape=[
            jax.ShapeDtypeStruct((QUADS, 2, BLOCK, D), bf16),
            jax.ShapeDtypeStruct((rows, OWN), bf16),
            jax.ShapeDtypeStruct((rows, OWN), bf16),
        ]
        + [jax.ShapeDtypeStruct(s, kind) for s, kind in ends],
        scratch_shapes=[
            pltpu.VMEM((OWN, D), f32), pltpu.VMEM((D, OWN), f32),
            pltpu.VMEM((OWN, GROUP), bf16), pltpu.VMEM((GROUP, D), bf16),
        ],
        compiler_params=pltpu.CompilerParams(vmem_limit_bytes=VMEM_GRANT),
    )(lens, stats, *grouped, w_out, gain_out)


def backward_group(live, dmix, conv_in, raw, act, conv, heads, skip, between):
    raw_v = raw[...]
    heads_v = heads[...]
    step, logdec = steps_of(raw_v, heads_v, live)
    spread, gather = (head_spread(), head_gather())
    rows0 = slice(0, BLOCK)
    cumul0 = mm_left(low16(lower_mask().astype(jnp.float32)), logdec[rows0])
    cumul0_w = mm_right(cumul0, spread)
    weighting = jnp.exp(cumul0_w[BLOCK - 1 :] - cumul0_w) * mm_right(step[rows0], spread, 2)
    state = low16(
        t_mm(act[rows0, OWN : OWN + NST], low16(weighting * act[rows0, :OWN].astype(jnp.float32)))
    )
    late = backward_block(1, act, dmix, step, logdec, skip[...], state, None, spread, gather)
    between()
    early = backward_block(0, act, dmix, step, logdec, skip[...], None, late[6], spread, gather)
    grad_act = jnp.concatenate([jnp.concatenate(part[:3], axis=1) for part in (early, late)], axis=0)
    grad_step = jnp.concatenate([early[3], late[3]], axis=0)
    grad_logdec = jnp.concatenate([early[4], late[4]], axis=0)
    rate = jnp.exp(heads_v[1:2])
    grad_raw = (grad_step - rate * grad_logdec) * live * heads_v[3:4] * sigmoid(raw_v + heads_v[0:1])
    u = conv_in[...]
    conv_v = conv[...]
    preact = preact_of(u, conv_v)
    sig_q = sigmoid(preact)
    grad_pre = grad_act * (sig_q * (1.0 + preact * (1.0 - sig_q)))
    grad_u = grad_pre * conv_v[KCONV - 1 : KCONV]
    taps = []
    for tap in range(KCONV):
        lag = KCONV - 1 - tap
        if lag:
            grad_u = grad_u + shift_up(grad_pre, lag) * conv_v[tap : tap + 1]
        taps.append(jnp.sum(grad_pre * shift_down(u, lag), axis=0, keepdims=True))
    taps.append(jnp.sum(grad_pre, axis=0, keepdims=True))
    small = (
        jnp.concatenate(taps + [jnp.zeros((3, MIX), jnp.float32)], axis=0),
        jnp.sum(grad_raw, axis=0, keepdims=True),
        jnp.sum(grad_logdec * logdec, axis=0, keepdims=True),
        early[5] + late[5],
    )
    return (grad_u, grad_raw, small)


PACK = 48


def back_kernel(
    lens, gate_grads, out_grads, branch_all, w_gate, w_x, w_com, conv, heads, skip, select, gain_in, g_gain,
    tok_own, normed, dgate, dmix, proj_x, proj_com, act,
    r_out, all_gate, all_x, sum_com, packs, sum_branch, grad_rows,
    acc_x, acc_com, small_conv, small_head, small_skip,
    branch_own, branch_sib, en_part, en_sib, branch_got, en_got, branch_relay, en_relay,
    gate_got, gate_own, sum_gate, x_send, x_got, x_passed, sum_x, com_send, com_sib, com_quad, com_z, com_got,
    pack_send, pack_got, pack_sum,
    sends, recvs, out_send, out_recv, local
):
    s = pl.program_id(0)
    slot = QUADS - 1 - s
    plane, quad, core = place()
    where = (plane, quad, core)
    rank = 2 * quad + core
    sibling = at(plane, quad, flip(core))
    f32 = jnp.float32
    sems = Sems(sends, recvs)
    to_x, to_y = (at(plane, xor4(quad, 1), core), at(plane, xor4(quad, 2), core))
    half = BLOCK // 2

    swaps = [
        [sems.copy(branch_all.at[k, flip(core)], branch_sib.at[k], sibling) for k in range(QUADS)],
        [sems.copy(en_part.at[k % 2, flip(core)], en_sib.at[k], sibling) for k in range(QUADS)],
    ]
    routes = []
    for sib, got, relay in ((branch_sib, branch_got, branch_relay), (en_sib, en_got, en_relay)):
        routes.append(
            {
                "relay_x": sems.copy(sib.at[3, pl.ds(0, half)], relay.at[0], to_x),
                "relay_y": sems.copy(sib.at[3, pl.ds(half, half)], relay.at[1], to_y),
                "x": sems.copy(sib.at[1], got.at[0], to_x),
                "y": sems.copy(sib.at[2], got.at[1], to_y),
            }
        )

    def z_push(source, target):
        return [
            sems.copy(source.at[xor4(plane, k)], target.at[k - 1], at(xor4(plane, k), quad, core))
            for k in (2, 3, 1)
        ]

    def rank_push(source, target):
        copies = []
        for k in range(1, RANKS):
            other_core = flip(core) if k % 2 else core
            other_quad = xor4(quad, k // 2)
            copies.append(
                sems.copy(source(2 * other_quad + other_core), target.at[rank], at(plane, other_quad, other_core))
            )
        return copies

    gate_z = z_push(gate_grads, gate_got)
    x_z = z_push(x_send, x_got)
    x_relay = sems.copy(x_send.at[xor4(plane, 3)], x_passed, at(xor4(plane, 1), quad, core))
    at_end = plane % (PLANES - 1) == 0
    part_rows = D // PLANES
    gate_ranks = rank_push(lambda r: sum_gate.at[r], all_gate)
    x_ranks = rank_push(lambda r: sum_x.at[r], all_x)
    com_swap = sems.copy(com_send.at[:, :, flip(core)], com_sib, sibling)
    com_quads = [
        sems.copy(com_sib.at[:, xor4(quad, k)], com_quad.at[k - 1], at(plane, xor4(quad, k), core))
        for k in (3, 1, 2)
    ]
    com_planes = z_push(com_z, com_got)
    pack_z = [
        sems.copy(pack_send, pack_got.at[k - 1], at(xor4(plane, k), quad, core)) for k in (2, 3, 1)
    ]
    pack_ranks = rank_push(lambda r: pack_sum, packs)

    def out_copy(near, side):
        return pltpu.make_async_remote_copy(
            src_ref=out_grads.at[near, side],
            dst_ref=r_out.at[plane],
            send_sem=out_send.at[2 * near + side],
            recv_sem=out_recv.at[plane],
            device_id=at(2 * core + near, quad, side),
            device_id_type=MESH_ID,
        )

    def out_landing(origin):
        return pltpu.make_async_remote_copy(
            src_ref=out_grads.at[0, 0],
            dst_ref=r_out.at[origin],
            send_sem=out_send.at[0],
            recv_sem=out_recv.at[origin],
            device_id=sibling,
            device_id_type=MESH_ID,
        )

    out_here = pltpu.make_async_copy(out_grads.at[plane % 2, core], r_out.at[plane], local.at[0])
    out_stays = plane // 2 == core
    gate_here = pltpu.make_async_copy(gate_grads.at[plane], gate_own, local.at[1])
    branch_here = [
        pltpu.make_async_copy(branch_all.at[k, core], branch_own.at[k], local.at[5 + k]) for k in range(QUADS)
    ]

    @pl.when(s == 0)
    def begin():
        peers = plane_mates(*where) + plane_others(*where)
        peers += [at(xor4(plane, k), quad, flip(core)) for k in range(1, PLANES)]
        greet(peers)
        for copy in gate_z:
            copy.start()
        for copy in swaps[0][::-1]:
            copy.start()
        for near in range(2):
            for side in range(2):

                @pl.when(jnp.logical_not((2 * core + near == plane) & (core == side)))
                def go():
                    out_copy(near, side).start()

        @pl.when(out_stays)
        def stay():
            out_here.start()

        for copy in branch_here[::-1]:
            copy.start()
        gate_here.start()
        for ref in (acc_x, acc_com, small_conv, small_head, small_skip):
            ref[...] = jnp.zeros_like(ref)

    def settle(kind, k, own, sib):
        route = routes[kind]
        relay = (branch_relay, en_relay)[kind]
        swaps[kind][k].wait_recv()
        sib[k] = low16(own.astype(f32) + sib[k].astype(f32))
        if k == 3:
            route["relay_x"].start()
            route["relay_y"].start()
        if k == 2:
            route["relay_x"].wait_recv()
            sib[k, :half] = low16(sib[k, :half].astype(f32) + relay[0].astype(f32))
            route["y"].start()
        if k == 1:
            route["relay_y"].wait_recv()
            sib[k, half:] = low16(sib[k, half:].astype(f32) + relay[1].astype(f32))
            route["x"].start()

    def settle_branch(k):
        branch_here[k].wait()
        settle(0, k, branch_own[k], branch_sib)

    def between():
        for k in range(QUADS):

            @pl.when(slot == k)
            def sums():
                if k < QUADS - 1:
                    settle(1, k + 1, en_part[(k + 1) % 2, core], en_sib)
                if k == 3:
                    settle_branch(3)
                if k == 2:
                    settle_branch(1)

    live = live_of(lens[...], slot)
    conv_in = jnp.concatenate([proj_x[...], proj_com[:, : 2 * NST]], axis=1)
    raw = mm_right(proj_com[:, 2 * NST :], low16(select[...]))
    grad_u, grad_raw, small = backward_group(
        live, dmix, conv_in, raw, act, conv, heads, skip, between
    )
    small_conv[...] += small[0]
    small_head[0:1] += small[1]
    small_head[1:2] += small[2]
    small_skip[0:1] += small[3]
    raw_wide = mm_t(low16(grad_raw), low16(select[...]))
    grad_x = low16(grad_u[:, :OWN])
    grad_com = low16(jnp.concatenate([grad_u[:, OWN:], raw_wide], axis=1))
    normed_v = normed[...]
    acc_x[...] += t_mm(normed_v, grad_x)

    @pl.when(s == QUADS - 1)
    def send_x():
        x_send[...] = low16(acc_x[...]).reshape(x_send.shape)

        @pl.when(at_end)
        def from_end():
            x_relay.start()

        @pl.when(jnp.logical_not(at_end))
        def from_middle():
            x_z[1].start()
            x_z[2].start()

    acc_com[...] += t_mm(normed_v, grad_com)

    @pl.when(s == QUADS - 1)
    def send_com():
        com_send[...] = low16(acc_com[...]).reshape(com_send.shape)
        com_swap.start()

    for k in range(2):

        @pl.when(slot == k)
        def free():
            swaps[1][k + 2].wait_send()

    for side in range(2):
        rows = slice(side * BLOCK, (side + 1) * BLOCK)
        en_part[slot % 2, side] = low16(
            mm_t(dgate[rows], w_gate[...]) + mm_t(grad_x[rows], w_x[...]) + mm_t(grad_com[rows], w_com[...])
        )
    for k in range(QUADS):

        @pl.when(slot == k)
        def swap_en():
            swaps[1][k].start()

    for k, done in ((3, 2), (2, 0)):

        @pl.when(slot == k)
        def settle_late():
            settle_branch(done)

    @pl.when(s == QUADS - 1)
    def tail():
        @pl.when(at_end)
        def rest_from_end():
            x_relay.wait_send()
            x_z[0].start()
            x_z[2].start()

        @pl.when(jnp.logical_not(at_end))
        def pass_on():
            x_relay.wait_recv()
            far = xor4(plane, 2)
            x_send[far] = low16(x_send[far].astype(f32) + x_passed[...].astype(f32))
            x_z[0].start()

        settle(1, 0, en_part[0, core], en_sib)
        gate_here.wait()
        for copy in gate_z:
            copy.wait_recv()
        sum_gate[...] = low16(
            gate_own[...].astype(f32) + gate_got[0].astype(f32) + gate_got[1].astype(f32) + gate_got[2].astype(f32)
        )
        for copy in gate_ranks:
            copy.start()
        gate_keep = pltpu.make_async_copy(sum_gate.at[rank], all_gate.at[rank], local.at[2])
        gate_keep.start()
        com_swap.wait_recv()
        com_sib[...] = low16(com_sib[...].astype(f32) + com_send[:, :, core].astype(f32))
        for copy in com_quads:
            copy.start()
        for name in ("x", "y"):
            routes[0][name].wait_recv()
        sum_branch[...] = (
            branch_sib[0].astype(f32) + branch_got[0].astype(f32) + branch_got[1].astype(f32)
        )
        for copy in com_quads:
            copy.wait_recv()
        com_z[...] = low16(
            com_sib[:, quad].astype(f32)
            + com_quad[0].astype(f32) + com_quad[1].astype(f32) + com_quad[2].astype(f32)
        )
        for copy in com_planes:
            copy.start()
        for name in ("x", "y"):
            routes[1][name].wait_recv()
        en = en_sib[0].astype(f32) + en_got[0].astype(f32) + en_got[1].astype(f32)
        rows = tok_own[...].astype(f32)
        scaling = lax.rsqrt(jnp.mean(rows * rows, axis=1, keepdims=True) + norm_eps)
        scaled = rows * scaling
        gain_grad = jnp.sum(en * scaled, axis=0, keepdims=True)
        weighted = en * gain_in[...]
        inner = jnp.mean(weighted * scaled, axis=1, keepdims=True)
        grad_rows[...] = scaling * (weighted - scaled * inner)
        pack_send[...] = jnp.zeros_like(pack_send)
        for i in range(D // LANES):
            pack_send[i : i + 1] = gain_grad[:, i * LANES : (i + 1) * LANES]
        gain_out_grad = g_gain[0:1]
        skip_grad = small_skip[0:1]
        for i in range(PAIRS):
            lanes = slice(i * LANES, (i + 1) * LANES)
            pack_send[12 + i : 13 + i] = gain_out_grad[:, lanes]
            pack_send[42 + i : 43 + i] = skip_grad[:, lanes]
            for tap in range(KCONV + 1):
                pack_send[15 + 3 * tap + i : 16 + 3 * tap + i] = small_conv[tap : tap + 1, lanes]
        for tap in range(KCONV + 1):
            for i in range(2):
                lanes = slice(OWN + i * LANES, OWN + (i + 1) * LANES)
                pack_send[30 + 2 * tap + i : 31 + 2 * tap + i] = small_conv[tap : tap + 1, lanes]
        pack_send[40:42] = small_head[0:2]
        for copy in pack_z:
            copy.start()
        for copy in com_planes:
            copy.wait_recv()
        sum_com[...] = (
            com_z[plane].astype(f32)
            + com_got[0].astype(f32) + com_got[1].astype(f32) + com_got[2].astype(f32)
        )
        for copy in pack_z:
            copy.wait_recv()
        pack_sum[...] = pack_send[...] + pack_got[0] + pack_got[1] + pack_got[2]
        for copy in pack_ranks:
            copy.start()
        pack_keep = pltpu.make_async_copy(pack_sum, packs.at[rank], local.at[3])
        pack_keep.start()
        x_z[0].wait_recv()
        x_z[2].wait_recv()
        acc_x[:part_rows] = (
            x_send[plane].astype(f32) + x_got[0].astype(f32) + x_got[1].astype(f32)
        ).reshape(part_rows, OWN)

        @pl.when(jnp.logical_not(at_end))
        def one_more():
            x_z[1].wait_recv()
            acc_x[:part_rows] += x_got[2].astype(f32).reshape(part_rows, OWN)

        sum_x[...] = low16(acc_x[:part_rows]).reshape(sum_x.shape)
        for copy in x_ranks:
            copy.start()
        x_keep = pltpu.make_async_copy(sum_x.at[rank], all_x.at[rank], local.at[4])
        x_keep.start()
        for origin in range(PLANES):

            @pl.when(jnp.logical_not((plane == origin) & out_stays))
            def arrived():
                out_landing(origin).wait_recv()

        @pl.when(out_stays)
        def kept():
            out_here.wait()

        for near in range(2):
            for side in range(2):

                @pl.when(jnp.logical_not((2 * core + near == plane) & (core == side)))
                def gone():
                    out_copy(near, side).wait_send()

        for copy in gate_ranks + pack_ranks + x_ranks:
            copy.wait_recv()
        @pl.when(jnp.logical_not(at_end))
        def middle_sent():
            x_z[1].wait_send()

        for copy in gate_z + [x_z[0], x_z[2]] + gate_ranks + x_ranks + [com_swap] + com_quads + com_planes + pack_z + pack_ranks:
            copy.wait_send()
        for copy in swaps[0] + swaps[1][:2] + list(routes[0].values()) + list(routes[1].values()):
            copy.wait_send()
        gate_keep.wait()
        pack_keep.wait()
        x_keep.wait()


def run_back(lens, gate_grads, out_grads, branch, w_gate, w_x, w_com, conv, heads, skip, select, gain_in, g_gain, tok_own,
             normed, dgate, dmix, proj_x, proj_com, act):
    f32, bf16 = (jnp.float32, jnp.bfloat16)
    rows_in = D // (PLANES * RANKS)
    rows_out = DIN // (PLANES * RANKS)
    gate_grads = gate_grads.reshape(PLANES, RANKS, rows_in, OWN)
    out_grads = out_grads.reshape(2, 2, rows_out, D)
    fixed = (w_gate, w_x, w_com, conv, heads, skip, select, gain_in, g_gain, tok_own)
    grouped = (normed, dgate, dmix, proj_x, proj_com, act)

    def turned(width):
        return pl.BlockSpec((GROUP, width), lambda s: (QUADS - 1 - s, 0))

    outs = (
        ((PLANES, rows_out, D), bf16, ANY),
        ((RANKS, rows_in, OWN), bf16, ANY),
        ((RANKS, rows_in, OWN), bf16, ANY),
        ((rows_in, COMMON_PAD), f32, None),
        ((RANKS, PACK, LANES), f32, ANY),
        ((BLOCK, D), f32, None),
        ((BLOCK, D), f32, None),
    )
    half = BLOCK // 2
    quarter = (RANKS, rows_in, OWN)
    com = (rows_in, COMMON_PAD)
    scratch = [
        ((D, OWN), f32), ((D, COMMON_PAD), f32), ((8, MIX), f32), ((8, LANES), f32), ((8, OWN), f32),
        ((QUADS, BLOCK, D), bf16),
        ((QUADS, BLOCK, D), bf16), ((2, 2, BLOCK, D), bf16), ((QUADS, BLOCK, D), bf16),
        ((2, BLOCK, D), bf16), ((2, BLOCK, D), bf16), ((2, half, D), bf16), ((2, half, D), bf16),
        ((PLANES - 1,) + quarter, bf16), (quarter, bf16), (quarter, bf16),
        ((PLANES,) + quarter, bf16), ((PLANES - 1,) + quarter, bf16), (quarter, bf16), (quarter, bf16),
        ((PLANES, QUADS, 2) + com, bf16), ((PLANES, QUADS) + com, bf16), ((QUADS - 1, PLANES) + com, bf16),
        ((PLANES,) + com, bf16), ((PLANES - 1,) + com, bf16),
        ((PACK, LANES), f32), ((PLANES - 1, PACK, LANES), f32), ((PACK, LANES), f32),
    ]
    return pl.pallas_call(
        back_kernel,
        grid=(QUADS,),
        in_specs=[full_spec(lens.shape), ANY, ANY, ANY]
        + [full_spec(a.shape) for a in fixed]
        + [turned(a.shape[1]) for a in grouped],
        out_specs=[full_spec(s) if spec is None else spec for s, kind, spec in outs],
        out_shape=[jax.ShapeDtypeStruct(s, kind) for s, kind, spec in outs],
        scratch_shapes=[pltpu.VMEM(s, kind) for s, kind in scratch]
        + [
            pltpu.SemaphoreType.DMA((64,)),
            pltpu.SemaphoreType.DMA((64,)),
            pltpu.SemaphoreType.DMA((4,)),
            pltpu.SemaphoreType.DMA((4,)),
            pltpu.SemaphoreType.DMA((9,)),
        ],
        compiler_params=pltpu.CompilerParams(
            vmem_limit_bytes=VMEM_GRANT, collective_id=2, has_side_effects=True
        ),
    )(lens, gate_grads, out_grads, branch, *fixed, *grouped)


def adam_refs(refs, index, gradient, rate):
    weight, first, second, weight_new, first_new, second_new = refs
    results = adam_update(weight[index], first[index], second[index], gradient, rate)
    for ref, value in zip((weight_new, first_new, second_new), results):
        ref[index] = value


def finish_kernel(
    lens, tok, cot, sum_branch, grad_rows, r_out, all_gate, all_x, sum_com,
    in_w, in_m, in_v, out_w, out_m, out_v,
    mixed_out, grad_input, in_wn, in_mn, in_vn, out_wn, out_mn, out_vn
):
    f32 = jnp.float32
    core = lax.axis_index("seq")
    position = (iota((BLOCK, 1), 0) + core * BLOCK).astype(f32)
    live = (position < lens[0:1, 0:1]).astype(f32)
    mixed_out[...] = (tok[...].astype(f32) + live * sum_branch[...]).astype(jnp.bfloat16)
    grad_input[...] = cot[...].astype(f32) + grad_rows[...]
    ins = (in_w, in_m, in_v, in_wn, in_mn, in_vn)
    rows = in_w.shape[0]
    lanes = iota((rows, LANES), 1)
    for part, source in ((0, all_gate), (1, all_x)):
        for run in range(PLANES):
            side, near = divmod(run, 2)
            tiles = []
            for t in range(2 * PAIRS):
                halves = []
                for b in range(2):
                    p, i = divmod(2 * t + b, 3)
                    index = 3 * near + i
                    tile = source[2 * p + side, :, (index // 2) * LANES : (index // 2 + 1) * LANES].astype(f32)
                    halves.append(tile if index % 2 == b else pltpu.roll(tile, HDIM, 1))
                tiles.append(jnp.where(lanes < HDIM, halves[0], halves[1]))
            start = part * DIN + run * 2 * OWN
            adam_refs(ins, (slice(None), slice(start, start + 2 * OWN)), jnp.concatenate(tiles, axis=1), rate_in)
    adam_refs(ins, (slice(None), slice(2 * DIN, 2 * DIN + COMMON)), sum_com[:, :COMMON], rate_in)
    total = r_out[0].astype(f32) + r_out[1].astype(f32) + r_out[2].astype(f32) + r_out[3].astype(f32)
    adam_refs((out_w, out_m, out_v, out_wn, out_mn, out_vn), (slice(None), slice(None)), total, rate_out)


def run_finish(*args):
    tok, cot, in_w, out_w = (args[1], args[2], args[9], args[12])
    shapes = [(tok.shape, jnp.bfloat16), (cot.shape, jnp.float32)]
    shapes += [(in_w.shape, jnp.float32)] * 3 + [(out_w.shape, jnp.float32)] * 3
    whole = pl.BlockSpec(memory_space=pltpu.VMEM)
    return pl.pallas_call(
        finish_kernel,
        in_specs=[whole] * len(args),
        out_specs=[whole] * len(shapes),
        out_shape=[jax.ShapeDtypeStruct(s, kind) for s, kind in shapes],
        compiler_params=pltpu.CompilerParams(vmem_limit_bytes=VMEM_GRANT),
    )(*args)


def pick_runs(array, plane_runs, quad, core):
    lead = array.shape[:-1]
    width = array.shape[-1] // (PLANES * QUADS)
    split = array.reshape(lead + (2, 2, QUADS, width))
    zero = 0
    n = len(lead)
    taken = lax.dynamic_slice(
        split, (zero,) * n + (core, 0, quad, 0), lead + (1, 2, 1, width)
    )
    return taken.reshape(lead + (2 * width,))


def put_runs(array, quad, core):
    lead = array.shape[:-1]
    width = array.shape[-1] // 2
    zeros = jnp.zeros(lead + (2, 2, QUADS, width), array.dtype)
    n = len(lead)
    full = lax.dynamic_update_slice(
        zeros, array.reshape(lead + (1, 2, 1, width)), (0,) * n + (core, 0, quad, 0)
    )
    return full.reshape(lead + (width * PLANES * QUADS,))


def rank_slices(array):
    rows = array.shape[0]
    split = array.reshape(rows, 2, 2, QUADS, RUN)
    return split.transpose(3, 1, 0, 2, 4).reshape(RANKS, rows, OWN)


def rank_join(array):
    rows = array.shape[1]
    split = array.reshape(QUADS, 2, rows, 2, RUN)
    return split.transpose(2, 1, 3, 0, 4).reshape(rows, DIN)


def per_device_quad(
    tokens_in,
    cotangent,
    seq_lens,
    in_weight,
    in_first,
    in_second,
    out_weight,
    out_first,
    out_second,
    conv_weight,
    conv_first,
    conv_second,
    gains,
    gain_first,
    gain_second,
    head_params,
    head_first,
    head_second,
):
    plane, quad, core = place()
    rank = 2 * quad + core
    (
        normed, cot, w_gate, w_x, w_com, w_out, gate_part, proj_x, proj_com, act, mixed, grad_normed_out,
        stats, gain_in, gain_out, conv, heads, skip, select, lens
    ) = run_fore(tokens_in, cotangent, seq_lens, in_weight, out_weight, conv_weight, gains, head_params)
    branch, dgate, dmix, g_out, g_gate, g_gain = run_gate(
        lens, stats, cot, normed, gate_part, mixed, grad_normed_out, w_out, gain_out
    )
    r_out, all_gate, all_x, sum_com, packs, sum_branch, grad_rows = run_back(
        lens, g_gate, g_out, branch, w_gate, w_x, w_com, conv, heads, skip, select, gain_in, g_gain,
        tokens_in, normed, dgate, dmix, proj_x, proj_com, act
    )
    finished = run_finish(
        lens, tokens_in, cotangent, sum_branch, grad_rows, r_out, all_gate, all_x, sum_com,
        in_weight, in_first, in_second, out_weight, out_first, out_second
    )
    mine = rank + RANKS * plane
    grad_gains = jnp.concatenate(
        [jnp.sum(packs[:, :12], axis=0).reshape(D), rank_join(packs[:, 12:15].reshape(RANKS, 1, OWN)).reshape(DIN)]
    )
    gain_sum = lax.dynamic_slice(grad_gains, (mine * gains.shape[0],), gains.shape)
    grad_conv = jnp.concatenate(
        [
            rank_join(packs[:, 15:30].reshape(RANKS, KCONV + 1, OWN)),
            jnp.sum(packs[:, 30:40], axis=0).reshape(KCONV + 1, 2 * NST),
        ],
        axis=1,
    )
    conv_sum = lax.dynamic_slice(grad_conv, (0, mine * conv_weight.shape[1]), conv_weight.shape)
    grad_skip = jnp.sum(packs[:, 42:45].reshape(RANKS, 1, OWN_HEADS, HDIM), axis=3)
    head_sum = jnp.concatenate([packs[:, 40:42, :OWN_HEADS], grad_skip], axis=1)
    head_sum = head_sum.reshape(QUADS, 2, 3, 2, 3).transpose(2, 1, 3, 0, 4).reshape(3, HEADS)
    new_conv = adam_update(conv_weight, conv_first, conv_second, conv_sum, rate_conv)
    new_gain = adam_update(gains, gain_first, gain_second, gain_sum, rate_gain)
    new_head = adam_update(head_params, head_first, head_second, head_sum, rate_head)
    return tuple(finished) + new_conv + new_gain + new_head


def solution(mesh):
    placed = (
        P(("dp", "seq"), None),
        P(("dp", "seq"), None),
        P("dp", None),
        P(("dp", "seq"), None),
        P(("dp", "seq"), None),
        P(("dp", "seq"), None),
        P(("dp", "seq"), None),
        P(("dp", "seq"), None),
        P(("dp", "seq"), None),
        P(None, ("dp", "seq")),
        P(None, ("dp", "seq")),
        P(None, ("dp", "seq")),
        P(("dp", "seq")),
        P(("dp", "seq")),
        P(("dp", "seq")),
        P(),
        P(),
        P(),
    )
    quad = dict(mesh.shape) == {"dp": PLANES * QUADS, "seq": 2}
    return jax.shard_map(
        per_device_quad if quad else per_device,
        mesh=mesh,
        in_specs=placed,
        out_specs=(
            P(("dp", "seq"), None),
            P(("dp", "seq"), None),
            P(("dp", "seq"), None),
            P(("dp", "seq"), None),
            P(("dp", "seq"), None),
            P(("dp", "seq"), None),
            P(("dp", "seq"), None),
            P(("dp", "seq"), None),
            P(None, ("dp", "seq")),
            P(None, ("dp", "seq")),
            P(None, ("dp", "seq")),
            P(("dp", "seq")),
            P(("dp", "seq")),
            P(("dp", "seq")),
            P(),
            P(),
            P(),
        ),
        check_vma=False,
    )
```

```python
import functools

import jax
import jax.numpy as jnp
from jax import lax
from jax.experimental import pallas as pl
from jax.experimental.pallas import tpu as pltpu
from jax.sharding import PartitionSpec as P

D = 1536
HEADS = 48
HDIM = 64
NST = 128
KCONV = 4
BLOCK = 256
SLOTS = 4
STEP = 10
DIN = 3072
CONVC = 3328


highest = lax.Precision.HIGHEST
norm_eps = 1e-05
beta_first = 0.9
beta_second = 0.95
adam_eps = 1e-08
weight_decay = 0.1
rate_in = 0.01
rate_out = 0.008
rate_conv = 0.2
rate_gain = 0.4
rate_head = 0.5


def from_behind(block, axis, distance):
    devices = range(lax.axis_size(axis))
    route = [(i - distance, i) for i in devices if i - distance in devices]
    return lax.ppermute(block, axis, route)


def prefix(value, axis, join, neutral):
    place = lax.axis_index(axis)
    gathered = jax.tree.map(
        lambda a, kind: lax.all_gather(a.astype(kind), axis),
        value,
        jax.tree.map(lambda a: jnp.bfloat16 if a.dtype == jnp.float32 else a.dtype, value),
    )
    state = jax.tree.map(lambda a, e: jnp.zeros_like(a) + jnp.asarray(e, a.dtype), value, neutral)

    def one(hop, state):
        return join(
            state,
            jax.tree.map(
                lambda a, own: lax.dynamic_index_in_dim(a, hop, 0, False).astype(own.dtype),
                gathered,
                value,
            ),
        )

    return lax.fori_loop(0, place, one, state)


def prefix_2(value, axis, combine, identity):
    devices, index = (lax.axis_size(axis), lax.axis_index(axis))
    everything = jax.tree.map(
        lambda part, kind: lax.all_gather(part.astype(kind), axis),
        value,
        (jnp.bfloat16, jnp.bfloat16),
    )
    start = jax.tree.map(
        lambda part, zero: jnp.broadcast_to(jnp.asarray(zero, part.dtype), part.shape),
        value,
        identity,
    )

    def hop(k, before):
        at = devices - 1 - k
        reached = at > index
        new = combine(
            before, jax.tree.map(lambda part, own: part[at].astype(own.dtype), everything, value)
        )
        return jax.tree.map(lambda a, b: jnp.where(reached, a, b), new, before)

    return lax.fori_loop(0, devices, hop, start)


def segment_of(seq_row, position):
    blocks = (seq_row + BLOCK - 1) // BLOCK
    ends = jnp.cumsum(blocks) * BLOCK
    starts = ends - blocks * BLOCK
    above = position[:, None] >= starts[None, :]
    inside = above & (position[:, None] < ends[None, :])
    numbers = jnp.arange(1, SLOTS + 1, dtype=jnp.int32)
    labels_of = jnp.sum(jnp.where(inside, numbers[None, :], 0), axis=1)
    live_rows = jnp.sum(
        (above & (position[:, None] < (starts + seq_row)[None, :])).astype(jnp.float32), axis=1
    )
    return (labels_of, live_rows)


def layout(seq_row, position):
    labels_of, live_rows = segment_of(seq_row, position)
    columns = []
    for conv_lag in range(KCONV):
        earlier, unused_live = segment_of(seq_row, position - conv_lag)
        columns.append(((earlier == labels_of) & (labels_of > 0)).astype(jnp.float32))
    return (live_rows, jnp.stack(columns, axis=1))


def pre_norm(token_rows, gain_row):
    scaling = lax.rsqrt(jnp.mean(token_rows * token_rows, axis=1, keepdims=True) + norm_eps)
    return token_rows * scaling * gain_row[None, :]


def gate_norm(mixed, gate_part, gain_row):
    gated = mixed * jax.nn.silu(gate_part)
    scaling = lax.rsqrt(jnp.mean(gated * gated, axis=1, keepdims=True) + norm_eps)
    return gated * scaling * gain_row[None, :]


def mixer_in(extended, step_raw, conv_par, head_values, factors, live_rows):
    row_count = step_raw.shape[0]
    preact = jnp.zeros((row_count, conv_par.shape[1]), jnp.float32) + conv_par[KCONV][None, :]
    for conv_tap in range(KCONV):
        window = lax.slice_in_dim(extended, conv_tap, conv_tap + row_count, axis=0)
        preact = (
            preact
            + conv_par[conv_tap][None, :] * window * factors[:, KCONV - 1 - conv_tap][:, None]
        )
    conv_act = jax.nn.silu(preact)
    step_size = jax.nn.softplus(step_raw + head_values[0][None, :]) * live_rows[:, None]
    logdec = -jnp.exp(head_values[1])[None, :] * step_size
    return (conv_act, step_size, logdec)


def lower_ones():
    row_ids = lax.broadcasted_iota(jnp.int32, (BLOCK, BLOCK), 0)
    col_ids = lax.broadcasted_iota(jnp.int32, (BLOCK, BLOCK), 1)
    return (row_ids >= col_ids).astype(jnp.float32)


def block_state(values, keys_in, step_size, logdec):
    cumul = jnp.dot(lower_ones(), logdec, precision=highest)
    totals = cumul[-1]
    weighting = jnp.exp(totals[None, :] - cumul) * step_size
    states = jnp.einsum("uhp,un->hpn", weighting[:, :, None] * values, keys_in, precision=highest)
    return (jnp.exp(totals), states)


def block_out(values, keys_in, queries, step_size, logdec, skip_gain, start_state):
    lower_tri = lower_ones()
    cumul = jnp.dot(lower_tri, logdec, precision=highest)
    across = cumul.T
    gap_matrix = across[:, :, None] - across[:, None, :]
    decays = jnp.exp(jnp.where(lower_tri[None, :, :] > 0, gap_matrix, -1e30))
    gram_matrix = jnp.dot(queries, keys_in.T, precision=highest)
    mixing = gram_matrix[None, :, :] * decays * step_size.T[:, None, :]
    intra_part = jnp.einsum("htu,uhp->thp", mixing, values, precision=highest)
    carried = jnp.exp(cumul)[:, :, None] * jnp.einsum(
        "tn,hpn->thp", queries, start_state, precision=highest
    )
    return intra_part + carried + skip_gain[None, :, None] * values


def block_full(values, keys_in, queries, step_size, logdec, skip_gain, start_state):
    factor_end, states = block_state(values, keys_in, step_size, logdec)
    outputs = block_out(values, keys_in, queries, step_size, logdec, skip_gain, start_state)
    return (outputs, factor_end[:, None, None] * start_state + states)


def adam_update(weight, first, second, gradient, step_rate):
    first_new = beta_first * first + (1.0 - beta_first) * gradient
    second_new = beta_second * second + (1.0 - beta_second) * gradient * gradient
    first_hat = first_new / (1.0 - beta_first**STEP)
    second_hat = second_new / (1.0 - beta_second**STEP)
    weight_new = weight - step_rate * (
        first_hat / (jnp.sqrt(second_hat) + adam_eps) + weight_decay * weight
    )
    return (weight_new, first_new, second_new)


def carry_join(earlier, later):
    return (earlier[0] * later[0], later[0][:, None, None] * earlier[1] + later[1])


def as_float(array_low):
    return lax.optimization_barrier(array_low).astype(jnp.float32)


def contract_rows(left, right):
    return lax.dot_general(
        left, right, (((0,), (0,)), ((), ())), preferred_element_type=jnp.float32
    )


def contract_cols(left, right):
    return lax.dot_general(
        left, right, (((1,), (1,)), ((), ())), preferred_element_type=jnp.float32
    )


def per_device(
    tokens_in,
    cotangent,
    seq_lens,
    in_weight,
    in_first,
    in_second,
    out_weight,
    out_first,
    out_second,
    conv_weight,
    conv_first,
    conv_second,
    gains,
    gain_first,
    gain_second,
    head_params,
    head_first,
    head_second,
):
    local_tok = tokens_in.shape[0]
    position = lax.axis_index("seq") * local_tok + jnp.arange(local_tok, dtype=jnp.int32)
    live_rows, factors = layout(seq_lens[0], position)
    low_weights = (
        in_weight.astype(jnp.bfloat16),
        out_weight.astype(jnp.bfloat16),
        conv_weight.astype(jnp.bfloat16),
        gains.astype(jnp.bfloat16),
    )
    in_full, out_full, conv_full, gain_full = (
        lax.all_gather(low_weights[0], ("dp", "seq"), axis=0, tiled=True),
        lax.all_gather(low_weights[1], ("dp", "seq"), axis=0, tiled=True),
        lax.all_gather(low_weights[2], ("dp", "seq"), axis=1, tiled=True),
        lax.all_gather(low_weights[3], ("dp", "seq"), axis=0, tiled=True),
    )
    conv_par = conv_full.astype(jnp.float32)
    gain_par = gain_full.astype(jnp.float32)
    token_rows = tokens_in.astype(jnp.float32)
    normed_value, pull_pre = jax.vjp(pre_norm, token_rows, gain_par[:D])
    normed = normed_value.astype(jnp.bfloat16)
    projected = jnp.dot(normed, in_full, preferred_element_type=jnp.float32)
    gate_part = projected[:, :DIN]
    conv_in = projected[:, DIN : DIN + CONVC]
    step_raw = projected[:, DIN + CONVC :]
    halo_rows = from_behind(conv_in[local_tok - KCONV + 1 :], "seq", 1)
    extended = jnp.concatenate([halo_rows, conv_in], axis=0)

    def mixer_local(extended_rows, raw_steps, conv_values, head_values):
        return mixer_in(extended_rows, raw_steps, conv_values, head_values, factors, live_rows)

    (conv_act, step_size, logdec), pull_mixer = jax.vjp(
        mixer_local, extended, step_raw, conv_par, head_params
    )
    conv_used = as_float(conv_act.astype(jnp.bfloat16))
    block_count = local_tok // BLOCK
    values = conv_used[:, :DIN].reshape(block_count, BLOCK, HEADS, HDIM)
    keys_in = conv_used[:, DIN : DIN + NST].reshape(block_count, BLOCK, NST)
    queries = conv_used[:, DIN + NST :].reshape(block_count, BLOCK, NST)
    steps_blk = step_size.reshape(block_count, BLOCK, HEADS)
    logdec_blk = logdec.reshape(block_count, BLOCK, HEADS)
    resets = factors[::BLOCK, 1]
    skip_gain = head_params[2]
    decays, block_states = jax.vmap(block_state)(values, keys_in, steps_blk, logdec_blk)

    def fold_local(carried, block_item):
        factor_now = block_item[0] * block_item[2]
        return (
            (carried[0] * factor_now, factor_now[:, None, None] * carried[1] + block_item[1]),
            None,
        )

    identity = (jnp.ones((HEADS,), jnp.float32), jnp.zeros((HEADS, HDIM, NST), jnp.float32))
    device_sum, unused_fold = lax.scan(fold_local, identity, (decays, block_states, resets))
    unused_dec, entering = prefix(device_sum, "seq", carry_join, identity)

    def start_states(states, block_item):
        begin = block_item[2] * states
        return (block_item[0][:, None, None] * begin + block_item[1], begin)

    unused_end, begins = lax.scan(start_states, entering, (decays, block_states, resets))

    def emit(block_item):
        return block_out(
            block_item[0],
            block_item[1],
            block_item[2],
            block_item[3],
            block_item[4],
            skip_gain,
            block_item[5],
        )

    mixed = lax.map(emit, (values, keys_in, queries, steps_blk, logdec_blk, begins)).reshape(
        local_tok, DIN
    )
    normed_out_value, pull_gate = jax.vjp(gate_norm, mixed, gate_part, gain_par[D:])
    normed_out = normed_out_value.astype(jnp.bfloat16)
    branch = jnp.dot(normed_out, out_full, preferred_element_type=jnp.float32)
    mixed_out = (token_rows + live_rows[:, None] * branch).astype(jnp.bfloat16)
    out_grad = (cotangent.astype(jnp.float32) * live_rows[:, None]).astype(jnp.bfloat16)
    in_back, out_back = (
        lax.all_gather(in_weight.astype(jnp.bfloat16), ("dp", "seq"), axis=0, tiled=True),
        lax.all_gather(out_weight.astype(jnp.bfloat16), ("dp", "seq"), axis=0, tiled=True),
    )
    grad_out_w = contract_rows(normed_out, out_grad)
    grad_normed_out = contract_cols(out_grad, out_back)
    grad_mixed, grad_gate, grad_gain_in = pull_gate(grad_normed_out)
    mixed_back = as_float(grad_mixed.astype(jnp.bfloat16)).reshape(block_count, BLOCK, HEADS, HDIM)

    def adjoint_local(carried, block_item):
        cumul = jnp.dot(lower_ones(), block_item[2], precision=highest)
        weighted = jnp.exp(cumul)[:, :, None] * block_item[0]
        direct = jnp.einsum("thp,tn->hpn", weighted, block_item[1], precision=highest)
        return (block_item[4] * (direct + block_item[3][:, None, None] * carried), None)

    local_adj, unused_adj = lax.scan(
        adjoint_local, identity[1], (mixed_back, queries, logdec_blk, decays, resets), reverse=True
    )
    unused_later, leaving = prefix_2((device_sum[0], local_adj), "seq", carry_join, identity)

    def adjoint_block(carried, block_item):
        unused_primal, pull_block = jax.vjp(
            block_full,
            block_item[0],
            block_item[1],
            block_item[2],
            block_item[3],
            block_item[4],
            skip_gain,
            block_item[5],
        )
        grads = pull_block((block_item[6], carried[0]))
        return ((block_item[7] * grads[6], carried[1] + grads[5]), grads[:5])

    (unused_state, grad_skip), block_grads = lax.scan(
        adjoint_block,
        (leaving, jnp.zeros((HEADS,), jnp.float32)),
        (values, keys_in, queries, steps_blk, logdec_blk, begins, mixed_back, resets),
        reverse=True,
    )
    grad_values, grad_keys, grad_queries, grad_step, grad_logdec = block_grads
    grad_act = jnp.concatenate(
        [
            grad_values.reshape(local_tok, DIN),
            grad_keys.reshape(local_tok, NST),
            grad_queries.reshape(local_tok, NST),
        ],
        axis=1,
    )
    grad_ext, grad_raw, grad_conv, grad_head_part = pull_mixer(
        (grad_act, grad_step.reshape(local_tok, HEADS), grad_logdec.reshape(local_tok, HEADS))
    )
    returned = from_behind(grad_ext[: KCONV - 1].astype(jnp.bfloat16), "seq", -1).astype(
        jnp.float32
    )
    grad_conv_in = grad_ext[KCONV - 1 :] + jnp.concatenate(
        [jnp.zeros((local_tok - KCONV + 1, CONVC), jnp.float32), returned], axis=0
    )
    grad_proj = jnp.concatenate([grad_gate, grad_conv_in, grad_raw], axis=1).astype(jnp.bfloat16)
    grad_normed = contract_cols(grad_proj, in_back)
    grad_rows, grad_gain_pre = pull_pre(grad_normed)
    grad_input = cotangent.astype(jnp.float32) + grad_rows
    grad_gains = jnp.concatenate([grad_gain_pre, grad_gain_in], axis=0)
    grad_head = jnp.concatenate(
        [grad_head_part[:2], (grad_head_part[2] + grad_skip)[None, :]], axis=0
    )
    grad_in_w = contract_rows(normed, grad_proj)
    in_sum, out_sum, conv_sum, gain_sum = (
        lax.psum_scatter(grad_in_w, ("dp", "seq"), scatter_dimension=0, tiled=True),
        lax.psum_scatter(grad_out_w, ("dp", "seq"), scatter_dimension=0, tiled=True),
        lax.psum_scatter(grad_conv, ("dp", "seq"), scatter_dimension=1, tiled=True),
        lax.psum_scatter(grad_gains, ("dp", "seq"), scatter_dimension=0, tiled=True),
    )
    head_sum = lax.psum(grad_head, ("dp", "seq"))
    new_in = adam_update(in_weight, in_first, in_second, in_sum, rate_in)
    new_out = adam_update(out_weight, out_first, out_second, out_sum, rate_out)
    new_conv = adam_update(conv_weight, conv_first, conv_second, conv_sum, rate_conv)
    new_gain = adam_update(gains, gain_first, gain_second, gain_sum, rate_gain)
    new_head = adam_update(head_params, head_first, head_second, head_sum, rate_head)
    return (
        mixed_out,
        grad_input,
        new_in[0],
        new_in[1],
        new_in[2],
        new_out[0],
        new_out[1],
        new_out[2],
        new_conv[0],
        new_conv[1],
        new_conv[2],
        new_gain[0],
        new_gain[1],
        new_gain[2],
        new_head[0],
        new_head[1],
        new_head[2],
    )


MESH_ID = pl.DeviceIdType.MESH
ANY = pl.BlockSpec(memory_space=pl.ANY)
PLANES = 4
QUADS = 4
RANKS = 8


def place():
    chip = lax.axis_index("dp")
    return (chip // QUADS, chip % QUADS, lax.axis_index("seq"))


def at(plane, quad, core):
    return (plane * QUADS + quad, core)


def flip(core):
    return 1 - core


def xor4(value, k):
    low, high = value % 2, value // 2
    if k % 2:
        low = 1 - low
    if k // 2:
        high = 1 - high
    return 2 * high + low


def greet(devices):
    barrier = pltpu.get_barrier_semaphore()
    for device in devices:
        pl.semaphore_signal(barrier, inc=1, device_id=device, device_id_type=MESH_ID)
    pl.semaphore_wait(barrier, len(devices))


def plane_mates(plane, quad, core):
    mates = []
    for k in range(QUADS):
        for other in (core, flip(core)):
            if not (k == 0 and other is core):
                mates.append(at(plane, xor4(quad, k), other))
    return mates


def plane_others(plane, quad, core):
    return [at(xor4(plane, k), quad, core) for k in range(1, PLANES)]


class Sems:
    def __init__(self, send, recv):
        self.send, self.recv, self.used = (send, recv, 0)

    def copy(self, source, target, device):
        index = self.used
        self.used += 1
        return pltpu.make_async_remote_copy(
            src_ref=source,
            dst_ref=target,
            send_sem=self.send.at[index],
            recv_sem=self.recv.at[index],
            device_id=device,
            device_id_type=MESH_ID,
        )


class PlaneGather:
    def __init__(self, sems, own, land, plane, quad, core):
        near_x, near_y, far = (xor4(quad, k) for k in (1, 2, 3))
        rank, rank_x, rank_y, rank_far = (2 * q + core for q in (quad, near_x, near_y, far))
        to_x, to_y = (at(plane, near_x, core), at(plane, near_y, core))
        sibling = at(plane, quad, flip(core))
        whole = [0, 1]
        self.own = [
            sems.copy(own(h), land(rank, slot, h), device)
            for device, slot in ((to_x, 1), (to_y, 2), (sibling, 0))
            for h in whole
        ]
        self.relay_x = [
            sems.copy(land(rank_x, 1, 0), land(rank_x, 3, 0), to_y),
        ] + [sems.copy(land(rank_x, 1, h), land(rank_x, 1, h), sibling) for h in whole]
        self.relay_y = [
            sems.copy(land(rank_y, 2, 1), land(rank_y, 3, 1), to_x),
        ] + [sems.copy(land(rank_y, 2, h), land(rank_y, 2, h), sibling) for h in whole]
        self.relay_far = [
            sems.copy(land(rank_far, 3, h), land(rank_far, 3, h), sibling) for h in whole
        ]

    def start(self):
        for copy in self.own:
            copy.start()

    def near(self):
        self.own[0].wait_recv()
        self.relay_x[0].start()
        self.own[3].wait_recv()
        self.relay_y[0].start()
        self.own[1].wait_recv()
        self.own[2].wait_recv()
        for copy in self.relay_x[1:] + self.relay_y[1:]:
            copy.start()

    def across(self):
        for h, relay in ((0, self.relay_x[0]), (1, self.relay_y[0])):
            relay.wait_recv()
            self.relay_far[h].start()

    def wait_slot(self, slot):
        for copy in (self.own[4:], self.relay_x[1:], self.relay_y[1:], self.relay_far)[slot]:
            copy.wait_recv()

    def sent(self):
        for copy in self.own + self.relay_x + self.relay_y + self.relay_far:
            copy.wait_send()


class LineGather:
    def __init__(self, sems, own, block, plane, quad, core):
        self.plane = plane
        self.right, self.left = ([], [])
        for hop in range(PLANES - 1):
            for copies, step in ((self.right, 1), (self.left, -1)):
                index = plane - step * hop
                source = own if hop == 0 else block(index)
                copies.append(sems.copy(source, block(index), at(plane + step, quad, core)))

    def sends(self, hop, step):
        if step > 0:
            return (self.plane - hop >= 0) & (self.plane < PLANES - 1)
        return (self.plane + hop < PLANES) & (self.plane > 0)

    def receives(self, hop, step):
        if step > 0:
            return self.plane - 1 - hop >= 0
        return self.plane + 1 + hop < PLANES

    def start(self, hop):
        for copies, step in ((self.right, 1), (self.left, -1)):

            @pl.when(self.sends(hop, step))
            def go():
                copies[hop].start()

    def arrive(self, hop):
        for copies, step in ((self.right, 1), (self.left, -1)):

            @pl.when(self.receives(hop, step))
            def landed():
                copies[hop].wait_recv()

    def sent(self):
        for hop in range(PLANES - 1):
            for copies, step in ((self.right, 1), (self.left, -1)):

                @pl.when(self.sends(hop, step))
                def left():
                    copies[hop].wait_send()


OWN_HEADS = HEADS // RANKS
OWN = OWN_HEADS * HDIM
PAIRS = OWN_HEADS // 2
RUN = OWN // 2
COMMON = 2 * NST + HEADS
COMMON_PAD = 384
GROUP = 2 * BLOCK
MIX = OWN + 2 * NST
LANES = 128
STRIP = 128


def mm(left, right):
    return lax.dot_general(left, right, (((1,), (0,)), ((), ())), preferred_element_type=jnp.float32)


def mm_t(left, right):
    return lax.dot_general(left, right, (((1,), (1,)), ((), ())), preferred_element_type=jnp.float32)


def t_mm(left, right):
    return lax.dot_general(left, right, (((0,), (0,)), ((), ())), preferred_element_type=jnp.float32)


def mm_full(left, right):
    return lax.dot_general(
        left, right, (((1,), (0,)), ((), ())), precision=highest, preferred_element_type=jnp.float32
    )


def low16(value):
    return value.astype(jnp.bfloat16)


def parts_of(value, terms):
    parts = []
    for unused in range(terms):
        parts.append(low16(value))
        value = value - parts[-1].astype(jnp.float32)
    return parts


def mm_right(left, ones, terms=3):
    return sum(mm(part, ones) for part in parts_of(left, terms))


def mm_left(ones, right, terms=3):
    return sum(mm(ones, part) for part in parts_of(right, terms))


def iota(shape, axis):
    return lax.broadcasted_iota(jnp.int32, shape, axis)


def head_spread():
    return low16((iota((LANES, OWN), 1) // HDIM == iota((LANES, OWN), 0)).astype(jnp.float32))


def head_gather():
    return low16((iota((OWN, LANES), 0) // HDIM == iota((OWN, LANES), 1)).astype(jnp.float32))


def lower_mask():
    return iota((BLOCK, BLOCK), 0) >= iota((BLOCK, BLOCK), 1)


def shift_down(value, k):
    if k == 0:
        return value
    rolled = pltpu.roll(value, k, 0)
    return jnp.where(iota(value.shape, 0) >= k, rolled, 0.0)


def shift_up(value, k):
    if k == 0:
        return value
    rows = value.shape[0]
    rolled = pltpu.roll(value, rows - k, 0)
    return jnp.where(iota(value.shape, 0) < rows - k, rolled, 0.0)


def sigmoid(value):
    return 1.0 / (1.0 + jnp.exp(-value))


def softplus(value):
    return jnp.maximum(value, 0.0) + jnp.log1p(jnp.exp(-jnp.abs(value)))


def preact_of(u, conv):
    total = u * conv[KCONV - 1 : KCONV] + conv[KCONV : KCONV + 1]
    for tap in range(KCONV - 1):
        total = total + shift_down(u, KCONV - 1 - tap) * conv[tap : tap + 1]
    return total


def steps_of(raw, heads, live):
    step = softplus(raw + heads[0:1]) * live * heads[3:4]
    return (step, -jnp.exp(heads[1:2]) * step)


def lane_half(value, side):
    lanes = iota(value.shape, 1)
    return jnp.where((lanes >= HDIM) == (side == 1), value, jnp.zeros_like(value))


def block_parts(step, logdec, spread):
    cumul = mm_left(low16(lower_mask().astype(jnp.float32)), logdec)
    return (cumul, jnp.transpose(cumul), mm_right(step, spread, 2), mm_right(cumul, spread))


def ssd_forward(act, step, logdec, skip, out):
    spread = head_spread()
    lower = lower_mask()
    state = None
    for k in range(2):
        rows = slice(k * BLOCK, (k + 1) * BLOCK)
        values, keys, queries = (act[rows, :OWN], act[rows, OWN : OWN + NST], act[rows, OWN + NST :])
        cumul, cumul_t, step_w, cumul_w = block_parts(step[rows], logdec[rows], spread)
        gram = jnp.where(lower, mm_t(queries, keys), 0.0)
        values_f = values.astype(jnp.float32)
        stepped = low16(values_f * step_w)
        base = skip * values_f
        if state is not None:
            base = base + jnp.exp(cumul_w) * mm(queries, state)
        else:
            weighting = jnp.exp(cumul_w[BLOCK - 1 :] - cumul_w) * step_w
            state = low16(t_mm(keys, low16(weighting * values_f)))

        for pair in range(PAIRS):
            lanes = slice(pair * LANES, (pair + 1) * LANES)
            sides = [lane_half(stepped[:, lanes], side) for side in range(2)]
            for start in range(0, BLOCK, STRIP):
                strip, wide = (slice(start, start + STRIP), start + STRIP)
                piece = base[strip, lanes]
                for side in range(2):
                    h = 2 * pair + side
                    decay = jnp.exp(jnp.minimum(cumul[strip, h : h + 1] - cumul_t[h : h + 1, :wide], 0.0))
                    piece = piece + mm(low16(gram[strip, :wide] * decay), sides[side][:wide])
                out[k * BLOCK + start : k * BLOCK + wide, lanes] = piece


def live_of(lens, g):
    rows = iota((GROUP, 1), 0).astype(jnp.float32)
    chosen = jnp.sum(jnp.where(iota(lens.shape, 0) == g, lens, 0.0), axis=0, keepdims=True)[:, :1]
    return (rows < chosen).astype(jnp.float32)


def quad_of(slot):
    quad = lax.axis_index("dp") % QUADS
    return (quad % 2 + slot % 2) % 2 + 2 * ((quad // 2 + slot // 2) % 2)


def full_spec(shape):
    return pl.BlockSpec(shape, lambda g: (0,) * len(shape))


def group_spec(width):
    return pl.BlockSpec((GROUP, width), lambda g: (g, 0))


VMEM_GRANT = 60 * 1024 * 1024


def backward_block(k, act, dmix, step, logdec, skip, state, state_grad, spread, gather):
    rows = slice(k * BLOCK, (k + 1) * BLOCK)
    values, keys, queries = (act[rows, :OWN], act[rows, OWN : OWN + NST], act[rows, OWN + NST :])
    step, logdec = (step[rows], logdec[rows])
    lower = lower_mask()
    cumul, cumul_t, step_w, cumul_w = block_parts(step, logdec, spread)
    step_t = jnp.transpose(step)
    gram = jnp.where(lower, mm_t(queries, keys), 0.0)
    values_f = values.astype(jnp.float32)
    dmix_f = dmix[rows].astype(jnp.float32)
    lanes_h = iota((BLOCK, LANES), 1)

    rows_h = iota((8, BLOCK), 0)
    strips = [slice(i * STRIP, (i + 1) * STRIP) for i in range(BLOCK // STRIP)]
    widths = [-(-strip.stop // LANES) * LANES for strip in strips]
    grams = [gram[strip, :wide] for strip, wide in zip(strips, widths)]
    grad_grams = [0.0] * len(strips)
    row_sums = [jnp.zeros((STRIP, LANES), jnp.float32)] * len(strips)
    lanes_h = iota((STRIP, LANES), 1)
    col_sums = jnp.zeros((8, BLOCK), jnp.float32)
    pieces = []
    for pair in range(PAIRS):
        lanes = slice(pair * LANES, (pair + 1) * LANES)
        dm, value = (dmix[rows, lanes], act[rows, lanes])
        piece = [0.0] * (BLOCK // LANES)
        for side in range(2):
            h = 2 * pair + side
            dm_half = lane_half(dm, side)
            sums = [0.0] * (BLOCK // LANES)
            for i, (strip, wide) in enumerate(zip(strips, widths)):
                decay = jnp.exp(jnp.minimum(cumul[strip, h : h + 1] - cumul_t[h : h + 1, :wide], 0.0))
                grad_mixing = mm_t(dm_half[strip], value[:wide])
                mixing = grams[i] * decay
                step_row = step_t[h : h + 1, :wide]
                grad_grams[i] = grad_grams[i] + grad_mixing * decay * step_row
                product = grad_mixing * mixing
                row_sums[i] = jnp.where(
                    lanes_h == h, jnp.sum(product * step_row, axis=1, keepdims=True), row_sums[i]
                )
                column = jnp.sum(product, axis=0, keepdims=True)
                part = t_mm(low16(mixing), dm_half[strip])
                for c in range(wide // LANES):
                    own = slice(c * LANES, (c + 1) * LANES)
                    sums[c] = sums[c] + column[:, own]
                    piece[c] = piece[c] + part[own]
            col_sums = jnp.where(rows_h == h, jnp.concatenate(sums, axis=1), col_sums)
        pieces.append(jnp.concatenate(piece, axis=0))
    row_sums = jnp.concatenate(row_sums, axis=0)
    grad_values = jnp.concatenate(pieces, axis=1) * step_w + skip * dmix_f
    grad_skip = jnp.sum(dmix_f * values_f, axis=0, keepdims=True)
    grad_queries, grad_keys = ([], [0.0] * (BLOCK // LANES))
    for strip, wide, grad_gram in zip(strips, widths, grad_grams):
        kept = low16(jnp.where(lower[strip, :wide], grad_gram, 0.0))
        grad_queries.append(mm(kept, keys[:wide]))
        part = t_mm(kept, queries[strip])
        for c in range(wide // LANES):
            grad_keys[c] = grad_keys[c] + part[c * LANES : (c + 1) * LANES]
    grad_queries = jnp.concatenate(grad_queries, axis=0)
    grad_keys = jnp.concatenate(grad_keys, axis=0)
    columns = jnp.transpose(
        jnp.concatenate([col_sums, jnp.zeros((LANES - 8, BLOCK), jnp.float32)], axis=0)
    )
    grad_step = columns
    grad_cumul = row_sums - columns * step
    if k == 1:
        entering = jnp.exp(cumul_w) * dmix_f
        entering_low = low16(entering)
        crossed = mm(queries, state)
        grad_cumul = grad_cumul + mm_right(entering * crossed, gather, 2)
        grad_queries = grad_queries + mm_t(entering_low, state)
        before = low16(t_mm(queries, entering_low))
    else:
        tail = jnp.exp(cumul_w[BLOCK - 1 :] - cumul_w)
        weighting = tail * step_w
        back = mm(keys, state_grad)
        grad_values = grad_values + weighting * back
        grad_keys = grad_keys + mm_t(low16(weighting * values_f), state_grad)
        grad_weight = mm_right(values_f * back, gather, 2)
        tail_h = jnp.exp(cumul[BLOCK - 1 :] - cumul)
        grad_step = grad_step + grad_weight * tail_h
        part = grad_weight * tail_h * step
        last = iota((BLOCK, LANES), 0) == BLOCK - 1
        grad_cumul = grad_cumul - part + jnp.where(last, jnp.sum(part, axis=0, keepdims=True), 0.0)
        before = None
    upper = low16((iota((BLOCK, BLOCK), 0) <= iota((BLOCK, BLOCK), 1)).astype(jnp.float32))
    grad_logdec = mm_left(upper, grad_cumul)
    return (grad_values, grad_keys, grad_queries, grad_step, grad_logdec, grad_skip, before)


ROWS_IN = D // (PLANES * RANKS)
ROWS_OUT = DIN // (PLANES * RANKS)
ROWS_ALL = ROWS_IN + 16
SHARD_CONV = CONVC // (PLANES * RANKS)
SHARD_GAIN = (D + DIN) // (PLANES * RANKS)
RUN_HALVES = RUN // HDIM


def place_lanes(pieces, tiles, rows):
    lanes = iota((rows, LANES), 1)
    out = [jnp.zeros((rows, LANES), jnp.float32) for unused in range(tiles)]
    for value, width, offset in pieces:
        tile, lane = divmod(offset, LANES)
        moved = pltpu.roll(value, lane, 1) if lane else value
        end = lane + width
        out[tile] = jnp.where((lanes >= lane) & (lanes < end), moved, out[tile])
        if end > LANES:
            out[tile + 1] = jnp.where(lanes < end - LANES, moved, out[tile + 1])
    return out


def own_lanes(tiles, quad, core):
    rows = tiles[0].shape[0]
    lanes = iota((rows, LANES), 1)

    def half_of(index):
        tile, odd = (index // 2, index % 2)
        chosen = tiles[0]
        for t in range(1, len(tiles)):
            chosen = jnp.where(tile == t, tiles[t], chosen)
        return (chosen, odd)

    out = []
    for pair in range(PAIRS):
        sides = []
        for b in range(2):
            near, i = divmod(2 * pair + b, RUN_HALVES)
            value, odd = half_of(2 * PLANES * RUN_HALVES * core + PLANES * RUN_HALVES * near + RUN_HALVES * quad + i)
            sides.append(jnp.where(odd == b, value, pltpu.roll(value, HDIM, 1)))
        out.append(jnp.where(lanes < HDIM, sides[0], sides[1]))
    return jnp.concatenate(out, axis=1)


def fill_sends(in_w, part, target):
    lanes = iota((ROWS_IN, LANES), 1)
    for j in range(RANKS):
        quad, core = divmod(j, 2)
        for pair in range(PAIRS):
            sides = []
            for b in range(2):
                near, i = divmod(2 * pair + b, RUN_HALVES)
                index = (2 * core + near) * PLANES * RUN_HALVES + RUN_HALVES * quad + i
                start = part * DIN + index // 2 * LANES
                tile = in_w[:, start : start + LANES]
                sides.append(tile if index % 2 == b else pltpu.roll(tile, HDIM, 1))
            lane = pair * LANES
            target[j, :, lane : lane + LANES] = low16(jnp.where(lanes < HDIM, sides[0], sides[1]))


def fill_common(in_w, conv_w, gains, lens, wc_send):
    wc_send[...] = jnp.zeros_like(wc_send)
    wc_send[:ROWS_IN, : 2 * NST] = low16(in_w[:, 2 * DIN : 2 * DIN + 2 * NST])
    tail = in_w[:, 2 * DIN + 2 * NST : 2 * DIN + COMMON]
    wide = jnp.concatenate([tail, jnp.zeros((ROWS_IN, LANES - HEADS), jnp.float32)], axis=1)
    wc_send[:ROWS_IN, 2 * NST :] = low16(wide)
    conv_v = jnp.concatenate([conv_w[...], jnp.zeros((KCONV + 1, COMMON_PAD - SHARD_CONV), jnp.float32)], axis=1)
    gain_v = jnp.concatenate([gains[...], jnp.zeros((1, COMMON_PAD - SHARD_GAIN), jnp.float32)], axis=1)
    extra = jnp.broadcast_to(lens[:, 0:1].astype(jnp.float32) - BLOCK, (1, COMMON_PAD))
    rows = jnp.concatenate([conv_v, gain_v, extra, jnp.zeros((9, COMMON_PAD), jnp.float32)], axis=0)
    wc_send[ROWS_IN:] = low16(rows)


def select_heads(quad, core):
    rows, columns = (iota((LANES, LANES), 0), iota((LANES, LANES), 1))
    head = HEADS // 2 * core + HEADS // 4 * (columns // 3) + 3 * quad + columns % 3
    return ((rows == head) & (columns < OWN_HEADS)).astype(jnp.float32)


def fore_kernel(
    tok, cot, seq_lens, in_w, out_w, conv_w, gains, head_params,
    o_normed, o_cot, o_gate_w, o_x_w, o_com, o_out, o_gate, o_proj, o_proj_com, o_act, o_mixed, o_gno,
    stats, gain_in, gain_out, conv, heads, skip, select, lens,
    wx_send, wg_send, wc_send, wo_send, all_tok, all_cot, normed, all_wx, all_wg, all_wc, w_com, line_wo, w_out,
    proj, gate, proj_com, act, mixed, gno, part, shared,
    send, recv, local
):
    plane, quad, core = place()
    where = (plane, quad, core)
    rank = 2 * quad + core
    sibling = at(plane, quad, flip(core))
    sems = Sems(send, recv)
    f32 = jnp.float32
    half = BLOCK // 2
    kept = []

    def keep(source, target):
        copy = pltpu.make_async_copy(source, target, local.at[len(kept)])
        kept.append(copy)
        copy.start()
        return copy

    def pieces(buffer):
        return lambda r, slot, h: buffer.at[slot, core, pl.ds(h * half, half)]

    def halves(buffer):
        return lambda h: buffer.at[pl.ds(h * half, half)]

    push_c = [
        sems.copy(wc_send, all_wc.at[plane, rank], at(xor4(plane, k), quad, core)) for k in (2, 3, 1)
    ]
    line_o = LineGather(sems, wo_send, lambda q: line_wo.at[q], *where)
    line_x = LineGather(sems, all_wx.at[plane], lambda q: all_wx.at[q], *where)
    line_g = LineGather(sems, all_wg.at[plane], lambda q: all_wg.at[q], *where)
    shuffles = []
    for source, target in ((wx_send, all_wx), (wg_send, all_wg)):
        copies = []
        for k in range(1, RANKS):
            other_core = flip(core) if k % 2 else core
            other_quad = xor4(quad, k // 2)
            copies.append(
                sems.copy(
                    source.at[2 * other_quad + other_core], target.at[plane, rank], at(plane, other_quad, other_core)
                )
            )
        shuffles.append(copies)
    tokens = PlaneGather(sems, halves(tok), pieces(all_tok), *where)
    grads = PlaneGather(sems, halves(cot), pieces(all_cot), *where)
    common = PlaneGather(
        sems,
        lambda h: all_wc.at[pl.ds(2 * h, 2), rank],
        lambda r, slot, h: all_wc.at[pl.ds(2 * h, 2), r],
        *where,
    )
    cross_o = [
        sems.copy(line_wo.at[2 * flip(core) + k], w_out.at[k, core], sibling) for k in range(2)
    ]
    mates = plane_mates(*where)
    swap = [sems.copy(part, shared.at[rank], device) for device in mates]

    greet(mates + plane_others(*where))
    fill_common(in_w, conv_w, gains, seq_lens, wc_send)
    for copy in push_c:
        copy.start()
    fill_sends(in_w, 1, wx_send)
    for copy in shuffles[0]:
        copy.start()
    wo_send[...] = low16(out_w[...])
    line_o.start(0)
    fill_sends(in_w, 0, wg_send)
    for copy in shuffles[1]:
        copy.start()
    own_wx = keep(wx_send.at[rank], all_wx.at[plane, rank])
    own_wg = keep(wg_send.at[rank], all_wg.at[plane, rank])
    own_wc = keep(wc_send, all_wc.at[plane, rank])
    own_tok = keep(tok, all_tok.at[0, core])
    own_cot = keep(cot, all_cot.at[0, core])
    own_wo = keep(wo_send, line_wo.at[plane])
    own_wc.wait()
    for copy in push_c:
        copy.wait_recv()
    common.start()
    own_wx.wait()
    for copy in shuffles[0]:
        copy.wait_recv()
    line_x.start(0)
    tokens.start()
    select[...] = select_heads(quad, core)
    wide = jnp.concatenate([head_params[...], jnp.zeros((3, LANES - HEADS), f32)], axis=1)
    wide = jnp.concatenate([wide, jnp.ones((1, LANES), f32), jnp.zeros((4, LANES), f32)], axis=0)
    heads[...] = mm_full(wide * (iota((8, LANES), 1) < HEADS).astype(f32), select[...])
    skip[...] = mm_right(heads[2:3], head_spread())

    common.near()
    common.across()
    for slot in range(QUADS):
        common.wait_slot(slot)
    line_x.arrive(0)
    line_x.start(1)
    for q in range(PLANES):
        for r in range(RANKS):
            start = (RANKS * q + r) * ROWS_IN
            w_com[start : start + ROWS_IN] = all_wc[q, r, :ROWS_IN]
    keep(w_com, o_com)
    extras = [all_wc[q, r, ROWS_IN:].astype(f32) for q in range(PLANES) for r in range(RANKS)]
    gain_tiles = place_lanes(
        [(e[5:6, :LANES], LANES, SHARD_GAIN * d) for d, e in enumerate(extras)]
        + [(e[5:6, LANES : 2 * LANES], SHARD_GAIN - LANES, SHARD_GAIN * d + LANES) for d, e in enumerate(extras)],
        (D + DIN) // LANES,
        1,
    )
    gain_in[...] = jnp.concatenate(gain_tiles[: D // LANES], axis=1)
    gain_out[...] = own_lanes(gain_tiles[D // LANES :], quad, core)
    conv_tiles = place_lanes(
        [(e[:8, :LANES], SHARD_CONV, SHARD_CONV * d) for d, e in enumerate(extras)], CONVC // LANES, 8
    )
    conv[...] = jnp.concatenate(
        [own_lanes(conv_tiles[: DIN // LANES], quad, core)] + conv_tiles[DIN // LANES :], axis=1
    )
    seats = []
    for slot in range(QUADS):
        chosen = jnp.zeros((1, LANES), f32)
        for q in range(PLANES):
            for p in range(QUADS):
                here = (plane == q) & (quad_of(slot) == p)
                chosen = jnp.where(here, extras[RANKS * q + 2 * p][6:7, :LANES], chosen)
        seats.append(chosen + BLOCK)
    lens[...] = jnp.concatenate(seats + [jnp.zeros((8 - QUADS, LANES), f32)], axis=0)

    def norm(slot):
        for side in range(2):
            rows = all_tok[slot, side].astype(f32)
            scaling = lax.rsqrt(jnp.mean(rows * rows, axis=1, keepdims=True) + norm_eps)
            normed[slot, pl.ds(side * BLOCK, BLOCK)] = low16(rows * scaling * gain_in[...])

    own_tok.wait()
    tokens.wait_slot(0)
    norm(0)
    line_x.arrive(1)
    line_x.start(2)
    own_wg.wait()
    for copy in shuffles[1]:
        copy.wait_recv()
    line_g.start(0)
    tokens.near()
    grads.start()
    line_x.arrive(2)
    keep(all_wx, o_x_w)

    @pl.loop(0, QUADS)
    def each(slot):
        @pl.when(slot == 1)
        def first():
            tokens.wait_slot(1)
            norm(1)
            line_g.arrive(0)
            line_g.start(1)

        @pl.when(slot == 2)
        def second():
            tokens.wait_slot(2)
            norm(2)
            tokens.across()
            line_g.arrive(1)
            line_g.start(2)

        @pl.when(slot == 3)
        def third():
            tokens.wait_slot(3)
            norm(3)
            line_o.arrive(0)
            line_o.start(1)

        proj[slot] = mm(normed[slot], all_wx[...].reshape(D, OWN))
        proj_com[slot] = mm(normed[slot], w_com[...])
        conv_in = jnp.concatenate([proj[slot], proj_com[slot, :, : 2 * NST]], axis=1)
        raw = mm_right(proj_com[slot, :, 2 * NST :], low16(select[...]))
        preact = preact_of(conv_in, conv[...])
        act[slot] = low16(preact * sigmoid(preact))
        step, logdec = steps_of(raw, heads[...], live_of(lens[...], slot))
        ssd_forward(act.at[slot], step, logdec, skip[...], mixed.at[slot])

    for slot in range(QUADS):
        keep(normed.at[slot], o_normed.at[pl.ds(slot * GROUP, GROUP)])
    for source, target in ((proj, o_proj), (proj_com, o_proj_com), (act, o_act), (mixed, o_mixed)):
        keep(source, target)
    line_g.arrive(2)
    line_o.arrive(1)
    line_o.start(2)
    keep(all_wg, o_gate_w)
    grads.near()

    @pl.loop(0, QUADS)
    def gates(slot):
        gate[slot] = mm(normed[slot], all_wg[...].reshape(D, OWN))

    keep(gate, o_gate)
    line_o.arrive(2)
    own_wo.wait()
    for copy in cross_o:
        copy.start()
    for k in range(2):
        w_out[k, core] = line_wo[2 * core + k]
    own_cot.wait()
    for copy in cross_o:
        copy.wait_recv()
    keep(w_out, o_out)
    part[...] = jnp.zeros_like(part)

    @pl.loop(0, QUADS)
    def measure(slot):
        for k in range(QUADS):

            @pl.when(slot == k)
            def here():
                if k == 1:
                    grads.across()
                grads.wait_slot(k)

        live = live_of(lens[...], slot)
        grad = all_cot[slot].reshape(GROUP, D)
        grad = jnp.where(live > 0.0, grad, jnp.zeros_like(grad))
        gno_v = mm_t(grad, w_out[...].reshape(OWN, D))
        gno[slot] = gno_v
        gate_part = gate[slot]
        gated = mixed[slot] * gate_part * sigmoid(gate_part)
        squares = jnp.sum(gated * gated, axis=1, keepdims=True)
        inner = jnp.sum(gno_v * gain_out[...] * gated, axis=1, keepdims=True)
        lanes = iota((GROUP, LANES), 1)
        seat = quad_of(slot)
        columns = jnp.where(lanes == 2 * seat, squares, 0.0) + jnp.where(lanes == 2 * seat + 1, inner, 0.0)
        part[...] += jnp.transpose(columns)[:8]

    for copy in swap:
        copy.start()
    keep(all_cot, o_cot)
    keep(gno, o_gno)
    shared[rank] = part[...]
    for copy in swap:
        copy.wait_recv()
    stats[...] = jnp.sum(shared[...], axis=0)
    for copy in shuffles[0] + shuffles[1] + push_c + cross_o + swap:
        copy.wait_send()
    for line in (line_o, line_x, line_g):
        line.sent()
    for gather in (tokens, grads, common):
        gather.sent()
    for copy in kept:
        if not any(copy is done for done in (own_wx, own_wg, own_wc, own_tok, own_cot, own_wo)):
            copy.wait()


def run_fore(tok, cot, seq_lens, in_w, out_w, conv_w, gains, head_params):
    f32, bf16 = (jnp.float32, jnp.bfloat16)
    whole = pl.BlockSpec(memory_space=pltpu.VMEM)
    outs = (
        ((QUADS * GROUP, D), bf16), ((QUADS, 2, BLOCK, D), bf16), ((PLANES, RANKS, ROWS_IN, OWN), bf16),
        ((PLANES, RANKS, ROWS_IN, OWN), bf16), ((D, COMMON_PAD), bf16), ((2, 2, ROWS_OUT, D), bf16),
        ((QUADS, GROUP, OWN), f32), ((QUADS, GROUP, OWN), f32), ((QUADS, GROUP, COMMON_PAD), f32), ((QUADS, GROUP, MIX), bf16),
        ((QUADS, GROUP, OWN), f32), ((QUADS, GROUP, OWN), f32),
    )
    small = (
        (8, GROUP), (1, D), (1, OWN), (8, MIX), (8, LANES), (1, OWN), (LANES, LANES), (8, LANES),
    )
    scratch = (
        ((RANKS, ROWS_IN, OWN), bf16), ((RANKS, ROWS_IN, OWN), bf16), ((ROWS_ALL, COMMON_PAD), bf16), ((ROWS_OUT, D), bf16),
        ((QUADS, 2, BLOCK, D), bf16), ((QUADS, 2, BLOCK, D), bf16), ((QUADS, GROUP, D), bf16),
        ((PLANES, RANKS, ROWS_IN, OWN), bf16), ((PLANES, RANKS, ROWS_IN, OWN), bf16),
        ((PLANES, RANKS, ROWS_ALL, COMMON_PAD), bf16),
        ((D, COMMON_PAD), bf16), ((PLANES, ROWS_OUT, D), bf16), ((2, 2, ROWS_OUT, D), bf16),
        ((QUADS, GROUP, OWN), f32), ((QUADS, GROUP, OWN), f32), ((QUADS, GROUP, COMMON_PAD), f32),
        ((QUADS, GROUP, MIX), bf16), ((QUADS, GROUP, OWN), f32), ((QUADS, GROUP, OWN), f32), ((8, GROUP), f32),
        ((RANKS, 8, GROUP), f32),
    )
    args = (tok, cot, seq_lens, in_w, out_w, conv_w, gains.reshape(1, -1), head_params)
    results = pl.pallas_call(
        fore_kernel,
        in_specs=[ANY, ANY] + [whole] * 6,
        out_specs=[ANY] * len(outs) + [whole] * len(small),
        out_shape=[jax.ShapeDtypeStruct(s, kind) for s, kind in outs]
        + [jax.ShapeDtypeStruct(s, f32) for s in small],
        scratch_shapes=[pltpu.VMEM(s, kind) for s, kind in scratch]
        + [
            pltpu.SemaphoreType.DMA((96,)),
            pltpu.SemaphoreType.DMA((96,)),
            pltpu.SemaphoreType.DMA((24,)),
        ],
        compiler_params=pltpu.CompilerParams(
            vmem_limit_bytes=VMEM_GRANT, collective_id=0, has_side_effects=True
        ),
    )(*args)
    rows = QUADS * GROUP
    widths = (D, D, None, None, None, None, OWN, OWN, COMMON_PAD, MIX, OWN, OWN)
    flat = [a if w is None else a.reshape(rows, w) for a, w in zip(results, widths)]
    flat[2], flat[3] = (flat[2].reshape(D, OWN), flat[3].reshape(D, OWN))
    flat[5] = flat[5].reshape(OWN, D)
    return flat + list(results[len(outs) :])


def gate_kernel(
    lens, stats, cot, normed, gate_part, mixed, grad_normed_out, w_out, gain_out,
    branch, dgate, dmix, g_out, g_gate, g_gain, acc_out, acc_gate, tmp_out_t, tmp_grad
):
    g = pl.program_id(0)
    live = live_of(lens[...], g)

    @pl.when(g == 0)
    def first():
        acc_out[...] = jnp.zeros_like(acc_out)
        acc_gate[...] = jnp.zeros_like(acc_gate)
        g_gain[...] = jnp.zeros_like(g_gain)

    columns = jnp.transpose(jnp.concatenate([stats[...], jnp.zeros((LANES - 8, GROUP), jnp.float32)], axis=0))
    lanes = iota((GROUP, LANES), 1)
    seat = quad_of(g)
    power = jnp.sum(jnp.where(lanes == 2 * seat, columns, 0.0), axis=1, keepdims=True)
    along = jnp.sum(jnp.where(lanes == 2 * seat + 1, columns, 0.0), axis=1, keepdims=True)
    scale_out = lax.rsqrt(power * (1.0 / DIN) + norm_eps)
    gate_v, mixed_v, gno = (gate_part[...], mixed[...], grad_normed_out[...])
    sig = sigmoid(gate_v)
    gate_act = gate_v * sig
    gated = mixed_v * gate_act
    normed_out = low16(gated * scale_out * gain_out[...])
    tmp_out_t[...] = jnp.transpose(normed_out)
    tmp_grad[...] = jnp.where(live > 0.0, cot[...], jnp.zeros_like(cot[...]))
    scaled = gno * scale_out
    grad_gated = scaled * gain_out[...] - gated * (scale_out * scale_out * scale_out * along * (1.0 / DIN))
    gain_sum = jnp.sum(scaled * gated, axis=0, keepdims=True)
    g_gain[...] += jnp.concatenate([gain_sum, jnp.zeros((7, OWN), jnp.float32)], axis=0)
    grad_gate = low16(grad_gated * mixed_v * (sig * (1.0 + gate_v * (1.0 - sig))))
    dgate[...] = grad_gate
    dmix[...] = low16(grad_gated * gate_act)
    wide = 4 * LANES
    for side in range(2):
        branch[0, side] = low16(mm(normed_out[side * BLOCK : (side + 1) * BLOCK], w_out[...]))

    @pl.loop(0, D // wide)
    def tile(i):
        lanes = pl.ds(pl.multiple_of(i * wide, wide), wide)
        acc_out[:, lanes] += mm(tmp_out_t[...], tmp_grad[:, lanes])
        acc_gate[lanes, :] += t_mm(normed[:, lanes], dgate[...])

    @pl.when(g == QUADS - 1)
    def last():
        g_out[...] = low16(acc_out[...])
        g_gate[...] = low16(acc_gate[...])


def run_gate(lens, stats, cot, normed, gate_part, mixed, grad_normed_out, w_out, gain_out):
    f32, bf16 = (jnp.float32, jnp.bfloat16)
    rows = QUADS * GROUP
    grouped = (cot, normed, gate_part, mixed, grad_normed_out)
    ends = (((OWN, D), bf16), ((D, OWN), bf16), ((8, OWN), f32))
    return pl.pallas_call(
        gate_kernel,
        grid=(QUADS,),
        in_specs=[full_spec(a.shape) for a in (lens, stats)]
        + [group_spec(a.shape[1]) for a in grouped]
        + [full_spec(w_out.shape), full_spec(gain_out.shape)],
        out_specs=[pl.BlockSpec((1, 2, BLOCK, D), lambda g: (g, 0, 0, 0)), group_spec(OWN), group_spec(OWN)]
        + [full_spec(s) for s, kind in ends],
        out_shape=[
            jax.ShapeDtypeStruct((QUADS, 2, BLOCK, D), bf16),
            jax.ShapeDtypeStruct((rows, OWN), bf16),
            jax.ShapeDtypeStruct((rows, OWN), bf16),
        ]
        + [jax.ShapeDtypeStruct(s, kind) for s, kind in ends],
        scratch_shapes=[
            pltpu.VMEM((OWN, D), f32), pltpu.VMEM((D, OWN), f32),
            pltpu.VMEM((OWN, GROUP), bf16), pltpu.VMEM((GROUP, D), bf16),
        ],
        compiler_params=pltpu.CompilerParams(vmem_limit_bytes=VMEM_GRANT),
    )(lens, stats, *grouped, w_out, gain_out)


def backward_group(live, dmix, conv_in, raw, act, conv, heads, skip, between):
    raw_v = raw[...]
    heads_v = heads[...]
    step, logdec = steps_of(raw_v, heads_v, live)
    spread, gather = (head_spread(), head_gather())
    rows0 = slice(0, BLOCK)
    cumul0 = mm_left(low16(lower_mask().astype(jnp.float32)), logdec[rows0])
    cumul0_w = mm_right(cumul0, spread)
    weighting = jnp.exp(cumul0_w[BLOCK - 1 :] - cumul0_w) * mm_right(step[rows0], spread, 2)
    state = low16(
        t_mm(act[rows0, OWN : OWN + NST], low16(weighting * act[rows0, :OWN].astype(jnp.float32)))
    )
    late = backward_block(1, act, dmix, step, logdec, skip[...], state, None, spread, gather)
    between()
    early = backward_block(0, act, dmix, step, logdec, skip[...], None, late[6], spread, gather)
    grad_act = jnp.concatenate([jnp.concatenate(part[:3], axis=1) for part in (early, late)], axis=0)
    grad_step = jnp.concatenate([early[3], late[3]], axis=0)
    grad_logdec = jnp.concatenate([early[4], late[4]], axis=0)
    rate = jnp.exp(heads_v[1:2])
    grad_raw = (grad_step - rate * grad_logdec) * live * heads_v[3:4] * sigmoid(raw_v + heads_v[0:1])
    u = conv_in[...]
    conv_v = conv[...]
    preact = preact_of(u, conv_v)
    sig_q = sigmoid(preact)
    grad_pre = grad_act * (sig_q * (1.0 + preact * (1.0 - sig_q)))
    grad_u = grad_pre * conv_v[KCONV - 1 : KCONV]
    taps = []
    for tap in range(KCONV):
        lag = KCONV - 1 - tap
        if lag:
            grad_u = grad_u + shift_up(grad_pre, lag) * conv_v[tap : tap + 1]
        taps.append(jnp.sum(grad_pre * shift_down(u, lag), axis=0, keepdims=True))
    taps.append(jnp.sum(grad_pre, axis=0, keepdims=True))
    small = (
        jnp.concatenate(taps + [jnp.zeros((3, MIX), jnp.float32)], axis=0),
        jnp.sum(grad_raw, axis=0, keepdims=True),
        jnp.sum(grad_logdec * logdec, axis=0, keepdims=True),
        early[5] + late[5],
    )
    return (grad_u, grad_raw, small)


PACK = 48


def back_kernel(
    lens, gate_grads, out_grads, branch_all, w_gate, w_x, w_com, conv, heads, skip, select, gain_in, g_gain,
    tok_own, normed, dgate, dmix, proj_x, proj_com, act,
    r_out, all_gate, all_x, sum_com, packs, sum_branch, grad_rows,
    acc_x, acc_com, small_conv, small_head, small_skip,
    branch_own, branch_sib, en_part, en_sib, branch_got, en_got, branch_relay, en_relay,
    gate_got, gate_own, sum_gate, x_send, x_got, x_passed, sum_x, com_send, com_sib, com_quad, com_z, com_got,
    pack_send, pack_got, pack_sum,
    sends, recvs, out_send, out_recv, local
):
    s = pl.program_id(0)
    slot = QUADS - 1 - s
    plane, quad, core = place()
    where = (plane, quad, core)
    rank = 2 * quad + core
    sibling = at(plane, quad, flip(core))
    f32 = jnp.float32
    sems = Sems(sends, recvs)
    to_x, to_y = (at(plane, xor4(quad, 1), core), at(plane, xor4(quad, 2), core))
    half = BLOCK // 2

    swaps = [
        [sems.copy(branch_all.at[k, flip(core)], branch_sib.at[k], sibling) for k in range(QUADS)],
        [sems.copy(en_part.at[k % 2, flip(core)], en_sib.at[k], sibling) for k in range(QUADS)],
    ]
    routes = []
    for sib, got, relay in ((branch_sib, branch_got, branch_relay), (en_sib, en_got, en_relay)):
        routes.append(
            {
                "relay_x": sems.copy(sib.at[3, pl.ds(0, half)], relay.at[0], to_x),
                "relay_y": sems.copy(sib.at[3, pl.ds(half, half)], relay.at[1], to_y),
                "x": sems.copy(sib.at[1], got.at[0], to_x),
                "y": sems.copy(sib.at[2], got.at[1], to_y),
            }
        )

    def z_push(source, target):
        return [
            sems.copy(source.at[xor4(plane, k)], target.at[k - 1], at(xor4(plane, k), quad, core))
            for k in (2, 3, 1)
        ]

    def rank_push(source, target):
        copies = []
        for k in range(1, RANKS):
            other_core = flip(core) if k % 2 else core
            other_quad = xor4(quad, k // 2)
            copies.append(
                sems.copy(source(2 * other_quad + other_core), target.at[rank], at(plane, other_quad, other_core))
            )
        return copies

    gate_z = z_push(gate_grads, gate_got)
    x_z = z_push(x_send, x_got)
    x_relay = sems.copy(x_send.at[xor4(plane, 3)], x_passed, at(xor4(plane, 1), quad, core))
    at_end = plane % (PLANES - 1) == 0
    part_rows = D // PLANES
    gate_ranks = rank_push(lambda r: sum_gate.at[r], all_gate)
    x_ranks = rank_push(lambda r: sum_x.at[r], all_x)
    com_swap = sems.copy(com_send.at[:, :, flip(core)], com_sib, sibling)
    com_quads = [
        sems.copy(com_sib.at[:, xor4(quad, k)], com_quad.at[k - 1], at(plane, xor4(quad, k), core))
        for k in (3, 1, 2)
    ]
    com_planes = z_push(com_z, com_got)
    pack_z = [
        sems.copy(pack_send, pack_got.at[k - 1], at(xor4(plane, k), quad, core)) for k in (2, 3, 1)
    ]
    pack_ranks = rank_push(lambda r: pack_sum, packs)

    def out_copy(near, side):
        return pltpu.make_async_remote_copy(
            src_ref=out_grads.at[near, side],
            dst_ref=r_out.at[plane],
            send_sem=out_send.at[2 * near + side],
            recv_sem=out_recv.at[plane],
            device_id=at(2 * core + near, quad, side),
            device_id_type=MESH_ID,
        )

    def out_landing(origin):
        return pltpu.make_async_remote_copy(
            src_ref=out_grads.at[0, 0],
            dst_ref=r_out.at[origin],
            send_sem=out_send.at[0],
            recv_sem=out_recv.at[origin],
            device_id=sibling,
            device_id_type=MESH_ID,
        )

    out_here = pltpu.make_async_copy(out_grads.at[plane % 2, core], r_out.at[plane], local.at[0])
    out_stays = plane // 2 == core
    gate_here = pltpu.make_async_copy(gate_grads.at[plane], gate_own, local.at[1])
    branch_here = [
        pltpu.make_async_copy(branch_all.at[k, core], branch_own.at[k], local.at[5 + k]) for k in range(QUADS)
    ]

    @pl.when(s == 0)
    def begin():
        peers = plane_mates(*where) + plane_others(*where)
        peers += [at(xor4(plane, k), quad, flip(core)) for k in range(1, PLANES)]
        greet(peers)
        for copy in gate_z:
            copy.start()
        for copy in swaps[0][::-1]:
            copy.start()
        for near in range(2):
            for side in range(2):

                @pl.when(jnp.logical_not((2 * core + near == plane) & (core == side)))
                def go():
                    out_copy(near, side).start()

        @pl.when(out_stays)
        def stay():
            out_here.start()

        for copy in branch_here[::-1]:
            copy.start()
        gate_here.start()
        for ref in (acc_x, acc_com, small_conv, small_head, small_skip):
            ref[...] = jnp.zeros_like(ref)

    def settle(kind, k, own, sib):
        route = routes[kind]
        relay = (branch_relay, en_relay)[kind]
        swaps[kind][k].wait_recv()
        sib[k] = low16(own.astype(f32) + sib[k].astype(f32))
        if k == 3:
            route["relay_x"].start()
            route["relay_y"].start()
        if k == 2:
            route["relay_x"].wait_recv()
            sib[k, :half] = low16(sib[k, :half].astype(f32) + relay[0].astype(f32))
            route["y"].start()
        if k == 1:
            route["relay_y"].wait_recv()
            sib[k, half:] = low16(sib[k, half:].astype(f32) + relay[1].astype(f32))
            route["x"].start()

    def settle_branch(k):
        branch_here[k].wait()
        settle(0, k, branch_own[k], branch_sib)

    def between():
        for k in range(QUADS):

            @pl.when(slot == k)
            def sums():
                if k < QUADS - 1:
                    settle(1, k + 1, en_part[(k + 1) % 2, core], en_sib)
                if k == 3:
                    settle_branch(3)
                if k == 2:
                    settle_branch(1)

    live = live_of(lens[...], slot)
    conv_in = jnp.concatenate([proj_x[...], proj_com[:, : 2 * NST]], axis=1)
    raw = mm_right(proj_com[:, 2 * NST :], low16(select[...]))
    grad_u, grad_raw, small = backward_group(
        live, dmix, conv_in, raw, act, conv, heads, skip, between
    )
    small_conv[...] += small[0]
    small_head[0:1] += small[1]
    small_head[1:2] += small[2]
    small_skip[0:1] += small[3]
    raw_wide = mm_t(low16(grad_raw), low16(select[...]))
    grad_x = low16(grad_u[:, :OWN])
    grad_com = low16(jnp.concatenate([grad_u[:, OWN:], raw_wide], axis=1))
    normed_v = normed[...]
    acc_x[...] += t_mm(normed_v, grad_x)

    @pl.when(s == QUADS - 1)
    def send_x():
        x_send[...] = low16(acc_x[...]).reshape(x_send.shape)

        @pl.when(at_end)
        def from_end():
            x_relay.start()

        @pl.when(jnp.logical_not(at_end))
        def from_middle():
            x_z[1].start()
            x_z[2].start()

    acc_com[...] += t_mm(normed_v, grad_com)

    @pl.when(s == QUADS - 1)
    def send_com():
        com_send[...] = low16(acc_com[...]).reshape(com_send.shape)
        com_swap.start()

    for k in range(2):

        @pl.when(slot == k)
        def free():
            swaps[1][k + 2].wait_send()

    grad_all = jnp.concatenate([dgate[...], grad_x, grad_com], axis=1)
    w_all = jnp.concatenate([w_gate[...], w_x[...], w_com[...]], axis=1)
    for side in range(2):
        en_part[slot % 2, side] = low16(mm_t(grad_all[side * BLOCK : (side + 1) * BLOCK], w_all))
    for k in range(QUADS):

        @pl.when(slot == k)
        def swap_en():
            swaps[1][k].start()

    for k, done in ((3, 2), (2, 0)):

        @pl.when(slot == k)
        def settle_late():
            settle_branch(done)

    @pl.when(s == QUADS - 1)
    def tail():
        @pl.when(at_end)
        def rest_from_end():
            x_relay.wait_send()
            x_z[0].start()
            x_z[2].start()

        @pl.when(jnp.logical_not(at_end))
        def pass_on():
            x_relay.wait_recv()
            far = xor4(plane, 2)
            x_send[far] = low16(x_send[far].astype(f32) + x_passed[...].astype(f32))
            x_z[0].start()

        settle(1, 0, en_part[0, core], en_sib)
        gate_here.wait()
        for copy in gate_z:
            copy.wait_recv()
        sum_gate[...] = low16(
            gate_own[...].astype(f32) + gate_got[0].astype(f32) + gate_got[1].astype(f32) + gate_got[2].astype(f32)
        )
        for copy in gate_ranks:
            copy.start()
        gate_keep = pltpu.make_async_copy(sum_gate.at[rank], all_gate.at[rank], local.at[2])
        gate_keep.start()
        com_swap.wait_recv()
        com_sib[...] = low16(com_sib[...].astype(f32) + com_send[:, :, core].astype(f32))
        for copy in com_quads:
            copy.start()
        for name in ("x", "y"):
            routes[0][name].wait_recv()
        sum_branch[...] = (
            branch_sib[0].astype(f32) + branch_got[0].astype(f32) + branch_got[1].astype(f32)
        )
        for copy in com_quads:
            copy.wait_recv()
        com_z[...] = low16(
            com_sib[:, quad].astype(f32)
            + com_quad[0].astype(f32) + com_quad[1].astype(f32) + com_quad[2].astype(f32)
        )
        for copy in com_planes:
            copy.start()
        for name in ("x", "y"):
            routes[1][name].wait_recv()
        en = en_sib[0].astype(f32) + en_got[0].astype(f32) + en_got[1].astype(f32)
        rows = tok_own[...].astype(f32)
        scaling = lax.rsqrt(jnp.mean(rows * rows, axis=1, keepdims=True) + norm_eps)
        scaled = rows * scaling
        gain_grad = jnp.sum(en * scaled, axis=0, keepdims=True)
        weighted = en * gain_in[...]
        inner = jnp.mean(weighted * scaled, axis=1, keepdims=True)
        grad_rows[...] = scaling * (weighted - scaled * inner)
        pack_send[...] = jnp.zeros_like(pack_send)
        for i in range(D // LANES):
            pack_send[i : i + 1] = gain_grad[:, i * LANES : (i + 1) * LANES]
        gain_out_grad = g_gain[0:1]
        skip_grad = small_skip[0:1]
        for i in range(PAIRS):
            lanes = slice(i * LANES, (i + 1) * LANES)
            pack_send[12 + i : 13 + i] = gain_out_grad[:, lanes]
            pack_send[42 + i : 43 + i] = skip_grad[:, lanes]
            for tap in range(KCONV + 1):
                pack_send[15 + 3 * tap + i : 16 + 3 * tap + i] = small_conv[tap : tap + 1, lanes]
        for tap in range(KCONV + 1):
            for i in range(2):
                lanes = slice(OWN + i * LANES, OWN + (i + 1) * LANES)
                pack_send[30 + 2 * tap + i : 31 + 2 * tap + i] = small_conv[tap : tap + 1, lanes]
        pack_send[40:42] = small_head[0:2]
        for copy in pack_z:
            copy.start()
        for copy in com_planes:
            copy.wait_recv()
        sum_com[...] = (
            com_z[plane].astype(f32)
            + com_got[0].astype(f32) + com_got[1].astype(f32) + com_got[2].astype(f32)
        )
        for copy in pack_z:
            copy.wait_recv()
        pack_sum[...] = pack_send[...] + pack_got[0] + pack_got[1] + pack_got[2]
        for copy in pack_ranks:
            copy.start()
        pack_keep = pltpu.make_async_copy(pack_sum, packs.at[rank], local.at[3])
        pack_keep.start()
        x_z[0].wait_recv()
        x_z[2].wait_recv()
        acc_x[:part_rows] = (
            x_send[plane].astype(f32) + x_got[0].astype(f32) + x_got[1].astype(f32)
        ).reshape(part_rows, OWN)

        @pl.when(jnp.logical_not(at_end))
        def one_more():
            x_z[1].wait_recv()
            acc_x[:part_rows] += x_got[2].astype(f32).reshape(part_rows, OWN)

        sum_x[...] = low16(acc_x[:part_rows]).reshape(sum_x.shape)
        for copy in x_ranks:
            copy.start()
        x_keep = pltpu.make_async_copy(sum_x.at[rank], all_x.at[rank], local.at[4])
        x_keep.start()
        for origin in range(PLANES):

            @pl.when(jnp.logical_not((plane == origin) & out_stays))
            def arrived():
                out_landing(origin).wait_recv()

        @pl.when(out_stays)
        def kept():
            out_here.wait()

        for near in range(2):
            for side in range(2):

                @pl.when(jnp.logical_not((2 * core + near == plane) & (core == side)))
                def gone():
                    out_copy(near, side).wait_send()

        for copy in gate_ranks + pack_ranks + x_ranks:
            copy.wait_recv()
        @pl.when(jnp.logical_not(at_end))
        def middle_sent():
            x_z[1].wait_send()

        for copy in gate_z + [x_z[0], x_z[2]] + gate_ranks + x_ranks + [com_swap] + com_quads + com_planes + pack_z + pack_ranks:
            copy.wait_send()
        for copy in swaps[0] + swaps[1][:2] + list(routes[0].values()) + list(routes[1].values()):
            copy.wait_send()
        gate_keep.wait()
        pack_keep.wait()
        x_keep.wait()


def run_back(lens, gate_grads, out_grads, branch, w_gate, w_x, w_com, conv, heads, skip, select, gain_in, g_gain, tok_own,
             normed, dgate, dmix, proj_x, proj_com, act):
    f32, bf16 = (jnp.float32, jnp.bfloat16)
    rows_in = D // (PLANES * RANKS)
    rows_out = DIN // (PLANES * RANKS)
    gate_grads = gate_grads.reshape(PLANES, RANKS, rows_in, OWN)
    out_grads = out_grads.reshape(2, 2, rows_out, D)
    fixed = (w_gate, w_x, w_com, conv, heads, skip, select, gain_in, g_gain, tok_own)
    grouped = (normed, dgate, dmix, proj_x, proj_com, act)

    def turned(width):
        return pl.BlockSpec((GROUP, width), lambda s: (QUADS - 1 - s, 0))

    outs = (
        ((PLANES, rows_out, D), bf16, ANY),
        ((RANKS, rows_in, OWN), bf16, ANY),
        ((RANKS, rows_in, OWN), bf16, ANY),
        ((rows_in, COMMON_PAD), f32, None),
        ((RANKS, PACK, LANES), f32, ANY),
        ((BLOCK, D), f32, None),
        ((BLOCK, D), f32, None),
    )
    half = BLOCK // 2
    quarter = (RANKS, rows_in, OWN)
    com = (rows_in, COMMON_PAD)
    scratch = [
        ((D, OWN), f32), ((D, COMMON_PAD), f32), ((8, MIX), f32), ((8, LANES), f32), ((8, OWN), f32),
        ((QUADS, BLOCK, D), bf16),
        ((QUADS, BLOCK, D), bf16), ((2, 2, BLOCK, D), bf16), ((QUADS, BLOCK, D), bf16),
        ((2, BLOCK, D), bf16), ((2, BLOCK, D), bf16), ((2, half, D), bf16), ((2, half, D), bf16),
        ((PLANES - 1,) + quarter, bf16), (quarter, bf16), (quarter, bf16),
        ((PLANES,) + quarter, bf16), ((PLANES - 1,) + quarter, bf16), (quarter, bf16), (quarter, bf16),
        ((PLANES, QUADS, 2) + com, bf16), ((PLANES, QUADS) + com, bf16), ((QUADS - 1, PLANES) + com, bf16),
        ((PLANES,) + com, bf16), ((PLANES - 1,) + com, bf16),
        ((PACK, LANES), f32), ((PLANES - 1, PACK, LANES), f32), ((PACK, LANES), f32),
    ]
    return pl.pallas_call(
        back_kernel,
        grid=(QUADS,),
        in_specs=[full_spec(lens.shape), ANY, ANY, ANY]
        + [full_spec(a.shape) for a in fixed]
        + [turned(a.shape[1]) for a in grouped],
        out_specs=[full_spec(s) if spec is None else spec for s, kind, spec in outs],
        out_shape=[jax.ShapeDtypeStruct(s, kind) for s, kind, spec in outs],
        scratch_shapes=[pltpu.VMEM(s, kind) for s, kind in scratch]
        + [
            pltpu.SemaphoreType.DMA((64,)),
            pltpu.SemaphoreType.DMA((64,)),
            pltpu.SemaphoreType.DMA((4,)),
            pltpu.SemaphoreType.DMA((4,)),
            pltpu.SemaphoreType.DMA((9,)),
        ],
        compiler_params=pltpu.CompilerParams(
            vmem_limit_bytes=VMEM_GRANT, collective_id=2, has_side_effects=True
        ),
    )(lens, gate_grads, out_grads, branch, *fixed, *grouped)


def adam_refs(refs, columns, gradient, rate):
    weight, first, second, weight_new, first_new, second_new = refs
    results = adam_update(weight[:, columns], first[:, columns], second[:, columns], gradient, rate)
    for ref, value in zip((weight_new, first_new, second_new), results):
        ref[:, columns] = value


RUNS = 2 * PLANES
PIECE = 2 * OWN
STEPS = 3
RUNS_STEP = 3


def finish_kernel(
    lens, all_gate, all_x, sum_com, tok, cot, sum_branch, grad_rows, r_out,
    in_w, in_m, in_v, out_w, out_m, out_v,
    mixed_out, grad_input, in_wn, in_mn, in_vn, out_wn, out_mn, out_vn
):
    f32 = jnp.float32
    step = pl.program_id(0)
    core = lax.axis_index("seq")
    ins = (in_w, in_m, in_v, in_wn, in_mn, in_vn)
    rows = in_w.shape[0]
    lanes = iota((rows, LANES), 1)

    @pl.when(step < 2)
    def positions():
        count = tok.shape[0]
        position = (iota((count, 1), 0) + core * BLOCK + step * count).astype(f32)
        live = (position < lens[0:1, 0:1]).astype(f32)
        mixed_out[...] = (tok[...].astype(f32) + live * sum_branch[...]).astype(jnp.bfloat16)
        grad_input[...] = cot[...].astype(f32) + grad_rows[...]

    total = r_out[0].astype(f32) + r_out[1].astype(f32) + r_out[2].astype(f32) + r_out[3].astype(f32)
    adam_refs((out_w, out_m, out_v, out_wn, out_mn, out_vn), slice(None), total, rate_out)

    for part, source in ((0, all_gate), (1, all_x)):
        for run in range(PLANES):

            place_at = PLANES * part + run
            start = place_at % RUNS_STEP * PIECE

            @pl.when(step == place_at // RUNS_STEP)
            def in_columns():
                side, near = divmod(run, 2)
                for t in range(2 * PAIRS):
                    halves = []
                    for b in range(2):
                        p, i = divmod(2 * t + b, RUN_HALVES)
                        index = RUN_HALVES * near + i
                        tile = source[2 * p + side, :, (index // 2) * LANES : (index // 2 + 1) * LANES].astype(f32)
                        halves.append(tile if index % 2 == b else pltpu.roll(tile, HDIM, 1))
                    gradient = jnp.where(lanes < HDIM, halves[0], halves[1])
                    adam_refs(ins, slice(start + t * LANES, start + (t + 1) * LANES), gradient, rate_in)

    @pl.when(step == RUNS // RUNS_STEP)
    def common_columns():
        start = RUNS % RUNS_STEP * PIECE
        adam_refs(ins, slice(start, start + COMMON_PAD), sum_com[...], rate_in)


def run_finish(lens, tok, cot, sum_branch, grad_rows, r_out, all_gate, all_x, sum_com, *weights):
    in_w, out_w = (weights[0], weights[3])
    f32 = jnp.float32
    rows = BLOCK // 2
    out_rows = out_w.shape[0] // STEPS

    def positions():
        return pl.BlockSpec((rows, D), lambda s: (jnp.minimum(s, 1), 0))

    def in_block():
        return pl.BlockSpec((in_w.shape[0], RUNS_STEP * PIECE), lambda s: (0, s))

    def out_block():
        return pl.BlockSpec((out_rows, D), lambda s: (s, 0))

    shapes = [(tok.shape, jnp.bfloat16), (cot.shape, f32)] + [(in_w.shape, f32)] * 3 + [(out_w.shape, f32)] * 3
    return pl.pallas_call(
        finish_kernel,
        grid=(STEPS,),
        in_specs=[full_spec(a.shape) for a in (lens, all_gate, all_x, sum_com)]
        + [positions() for unused in range(4)]
        + [pl.BlockSpec((PLANES, out_rows, D), lambda s: (0, s, 0))]
        + [in_block() for unused in range(3)]
        + [out_block() for unused in range(3)],
        out_specs=[positions(), positions()]
        + [in_block() for unused in range(3)]
        + [out_block() for unused in range(3)],
        out_shape=[jax.ShapeDtypeStruct(s, kind) for s, kind in shapes],
        compiler_params=pltpu.CompilerParams(vmem_limit_bytes=VMEM_GRANT),
    )(lens, all_gate, all_x, sum_com, tok, cot, sum_branch, grad_rows, r_out, *weights)


def rank_join(array):
    rows = array.shape[1]
    split = array.reshape(QUADS, 2, rows, 2, RUN)
    return split.transpose(2, 1, 3, 0, 4).reshape(rows, DIN)


def per_device_quad(
    tokens_in,
    cotangent,
    seq_lens,
    in_weight,
    in_first,
    in_second,
    out_weight,
    out_first,
    out_second,
    conv_weight,
    conv_first,
    conv_second,
    gains,
    gain_first,
    gain_second,
    head_params,
    head_first,
    head_second,
):
    plane, quad, core = place()
    rank = 2 * quad + core
    (
        normed, cot, w_gate, w_x, w_com, w_out, gate_part, proj_x, proj_com, act, mixed, grad_normed_out,
        stats, gain_in, gain_out, conv, heads, skip, select, lens
    ) = run_fore(tokens_in, cotangent, seq_lens, in_weight, out_weight, conv_weight, gains, head_params)
    branch, dgate, dmix, g_out, g_gate, g_gain = run_gate(
        lens, stats, cot, normed, gate_part, mixed, grad_normed_out, w_out, gain_out
    )
    r_out, all_gate, all_x, sum_com, packs, sum_branch, grad_rows = run_back(
        lens, g_gate, g_out, branch, w_gate, w_x, w_com, conv, heads, skip, select, gain_in, g_gain,
        tokens_in, normed, dgate, dmix, proj_x, proj_com, act
    )
    finished = run_finish(
        lens, tokens_in, cotangent, sum_branch, grad_rows, r_out, all_gate, all_x, sum_com,
        in_weight, in_first, in_second, out_weight, out_first, out_second
    )
    mine = rank + RANKS * plane
    grad_gains = jnp.concatenate(
        [jnp.sum(packs[:, :12], axis=0).reshape(D), rank_join(packs[:, 12:15].reshape(RANKS, 1, OWN)).reshape(DIN)]
    )
    gain_sum = lax.dynamic_slice(grad_gains, (mine * gains.shape[0],), gains.shape)
    grad_conv = jnp.concatenate(
        [
            rank_join(packs[:, 15:30].reshape(RANKS, KCONV + 1, OWN)),
            jnp.sum(packs[:, 30:40], axis=0).reshape(KCONV + 1, 2 * NST),
        ],
        axis=1,
    )
    conv_sum = lax.dynamic_slice(grad_conv, (0, mine * conv_weight.shape[1]), conv_weight.shape)
    grad_skip = jnp.sum(packs[:, 42:45].reshape(RANKS, 1, OWN_HEADS, HDIM), axis=3)
    head_sum = jnp.concatenate([packs[:, 40:42, :OWN_HEADS], grad_skip], axis=1)
    head_sum = head_sum.reshape(QUADS, 2, 3, 2, 3).transpose(2, 1, 3, 0, 4).reshape(3, HEADS)
    new_conv = adam_update(conv_weight, conv_first, conv_second, conv_sum, rate_conv)
    new_gain = adam_update(gains, gain_first, gain_second, gain_sum, rate_gain)
    new_head = adam_update(head_params, head_first, head_second, head_sum, rate_head)
    return tuple(finished) + new_conv + new_gain + new_head


def solution(mesh):
    placed = (
        P(("dp", "seq"), None),
        P(("dp", "seq"), None),
        P("dp", None),
        P(("dp", "seq"), None),
        P(("dp", "seq"), None),
        P(("dp", "seq"), None),
        P(("dp", "seq"), None),
        P(("dp", "seq"), None),
        P(("dp", "seq"), None),
        P(None, ("dp", "seq")),
        P(None, ("dp", "seq")),
        P(None, ("dp", "seq")),
        P(("dp", "seq")),
        P(("dp", "seq")),
        P(("dp", "seq")),
        P(),
        P(),
        P(),
    )
    quad = dict(mesh.shape) == {"dp": PLANES * QUADS, "seq": 2}
    return jax.shard_map(
        per_device_quad if quad else per_device,
        mesh=mesh,
        in_specs=placed,
        out_specs=(
            P(("dp", "seq"), None),
            P(("dp", "seq"), None),
            P(("dp", "seq"), None),
            P(("dp", "seq"), None),
            P(("dp", "seq"), None),
            P(("dp", "seq"), None),
            P(("dp", "seq"), None),
            P(("dp", "seq"), None),
            P(None, ("dp", "seq")),
            P(None, ("dp", "seq")),
            P(None, ("dp", "seq")),
            P(("dp", "seq")),
            P(("dp", "seq")),
            P(("dp", "seq")),
            P(),
            P(),
            P(),
        ),
        check_vma=False,
    )
```
